32 devices in a mesh: gx: 2 (over y), gy: 4 (over z), gz: 4 (over x, core).
Axes of the slice: x: 2, y: 2, z: 4, core: 2. Of those that a mesh axis runs over, the one named last changes fastest.
Arguments:
- divergence: float32 [64, 32, 512], P('gz', 'gx', 'gy'), may hold values from -6 to 6
- pressure_prev: float32 [64, 32, 512], P('gz', 'gx', 'gy'), may hold values from -6 to 6
Outputs:
- pressure: float32 [64, 32, 512], P('gz', 'gx', 'gy')
- residual: float32 [64, 32, 512], P('gz', 'gx', 'gy')
- coarse_correction: float32 [2, 1, 16], replicated
The draws below stay inside these ranges and needn't reach their ends.
All inputs are finite; a program needn't handle non-finite values.
Results may differ from the reference program's by a relative error of at most 0.0004.
Values sent between devices are 32-bit elements; how exact they have to be, the bound alone decides.
No kernel may reach another device: no remote copies, remote signals or barrier semaphores. Data moves between devices by JAX's collectives and lax.ppermute only.
A program may use at most 64 MiB of HBM per device.

```python
import jax
import jax.numpy as jnp

LEVELS = 6
NX = 32
NY = 512
NZ = 64


def draw_divergence(key, part):
    key = jax.random.fold_in(key, 3)
    first_key = jax.random.fold_in(key, 0)
    return jax.random.truncated_normal(first_key, -6.0, 6.0, (NZ, NX, NY), jnp.float32)


def level_of(rng, shape, shards, smallest, high):
    def one(position, shards_of):
        steps = jax.random.uniform(jax.random.fold_in(jax.random.fold_in(rng, 6), position), (shards_of,), jnp.float32, smallest / len(shards), high / len(shards))
        return jnp.repeat(jnp.exp(steps), shape[position] // shards_of).reshape((-1,) + (1,) * (len(shape) - position - 1))

    gain = one(*shards[0])
    for cut in shards[1:]:
        gain = gain * one(*cut)
    return gain


def bell_draw(key, shape, deviation, bound, cuts=(), kind=jnp.bfloat16):
    entries = deviation * jax.random.normal(key, shape, jnp.float32)
    if cuts:
        entries = entries * level_of(key, shape, cuts, -0.22, 0.18)
    return jnp.clip(entries, -bound, bound).astype(kind)


def setup_inputs(seed: int = 0) -> dict:
    seeds = jax.random.split(jax.random.key(seed), 3)
    return {
        "divergence": draw_divergence(jax.random.fold_in(seeds[2], 71), 0),
        "pressure_prev": bell_draw(seeds[1], (NZ, NX, NY), 1.0, 6.0, ((0, 4), (1, 2), (2, 4)), jnp.float32),
    }


first_scale = 1.0 / 7.5
rho_one = 1.0 / (2.0 * (5.0 / 3.0) - 0.6)
carry_coef = 0.6 * rho_one
fresh_coef = 2.0 * rho_one / (0.75 * 6.0)


def stencil(values):
    padded = jnp.pad(values, 1)
    beside = padded[2:, 1:-1, 1:-1] + padded[:-2, 1:-1, 1:-1]
    beside = beside + padded[1:-1, 2:, 1:-1] + padded[1:-1, :-2, 1:-1]
    beside = beside + padded[1:-1, 1:-1, 2:] + padded[1:-1, 1:-1, :-2]
    return 6.0 * values - beside


def smooth_pass(iterate, source, apply_op, from_zero):
    residue = source if from_zero else source - apply_op(iterate)
    update = residue * first_scale
    iterate = update if from_zero else iterate + update
    residue = source - apply_op(iterate)
    update = carry_coef * update + fresh_coef * residue
    return iterate + update


def restrict(values):
    shape_a, shape_b, shape_c = values.shape
    blocks = values.reshape(shape_a // 2, 2, shape_b // 2, 2, shape_c // 2, 2)
    return 0.5 * jnp.sum(blocks, axis=(1, 3, 5))


def prolong(values):
    shape_a, shape_b, shape_c = values.shape
    spread = jnp.broadcast_to(values[:, None, :, None, :, None], (shape_a, 2, shape_b, 2, shape_c, 2))
    return spread.reshape(2 * shape_a, 2 * shape_b, 2 * shape_c)


def vcycle(level_num, iterate, source, from_zero):
    iterate = smooth_pass(iterate, source, stencil, from_zero)
    coarsest = None
    if level_num < LEVELS - 1:
        residue = source - stencil(iterate)
        coarse, coarsest = vcycle(level_num + 1, None, restrict(residue), True)
        iterate = iterate + prolong(coarse)
    result = smooth_pass(iterate, source, stencil, False)
    if level_num == LEVELS - 1:
        coarsest = result
    return result, coarsest


def reference(divergence, pressure_prev):
    pressure, coarse_correction = vcycle(0, pressure_prev, divergence, False)
    residual = divergence - stencil(pressure)
    return (pressure, residual, coarse_correction)
```

```python
import jax
import jax.numpy as jnp
from jax import lax
from jax.sharding import PartitionSpec as P

LEVELS = 6


first_scale = 1.0 / 7.5
rho_one = 1.0 / (2.0 * (5.0 / 3.0) - 0.6)
carry_coef = 0.6 * rho_one
fresh_coef = 2.0 * rho_one / (0.75 * 6.0)

AXES = (("gz", 0), ("gx", 1), ("gy", 2))


def extended(x, width):
    for axis, dim in AXES:
        peers, length = (lax.axis_size(axis), x.shape[dim + 1])
        up = [(i, (i + 1) % peers) for i in range(peers - 1)]
        down = [(j, i) for i, j in up]
        last = lax.slice_in_dim(x, length - width, length, axis=dim + 1)
        first = lax.slice_in_dim(x, 0, width, axis=dim + 1)
        before = lax.ppermute(last, axis, up)
        after = lax.ppermute(first, axis, down)
        x = jnp.concatenate([before, x, after], axis=dim + 1)
    return x


def stencil(values):
    padded = jnp.pad(values, 1)
    return valid_op(padded)


def valid_op(padded):
    beside = padded[2:, 1:-1, 1:-1] + padded[:-2, 1:-1, 1:-1]
    beside = beside + padded[1:-1, 2:, 1:-1] + padded[1:-1, :-2, 1:-1]
    beside = beside + padded[1:-1, 1:-1, 2:] + padded[1:-1, 1:-1, :-2]
    return 6.0 * padded[1:-1, 1:-1, 1:-1] - beside


def smooth_pass(iterate, source, apply_op, from_zero):
    residue = source if from_zero else source - apply_op(iterate)
    update = residue * first_scale
    iterate = update if from_zero else iterate + update
    residue = source - apply_op(iterate)
    update = carry_coef * update + fresh_coef * residue
    return iterate + update


def restrict(values):
    shape_a, shape_b, shape_c = values.shape
    blocks = values.reshape(shape_a // 2, 2, shape_b // 2, 2, shape_c // 2, 2)
    return 0.5 * jnp.sum(blocks, axis=(1, 3, 5))


def prolong(values):
    shape_a, shape_b, shape_c = values.shape
    spread = jnp.broadcast_to(
        values[:, None, :, None, :, None], (shape_a, 2, shape_b, 2, shape_c, 2)
    )
    return spread.reshape(2 * shape_a, 2 * shape_b, 2 * shape_c)


def vcycle(level_num, iterate, source):
    iterate = smooth_pass(iterate, source, stencil, True)
    coarsest = None
    if level_num < LEVELS - 1:
        residue = source - stencil(iterate)
        coarse, coarsest = vcycle(level_num + 1, None, restrict(residue))
        iterate = iterate + prolong(coarse)
    result = smooth_pass(iterate, source, stencil, False)
    if level_num == LEVELS - 1:
        coarsest = result
    return (result, coarsest)


def collect(values):
    gathered = lax.all_gather(values, "gz", axis=0, tiled=True)
    gathered = lax.all_gather(gathered, "gy", axis=2, tiled=True)
    return lax.all_gather(gathered, "gx", axis=1, tiled=True)


def local_stencil(values):
    return valid_op(extended(values[None], 1)[0])


def own_block(whole, block_shape):
    start_z = lax.axis_index("gz") * block_shape[0]
    start_x = lax.axis_index("gx") * block_shape[1]
    start_y = lax.axis_index("gy") * block_shape[2]
    return lax.dynamic_slice(whole, (start_z, start_x, start_y), block_shape)


def body_cycle(level_num, iterate, source, from_zero, gather_at):
    if level_num == gather_at:
        whole_source = collect(source)
        coarse, coarsest = vcycle(level_num, None, whole_source)
        return (own_block(coarse, source.shape), coarsest)
    iterate = smooth_pass(iterate, source, local_stencil, from_zero)
    residue = source - local_stencil(iterate)
    coarse, coarsest = body_cycle(level_num + 1, None, restrict(residue), True, gather_at)
    iterate = iterate + prolong(coarse)
    return (smooth_pass(iterate, source, local_stencil, False), coarsest)


def body_levels(divergence, pressure_prev):
    pressure, coarse_correction = body_cycle(0, pressure_prev, divergence, False, 3)
    residual = divergence - local_stencil(pressure)
    return (pressure, residual, coarse_correction)


def crop(x, n):
    return x[n:-n, n:-n, n:-n]


def body_wide(divergence, pressure_prev):
    block = divergence.shape
    wide = 5
    both = extended(jnp.stack([pressure_prev, divergence]), wide)
    x, b = both[0], both[1]

    def inside(width):
        keep = None
        for axis, dim in AXES:
            at = lax.broadcasted_iota(jnp.int32, tuple(n + 2 * width for n in block), dim) - width
            at = at + lax.axis_index(axis) * block[dim]
            good = (at >= 0) & (at < lax.axis_size(axis) * block[dim])
            keep = good if keep is None else keep & good
        return keep

    def masked(values, width):
        return jnp.where(inside(width), values, 0.0)

    r = crop(b, 1) - valid_op(x)
    d = masked(r * first_scale, 4)
    r = crop(r, 1) - valid_op(d)
    d2 = masked(carry_coef * crop(d, 1) + fresh_coef * r, 3)
    r = crop(r, 1) - valid_op(d2)
    x = pressure_prev + crop(d, 4) + crop(d2, 3)
    coarse_source = collect(restrict(crop(r, 2)))
    coarse, coarsest = vcycle(1, None, coarse_source)
    half = tuple(n // 2 for n in block)
    starts = tuple(lax.axis_index(axis) * half[dim] for axis, dim in AXES)
    local = lax.dynamic_slice(jnp.pad(coarse, 2), starts, tuple(n + 4 for n in half))
    e = prolong(local)
    r = r - valid_op(crop(e, 1))
    x = x + crop(e, 4)
    d = masked(r * first_scale, 2)
    r = crop(r, 1) - valid_op(d)
    d2 = masked(carry_coef * crop(d, 1) + fresh_coef * r, 1)
    r = crop(r, 1) - valid_op(d2)
    return (x + crop(d, 2) + crop(d2, 1), r, coarsest)


WHOLE_CELLS = 1 << 18


def body(divergence, pressure_prev):
    cells = lax.axis_size("gz") * lax.axis_size("gx") * lax.axis_size("gy") * divergence.size // 8
    if cells <= WHOLE_CELLS and min(divergence.shape) > 5:
        return body_wide(divergence, pressure_prev)
    return body_levels(divergence, pressure_prev)


def solution(mesh):
    in_specs = (P("gz", "gx", "gy"), P("gz", "gx", "gy"))
    out_specs = (P("gz", "gx", "gy"), P("gz", "gx", "gy"), P())
    return jax.shard_map(body, mesh=mesh, in_specs=in_specs, out_specs=out_specs, check_vma=False)
```

```python
import jax
import jax.numpy as jnp
from jax import lax
from jax.experimental import pallas as pl
from jax.experimental.pallas import tpu as pltpu
from jax.sharding import PartitionSpec as P

LEVELS = 6


first_scale = 1.0 / 7.5
rho_one = 1.0 / (2.0 * (5.0 / 3.0) - 0.6)
carry_coef = 0.6 * rho_one
fresh_coef = 2.0 * rho_one / (0.75 * 6.0)

LANES = 128
F32 = jnp.float32
AXES = (("gz", 0), ("gx", 1), ("gy", 2))


def extended(x, width):
    for axis, dim in AXES:
        peers, length = (lax.axis_size(axis), x.shape[dim + 1])
        up = [(i, (i + 1) % peers) for i in range(peers - 1)]
        down = [(j, i) for i, j in up]
        last = lax.slice_in_dim(x, length - width, length, axis=dim + 1)
        first = lax.slice_in_dim(x, 0, width, axis=dim + 1)
        before = lax.ppermute(last, axis, up)
        after = lax.ppermute(first, axis, down)
        x = jnp.concatenate([before, x, after], axis=dim + 1)
    return x


def stencil(values):
    padded = jnp.pad(values, 1)
    return valid_op(padded)


def valid_op(padded):
    beside = padded[2:, 1:-1, 1:-1] + padded[:-2, 1:-1, 1:-1]
    beside = beside + padded[1:-1, 2:, 1:-1] + padded[1:-1, :-2, 1:-1]
    beside = beside + padded[1:-1, 1:-1, 2:] + padded[1:-1, 1:-1, :-2]
    return 6.0 * padded[1:-1, 1:-1, 1:-1] - beside


def smooth_pass(iterate, source, apply_op, from_zero):
    residue = source if from_zero else source - apply_op(iterate)
    update = residue * first_scale
    iterate = update if from_zero else iterate + update
    residue = source - apply_op(iterate)
    update = carry_coef * update + fresh_coef * residue
    return iterate + update


def restrict(values):
    shape_a, shape_b, shape_c = values.shape
    blocks = values.reshape(shape_a // 2, 2, shape_b // 2, 2, shape_c // 2, 2)
    return 0.5 * jnp.sum(blocks, axis=(1, 3, 5))


def prolong(values):
    shape_a, shape_b, shape_c = values.shape
    spread = jnp.broadcast_to(
        values[:, None, :, None, :, None], (shape_a, 2, shape_b, 2, shape_c, 2)
    )
    return spread.reshape(2 * shape_a, 2 * shape_b, 2 * shape_c)


def vcycle(level_num, iterate, source):
    iterate = smooth_pass(iterate, source, stencil, True)
    coarsest = None
    if level_num < LEVELS - 1:
        residue = source - stencil(iterate)
        coarse, coarsest = vcycle(level_num + 1, None, restrict(residue))
        iterate = iterate + prolong(coarse)
    result = smooth_pass(iterate, source, stencil, False)
    if level_num == LEVELS - 1:
        coarsest = result
    return (result, coarsest)


def collect(values):
    gathered = lax.all_gather(values, "gz", axis=0, tiled=True)
    gathered = lax.all_gather(gathered, "gy", axis=2, tiled=True)
    return lax.all_gather(gathered, "gx", axis=1, tiled=True)


def local_stencil(values):
    return valid_op(extended(values[None], 1)[0])


def own_block(whole, block_shape):
    start_z = lax.axis_index("gz") * block_shape[0]
    start_x = lax.axis_index("gx") * block_shape[1]
    start_y = lax.axis_index("gy") * block_shape[2]
    return lax.dynamic_slice(whole, (start_z, start_x, start_y), block_shape)


def body_cycle(level_num, iterate, source, from_zero, gather_at):
    if level_num == gather_at:
        whole_source = collect(source)
        coarse, coarsest = vcycle(level_num, None, whole_source)
        return (own_block(coarse, source.shape), coarsest)
    iterate = smooth_pass(iterate, source, local_stencil, from_zero)
    residue = source - local_stencil(iterate)
    coarse, coarsest = body_cycle(level_num + 1, None, restrict(residue), True, gather_at)
    iterate = iterate + prolong(coarse)
    return (smooth_pass(iterate, source, local_stencil, False), coarsest)


def body_levels(divergence, pressure_prev):
    pressure, coarse_correction = body_cycle(0, pressure_prev, divergence, False, 3)
    residual = divergence - local_stencil(pressure)
    return (pressure, residual, coarse_correction)


def iota(shape, dim):
    return lax.broadcasted_iota(jnp.int32, shape, dim)


def signed(index, size, extent):
    return jnp.where(index >= (size + extent) // 2, index - extent, index)


def split(values):
    terms = []
    for _ in range(3):
        term = values.astype(jnp.bfloat16)
        terms.append(term)
        values = values - term.astype(F32)
    return terms


def right_dot(values, table):
    parts = [jnp.dot(t, table, preferred_element_type=F32) for t in split(values)]
    return parts[0] + parts[1] + parts[2]


def left_dot(table, values):
    parts = [jnp.dot(table, t, preferred_element_type=F32) for t in split(values)]
    return parts[0] + parts[1] + parts[2]


def as_table(keep, value=1.0):
    return jnp.where(keep, value, 0.0).astype(jnp.bfloat16)


def lateral(v):
    rows, lanes = v.shape
    return (
        pltpu.roll(v, 1, 0) + pltpu.roll(v, rows - 1, 0)
        + pltpu.roll(v, 1, 1) + pltpu.roll(v, lanes - 1, 1)
    )


def apply_at(ref, k, lateral_of=lateral):
    centre = ref[k]
    beside = lateral_of(centre)
    if k > 0:
        beside = beside + ref[k - 1]
    if k < ref.shape[0] - 1:
        beside = beside + ref[k + 1]
    return 6.0 * centre - beside


def wrapped_mask(shape, sizes, low, high):
    keep = None
    for dim, size in sizes.items():
        at = signed(iota(shape, dim), size, shape[dim])
        good = ((at >= 0) | low[dim]) & ((at < size) | high[dim])
        keep = good if keep is None else keep & good
    return jnp.where(keep, 1.0, 0.0).astype(F32)


def side(index, step):
    low_bits = (1 << step) - 1
    above = ((index >> step) & 1) == 0
    near = jnp.where(above, (index & low_bits) == low_bits, (index & low_bits) == 0)
    return above, near


def place(axis, count):
    index = lax.axis_index(axis)
    return index, index > 0, index < count - 1


def first_kernel(peers, steps, b_ref, p_ref, r_ref, x_ref, coarse_ref, *rest):
    slabs, (b_ext, p_ext, d_one, d_two, pairs, lines) = rest[:steps], rest[steps:]
    bz, bx, by = b_ref.shape
    ez, ex, ey = r_ref.shape
    iz, z_low, z_high = place("gz", peers[0])
    _, x_low, x_high = place("gx", peers[1])
    _, y_low, y_high = place("gy", peers[2])
    flat = wrapped_mask((ex, ey), {0: bx, 1: by}, (x_low, y_low), (x_high, y_high))
    below = jnp.where(z_low, 1.0, 0.0).astype(F32)
    above = jnp.where(z_high, 1.0, 0.0).astype(F32)

    def masked(k, v):
        v = v * flat
        if k < 3:
            v = v * below
        if k >= 3 + bz:
            v = v * above
        return v

    zero = jnp.zeros((ex, ey), F32)
    for k in range(ez):
        p_ext[k] = zero
        b_ext[k] = zero
        if 3 <= k < 3 + bz:
            b_ext[k, 0:bx, 0:by] = b_ref[k - 3]
            p_ext[k, 0:bx, 0:by] = p_ref[k - 3]
    for k in range(ez):
        if 2 <= k < ez - 2:
            r = b_ext[k] - apply_at(p_ext, k)
            r_ref[k] = r
            d_one[k] = masked(k, r * first_scale)
        else:
            d_one[k] = zero
    for k in range(ez):
        if 1 <= k < ez - 1:
            r = -apply_at(d_one, k)
            if 2 <= k < ez - 2:
                r = r + r_ref[k]
            r_ref[k] = r
            d_two[k] = masked(k, carry_coef * d_one[k] + fresh_coef * r)
        else:
            d_two[k] = zero
    for k in range(ez):
        r = -apply_at(d_two, k)
        if 1 <= k < ez - 1:
            r = r + r_ref[k]
        r_ref[k] = masked(k, r)
        x_ref[k] = p_ext[k] + d_one[k] + d_two[k]

    for step, out in enumerate(slabs):
        up, _ = side(iz, step)
        start = jnp.where(up, ez - 5, 0)
        start_x = jnp.where(up, ez - 3, 1)
        for j in range(5):
            out[j * ex:(j + 1) * ex, :] = r_ref[start + j]
        for j in range(2):
            out[(5 + j) * ex:(6 + j) * ex, :] = x_ref[start_x + j]

    coarse_z, rows, lanes = bz // 2 + 4, bx // 2, coarse_ref.shape[1] // 2
    half = coarse_z // 2
    for zc in range(coarse_z):
        low, high = 2 * zc - 1, 2 * zc
        if low < 0:
            total = r_ref[high]
        elif high >= ez:
            total = r_ref[low]
        else:
            total = r_ref[low] + r_ref[high]
        base = zc * ex
        for tile in range(ey // LANES):
            here = slice(tile * LANES, (tile + 1) * LANES)
            pairs[tile, base:base + ex, :] = total[:, here]
            even = pairs.at[tile][pl.ds(base, ex // 2, 2), :]
            odd = pairs.at[tile][pl.ds(base + 1, ex // 2, 2), :]
            sums = even + odd
            at = zc // 2 * rows
            lines[zc % 2, at:at + rows, here] = sums[0:rows]
            at = half * rows + zc // 2 * 4
            lines[zc % 2, at:at + 4, here] = sums[rows:rows + 4]
    fine = signed(iota((ey, lanes), 0), by, ey)
    coarse = signed(iota((ey, lanes), 1), by // 2, lanes)
    table = as_table((fine >> 1) == coarse, 0.5)
    for part in range(2):
        coarse_ref[:, part * lanes:(part + 1) * lanes] = right_dot(lines[part], table)


def z_kernel(peers, steps, *refs):
    r_in, x_in = refs[0:2]
    slabs = refs[2:2 + steps]
    r_ref, x_ref, slab_ref = refs[2 + steps:]
    ez, ex, ey = r_in.shape
    iz, _, _ = place("gz", peers[0])
    ix, _, _ = place("gx", peers[1])
    for k in range(r_ref.shape[0]):
        r_ref[k] = r_in[k + 1]
    for k in range(x_ref.shape[0]):
        x_ref[k] = x_in[k + 3]
    for step, slab in enumerate(slabs):
        up, near = side(iz, step)

        @pl.when(near)
        def _():
            start = jnp.where(up, r_ref.shape[0] - 5, 0)
            start_x = jnp.where(up, x_ref.shape[0] - 2, 0)
            for j in range(5):
                r_ref[start + j] += slab[j * ex:(j + 1) * ex, :]
            for j in range(2):
                x_ref[start_x + j] += slab[(5 + j) * ex:(6 + j) * ex, :]

    bx = ex - 8
    up = (ix & 1) == 0
    row = iota((8, ey), 0)
    for k in range(r_ref.shape[0]):
        first, last, spill = r_ref[k, 0:8], r_ref[k, bx - 8:bx], r_ref[k, bx:ex]
        to_high = pltpu.roll(jnp.where(row >= 6, last, spill), 2, 0)
        to_low = pltpu.roll(jnp.where(row >= 5, spill, first), 3, 0)
        out = jnp.where(up, to_high, to_low)
        if 2 <= k < 2 + x_ref.shape[0]:
            spill = x_ref[k - 2, bx:ex]
            extra = jnp.where(up, pltpu.roll(spill, 5, 0), pltpu.roll(spill, 7, 0))
            out = jnp.where((row == 5) | (row == 6), extra, out)
        slab_ref[8 * k:8 * k + 8, :] = out


def edge_lanes(low_tile, high_tile, first, count, slot):
    lane = iota(low_tile.shape, 1)
    at = first % LANES
    source = low_tile if first < LANES else high_tile
    after = high_tile if first < LANES else low_tile
    taken = jnp.where(lane >= at, source, after)
    keep = (lane - at) % LANES if at == 0 else jnp.where(lane >= at, lane - at, lane + LANES - at)
    taken = jnp.where(keep < count, taken, 0.0)
    return pltpu.roll(taken, (slot - at) % LANES, 1)


def one_tile_lanes(tile, first, count, slot):
    lane = iota(tile.shape, 1)
    at = first % LANES
    gone = jnp.where(lane >= at, lane - at, lane + LANES - at)
    return pltpu.roll(jnp.where(gone < count, tile, 0.0), (slot - at) % LANES, 1)


def y_kernel(peers, steps, r_in, x_in, mine, got, r_ref, x_ref, r1_ref, x1_ref, sum_ref, *rest):
    slabs = rest[:steps]
    b1, d1, d2, x_all, pairs, lines, edges = rest[steps:]
    layers, ex, ey = r_in.shape
    bx, by = ex - 8, ey - LANES
    ix, _, _ = place("gx", peers[1])
    iy, y_low, y_high = place("gy", peers[2])
    up = (ix & 1) == 0
    row = iota((8, ey), 0)
    own_z = x_in.shape[0]

    for k in range(layers):
        slab = got[8 * k:8 * k + 8, :]
        from_high = pltpu.roll(slab, 5, 0)
        from_low = pltpu.roll(slab, 6, 0)
        first, last, spill = r_in[k, 0:8], r_in[k, bx - 8:bx], r_in[k, bx:ex]
        if bx > 16:
            r_ref[k] = r_in[k]
        r_ref[k, 0:8] = first + jnp.where(up | (row >= 3), 0.0, from_low)
        r_ref[k, bx - 8:bx] = last + jnp.where(up & (row >= 5), from_high, 0.0)
        r_ref[k, bx:ex] = spill + jnp.where(
            up, jnp.where(row < 2, from_high, 0.0), jnp.where(row >= 6, from_low, 0.0)
        )
        if 2 <= k < 2 + own_z:
            j = k - 2
            if bx > 16:
                x_all[j] = x_in[j, 0:bx]
            x_all[j, 0:8] = x_in[j, 0:8] + jnp.where(up | (row >= 2), 0.0, pltpu.roll(slab, 3, 0))
            x_all[j, bx - 8:bx] = x_in[j, bx - 8:bx] + jnp.where(
                up & (row >= 6), pltpu.roll(slab, 1, 0), 0.0
            )
            x_ref[j] = x_all[j, :, 0:by]

    per_tile = LANES // 8
    groups = -(-layers // per_tile)
    tall = edges.shape[1]
    for which in range(2):
        for group in range(groups):
            total = jnp.zeros((ex, LANES), F32)
            total_x = jnp.zeros((bx, LANES), F32)
            for k in range(group * per_tile, min(layers, (group + 1) * per_tile)):
                slot = 8 * (k % per_tile)
                a, c = r_ref[k, :, by - LANES:by], r_ref[k, :, by:ey]
                if which == 0:
                    total = total + edge_lanes(a, c, LANES - 2, 5, slot)
                else:
                    total = total + edge_lanes(r_ref[k, :, 0:LANES], c, 2 * LANES - 3, 5, slot)
                if 2 <= k < 2 + own_z:
                    v = x_all[k - 2, :, by:ey]
                    total_x = total_x + one_tile_lanes(v, 0 if which == 0 else LANES - 2, 2, slot + 5)
            edges[which, group * ex:(group + 1) * ex, :] = total
            edges[which, group * ex:group * ex + bx, :] += total_x

    nz1, nx1, _ = b1.shape
    zp_rows = nz1 // 2 * nx1 // 2
    own_rows = nx1 // 2
    base = 8 * layers
    row = iota((own_rows, ey), 0)
    row8 = iota((8, ey), 0)
    for zp in range(nz1 // 2):
        at = base + zp * own_rows
        ours, theirs = mine[at - base:at - base + own_rows, :], got[at:at + own_rows, :]
        low, high = jnp.where(up, ours, theirs), jnp.where(up, theirs, ours)
        at = zp_rows + (zp // 2) * 8
        ours, theirs = mine[at:at + 8, :], got[base + at:base + at + 8, :]
        low_spill, high_spill = jnp.where(up, ours, theirs), jnp.where(up, theirs, ours)
        if zp % 2 == 0:
            high_spill = pltpu.roll(high_spill, 4, 0)
        else:
            low_spill = pltpu.roll(low_spill, 4, 0)
        low_add = jnp.where(row8 >= 6, high_spill, 0.0)
        high_add = jnp.where(row8 < 2, low_spill, 0.0)
        for part in range(2):
            lanes = slice(part * LANES, (part + 1) * LANES)
            b1[2 * zp + part, 0:own_rows, :] = low[:, lanes]
            b1[2 * zp + part, own_rows:nx1, :] = high[:, lanes]
            b1[2 * zp + part, own_rows - 8:own_rows, :] += low_add[:, lanes]
            b1[2 * zp + part, own_rows:own_rows + 8, :] += high_add[:, lanes]

    lateral1 = level_lateral((nx1, LANES))
    keep = wrapped_mask((nx1, LANES), {1: by // 2}, (None, y_low), (None, y_high))
    for k in range(nz1):
        d1[k] = b1[k] * first_scale
    for k in range(nz1):
        r = b1[k] - apply_at(d1, k, lateral1)
        r1_ref[k] = r
        d2[k] = keep * (carry_coef * d1[k] + fresh_coef * r)
    for k in range(nz1):
        r1_ref[k] = keep * (r1_ref[k] - apply_at(d2, k, lateral1))
        x1_ref[k] = d1[k] + d2[k]

    for zc in range(nz1 // 2):
        pairs[zc * nx1:(zc + 1) * nx1, :] = r1_ref[2 * zc] + r1_ref[2 * zc + 1]
        lines[zc * own_rows:(zc + 1) * own_rows, :] = (
            pairs[pl.ds(zc * nx1, own_rows, 2), :] + pairs[pl.ds(zc * nx1 + 1, own_rows, 2), :]
        )
    fine = signed(iota((LANES, LANES), 0), by // 2, LANES)
    coarse = iota((LANES, LANES), 1) - iy * (by // 4)
    sum_ref[...] = right_dot(lines[...], as_table((fine >> 1) == coarse, 0.5))

    fine_rows = groups * ex
    per_tile = LANES // 16
    for which in range(2):
        for group in range(nz1 // per_tile):
            total = jnp.zeros((nx1, LANES), F32)
            for j in range(per_tile):
                k = group * per_tile + j
                first = by // 2 - 3 if which == 0 else LANES - 4
                total = total + one_tile_lanes(r1_ref[k], first, 7, 16 * j)
                first = by // 2 - 2 if which == 0 else LANES - 3
                total = total + one_tile_lanes(x1_ref[k], first, 5, 16 * j + 7)
            at = fine_rows + group * nx1
            edges[which, at:at + nx1, :] = total
    for step, out in enumerate(slabs):
        above, _ = side(iy, step)
        out[...] = jnp.where(above, edges[0], edges[1])


def level_lateral(shape):
    row = iota(shape, 0)
    not_first = jnp.where(row > 0, 1.0, 0.0).astype(F32)
    not_last = jnp.where(row < shape[0] - 1, 1.0, 0.0).astype(F32)

    def beside(v):
        return (
            not_first * pltpu.roll(v, 1, 0) + not_last * pltpu.roll(v, shape[0] - 1, 0)
            + pltpu.roll(v, 1, 1) + pltpu.roll(v, LANES - 1, 1)
        )

    return beside


def small_cycle(level, source, sizes):
    nz, nx, ny = sizes
    rows = source.shape[0]
    row, lane = iota((rows, LANES), 0), iota((rows, LANES), 1)
    inside = (row < nz * nx) & (lane < ny)

    def factor(keep):
        return jnp.where(keep & inside, 1.0, 0.0).astype(F32)

    shifts = [(nx, 0, factor(row >= nx)), (rows - nx, 0, factor(row < (nz - 1) * nx))]
    if nx > 1:
        shifts += [(1, 0, factor(row % nx > 0)), (rows - 1, 0, factor(row % nx < nx - 1))]
    shifts += [(1, 1, factor(lane > 0)), (LANES - 1, 1, factor(lane < ny - 1))]

    def op(v):
        beside = None
        for shift, dim, keep in shifts:
            moved = keep * (v if shift % v.shape[dim] == 0 else pltpu.roll(v, shift, dim))
            beside = moved if beside is None else beside + moved
        return 6.0 * v - beside

    d = source * first_scale
    r = source - op(d)
    d2 = carry_coef * d + fresh_coef * r
    x = d + d2
    r = r - op(d2)
    coarsest = None
    if level < LEVELS - 1:
        half = tuple(max(n // 2, 1) for n in sizes)
        coarse_rows = max(half[0] * half[1], 8)
        shape = (coarse_rows, rows)
        fine, coarse = iota(shape, 1), iota(shape, 0)
        wanted = (fine // nx // 2) * half[1] + fine % nx // 2
        gather = (wanted == coarse) & (fine < nz * nx)
        fine, coarse = iota((LANES, LANES), 0), iota((LANES, LANES), 1)
        halve = as_table((fine // 2 == coarse) & (fine < ny), 0.5)
        shape = (rows, coarse_rows)
        fine, coarse = iota(shape, 0), iota(shape, 1)
        wanted = (fine // nx // 2) * half[1] + fine % nx // 2
        spread = as_table((wanted == coarse) & (fine < nz * nx))
        fine, coarse = iota((LANES, LANES), 1), iota((LANES, LANES), 0)
        double = as_table((fine // 2 == coarse) & (fine < ny))
        e, coarsest = small_cycle(
            level + 1, right_dot(left_dot(as_table(gather), r), halve), half
        )
        e = right_dot(left_dot(spread, e), double)
        x = x + e
        r = r - op(e)
    d = r * first_scale
    r = r - op(d)
    x = x + d + (carry_coef * d + fresh_coef * r)
    return x, (x if level == LEVELS - 1 else coarsest)


def last_kernel(peers, steps, sizes, r_in, x_in, r1_in, x1_in, *refs):
    slabs, (part_a, part_b) = refs[:steps], refs[steps:steps + 2]
    p_ref, res_ref, last_ref = refs[steps + 2:steps + 5]
    r, x, q1, e1, e0, d0, d1, r1, lines, wide = refs[steps + 5:]
    layers, ex, ey = r_in.shape
    nz1, nx1, _ = r1_in.shape
    bz, bx, by = p_ref.shape
    iz, z_low, z_high = place("gz", peers[0])
    ix, x_low, x_high = place("gx", peers[1])
    iy, y_low, y_high = place("gy", peers[2])

    def pick(wanted_above, rows):
        total = None
        for step, slab in enumerate(slabs):
            above, near = side(iy, step)
            good = near & (above if wanted_above else jnp.logical_not(above))
            term = jnp.where(good, slab[rows[0]:rows[1], :], 0.0)
            total = term if total is None else total + term
        return total

    e2, coarsest = small_cycle(2, part_a[...] + part_b[...], sizes)
    last_ref[...] = coarsest

    fine = signed(iota((LANES, LANES), 1), by // 2, LANES)
    coarse = iota((LANES, LANES), 0) - iy * (by // 4)
    e2 = right_dot(e2, as_table((fine >> 1) == coarse))
    half_x = nx1 // 2
    lines[...] = e2
    for zc in range(nz1 // 2):
        v = lines[zc * half_x:(zc + 1) * half_x, :]
        for part in range(2):
            q1.at[2 * zc + part][pl.ds(0, half_x, 2), :] = v
            q1.at[2 * zc + part][pl.ds(1, half_x, 2), :] = v
    fine_rows = -(-layers // (LANES // 8)) * ex
    per_tile = LANES // 16
    lane = iota((nx1, LANES), 1)

    def landed(v, slot, at, count):
        gone = jnp.where(lane_of(v) >= at, lane_of(v) - at, lane_of(v) + LANES - at)
        return jnp.where(gone < count, pltpu.roll(v, (at - slot) % LANES, 1), 0.0)

    def lane_of(v):
        return iota(v.shape, 1)

    lateral1 = level_lateral((nx1, LANES))
    keep = wrapped_mask((nx1, LANES), {1: by // 2}, (None, y_low), (None, y_high))
    for group in range(nz1 // per_tile):
        at = fine_rows + group * nx1
        high, low = pick(True, (at, at + nx1)), pick(False, (at, at + nx1))
        for j in range(per_tile):
            k = group * per_tile + j
            s = 16 * j
            r1[k] = (
                r1_in[k] + landed(high, s, by // 2 - 4, 7) + landed(low, s, LANES - 3, 7)
                - apply_at(q1, k, lateral1)
            )
            e1[k + 2, 8:8 + nx1, :] = (
                x1_in[k] + q1[k]
                + landed(high, s + 7, by // 2 - 3, 5) + landed(low, s + 7, LANES - 2, 5)
            )
    for k in range(nz1):
        d1[k] = keep * (r1[k] * first_scale)
    nothing = jnp.zeros((8, LANES), F32)
    for k in range(nz1 + 4):
        e1[k, 0:8, :] = nothing
        e1[k, 8 + nx1:16 + nx1, :] = nothing
        if not 2 <= k < nz1 + 2:
            e1[k, 8:8 + nx1, :] = jnp.zeros((nx1, LANES), F32)
    for k in range(nz1):
        v = r1[k] - apply_at(d1, k, lateral1)
        e1[k + 2, 8:8 + nx1, :] += d1[k] + keep * (carry_coef * d1[k] + fresh_coef * v)

    coarse = signed(iota((LANES, ey), 0), by // 2, LANES)
    fine = signed(iota((LANES, ey), 1), by, ey)
    double = as_table((fine >> 1) == coarse)
    half_z, half_x = bz // 2, bx // 2
    for zc in range(half_z + 4):
        start = pl.multiple_of(ix * half_x, 8)
        v = e1[iz * half_z + zc, pl.ds(start, half_x + 16), :]
        own, low, high = v[8:8 + half_x], v[0:8], v[8 + half_x:16 + half_x]
        at = zc * ex
        wide[pl.ds(at, half_x, 2), :] = own
        wide[pl.ds(at + 1, half_x, 2), :] = own
        for j in range(2):
            for twin in range(2):
                row = at + bx + 2 * j + twin
                wide[row:row + 1, :] = high[j:j + 1]
                row = at + ex - 4 + 2 * j + twin
                wide[row:row + 1, :] = low[6 + j:7 + j]
    for zc in range(half_z + 4):
        v = right_dot(wide[zc * ex:(zc + 1) * ex, :], double)
        for k in (2 * zc - 1, 2 * zc):
            if 0 <= k < bz + 6:
                e0[k] = v
    flat = wrapped_mask((ex, ey), {0: bx, 1: by}, (x_low, y_low), (x_high, y_high))
    below = jnp.where(z_low, 1.0, 0.0).astype(F32)
    above = jnp.where(z_high, 1.0, 0.0).astype(F32)

    def masked(k, v):
        v = v * flat
        if k < 3:
            v = v * below
        if k >= 3 + bz:
            v = v * above
        return v

    per_tile = LANES // 8
    for group in range(-(-layers // per_tile)):
        rows = (group * ex, (group + 1) * ex)
        high, low = pick(True, rows), pick(False, rows)
        for k in range(group * per_tile, min(layers, (group + 1) * per_tile)):
            s = 8 * (k % per_tile)
            v = r_in[k] - apply_at(e0, k + 1)
            own, spill = v[:, by - LANES:by], v[:, by:ey]
            own = own + landed(high, s, LANES - 3, 3)
            spill = spill + landed(high, s + 3, 0, 2) + landed(low, s, LANES - 2, 2)
            if by > LANES:
                r[k, :, 0:by - LANES] = v[:, 0:by - LANES]
                r[k, :, by - LANES:by] = own
                r[k, :, 0:LANES] += landed(low, s + 2, 0, 3)
            else:
                r[k, :, 0:LANES] = own + landed(low, s + 2, 0, 3)
            r[k, :, by:ey] = spill
            d0[k] = masked(k + 1, r[k] * first_scale)
            if 2 <= k < 2 + bz:
                x[k - 2] = x_in[k - 2] + e0[k + 1, 0:bx, 0:by]
                x[k - 2, :, by - LANES:by] += landed(high, s + 5, LANES - 2, 2)[0:bx]
                x[k - 2, :, 0:LANES] += landed(low, s + 5, 0, 2)[0:bx]
    for k in range(1, layers - 1):
        v = r[k] - apply_at(d0, k)
        r[k] = v
        e0[k] = masked(k + 1, carry_coef * d0[k] + fresh_coef * v)
    for k in range(2, layers - 2):
        p_ref[k - 2] = x[k - 2] + (d0[k, 0:bx, 0:by] + e0[k, 0:bx, 0:by])
        v = r[k] - apply_at(e0, k)
        res_ref[k - 2] = v[0:bx, 0:by]


def whole(shape, dtype=F32):
    return jax.ShapeDtypeStruct(shape, dtype)


def run(kernel, outs, scratch, *operands):
    return pl.pallas_call(
        kernel,
        out_shape=[whole(s) for s in outs],
        in_specs=[pl.BlockSpec(memory_space=pltpu.VMEM)] * len(operands),
        out_specs=[pl.BlockSpec(memory_space=pltpu.VMEM)] * len(outs),
        scratch_shapes=[pltpu.VMEM(s, F32) for s in scratch],
        compiler_params=pltpu.CompilerParams(vmem_limit_bytes=VMEM_BYTES),
    )(*operands)


def swap(values, axis, step):
    count = lax.axis_size(axis)
    flip = (2 << step) - 1
    return lax.ppermute(values, axis, [(i, i ^ flip) for i in range(count)])


def join_z(mine, got, index, step, half, rows):
    above, _ = side(index, step)
    out = []
    at = 0
    for width in (rows, 4):
        a, b = mine[at:at + half * width], got[at:at + half * width]
        low, high = jnp.where(above, a, b), jnp.where(above, b, a)
        meet = 2 * width
        out += [low[:-meet], low[-meet:] + high[:meet], high[meet:]]
        at += half * width
    return jnp.concatenate(out, axis=0)


def body_fast(divergence, pressure_prev):
    bz, bx, by = divergence.shape
    peers = tuple(lax.axis_size(a) for a in ("gz", "gx", "gy"))
    nz, nx, ny = peers
    steps_z, steps_y = nz.bit_length() - 1, ny.bit_length() - 1
    ez, ex, ey = bz + 6, bx + 8, by + LANES
    rows, half = bx // 2, bz // 4 + 2
    ext, slab = (ez, ex, ey), (7 * ex, ey)
    coarse_rows = half * (rows + 4)
    r, x, coarse, *slabs = run(
        lambda *refs: first_kernel(peers, steps_z, *refs),
        [ext, ext, (coarse_rows, 2 * LANES)] + [slab] * steps_z,
        [ext, ext, ext, ext, (ey // LANES, (bz // 2 + 4) * ex, LANES),
         (2, coarse_rows, ey)],
        divergence, pressure_prev,
    )
    got = []
    iz = lax.axis_index("gz")
    for step in range(steps_z):
        there = swap(jnp.concatenate([slabs[step], coarse], axis=0), "gz", step)
        got.append(there[:7 * ex])
        coarse = join_z(coarse, there[7 * ex:], iz, step, half, rows)
        half = 2 * half - 2
    inner = half - 2
    coarse = jnp.concatenate(
        [coarse[rows:half * rows - rows], coarse[half * rows + 4:half * (rows + 4) - 4]], axis=0
    )
    layers = bz + 4
    r, x, slab_x = run(
        lambda *refs: z_kernel(peers, steps_z, *refs),
        [(layers, ex, ey), (bz, ex, ey), (layers * 8, ey)],
        [],
        r, x, *got,
    )
    there = swap(jnp.concatenate([slab_x, coarse], axis=0), "gx", 0)
    nz1, nx1 = nz * bz // 2, nx * bx // 2
    level1 = (nz1, nx1, LANES)
    edge_rows = -(-layers // (LANES // 8)) * ex + nz1 // (LANES // 16) * nx1
    level2_rows = nz1 // 2 * nx1 // 2
    r, x, r1, x1, total, *slabs = run(
        lambda *refs: y_kernel(peers, steps_y, *refs),
        [(layers, ex, ey), (bz, bx, by), level1, level1, (level2_rows, LANES)]
        + [(edge_rows, LANES)] * steps_y,
        [level1, level1, level1, (bz, bx, ey), (nz1 // 2 * nx1, LANES), (level2_rows, LANES),
         (2, edge_rows, LANES)],
        r, x, coarse, there,
    )
    got = []
    other = None
    for step in range(steps_y):
        if other is not None:
            total = total + other
        there = swap(jnp.concatenate([slabs[step], total], axis=0), "gy", step)
        got.append(there[:edge_rows])
        other = there[edge_rows:]
    sizes = (nz1 // 2, nx1 // 2, ny * by // 4)
    pressure, residual, last = run(
        lambda *refs: last_kernel(peers, steps_y, sizes, *refs),
        [divergence.shape, divergence.shape, (8, LANES)],
        [(layers, ex, ey), divergence.shape, level1, (nz1 + 4, nx1 + 16, LANES), ext,
         (layers, ex, ey), level1, level1, (level2_rows, LANES), ((bz // 2 + 4) * ex, LANES)],
        r, x, r1, x1, *got, total, other,
    )
    z5, x5, y5 = (n >> 3 for n in sizes)
    coarsest = last[:z5 * x5, :y5].reshape(z5, x5, y5)
    return pressure, residual, coarsest


VMEM_BYTES = 24 << 20


def fits_fast(shape, peers):
    bz, bx, by = shape
    nz, nx, ny = peers
    return (
        nx == 2 and nz > 1 and ny > 1 and not (nz & (nz - 1) or ny & (ny - 1))
        and bz % 16 == 0 and bx == 16 and by == LANES and ny * by // 4 <= LANES
        and nz * bz <= 128
    )


def body(divergence, pressure_prev):
    peers = tuple(lax.axis_size(a) for a in ("gz", "gx", "gy"))
    if fits_fast(divergence.shape, peers):
        return body_fast(divergence, pressure_prev)
    return body_levels(divergence, pressure_prev)


def solution(mesh):
    in_specs = (P("gz", "gx", "gy"), P("gz", "gx", "gy"))
    out_specs = (P("gz", "gx", "gy"), P("gz", "gx", "gy"), P())
    return jax.shard_map(body, mesh=mesh, in_specs=in_specs, out_specs=out_specs, check_vma=False)
```

```python
import functools

import jax
import jax.numpy as jnp
from jax import lax
from jax.experimental import pallas as pl
from jax.experimental.pallas import tpu as pltpu
from jax.sharding import PartitionSpec as P

LEVELS = 6


first_scale = 1.0 / 7.5
rho_one = 1.0 / (2.0 * (5.0 / 3.0) - 0.6)
carry_coef = 0.6 * rho_one
fresh_coef = 2.0 * rho_one / (0.75 * 6.0)

LANES = 128
F32 = jnp.float32
AXES = (("gz", 0), ("gx", 1), ("gy", 2))


def extended(x, width):
    for axis, dim in AXES:
        peers, length = (lax.axis_size(axis), x.shape[dim + 1])
        up = [(i, (i + 1) % peers) for i in range(peers - 1)]
        down = [(j, i) for i, j in up]
        last = lax.slice_in_dim(x, length - width, length, axis=dim + 1)
        first = lax.slice_in_dim(x, 0, width, axis=dim + 1)
        before = lax.ppermute(last, axis, up)
        after = lax.ppermute(first, axis, down)
        x = jnp.concatenate([before, x, after], axis=dim + 1)
    return x


def stencil(values):
    padded = jnp.pad(values, 1)
    return valid_op(padded)


def valid_op(padded):
    beside = padded[2:, 1:-1, 1:-1] + padded[:-2, 1:-1, 1:-1]
    beside = beside + padded[1:-1, 2:, 1:-1] + padded[1:-1, :-2, 1:-1]
    beside = beside + padded[1:-1, 1:-1, 2:] + padded[1:-1, 1:-1, :-2]
    return 6.0 * padded[1:-1, 1:-1, 1:-1] - beside


def smooth_pass(iterate, source, apply_op, from_zero):
    residue = source if from_zero else source - apply_op(iterate)
    update = residue * first_scale
    iterate = update if from_zero else iterate + update
    residue = source - apply_op(iterate)
    update = carry_coef * update + fresh_coef * residue
    return iterate + update


def restrict(values):
    shape_a, shape_b, shape_c = values.shape
    blocks = values.reshape(shape_a // 2, 2, shape_b // 2, 2, shape_c // 2, 2)
    return 0.5 * jnp.sum(blocks, axis=(1, 3, 5))


def prolong(values):
    shape_a, shape_b, shape_c = values.shape
    spread = jnp.broadcast_to(
        values[:, None, :, None, :, None], (shape_a, 2, shape_b, 2, shape_c, 2)
    )
    return spread.reshape(2 * shape_a, 2 * shape_b, 2 * shape_c)


def vcycle(level_num, iterate, source):
    iterate = smooth_pass(iterate, source, stencil, True)
    coarsest = None
    if level_num < LEVELS - 1:
        residue = source - stencil(iterate)
        coarse, coarsest = vcycle(level_num + 1, None, restrict(residue))
        iterate = iterate + prolong(coarse)
    result = smooth_pass(iterate, source, stencil, False)
    if level_num == LEVELS - 1:
        coarsest = result
    return (result, coarsest)


def collect(values):
    gathered = lax.all_gather(values, "gz", axis=0, tiled=True)
    gathered = lax.all_gather(gathered, "gy", axis=2, tiled=True)
    return lax.all_gather(gathered, "gx", axis=1, tiled=True)


def local_stencil(values):
    return valid_op(extended(values[None], 1)[0])


def own_block(whole, block_shape):
    start_z = lax.axis_index("gz") * block_shape[0]
    start_x = lax.axis_index("gx") * block_shape[1]
    start_y = lax.axis_index("gy") * block_shape[2]
    return lax.dynamic_slice(whole, (start_z, start_x, start_y), block_shape)


def body_cycle(level_num, iterate, source, from_zero, gather_at):
    if level_num == gather_at:
        whole_source = collect(source)
        coarse, coarsest = vcycle(level_num, None, whole_source)
        return (own_block(coarse, source.shape), coarsest)
    iterate = smooth_pass(iterate, source, local_stencil, from_zero)
    residue = source - local_stencil(iterate)
    coarse, coarsest = body_cycle(level_num + 1, None, restrict(residue), True, gather_at)
    iterate = iterate + prolong(coarse)
    return (smooth_pass(iterate, source, local_stencil, False), coarsest)


def body_levels(divergence, pressure_prev):
    pressure, coarse_correction = body_cycle(0, pressure_prev, divergence, False, 3)
    residual = divergence - local_stencil(pressure)
    return (pressure, residual, coarse_correction)


def iota(shape, dim):
    return lax.broadcasted_iota(jnp.int32, shape, dim)


def signed(index, size, extent):
    return jnp.where(index >= (size + extent) // 2, index - extent, index)


def split(values):
    terms = []
    for _ in range(3):
        term = values.astype(jnp.bfloat16)
        terms.append(term)
        values = values - term.astype(F32)
    return terms


def right_dot(values, table):
    parts = [jnp.dot(t, table, preferred_element_type=F32) for t in split(values)]
    return parts[0] + parts[1] + parts[2]


def left_dot(table, values):
    parts = [jnp.dot(table, t, preferred_element_type=F32) for t in split(values)]
    return parts[0] + parts[1] + parts[2]


def as_table(keep, value=1.0):
    return jnp.where(keep, value, 0.0).astype(jnp.bfloat16)


def lateral(v):
    rows, lanes = v.shape
    return (
        pltpu.roll(v, 1, 0) + pltpu.roll(v, rows - 1, 0)
        + pltpu.roll(v, 1, 1) + pltpu.roll(v, lanes - 1, 1)
    )


def apply_at(ref, k, lateral_of=lateral):
    centre = ref[k]
    beside = lateral_of(centre)
    if k > 0:
        beside = beside + ref[k - 1]
    if k < ref.shape[0] - 1:
        beside = beside + ref[k + 1]
    return 6.0 * centre - beside


def wrapped_mask(shape, sizes, low, high):
    keep = None
    for dim, size in sizes.items():
        at = signed(iota(shape, dim), size, shape[dim])
        good = ((at >= 0) | low[dim]) & ((at < size) | high[dim])
        keep = good if keep is None else keep & good
    return jnp.where(keep, 1.0, 0.0).astype(F32)


def side(index, flip):
    if flip == 1:
        return (index & 1) == 0, None
    return index < 2, (index == 1) | (index == 2)


def place(axis, count):
    index = lax.axis_index(axis)
    return index, index > 0, index < count - 1


def only(keep, v):
    return jnp.where(keep, v, 0.0)


def shifted(v, lanes):
    lanes = lanes % LANES
    return v if lanes == 0 else pltpu.roll(v, lanes, 1)


def lanes_of(v, first, count):
    lane = iota(v.shape, 1)
    last = first + count
    if last <= LANES:
        return (lane >= first) & (lane < last)
    return (lane >= first) | (lane < last - LANES)


def moved(v, first, count, to):
    first = first % LANES
    return shifted(only(lanes_of(v, first, count), v), to - first)


def side_pack(tile, slot):
    return moved(tile, LANES - 3, 6, 8 * slot)


def side_unpack(packed, slot):
    return moved(packed, 8 * slot, 6, LANES - 3)


SLOTS = LANES // 8


def slab_emit(r_ref, x_ref, out, at, up):
    ez, ex, _ = r_ref.shape
    start = jnp.where(up, ez - 5, 0)
    start_x = jnp.where(up, ez - 3, 1)
    lat = None
    for j in range(7):
        v = r_ref[start + j] if j < 5 else x_ref[start_x + j - 5]
        out[at + j * ex:at + (j + 1) * ex, :] = v[:, 0:LANES]
        part = side_pack(v[:, LANES:], j)
        lat = part if lat is None else lat + part
    out[at + 7 * ex:at + 8 * ex, :] = lat


def slab_add(r_ref, x_ref, slab, at, up):
    ez, ex, _ = r_ref.shape
    start = jnp.where(up, ez - 6, 1)
    start_x = jnp.where(up, ez - 5, 3)
    lat = slab[at + 7 * ex:at + 8 * ex, :]
    for j in range(7):
        ref, k = (r_ref, start + j) if j < 5 else (x_ref, start_x + j - 5)
        ref[k, :, 0:LANES] += slab[at + j * ex:at + (j + 1) * ex, :]
        ref[k, :, LANES:] += side_unpack(lat, j)


def rows_out(r, x, up):
    bx = r.shape[0] - 8
    row = iota((8, r.shape[1]), 0)
    first, last, spill = r[0:8], r[bx - 8:bx], r[bx:]
    to_high = pltpu.roll(jnp.where(row >= 6, last, spill), 2, 0)
    to_low = pltpu.roll(jnp.where(row >= 5, spill, first), 3, 0)
    out = jnp.where(up, to_high, to_low)
    if x is None:
        return only(row < 5, out)
    spill = x[bx:]
    extra = jnp.where(up, pltpu.roll(spill, 5, 0), pltpu.roll(spill, 7, 0))
    return jnp.where(row < 5, out, only(row < 7, extra))


def rows_in(r_ref, x_ref, k, rows, up):
    bx = r_ref.shape[1] - 8
    row = iota(rows.shape, 0)
    high, low = pltpu.roll(rows, 5, 0), pltpu.roll(rows, 6, 0)
    r_ref[k, 0:8] += only(jnp.logical_not(up) & (row < 3), low)
    r_ref[k, bx - 8:bx] += only(up & (row >= 5), high)
    r_ref[k, bx:] += jnp.where(up, only(row < 2, high), only(row >= 6, low))
    if x_ref is not None:
        x_ref[k, 0:8] += only(jnp.logical_not(up) & (row < 2), pltpu.roll(rows, 3, 0))
        x_ref[k, bx - 8:bx] += only(up & (row >= 6), pltpu.roll(rows, 1, 0))


class Plan:
    def __init__(self, shape, peers):
        self.peers = peers
        self.block = bz, bx, by = shape
        self.ext = self.ez, self.ex, self.ey = bz + 6, bx + 8, by + LANES
        self.rows, self.pairs = bx // 2, bz // 4 + 2
        self.lat_at = self.pairs * (self.rows + 4)
        self.coarse = self.lat_at + 16
        self.slab = 8 * self.ex
        self.x_groups = -(-self.ez // SLOTS)
        self.x_rows = (self.ez + self.x_groups) * 8
        self.corner = 6 * 8
        self.layers = bz + 4
        self.level1 = (peers[0] * bz // 2, peers[1] * bx // 2, LANES)
        self.level2 = (peers[0] * bz // 4, peers[1] * bx // 4, peers[2] * by // 4)
        self.y_groups = -(-self.layers // SLOTS)
        self.fine_rows = self.y_groups * self.ex
        self.edge = self.fine_rows + self.level1[0] * self.level1[1] // 8
        self.share = self.level2[0] * self.level2[1] // 2


def first_kernel(plan, b_in, p_in, r_ref, x_ref, pay_z, pay_x, pay_d, *scratch):
    b_own, p_own, b_ext, p_ext, d_one, d_two, pairs, lines, sem = scratch
    bz, bx, by = plan.block
    ez, ex, ey = plan.ext
    peers = plan.peers
    copies = [
        pltpu.make_async_copy(p_in, p_own, sem.at[0]),
        pltpu.make_async_copy(b_in, b_own, sem.at[1]),
    ]
    for copy in copies:
        copy.start()
    iz, z_low, z_high = place("gz", peers[0])
    ix, x_low, x_high = place("gx", peers[1])
    _, y_low, y_high = place("gy", peers[2])
    flat = wrapped_mask((ex, ey), {0: bx, 1: by}, (x_low, y_low), (x_high, y_high))
    below = jnp.where(z_low, 1.0, 0.0).astype(F32)
    above = jnp.where(z_high, 1.0, 0.0).astype(F32)

    def masked(k, v):
        v = v * flat
        if k < 3:
            v = v * below
        if k >= 3 + bz:
            v = v * above
        return v

    zero = jnp.zeros((ex, ey), F32)
    for k in range(ez):
        p_ext[k] = zero
        b_ext[k] = zero
    for copy in copies:
        copy.wait()
    for k in range(bz):
        b_ext[k + 3, 0:bx, 0:by] = b_own[k]
        p_ext[k + 3, 0:bx, 0:by] = p_own[k]
    for k in range(ez):
        if 2 <= k < ez - 2:
            r = b_ext[k] - apply_at(p_ext, k)
            r_ref[k] = r
            d_one[k] = masked(k, r * first_scale)
        else:
            d_one[k] = zero
    for k in range(ez):
        if 1 <= k < ez - 1:
            r = -apply_at(d_one, k)
            if 2 <= k < ez - 2:
                r = r + r_ref[k]
            r_ref[k] = r
            d_two[k] = masked(k, carry_coef * d_one[k] + fresh_coef * r)
        else:
            d_two[k] = zero
    for k in range(ez):
        r = -apply_at(d_two, k)
        if 1 <= k < ez - 1:
            r = r + r_ref[k]
        r_ref[k] = masked(k, r)
        x_ref[k] = p_ext[k] + d_one[k] + d_two[k]


    coarse_z, rows = 2 * plan.pairs, plan.rows
    for zc in range(coarse_z):
        low, high = 2 * zc - 1, 2 * zc
        if low < 0:
            total = r_ref[high]
        elif high >= ez:
            total = r_ref[low]
        else:
            total = r_ref[low] + r_ref[high]
        base = zc * ex
        for tile in range(ey // LANES):
            here = slice(tile * LANES, (tile + 1) * LANES)
            pairs[tile, base:base + ex, :] = total[:, here]
            even = pairs.at[tile][pl.ds(base, ex // 2, 2), :]
            odd = pairs.at[tile][pl.ds(base + 1, ex // 2, 2), :]
            sums = even + odd
            at = zc // 2 * rows
            lines[zc % 2, at:at + rows, here] = sums[0:rows]
            at = plan.pairs * rows + zc // 2 * 4
            lines[zc % 2, at:at + 4, here] = sums[rows:rows + 4]
    fine = signed(iota((ey, LANES), 0), by, ey)
    coarse = signed(iota((ey, LANES), 1), by // 2, LANES)
    table = as_table((fine >> 1) == coarse, 0.5)
    even, odd = right_dot(lines[0], table), right_dot(lines[1], table)
    lane = iota(even.shape, 1)
    at = plan.slab
    pay_z[at:at + plan.lat_at, :] = jnp.where(lane < LANES // 2, even, shifted(odd, LANES // 2))
    own_lat = spill_lat = None
    row = iota((8, LANES), 0)
    for zc in range(coarse_z):
        source = (even, odd)[zc % 2]
        base = zc // 2 * rows
        tile = source[base:base + rows]
        part = moved(tile, by // 2, 2, 4 * zc) + moved(tile, LANES - 2, 2, 4 * zc + 2)
        own_lat = part if own_lat is None else own_lat + part
        base = plan.pairs * rows + zc // 4 * 8
        tile = source[base:base + 8]
        if zc // 2 % 2:
            tile = pltpu.roll(tile, 4, 0)
        tile = only(row < 4, tile)
        part = moved(tile, by // 2, 2, 4 * zc) + moved(tile, LANES - 2, 2, 4 * zc + 2)
        spill_lat = part if spill_lat is None else spill_lat + part
    at = plan.slab + plan.lat_at
    pay_z[at:at + 8, :] = own_lat
    pay_z[at + 8:at + 16, :] = spill_lat
    block = pay_z[plan.slab:plan.slab + plan.coarse, :]
    pay_x[plan.x_rows:plan.x_rows + plan.coarse, :] = block
    pay_d[plan.corner:plan.corner + plan.coarse, :] = block

    up_z, _ = side(iz, 3)
    up_x, _ = side(ix, 1)
    slab_emit(r_ref, x_ref, pay_z, 0, up_z)
    for group in range(plan.x_groups):
        lat = jnp.zeros((8, LANES), F32)
        for k in range(group * SLOTS, min(ez, (group + 1) * SLOTS)):
            out = rows_out(r_ref[k], x_ref[k], up_x)
            pay_x[8 * k:8 * k + 8, :] = out[:, 0:LANES]
            lat = lat + side_pack(out[:, LANES:], k - group * SLOTS)
        pay_x[8 * (ez + group):8 * (ez + group) + 8, :] = lat
    start = jnp.where(up_z, ez - 5, 0)
    lat = jnp.zeros((8, LANES), F32)
    for j in range(5):
        out = rows_out(r_ref[start + j], x_ref[start + j] if j == 2 else None, up_x)
        pay_d[8 * j:8 * j + 8, :] = out[:, 0:LANES]
        lat = lat + side_pack(out[:, LANES:], j)
    pay_d[40:48, :] = lat


def chip_kernel(plan, r_in, x_in, ours, from_z, from_x, from_d, r_ref, x_ref, pay):
    ez, ex, ey = plan.ext
    iz, _, _ = place("gz", plan.peers[0])
    ix, _, _ = place("gx", plan.peers[1])
    up_z, near = side(iz, 3)
    up_x, _ = side(ix, 1)
    for k in range(ez):
        r_ref[k] = r_in[k]
        x_ref[k] = x_in[k]
        lat = from_x[8 * (ez + k // SLOTS):8 * (ez + k // SLOTS) + 8, :]
        rows = from_x[8 * k:8 * k + 8, :]
        rows = jnp.concatenate([rows, side_unpack(lat, k % SLOTS)], axis=1)
        rows_in(r_ref, x_ref, k, rows, up_x)

    @pl.when(near)
    def _():
        slab_add(r_ref, x_ref, from_z, 0, up_z)
        start = jnp.where(up_z, ez - 6, 1)
        lat = from_d[40:48, :]
        for j in range(5):
            rows = from_d[8 * j:8 * j + 8, :]
            rows = jnp.concatenate([rows, side_unpack(lat, j)], axis=1)
            rows_in(r_ref, x_ref if j == 2 else None, start + j, rows, up_x)

    up, _ = side(iz, 1)
    slab_emit(r_ref, x_ref, pay, 0, up)
    for j, (ref, at) in enumerate(
        ((ours, plan.slab), (from_z, plan.slab), (from_x, plan.x_rows), (from_d, plan.corner))
    ):
        here = plan.slab + j * plan.coarse
        pay[here:here + plan.coarse, :] = ref[at:at + plan.coarse, :]


def plane_kernel(plan, r_in, x_in, ours, theirs, r_ref, x_ref, r1_ref, x1_ref, pay_a, pay_b, pay_c,
                 r_all, x_all, b1, d1, d2, pairs, lines):
    bz, bx, by = plan.block
    ez, ex, ey = plan.ext
    layers = plan.layers
    iz, _, _ = place("gz", plan.peers[0])
    ix, _, _ = place("gx", plan.peers[1])
    iy, y_low, y_high = place("gy", plan.peers[2])
    up, _ = side(iz, 1)
    for k in range(ez):
        r_all[k] = r_in[k]
        x_all[k] = x_in[k]
    slab_add(r_all, x_all, theirs, 0, up)
    for k in range(layers):
        r_ref[k] = r_all[k + 1]
    for k in range(bz):
        x_ref[k] = x_all[k + 3, 0:bx, 0:by]

    up_a, _ = side(iy, 1)
    up_b, _ = side(iy, 3)
    edges = []
    for which in range(2):
        tiles = []
        for group in range(plan.y_groups):
            total = jnp.zeros((ex, LANES), F32)
            for k in range(group * SLOTS, min(layers, (group + 1) * SLOTS)):
                slot = 8 * (k - group * SLOTS)
                v, spill = r_all[k + 1, :, 0:by], r_all[k + 1, :, by:ey]
                if which == 0:
                    total = total + moved(jnp.where(lanes_of(v, 0, 3), spill, v), LANES - 2, 5, slot)
                else:
                    total = total + moved(jnp.where(lanes_of(v, 0, 2), v, spill), LANES - 3, 5, slot)
                if 2 <= k < 2 + bz:
                    spill = x_all[k + 1, :, by:ey]
                    total = total + moved(spill, 0 if which == 0 else LANES - 2, 2, slot + 5)
            tiles.append(total)
        edges.append(tiles)
    for group in range(plan.y_groups):
        here = slice(group * ex, (group + 1) * ex)
        pay_a[here, :] = jnp.where(up_a, edges[0][group], edges[1][group])
        pay_b[here, :] = jnp.where(up_b, edges[0][group], edges[1][group])

    nz1, nx1, _ = plan.level1
    rows, half = plan.rows, by // 2
    for k in range(nz1):
        b1[k] = jnp.zeros((nx1, LANES), F32)
    row = iota((8, LANES), 0)
    for j in range(plan.peers[0]):
        for i in range(plan.peers[1]):
            flip = iz ^ j
            chip = (flip >> 1) + 2 * (ix ^ i)
            other = ((flip ^ (flip >> 1)) & 1) == 1
            at = pl.multiple_of(plan.slab + chip * plan.coarse, 8)

            def rows_at(offset, count):
                here = pl.ds(pl.multiple_of(at + offset, 8), count)
                return jnp.where(other, theirs[here, :], ours[here, :])

            own_lat = rows_at(plan.lat_at, 8)
            spill_lat = rows_at(plan.lat_at + 8, 8)
            for zp in range(plan.pairs):
                own = rows_at(zp * rows, rows)
                if zp % 2 == 0:
                    spill_two = rows_at(plan.pairs * rows + zp * 4, 8)
                spill = spill_two if zp % 2 == 0 else pltpu.roll(spill_two, 4, 0)
                for part in range(2):
                    zc = 2 * zp + part
                    k = j * (bz // 2) + zc - 2
                    if not 0 <= k < nz1:
                        continue

                    def wide(main, lat):
                        return (
                            moved(main, part * half, half, 0)
                            + moved(lat, 4 * zc, 2, half) + moved(lat, 4 * zc + 2, 2, LANES - 2)
                        )

                    b1[k, i * rows:(i + 1) * rows, :] += wide(own, own_lat)
                    v = wide(spill, spill_lat)
                    if i + 1 < plan.peers[1]:
                        at_row = (i + 1) * rows
                        b1[k, at_row:at_row + 8, :] += only(row < 2, v)
                    if i > 0:
                        at_row = i * rows - 8
                        b1[k, at_row:at_row + 8, :] += only(row >= 6, pltpu.roll(v, 4, 0))

    lateral1 = level_lateral((nx1, LANES))
    keep = wrapped_mask((nx1, LANES), {1: half}, (None, y_low), (None, y_high))
    for k in range(nz1):
        d1[k] = b1[k] * first_scale
    for k in range(nz1):
        r = b1[k] - apply_at(d1, k, lateral1)
        r1_ref[k] = r
        d2[k] = keep * (carry_coef * d1[k] + fresh_coef * r)
    for k in range(nz1):
        r1_ref[k] = keep * (r1_ref[k] - apply_at(d2, k, lateral1))
        x1_ref[k] = d1[k] + d2[k]

    nz2, nx2, _ = plan.level2
    for zc in range(nz2):
        pairs[zc * nx1:(zc + 1) * nx1, :] = r1_ref[2 * zc] + r1_ref[2 * zc + 1]
        part, at = divmod(zc, nz2 // 2)
        lines[at * nx2:(at + 1) * nx2, part * LANES:(part + 1) * LANES] = (
            pairs[pl.ds(zc * nx1, nx2, 2), :] + pairs[pl.ds(zc * nx1 + 1, nx2, 2), :]
        )
    fine = iota((2 * LANES, LANES), 0)
    part, fine = fine // LANES, signed(fine % LANES, half, LANES)
    coarse = iota((2 * LANES, LANES), 1)
    table = as_table(
        (coarse // (LANES // 2) == part)
        & (signed(coarse % (LANES // 2), half // 2, LANES // 2) == (fine >> 1)), 0.5
    )
    share = right_dot(lines[...], table)
    pay_c[...] = share
    pay_a[plan.edge:plan.edge + plan.share, :] = share
    pay_b[plan.edge:plan.edge + plan.share, :] = share

    per_tile = LANES // 16
    for group in range(nz1 // per_tile):
        tiles = []
        for which in range(2):
            total = jnp.zeros((nx1, LANES), F32)
            for j in range(per_tile):
                k = group * per_tile + j
                first = half - 3 if which == 0 else LANES - 4
                total = total + moved(r1_ref[k], first, 7, 16 * j)
                first = half - 2 if which == 0 else LANES - 3
                total = total + moved(x1_ref[k], first, 5, 16 * j + 7)
            tiles.append(total)
        here = slice(plan.fine_rows + group * nx1, plan.fine_rows + (group + 1) * nx1)
        pay_a[here, :] = jnp.where(up_a, tiles[0], tiles[1])
        pay_b[here, :] = jnp.where(up_b, tiles[0], tiles[1])


def level_lateral(shape):
    row = iota(shape, 0)
    not_first = jnp.where(row > 0, 1.0, 0.0).astype(F32)
    not_last = jnp.where(row < shape[0] - 1, 1.0, 0.0).astype(F32)

    def beside(v):
        return (
            not_first * pltpu.roll(v, 1, 0) + not_last * pltpu.roll(v, shape[0] - 1, 0)
            + pltpu.roll(v, 1, 1) + pltpu.roll(v, LANES - 1, 1)
        )

    return beside


def small_cycle(level, source):
    step = 1 << (level - 2)
    row, lane = iota((8, LANES), 0), iota((8, LANES), 1)
    count = len(source)
    shifts = []
    if step < 8:
        shifts += [(step, 0, row >= step), (8 - step, 0, row < 8 - step)]
    shifts += [(step, 1, lane >= step), (LANES - step, 1, lane < LANES - step)]

    def op(v):
        out = []
        for k in range(count):
            beside = None
            for shift, dim, keep in shifts:
                part = only(keep, pltpu.roll(v[k], shift, dim))
                beside = part if beside is None else beside + part
            if k > 0:
                beside = beside + v[k - 1]
            if k < count - 1:
                beside = beside + v[k + 1]
            out.append(6.0 * v[k] - beside)
        return out

    d = [first_scale * v for v in source]
    r = [b - t for b, t in zip(source, op(d))]
    d2 = [carry_coef * v + fresh_coef * t for v, t in zip(d, r)]
    x = [v + t for v, t in zip(d, d2)]
    r = [v - t for v, t in zip(r, op(d2))]
    coarsest = None
    if level < LEVELS - 1:
        keep = only((row % (2 * step) == 0) & (lane % (2 * step) == 0), 0.5)
        coarse = []
        for k in range(0, count, 2):
            v = r[k] + r[k + 1]
            v = v + pltpu.roll(v, 8 - step, 0)
            coarse.append(keep * (v + pltpu.roll(v, LANES - step, 1)))
        coarse, coarsest = small_cycle(level + 1, coarse)
        e = []
        for v in coarse:
            v = v + pltpu.roll(v, step, 0)
            e += [v + pltpu.roll(v, step, 1)] * 2
        x = [v + t for v, t in zip(x, e)]
        r = [v - t for v, t in zip(r, op(e))]
    d = [first_scale * v for v in r]
    r = [v - t for v, t in zip(r, op(d))]
    x = [v + (t + (carry_coef * t + fresh_coef * u)) for v, t, u in zip(x, d, r)]
    return x, (x if level == LEVELS - 1 else coarsest)


def last_kernel(plan, r_in, x_in, r1_in, x1_in, share, from_a, from_b, from_c, p_out, res_out, last_ref, *scratch):
    shares, p_ref, res_ref, r, q1, e1, e0, d0, d1, r1, lines, wide, sem = scratch
    bz, bx, by = plan.block
    ez, ex, ey = plan.ext
    nz1, nx1, _ = plan.level1
    nz2, nx2, ny2 = plan.level2
    layers, half = plan.layers, by // 2
    iz, z_low, z_high = place("gz", plan.peers[0])
    ix, x_low, x_high = place("gx", plan.peers[1])
    iy, y_low, y_high = place("gy", plan.peers[2])

    shares[0] = share[...]
    shares[1] = from_a[plan.edge:plan.edge + plan.share, :]
    shares[3] = from_b[plan.edge:plan.edge + plan.share, :]
    shares[2] = from_c[...]
    lower = upper = None
    own2 = half // 2
    for j in range(plan.peers[2]):
        v = shares[iy ^ j]
        at = own2 * j
        mid = LANES // 2
        low = moved(v, 0, own2 + 2, at) + moved(v, mid - 2, 2, at - 2)
        high = moved(v, mid, own2 + 2, at) + moved(v, LANES - 2, 2, at - 2)
        lower = low if lower is None else lower + low
        upper = high if upper is None else upper + high
    source = [lower[8 * k:8 * k + 8] for k in range(nz2 // 2)]
    source += [upper[8 * k:8 * k + 8] for k in range(nz2 // 2)]
    e2, coarsest = small_cycle(2, source)
    for k in range(nz2):
        lines[k * nx2:(k + 1) * nx2, :] = e2[k]
    thin = as_table(iota((LANES, LANES), 0) == 8 * iota((LANES, LANES), 1))
    for k in range(last_ref.shape[0]):
        last_ref[k] = right_dot(coarsest[k], thin)[0:1, 0:last_ref.shape[2]]

    up_a, _ = side(iy, 1)
    _, near_b = side(iy, 3)
    a_low = jnp.logical_not(up_a)

    def sent(rows):
        a, b = from_a[rows[0]:rows[1], :], from_b[rows[0]:rows[1], :]
        b = only(near_b, b)
        return jnp.where(up_a, a, b), jnp.where(up_a, b, a)

    fine = signed(iota((LANES, LANES), 1), half, LANES)
    coarse = iota((LANES, LANES), 0) - iy * own2
    e2 = right_dot(lines[...], as_table((fine >> 1) == coarse))
    for zc in range(nz2):
        v = e2[zc * nx2:(zc + 1) * nx2]
        for part in range(2):
            q1.at[2 * zc + part][pl.ds(0, nx2, 2), :] = v
            q1.at[2 * zc + part][pl.ds(1, nx2, 2), :] = v
    per_tile = LANES // 16
    lateral1 = level_lateral((nx1, LANES))
    keep = wrapped_mask((nx1, LANES), {1: half}, (None, y_low), (None, y_high))
    for group in range(nz1 // per_tile):
        at = plan.fine_rows + group * nx1
        high, low = sent((at, at + nx1))
        for j in range(per_tile):
            k = group * per_tile + j
            s = 16 * j
            r1[k] = (
                r1_in[k] + moved(high, s, 7, half - 4) + moved(low, s, 7, LANES - 3)
                - apply_at(q1, k, lateral1)
            )
            e1[k + 2, 8:8 + nx1, :] = (
                x1_in[k] + q1[k]
                + moved(high, s + 7, 5, half - 3) + moved(low, s + 7, 5, LANES - 2)
            )
    for k in range(nz1):
        d1[k] = keep * (r1[k] * first_scale)
    nothing = jnp.zeros((8, LANES), F32)
    for k in range(nz1 + 4):
        e1[k, 0:8, :] = nothing
        e1[k, 8 + nx1:16 + nx1, :] = nothing
        if not 2 <= k < nz1 + 2:
            e1[k, 8:8 + nx1, :] = jnp.zeros((nx1, LANES), F32)
    for k in range(nz1):
        v = r1[k] - apply_at(d1, k, lateral1)
        e1[k + 2, 8:8 + nx1, :] += d1[k] + keep * (carry_coef * d1[k] + fresh_coef * v)

    coarse = signed(iota((LANES, ey), 0), half, LANES)
    fine = signed(iota((LANES, ey), 1), by, ey)
    double = as_table((fine >> 1) == coarse)
    half_z, half_x = bz // 2, bx // 2
    for zc in range(half_z + 4):
        start = pl.multiple_of(ix * half_x, 8)
        v = e1[iz * half_z + zc, pl.ds(start, half_x + 16), :]
        own, low, high = v[8:8 + half_x], v[0:8], v[8 + half_x:16 + half_x]
        at = zc * ex
        wide[pl.ds(at, half_x, 2), :] = own
        wide[pl.ds(at + 1, half_x, 2), :] = own
        for j in range(2):
            for twin in range(2):
                row = at + bx + 2 * j + twin
                wide[row:row + 1, :] = high[j:j + 1]
                row = at + ex - 4 + 2 * j + twin
                wide[row:row + 1, :] = low[6 + j:7 + j]
    for zc in range(half_z + 4):
        v = right_dot(wide[zc * ex:(zc + 1) * ex, :], double)
        for k in (2 * zc - 1, 2 * zc):
            if 0 <= k < ez:
                e0[k] = v
    flat = wrapped_mask((ex, ey), {0: bx, 1: by}, (x_low, y_low), (x_high, y_high))
    below = jnp.where(z_low, 1.0, 0.0).astype(F32)
    above = jnp.where(z_high, 1.0, 0.0).astype(F32)

    def masked(k, v):
        v = v * flat
        if k < 3:
            v = v * below
        if k >= 3 + bz:
            v = v * above
        return v

    for group in range(plan.y_groups):
        high, low = sent((group * ex, (group + 1) * ex))
        for k in range(group * SLOTS, min(layers, (group + 1) * SLOTS)):
            s = 8 * (k - group * SLOTS)
            v = r_in[k] - apply_at(e0, k + 1)
            r[k, :, 0:by] = v[:, 0:by] + moved(high, s, 3, LANES - 3) + moved(low, s + 2, 3, 0)
            r[k, :, by:ey] = v[:, by:ey] + moved(high, s + 3, 2, 0) + moved(low, s, 2, LANES - 2)
            d0[k] = masked(k + 1, r[k] * first_scale)
            if 2 <= k < 2 + bz:
                p_ref[k - 2] = (
                    x_in[k - 2] + e0[k + 1, 0:bx, 0:by]
                    + (moved(high, s + 5, 2, LANES - 2) + moved(low, s + 5, 2, 0))[0:bx]
                )
    for k in range(1, layers - 1):
        v = r[k] - apply_at(d0, k)
        r[k] = v
        v = masked(k + 1, carry_coef * d0[k] + fresh_coef * v)
        e0[k] = v
        if 2 <= k < 2 + bz:
            p_ref[k - 2] += d0[k, 0:bx, 0:by] + v[0:bx, 0:by]
    copy = pltpu.make_async_copy(p_ref, p_out, sem.at[0])
    copy.start()
    copies = [copy]
    parts = 2
    for part in range(parts):
        here = range(part * bz // parts, (part + 1) * bz // parts)
        for j in here:
            v = r[j + 2] - apply_at(e0, j + 2)
            res_ref[j] = v[0:bx, 0:by]
        here = pl.ds(here[0], bz // parts)
        copy = pltpu.make_async_copy(res_ref.at[here], res_out.at[here], sem.at[1 + part])
        copy.start()
        copies.append(copy)
    for copy in copies:
        copy.wait()


def whole(shape):
    return jax.ShapeDtypeStruct(shape, F32)


VMEM = pl.BlockSpec(memory_space=pltpu.VMEM)
ANY = pl.BlockSpec(memory_space=pl.ANY)
VMEM_BYTES = 24 << 20


def run(kernel, plan, outs, scratch, *operands, in_specs=None, out_specs=None, semaphores=0):
    scratch = [pltpu.VMEM(s, F32) for s in scratch]
    if semaphores:
        scratch.append(pltpu.SemaphoreType.DMA((semaphores,)))
    return pl.pallas_call(
        functools.partial(kernel, plan),
        out_shape=[whole(s) for s in outs],
        in_specs=in_specs or [VMEM] * len(operands),
        out_specs=out_specs or [VMEM] * len(outs),
        scratch_shapes=scratch,
        compiler_params=pltpu.CompilerParams(vmem_limit_bytes=VMEM_BYTES),
    )(*operands)


def swap(values, **flips):
    axes = ("gx", "gy", "gz")
    counts = [lax.axis_size(a) for a in axes]
    pairs = []
    for i in range(counts[0] * counts[1] * counts[2]):
        at = [i // (counts[1] * counts[2]), i // counts[2] % counts[1], i % counts[2]]
        to = [n ^ flips.get(a, 0) for n, a in zip(at, axes)]
        pairs.append((i, (to[0] * counts[1] + to[1]) * counts[2] + to[2]))
    return lax.ppermute(values, axes, pairs)


def body_fast(divergence, pressure_prev):
    plan = Plan(divergence.shape, tuple(lax.axis_size(a) for a in ("gz", "gx", "gy")))
    bz, bx, by = plan.block
    ext, lines = plan.ext, plan.lat_at
    flat = (plan.ex, plan.ey)
    level1 = plan.level1
    r, x, pay_z, pay_x, pay_d = run(
        first_kernel, plan,
        [ext, ext, (plan.slab + plan.coarse, LANES), (plan.x_rows + plan.coarse, LANES),
         (plan.corner + plan.coarse, LANES)],
        [plan.block, plan.block, ext, ext, ext, ext, (2, 2 * plan.pairs * plan.ex, LANES),
         (2, plan.lat_at, plan.ey)],
        divergence, pressure_prev, in_specs=[ANY, ANY], semaphores=2,
    )
    from_z, from_x = swap(pay_z, gz=3), swap(pay_x, gx=1)
    from_d = swap(pay_d, gz=3, gx=1)
    r, x, ours = run(
        chip_kernel, plan, [ext, ext, (plan.slab + 4 * plan.coarse, LANES)], [],
        r, x, pay_z, from_z, from_x, from_d,
    )
    theirs = swap(ours, gz=1)
    nz2, nx2, _ = plan.level2
    edge = plan.edge + plan.share
    r, x, r1, x1, pay_a, pay_b, share = run(
        plane_kernel, plan,
        [(plan.layers,) + flat, plan.block, level1, level1, (edge, LANES), (edge, LANES),
         (plan.share, LANES)],
        [ext, ext, level1, level1, level1, (nz2 * level1[1], LANES), (plan.share, 2 * LANES)],
        r, x, ours, theirs,
    )
    from_a, from_b, from_c = swap(pay_a, gy=1), swap(pay_b, gy=3), swap(share, gy=2)
    return run(
        last_kernel, plan,
        [plan.block, plan.block, tuple(n >> 3 for n in plan.level2)],
        [(4, plan.share, LANES), plan.block, plan.block, (plan.layers,) + flat, level1,
         (level1[0] + 4, level1[1] + 16, LANES), ext, (plan.layers,) + flat, level1, level1,
         (nz2 * nx2, LANES), (2 * plan.pairs * plan.ex, LANES)],
        r, x, r1, x1, share, from_a, from_b, from_c,
        out_specs=[ANY, ANY, VMEM], semaphores=3,
    )


def fits_fast(shape, peers):
    bz, bx, by = shape
    nz, nx, ny = peers
    return (
        nz == 4 and nx == 2 and ny == 4 and bz == 16 and by == LANES
        and nx * bx == 4 * 8 and ny * by == 4 * LANES
    )


def body(divergence, pressure_prev):
    peers = tuple(lax.axis_size(a) for a in ("gz", "gx", "gy"))
    if fits_fast(divergence.shape, peers):
        return tuple(body_fast(divergence, pressure_prev))
    return body_levels(divergence, pressure_prev)


def solution(mesh):
    in_specs = (P("gz", "gx", "gy"), P("gz", "gx", "gy"))
    out_specs = (P("gz", "gx", "gy"), P("gz", "gx", "gy"), P())
    return jax.shard_map(body, mesh=mesh, in_specs=in_specs, out_specs=out_specs, check_vma=False)
```

```python
import functools

import jax
import jax.numpy as jnp
from jax import lax
from jax.experimental import pallas as pl
from jax.experimental.pallas import tpu as pltpu
from jax.sharding import PartitionSpec as P

LEVELS = 6


first_scale = 1.0 / 7.5
rho_one = 1.0 / (2.0 * (5.0 / 3.0) - 0.6)
carry_coef = 0.6 * rho_one
fresh_coef = 2.0 * rho_one / (0.75 * 6.0)

LANES = 128
F32 = jnp.float32
AXES = (("gz", 0), ("gx", 1), ("gy", 2))


def extended(x, width):
    for axis, dim in AXES:
        peers, length = (lax.axis_size(axis), x.shape[dim + 1])
        up = [(i, (i + 1) % peers) for i in range(peers - 1)]
        down = [(j, i) for i, j in up]
        last = lax.slice_in_dim(x, length - width, length, axis=dim + 1)
        first = lax.slice_in_dim(x, 0, width, axis=dim + 1)
        before = lax.ppermute(last, axis, up)
        after = lax.ppermute(first, axis, down)
        x = jnp.concatenate([before, x, after], axis=dim + 1)
    return x


def stencil(values):
    padded = jnp.pad(values, 1)
    return valid_op(padded)


def valid_op(padded):
    beside = padded[2:, 1:-1, 1:-1] + padded[:-2, 1:-1, 1:-1]
    beside = beside + padded[1:-1, 2:, 1:-1] + padded[1:-1, :-2, 1:-1]
    beside = beside + padded[1:-1, 1:-1, 2:] + padded[1:-1, 1:-1, :-2]
    return 6.0 * padded[1:-1, 1:-1, 1:-1] - beside


def smooth_pass(iterate, source, apply_op, from_zero):
    residue = source if from_zero else source - apply_op(iterate)
    update = residue * first_scale
    iterate = update if from_zero else iterate + update
    residue = source - apply_op(iterate)
    update = carry_coef * update + fresh_coef * residue
    return iterate + update


def restrict(values):
    shape_a, shape_b, shape_c = values.shape
    blocks = values.reshape(shape_a // 2, 2, shape_b // 2, 2, shape_c // 2, 2)
    return 0.5 * jnp.sum(blocks, axis=(1, 3, 5))


def prolong(values):
    shape_a, shape_b, shape_c = values.shape
    spread = jnp.broadcast_to(
        values[:, None, :, None, :, None], (shape_a, 2, shape_b, 2, shape_c, 2)
    )
    return spread.reshape(2 * shape_a, 2 * shape_b, 2 * shape_c)


def vcycle(level_num, iterate, source):
    iterate = smooth_pass(iterate, source, stencil, True)
    coarsest = None
    if level_num < LEVELS - 1:
        residue = source - stencil(iterate)
        coarse, coarsest = vcycle(level_num + 1, None, restrict(residue))
        iterate = iterate + prolong(coarse)
    result = smooth_pass(iterate, source, stencil, False)
    if level_num == LEVELS - 1:
        coarsest = result
    return (result, coarsest)


def collect(values):
    gathered = lax.all_gather(values, "gz", axis=0, tiled=True)
    gathered = lax.all_gather(gathered, "gy", axis=2, tiled=True)
    return lax.all_gather(gathered, "gx", axis=1, tiled=True)


def local_stencil(values):
    return valid_op(extended(values[None], 1)[0])


def own_block(whole, block_shape):
    start_z = lax.axis_index("gz") * block_shape[0]
    start_x = lax.axis_index("gx") * block_shape[1]
    start_y = lax.axis_index("gy") * block_shape[2]
    return lax.dynamic_slice(whole, (start_z, start_x, start_y), block_shape)


def body_cycle(level_num, iterate, source, from_zero, gather_at):
    if level_num == gather_at:
        whole_source = collect(source)
        coarse, coarsest = vcycle(level_num, None, whole_source)
        return (own_block(coarse, source.shape), coarsest)
    iterate = smooth_pass(iterate, source, local_stencil, from_zero)
    residue = source - local_stencil(iterate)
    coarse, coarsest = body_cycle(level_num + 1, None, restrict(residue), True, gather_at)
    iterate = iterate + prolong(coarse)
    return (smooth_pass(iterate, source, local_stencil, False), coarsest)


def body_levels(divergence, pressure_prev):
    pressure, coarse_correction = body_cycle(0, pressure_prev, divergence, False, 3)
    residual = divergence - local_stencil(pressure)
    return (pressure, residual, coarse_correction)


def iota(shape, dim):
    return lax.broadcasted_iota(jnp.int32, shape, dim)


def signed(index, size, extent):
    return jnp.where(index >= (size + extent) // 2, index - extent, index)


def split(values):
    terms = []
    for _ in range(3):
        term = values.astype(jnp.bfloat16)
        terms.append(term)
        values = values - term.astype(F32)
    return terms


def right_dot(values, table):
    parts = [jnp.dot(t, table, preferred_element_type=F32) for t in split(values)]
    return parts[0] + parts[1] + parts[2]


def left_dot(table, values):
    parts = [jnp.dot(table, t, preferred_element_type=F32) for t in split(values)]
    return parts[0] + parts[1] + parts[2]


def as_table(keep, value=1.0):
    return jnp.where(keep, value, 0.0).astype(jnp.bfloat16)


def lateral(v):
    rows, lanes = v.shape
    return (
        pltpu.roll(v, 1, 0) + pltpu.roll(v, rows - 1, 0)
        + pltpu.roll(v, 1, 1) + pltpu.roll(v, lanes - 1, 1)
    )


def apply_at(ref, k, lateral_of=lateral):
    centre = ref[k]
    beside = lateral_of(centre)
    if k > 0:
        beside = beside + ref[k - 1]
    if k < ref.shape[0] - 1:
        beside = beside + ref[k + 1]
    return 6.0 * centre - beside


def wrapped_mask(shape, sizes, low, high):
    keep = None
    for dim, size in sizes.items():
        at = signed(iota(shape, dim), size, shape[dim])
        good = ((at >= 0) | low[dim]) & ((at < size) | high[dim])
        keep = good if keep is None else keep & good
    return jnp.where(keep, 1.0, 0.0).astype(F32)


def side(index, flip):
    if flip == 1:
        return (index & 1) == 0, None
    return index < 2, (index == 1) | (index == 2)


def place(axis, count):
    index = lax.axis_index(axis)
    return index, index > 0, index < count - 1


def only(keep, v):
    return jnp.where(keep, v, 0.0)


def shifted(v, lanes):
    lanes = lanes % LANES
    return v if lanes == 0 else pltpu.roll(v, lanes, 1)


def lanes_of(v, first, count):
    lane = iota(v.shape, 1)
    last = first + count
    if last <= LANES:
        return (lane >= first) & (lane < last)
    return (lane >= first) | (lane < last - LANES)


def moved(v, first, count, to):
    first = first % LANES
    return shifted(only(lanes_of(v, first, count), v), to - first)


def side_pack(tile, slot):
    return moved(tile, LANES - 3, 6, 8 * slot)


def side_unpack(packed, slot):
    return moved(packed, 8 * slot, 6, LANES - 3)


SLOTS = LANES // 8


def slab_emit(r_ref, x_ref, out, at, up):
    ez, ex, _ = r_ref.shape
    start = jnp.where(up, ez - 5, 0)
    start_x = jnp.where(up, ez - 3, 1)
    lat = None
    for j in range(7):
        v = r_ref[start + j] if j < 5 else x_ref[start_x + j - 5]
        out[at + j * ex:at + (j + 1) * ex, :] = v[:, 0:LANES]
        part = side_pack(v[:, LANES:], j)
        lat = part if lat is None else lat + part
    out[at + 7 * ex:at + 8 * ex, :] = lat


def slab_add(r_ref, x_ref, slab, at, up):
    ez, ex, _ = r_ref.shape
    start = jnp.where(up, ez - 6, 1)
    start_x = jnp.where(up, ez - 5, 3)
    lat = slab[at + 7 * ex:at + 8 * ex, :]
    for j in range(7):
        ref, k = (r_ref, start + j) if j < 5 else (x_ref, start_x + j - 5)
        ref[k, :, 0:LANES] += slab[at + j * ex:at + (j + 1) * ex, :]
        ref[k, :, LANES:] += side_unpack(lat, j)


def rows_out(r, x, up):
    bx = r.shape[0] - 8
    row = iota((8, r.shape[1]), 0)
    first, last, spill = r[0:8], r[bx - 8:bx], r[bx:]
    to_high = pltpu.roll(jnp.where(row >= 6, last, spill), 2, 0)
    to_low = pltpu.roll(jnp.where(row >= 5, spill, first), 3, 0)
    out = jnp.where(up, to_high, to_low)
    if x is None:
        return only(row < 5, out)
    spill = x[bx:]
    extra = jnp.where(up, pltpu.roll(spill, 5, 0), pltpu.roll(spill, 7, 0))
    return jnp.where(row < 5, out, only(row < 7, extra))


def rows_in(r_ref, x_ref, k, rows, up):
    bx = r_ref.shape[1] - 8
    row = iota(rows.shape, 0)
    high, low = pltpu.roll(rows, 5, 0), pltpu.roll(rows, 6, 0)
    r_ref[k, 0:8] += only(jnp.logical_not(up) & (row < 3), low)
    r_ref[k, bx - 8:bx] += only(up & (row >= 5), high)
    r_ref[k, bx:] += jnp.where(up, only(row < 2, high), only(row >= 6, low))
    if x_ref is not None:
        x_ref[k, 0:8] += only(jnp.logical_not(up) & (row < 2), pltpu.roll(rows, 3, 0))
        x_ref[k, bx - 8:bx] += only(up & (row >= 6), pltpu.roll(rows, 1, 0))


def rows_emit(r_ref, x_ref, out, up):
    ez = r_ref.shape[0]
    for group in range(-(-ez // SLOTS)):
        lat = jnp.zeros((8, LANES), F32)
        for k in range(group * SLOTS, min(ez, (group + 1) * SLOTS)):
            rows = rows_out(r_ref[k], x_ref[k], up)
            out[8 * k:8 * k + 8, :] = rows[:, 0:LANES]
            lat = lat + side_pack(rows[:, LANES:], k - group * SLOTS)
        out[8 * (ez + group):8 * (ez + group) + 8, :] = lat


def rows_add(r_ref, x_ref, slab, up):
    ez = r_ref.shape[0]
    for k in range(ez):
        at = 8 * (ez + k // SLOTS)
        lat = side_unpack(slab[at:at + 8, :], k % SLOTS)
        rows = jnp.concatenate([slab[8 * k:8 * k + 8, :], lat], axis=1)
        rows_in(r_ref, x_ref, k, rows, up)


class Plan:
    def __init__(self, shape, peers):
        self.peers = peers
        self.block = bz, bx, by = shape
        self.ext = self.ez, self.ex, self.ey = bz + 6, bx + 8, by + LANES
        self.rows, self.pairs = bx // 2, bz // 4 + 2
        self.lat_at = self.pairs * (self.rows + 4)
        self.coarse = self.lat_at + 16
        self.x_groups = -(-self.ez // SLOTS)
        self.slab = max(8 * self.ex, (self.ez + self.x_groups) * 8)
        self.layers = bz + 4
        self.level1 = (peers[0] * bz // 2, peers[1] * bx // 2, LANES)
        self.level2 = (peers[0] * bz // 4, peers[1] * bx // 4, peers[2] * by // 4)
        self.y_groups = -(-self.layers // SLOTS)
        self.fine_rows = self.y_groups * self.ex
        self.edge = self.fine_rows + self.level1[0] * self.level1[1] // 8
        self.share = self.level2[0] * self.level2[1] // 2


def first_kernel(plan, b_in, p_in, r_ref, x_ref, pay, *scratch):
    b_own, p_own, b_ext, p_ext, d_one, d_two, pairs, lines, sem = scratch
    bz, bx, by = plan.block
    ez, ex, ey = plan.ext
    peers = plan.peers
    copies = [
        pltpu.make_async_copy(p_in, p_own, sem.at[0]),
        pltpu.make_async_copy(b_in, b_own, sem.at[1]),
    ]
    for copy in copies:
        copy.start()
    iz, z_low, z_high = place("gz", peers[0])
    ix, x_low, x_high = place("gx", peers[1])
    _, y_low, y_high = place("gy", peers[2])
    flat = wrapped_mask((ex, ey), {0: bx, 1: by}, (x_low, y_low), (x_high, y_high))
    below = jnp.where(z_low, 1.0, 0.0).astype(F32)
    above = jnp.where(z_high, 1.0, 0.0).astype(F32)

    def masked(k, v):
        v = v * flat
        if k < 3:
            v = v * below
        if k >= 3 + bz:
            v = v * above
        return v

    zero = jnp.zeros((ex, ey), F32)
    for k in range(ez):
        p_ext[k] = zero
        b_ext[k] = zero
    for copy in copies:
        copy.wait()
    for k in range(bz):
        b_ext[k + 3, 0:bx, 0:by] = b_own[k]
        p_ext[k + 3, 0:bx, 0:by] = p_own[k]
    for k in range(ez):
        if 2 <= k < ez - 2:
            r = b_ext[k] - apply_at(p_ext, k)
            r_ref[k] = r
            d_one[k] = masked(k, r * first_scale)
        else:
            d_one[k] = zero
    for k in range(ez):
        if 1 <= k < ez - 1:
            r = -apply_at(d_one, k)
            if 2 <= k < ez - 2:
                r = r + r_ref[k]
            r_ref[k] = r
            d_two[k] = masked(k, carry_coef * d_one[k] + fresh_coef * r)
        else:
            d_two[k] = zero
    for k in range(ez):
        r = -apply_at(d_two, k)
        if 1 <= k < ez - 1:
            r = r + r_ref[k]
        r_ref[k] = masked(k, r)
        x_ref[k] = p_ext[k] + d_one[k] + d_two[k]


    coarse_z, rows = 2 * plan.pairs, plan.rows
    for zc in range(coarse_z):
        low, high = 2 * zc - 1, 2 * zc
        if low < 0:
            total = r_ref[high]
        elif high >= ez:
            total = r_ref[low]
        else:
            total = r_ref[low] + r_ref[high]
        base = zc * ex
        for tile in range(ey // LANES):
            here = slice(tile * LANES, (tile + 1) * LANES)
            pairs[tile, base:base + ex, :] = total[:, here]
            even = pairs.at[tile][pl.ds(base, ex // 2, 2), :]
            odd = pairs.at[tile][pl.ds(base + 1, ex // 2, 2), :]
            sums = even + odd
            at = zc // 2 * rows
            lines[zc % 2, at:at + rows, here] = sums[0:rows]
            at = plan.pairs * rows + zc // 2 * 4
            lines[zc % 2, at:at + 4, here] = sums[rows:rows + 4]
    fine = signed(iota((ey, LANES), 0), by, ey)
    coarse = signed(iota((ey, LANES), 1), by // 2, LANES)
    table = as_table((fine >> 1) == coarse, 0.5)
    even, odd = right_dot(lines[0], table), right_dot(lines[1], table)
    lane = iota(even.shape, 1)
    at = plan.slab
    pay[at:at + plan.lat_at, :] = jnp.where(lane < LANES // 2, even, shifted(odd, LANES // 2))
    own_lat = spill_lat = None
    row = iota((8, LANES), 0)
    for zc in range(coarse_z):
        source = (even, odd)[zc % 2]
        base = zc // 2 * rows
        tile = source[base:base + rows]
        part = moved(tile, by // 2, 2, 4 * zc) + moved(tile, LANES - 2, 2, 4 * zc + 2)
        own_lat = part if own_lat is None else own_lat + part
        base = plan.pairs * rows + zc // 4 * 8
        tile = source[base:base + 8]
        if zc // 2 % 2:
            tile = pltpu.roll(tile, 4, 0)
        tile = only(row < 4, tile)
        part = moved(tile, by // 2, 2, 4 * zc) + moved(tile, LANES - 2, 2, 4 * zc + 2)
        spill_lat = part if spill_lat is None else spill_lat + part
    at = plan.slab + plan.lat_at
    pay[at:at + 8, :] = own_lat
    pay[at + 8:at + 16, :] = spill_lat
    inner = (iz == 1) | (iz == 2)

    @pl.when(inner)
    def _():
        slab_emit(r_ref, x_ref, pay, 0, side(iz, 3)[0])

    @pl.when(jnp.logical_not(inner))
    def _():
        rows_emit(r_ref, x_ref, pay, side(ix, 1)[0])


def step_kernel(plan, r_in, x_in, ours, got, r_ref, x_ref, pay):
    iz, _, _ = place("gz", plan.peers[0])
    ix, _, _ = place("gx", plan.peers[1])
    up_z, inner = side(iz, 3)
    up_x, _ = side(ix, 1)
    for k in range(plan.ez):
        r_ref[k] = r_in[k]
        x_ref[k] = x_in[k]

    @pl.when(inner)
    def _():
        slab_add(r_ref, x_ref, got, 0, up_z)
        rows_emit(r_ref, x_ref, pay, up_x)

    @pl.when(jnp.logical_not(inner))
    def _():
        rows_add(r_ref, x_ref, got, up_x)
        pay[0:plan.slab, :] = jnp.zeros((plan.slab, LANES), F32)

    for j, ref in enumerate((ours, got)):
        here = plan.slab + j * plan.coarse
        pay[here:here + plan.coarse, :] = ref[plan.slab:plan.slab + plan.coarse, :]


def core_kernel(plan, r_in, x_in, ours, got, r_ref, x_ref, pay):
    iz, _, _ = place("gz", plan.peers[0])
    ix, _, _ = place("gx", plan.peers[1])
    _, inner = side(iz, 3)
    up_x, _ = side(ix, 1)
    for k in range(plan.ez):
        r_ref[k] = r_in[k]
        x_ref[k] = x_in[k]

    @pl.when(inner)
    def _():
        rows_add(r_ref, x_ref, got, up_x)

    slab_emit(r_ref, x_ref, pay, 0, side(iz, 1)[0])
    for j, ref in enumerate((ours, got)):
        here = plan.slab + 2 * j * plan.coarse
        pay[here:here + 2 * plan.coarse, :] = ref[plan.slab:plan.slab + 2 * plan.coarse, :]


def plane_kernel(plan, r_in, x_in, ours, theirs, r_ref, x_ref, r1_ref, x1_ref, pay, later,
                 r_all, x_all, b1, d1, d2, pairs, lines):
    bz, bx, by = plan.block
    ez, ex, ey = plan.ext
    layers = plan.layers
    iz, _, _ = place("gz", plan.peers[0])
    ix, _, _ = place("gx", plan.peers[1])
    iy, y_low, y_high = place("gy", plan.peers[2])
    up, _ = side(iz, 1)
    for k in range(ez):
        r_all[k] = r_in[k]
        x_all[k] = x_in[k]
    slab_add(r_all, x_all, theirs, 0, up)
    for k in range(layers):
        r_ref[k] = r_all[k + 1]
    for k in range(bz):
        x_ref[k] = x_all[k + 3, 0:bx, 0:by]

    even = (iz & 1) == 0
    up_a, up_b = side(iy, 1)[0], side(iy, 3)[0]
    up_now = (even & up_a) | (jnp.logical_not(even) & up_b)
    up_later = (even & up_b) | (jnp.logical_not(even) & up_a)
    edges = []
    for which in range(2):
        tiles = []
        for group in range(plan.y_groups):
            total = jnp.zeros((ex, LANES), F32)
            for k in range(group * SLOTS, min(layers, (group + 1) * SLOTS)):
                slot = 8 * (k - group * SLOTS)
                v, spill = r_all[k + 1, :, 0:by], r_all[k + 1, :, by:ey]
                if which == 0:
                    total = total + moved(jnp.where(lanes_of(v, 0, 3), spill, v), LANES - 2, 5, slot)
                else:
                    total = total + moved(jnp.where(lanes_of(v, 0, 2), v, spill), LANES - 3, 5, slot)
                if 2 <= k < 2 + bz:
                    spill = x_all[k + 1, :, by:ey]
                    total = total + moved(spill, 0 if which == 0 else LANES - 2, 2, slot + 5)
            tiles.append(total)
        edges.append(tiles)
    for group in range(plan.y_groups):
        here = slice(group * ex, (group + 1) * ex)
        pay[here, :] = jnp.where(up_now, edges[0][group], edges[1][group])
        later[here, :] = jnp.where(up_later, edges[0][group], edges[1][group])

    nz1, nx1, _ = plan.level1
    rows, half = plan.rows, by // 2
    for k in range(nz1):
        b1[k] = jnp.zeros((nx1, LANES), F32)
    row = iota((8, LANES), 0)
    for j in range(plan.peers[0]):
        for i in range(plan.peers[1]):
            flip = iz ^ j
            other = ((flip ^ (flip >> 1)) & 1) == 1
            along_z, along_x = flip >> 1, ix ^ i
            met_z = ((iz == 1) | (iz == 2)) ^ other
            chip = jnp.where(met_z, along_z + 2 * along_x, along_x + 2 * along_z)
            at = pl.multiple_of(plan.slab + chip * plan.coarse, 8)

            def rows_at(offset, count):
                here = pl.ds(pl.multiple_of(at + offset, 8), count)
                return jnp.where(other, theirs[here, :], ours[here, :])

            own_lat = rows_at(plan.lat_at, 8)
            spill_lat = rows_at(plan.lat_at + 8, 8)
            for zp in range(plan.pairs):
                own = rows_at(zp * rows, rows)
                if zp % 2 == 0:
                    spill_two = rows_at(plan.pairs * rows + zp * 4, 8)
                spill = spill_two if zp % 2 == 0 else pltpu.roll(spill_two, 4, 0)
                for part in range(2):
                    zc = 2 * zp + part
                    k = j * (bz // 2) + zc - 2
                    if not 0 <= k < nz1:
                        continue

                    def wide(main, lat):
                        return (
                            moved(main, part * half, half, 0)
                            + moved(lat, 4 * zc, 2, half) + moved(lat, 4 * zc + 2, 2, LANES - 2)
                        )

                    b1[k, i * rows:(i + 1) * rows, :] += wide(own, own_lat)
                    v = wide(spill, spill_lat)
                    if i + 1 < plan.peers[1]:
                        at_row = (i + 1) * rows
                        b1[k, at_row:at_row + 8, :] += only(row < 2, v)
                    if i > 0:
                        at_row = i * rows - 8
                        b1[k, at_row:at_row + 8, :] += only(row >= 6, pltpu.roll(v, 4, 0))

    lateral1 = level_lateral((nx1, LANES))
    keep = wrapped_mask((nx1, LANES), {1: half}, (None, y_low), (None, y_high))
    for k in range(nz1):
        d1[k] = b1[k] * first_scale
    for k in range(nz1):
        r = b1[k] - apply_at(d1, k, lateral1)
        r1_ref[k] = r
        d2[k] = keep * (carry_coef * d1[k] + fresh_coef * r)
    for k in range(nz1):
        r1_ref[k] = keep * (r1_ref[k] - apply_at(d2, k, lateral1))
        x1_ref[k] = d1[k] + d2[k]

    nz2, nx2, _ = plan.level2
    for zc in range(nz2):
        pairs[zc * nx1:(zc + 1) * nx1, :] = r1_ref[2 * zc] + r1_ref[2 * zc + 1]
        part, at = divmod(zc, nz2 // 2)
        lines[at * nx2:(at + 1) * nx2, part * LANES:(part + 1) * LANES] = (
            pairs[pl.ds(zc * nx1, nx2, 2), :] + pairs[pl.ds(zc * nx1 + 1, nx2, 2), :]
        )
    fine = iota((2 * LANES, LANES), 0)
    part, fine = fine // LANES, signed(fine % LANES, half, LANES)
    coarse = iota((2 * LANES, LANES), 1)
    table = as_table(
        (coarse // (LANES // 2) == part)
        & (signed(coarse % (LANES // 2), half // 2, LANES // 2) == (fine >> 1)), 0.5
    )
    share = right_dot(lines[...], table)
    pay[plan.edge:plan.edge + plan.share, :] = share

    per_tile = LANES // 16
    for group in range(nz1 // per_tile):
        tiles = []
        for which in range(2):
            total = jnp.zeros((nx1, LANES), F32)
            for j in range(per_tile):
                k = group * per_tile + j
                first = half - 3 if which == 0 else LANES - 4
                total = total + moved(r1_ref[k], first, 7, 16 * j)
                first = half - 2 if which == 0 else LANES - 3
                total = total + moved(x1_ref[k], first, 5, 16 * j + 7)
            tiles.append(total)
        here = slice(plan.fine_rows + group * nx1, plan.fine_rows + (group + 1) * nx1)
        pay[here, :] = jnp.where(up_now, tiles[0], tiles[1])
        later[here, :] = jnp.where(up_later, tiles[0], tiles[1])


def level_lateral(shape):
    row = iota(shape, 0)
    not_first = jnp.where(row > 0, 1.0, 0.0).astype(F32)
    not_last = jnp.where(row < shape[0] - 1, 1.0, 0.0).astype(F32)

    def beside(v):
        return (
            not_first * pltpu.roll(v, 1, 0) + not_last * pltpu.roll(v, shape[0] - 1, 0)
            + pltpu.roll(v, 1, 1) + pltpu.roll(v, LANES - 1, 1)
        )

    return beside


def small_cycle(level, source):
    step = 1 << (level - 2)
    row, lane = iota((8, LANES), 0), iota((8, LANES), 1)
    count = len(source)
    shifts = []
    if step < 8:
        shifts += [(step, 0, row >= step), (8 - step, 0, row < 8 - step)]
    shifts += [(step, 1, lane >= step), (LANES - step, 1, lane < LANES - step)]

    def op(v):
        out = []
        for k in range(count):
            beside = None
            for shift, dim, keep in shifts:
                part = only(keep, pltpu.roll(v[k], shift, dim))
                beside = part if beside is None else beside + part
            if k > 0:
                beside = beside + v[k - 1]
            if k < count - 1:
                beside = beside + v[k + 1]
            out.append(6.0 * v[k] - beside)
        return out

    d = [first_scale * v for v in source]
    r = [b - t for b, t in zip(source, op(d))]
    d2 = [carry_coef * v + fresh_coef * t for v, t in zip(d, r)]
    x = [v + t for v, t in zip(d, d2)]
    r = [v - t for v, t in zip(r, op(d2))]
    coarsest = None
    if level < LEVELS - 1:
        keep = only((row % (2 * step) == 0) & (lane % (2 * step) == 0), 0.5)
        coarse = []
        for k in range(0, count, 2):
            v = r[k] + r[k + 1]
            v = v + pltpu.roll(v, 8 - step, 0)
            coarse.append(keep * (v + pltpu.roll(v, LANES - step, 1)))
        coarse, coarsest = small_cycle(level + 1, coarse)
        e = []
        for v in coarse:
            v = v + pltpu.roll(v, step, 0)
            e += [v + pltpu.roll(v, step, 1)] * 2
        x = [v + t for v, t in zip(x, e)]
        r = [v - t for v, t in zip(r, op(e))]
    d = [first_scale * v for v in r]
    r = [v - t for v, t in zip(r, op(d))]
    x = [v + (t + (carry_coef * t + fresh_coef * u)) for v, t, u in zip(x, d, r)]
    return x, (x if level == LEVELS - 1 else coarsest)


def last_kernel(plan, r_in, x_in, r1_in, x1_in, ours, got, then, p_out, res_out, last_ref, *scratch):
    shares, p_ref, res_ref, r, q1, e1, e0, d0, d1, r1, lines, wide, sem = scratch
    bz, bx, by = plan.block
    ez, ex, ey = plan.ext
    nz1, nx1, _ = plan.level1
    nz2, nx2, ny2 = plan.level2
    layers, half = plan.layers, by // 2
    iz, z_low, z_high = place("gz", plan.peers[0])
    ix, x_low, x_high = place("gx", plan.peers[1])
    iy, y_low, y_high = place("gy", plan.peers[2])

    even = (iz & 1) == 0
    first = jnp.where(even, 1, 3)
    here = plan.edge + plan.share
    shares[0] = ours[plan.edge:here, :]
    shares[first] = got[plan.edge:here, :]
    shares[4 - first] = then[plan.edge:here, :]
    shares[2] = then[here:here + plan.share, :]
    lower = upper = None
    own2 = half // 2
    for j in range(plan.peers[2]):
        v = shares[iy ^ j]
        at = own2 * j
        mid = LANES // 2
        low = moved(v, 0, own2 + 2, at) + moved(v, mid - 2, 2, at - 2)
        high = moved(v, mid, own2 + 2, at) + moved(v, LANES - 2, 2, at - 2)
        lower = low if lower is None else lower + low
        upper = high if upper is None else upper + high
    source = [lower[8 * k:8 * k + 8] for k in range(nz2 // 2)]
    source += [upper[8 * k:8 * k + 8] for k in range(nz2 // 2)]
    e2, coarsest = small_cycle(2, source)
    for k in range(nz2):
        lines[k * nx2:(k + 1) * nx2, :] = e2[k]
    thin = as_table(iota((LANES, LANES), 0) == 8 * iota((LANES, LANES), 1))
    for k in range(last_ref.shape[0]):
        last_ref[k] = right_dot(coarsest[k], thin)[0:1, 0:last_ref.shape[2]]

    up_a, _ = side(iy, 1)
    _, near_b = side(iy, 3)

    def sent(rows):
        a, b = got[rows[0]:rows[1], :], then[rows[0]:rows[1], :]
        a, b = jnp.where(even, a, b), only(near_b, jnp.where(even, b, a))
        return jnp.where(up_a, a, b), jnp.where(up_a, b, a)

    fine = signed(iota((LANES, LANES), 1), half, LANES)
    coarse = iota((LANES, LANES), 0) - iy * own2
    e2 = right_dot(lines[...], as_table((fine >> 1) == coarse))
    for zc in range(nz2):
        v = e2[zc * nx2:(zc + 1) * nx2]
        for part in range(2):
            q1.at[2 * zc + part][pl.ds(0, nx2, 2), :] = v
            q1.at[2 * zc + part][pl.ds(1, nx2, 2), :] = v
    per_tile = LANES // 16
    lateral1 = level_lateral((nx1, LANES))
    keep = wrapped_mask((nx1, LANES), {1: half}, (None, y_low), (None, y_high))
    for group in range(nz1 // per_tile):
        at = plan.fine_rows + group * nx1
        high, low = sent((at, at + nx1))
        for j in range(per_tile):
            k = group * per_tile + j
            s = 16 * j
            r1[k] = (
                r1_in[k] + moved(high, s, 7, half - 4) + moved(low, s, 7, LANES - 3)
                - apply_at(q1, k, lateral1)
            )
            e1[k + 2, 8:8 + nx1, :] = (
                x1_in[k] + q1[k]
                + moved(high, s + 7, 5, half - 3) + moved(low, s + 7, 5, LANES - 2)
            )
    for k in range(nz1):
        d1[k] = keep * (r1[k] * first_scale)
    nothing = jnp.zeros((8, LANES), F32)
    for k in range(nz1 + 4):
        e1[k, 0:8, :] = nothing
        e1[k, 8 + nx1:16 + nx1, :] = nothing
        if not 2 <= k < nz1 + 2:
            e1[k, 8:8 + nx1, :] = jnp.zeros((nx1, LANES), F32)
    for k in range(nz1):
        v = r1[k] - apply_at(d1, k, lateral1)
        e1[k + 2, 8:8 + nx1, :] += d1[k] + keep * (carry_coef * d1[k] + fresh_coef * v)

    coarse = signed(iota((LANES, ey), 0), half, LANES)
    fine = signed(iota((LANES, ey), 1), by, ey)
    double = as_table((fine >> 1) == coarse)
    half_z, half_x = bz // 2, bx // 2
    for zc in range(half_z + 4):
        start = pl.multiple_of(ix * half_x, 8)
        v = e1[iz * half_z + zc, pl.ds(start, half_x + 16), :]
        own, low, high = v[8:8 + half_x], v[0:8], v[8 + half_x:16 + half_x]
        at = zc * ex
        wide[pl.ds(at, half_x, 2), :] = own
        wide[pl.ds(at + 1, half_x, 2), :] = own
        for j in range(2):
            for twin in range(2):
                row = at + bx + 2 * j + twin
                wide[row:row + 1, :] = high[j:j + 1]
                row = at + ex - 4 + 2 * j + twin
                wide[row:row + 1, :] = low[6 + j:7 + j]
    for zc in range(half_z + 4):
        v = right_dot(wide[zc * ex:(zc + 1) * ex, :], double)
        for k in (2 * zc - 1, 2 * zc):
            if 0 <= k < ez:
                e0[k] = v
    flat = wrapped_mask((ex, ey), {0: bx, 1: by}, (x_low, y_low), (x_high, y_high))
    below = jnp.where(z_low, 1.0, 0.0).astype(F32)
    above = jnp.where(z_high, 1.0, 0.0).astype(F32)

    def masked(k, v):
        v = v * flat
        if k < 3:
            v = v * below
        if k >= 3 + bz:
            v = v * above
        return v

    for group in range(plan.y_groups):
        high, low = sent((group * ex, (group + 1) * ex))
        for k in range(group * SLOTS, min(layers, (group + 1) * SLOTS)):
            s = 8 * (k - group * SLOTS)
            v = r_in[k] - apply_at(e0, k + 1)
            r[k, :, 0:by] = v[:, 0:by] + moved(high, s, 3, LANES - 3) + moved(low, s + 2, 3, 0)
            r[k, :, by:ey] = v[:, by:ey] + moved(high, s + 3, 2, 0) + moved(low, s, 2, LANES - 2)
            d0[k] = masked(k + 1, r[k] * first_scale)
            if 2 <= k < 2 + bz:
                p_ref[k - 2] = (
                    x_in[k - 2] + e0[k + 1, 0:bx, 0:by]
                    + (moved(high, s + 5, 2, LANES - 2) + moved(low, s + 5, 2, 0))[0:bx]
                )
    for k in range(1, layers - 1):
        v = r[k] - apply_at(d0, k)
        r[k] = v
        v = masked(k + 1, carry_coef * d0[k] + fresh_coef * v)
        e0[k] = v
        if 2 <= k < 2 + bz:
            p_ref[k - 2] += d0[k, 0:bx, 0:by] + v[0:bx, 0:by]
    copy = pltpu.make_async_copy(p_ref, p_out, sem.at[0])
    copy.start()
    copies = [copy]
    parts = 2
    for part in range(parts):
        here = range(part * bz // parts, (part + 1) * bz // parts)
        for j in here:
            v = r[j + 2] - apply_at(e0, j + 2)
            res_ref[j] = v[0:bx, 0:by]
        here = pl.ds(here[0], bz // parts)
        copy = pltpu.make_async_copy(res_ref.at[here], res_out.at[here], sem.at[1 + part])
        copy.start()
        copies.append(copy)
    for copy in copies:
        copy.wait()


def whole(shape):
    return jax.ShapeDtypeStruct(shape, F32)


VMEM = pl.BlockSpec(memory_space=pltpu.VMEM)
ANY = pl.BlockSpec(memory_space=pl.ANY)
HBM = pl.BlockSpec(memory_space=pltpu.HBM)
VMEM_BYTES = 24 << 20


def run(kernel, plan, outs, scratch, *operands, in_specs=None, out_specs=None, semaphores=0):
    scratch = [pltpu.VMEM(s, F32) for s in scratch]
    if semaphores:
        scratch.append(pltpu.SemaphoreType.DMA((semaphores,)))
    return pl.pallas_call(
        functools.partial(kernel, plan),
        out_shape=[whole(s) for s in outs],
        in_specs=in_specs or [VMEM] * len(operands),
        out_specs=out_specs or [VMEM] * len(outs),
        scratch_shapes=scratch,
        compiler_params=pltpu.CompilerParams(vmem_limit_bytes=VMEM_BYTES),
    )(*operands)


def swap(values, partner):
    axes = ("gx", "gy", "gz")
    counts = [lax.axis_size(a) for a in axes]
    pairs = []
    for i in range(counts[0] * counts[1] * counts[2]):
        x, y, z = partner(i // (counts[1] * counts[2]), i // counts[2] % counts[1], i % counts[2])
        pairs.append((i, (x * counts[1] + y) * counts[2] + z))
    return lax.ppermute(values, axes, pairs)


def body_fast(divergence, pressure_prev):
    plan = Plan(divergence.shape, tuple(lax.axis_size(a) for a in ("gz", "gx", "gy")))
    ext, level1 = plan.ext, plan.level1
    payload = [(plan.slab + n * plan.coarse, LANES) for n in (1, 2, 4)]
    r, x, ours = run(
        first_kernel, plan, [ext, ext, payload[0]],
        [plan.block, plan.block, ext, ext, ext, ext, (2, 2 * plan.pairs * plan.ex, LANES),
         (2, plan.lat_at, plan.ey)],
        divergence, pressure_prev, in_specs=[HBM, HBM], semaphores=2,
    )
    got = swap(ours, lambda x, y, z: (x, y, z ^ 3) if z in (1, 2) else (x ^ 1, y, z))
    r, x, ours = run(step_kernel, plan, [ext, ext, payload[1]], [], r, x, ours, got)
    got = swap(ours, lambda x, y, z: (x ^ 1, y, z) if z in (1, 2) else (x, y, z ^ 3))
    r, x, ours = run(core_kernel, plan, [ext, ext, payload[2]], [], r, x, ours, got)
    got = swap(ours, lambda x, y, z: (x, y, z ^ 1))
    nz2, nx2, _ = plan.level2
    layers = (plan.layers, plan.ex, plan.ey)
    r, x, r1, x1, ours, later = run(
        plane_kernel, plan,
        [layers, plan.block, level1, level1, (plan.edge + plan.share, LANES), (plan.edge, LANES)],
        [ext, ext, level1, level1, level1, (nz2 * level1[1], LANES), (plan.share, 2 * LANES)],
        r, x, ours, got,
    )
    got = swap(ours, lambda x, y, z: (x, y ^ (1, 3)[z & 1], z))
    then = jnp.concatenate([later, ours[plan.edge:], got[plan.edge:]], axis=0)
    then = swap(then, lambda x, y, z: (x, y ^ (3, 1)[z & 1], z))
    return run(
        last_kernel, plan,
        [plan.block, plan.block, tuple(n >> 3 for n in plan.level2)],
        [(4, plan.share, LANES), plan.block, plan.block, layers, level1,
         (level1[0] + 4, level1[1] + 16, LANES), ext, layers, level1, level1,
         (nz2 * nx2, LANES), (2 * plan.pairs * plan.ex, LANES)],
        r, x, r1, x1, ours, got, then,
        out_specs=[ANY, ANY, VMEM], semaphores=3,
    )


def fits_fast(shape, peers):
    bz, bx, by = shape
    nz, nx, ny = peers
    return (
        nz == 4 and nx == 2 and ny == 4 and bz == 16 and by == LANES
        and nx * bx == 4 * 8 and ny * by == 4 * LANES
    )


def body(divergence, pressure_prev):
    peers = tuple(lax.axis_size(a) for a in ("gz", "gx", "gy"))
    if fits_fast(divergence.shape, peers):
        return tuple(body_fast(divergence, pressure_prev))
    return body_levels(divergence, pressure_prev)


def solution(mesh):
    in_specs = (P("gz", "gx", "gy"), P("gz", "gx", "gy"))
    out_specs = (P("gz", "gx", "gy"), P("gz", "gx", "gy"), P())
    return jax.shard_map(body, mesh=mesh, in_specs=in_specs, out_specs=out_specs, check_vma=False)
```

```python
import functools

import jax
import jax.numpy as jnp
from jax import lax
from jax.experimental import pallas as pl
from jax.experimental.pallas import tpu as pltpu
from jax.sharding import PartitionSpec as P

LEVELS = 6


first_scale = 1.0 / 7.5
rho_one = 1.0 / (2.0 * (5.0 / 3.0) - 0.6)
carry_coef = 0.6 * rho_one
fresh_coef = 2.0 * rho_one / (0.75 * 6.0)

LANES = 128
F32 = jnp.float32
AXES = (("gz", 0), ("gx", 1), ("gy", 2))


def extended(x, width):
    for axis, dim in AXES:
        peers, length = (lax.axis_size(axis), x.shape[dim + 1])
        up = [(i, (i + 1) % peers) for i in range(peers - 1)]
        down = [(j, i) for i, j in up]
        last = lax.slice_in_dim(x, length - width, length, axis=dim + 1)
        first = lax.slice_in_dim(x, 0, width, axis=dim + 1)
        before = lax.ppermute(last, axis, up)
        after = lax.ppermute(first, axis, down)
        x = jnp.concatenate([before, x, after], axis=dim + 1)
    return x


def stencil(values):
    padded = jnp.pad(values, 1)
    return valid_op(padded)


def valid_op(padded):
    beside = padded[2:, 1:-1, 1:-1] + padded[:-2, 1:-1, 1:-1]
    beside = beside + padded[1:-1, 2:, 1:-1] + padded[1:-1, :-2, 1:-1]
    beside = beside + padded[1:-1, 1:-1, 2:] + padded[1:-1, 1:-1, :-2]
    return 6.0 * padded[1:-1, 1:-1, 1:-1] - beside


def smooth_pass(iterate, source, apply_op, from_zero):
    residue = source if from_zero else source - apply_op(iterate)
    update = residue * first_scale
    iterate = update if from_zero else iterate + update
    residue = source - apply_op(iterate)
    update = carry_coef * update + fresh_coef * residue
    return iterate + update


def restrict(values):
    shape_a, shape_b, shape_c = values.shape
    blocks = values.reshape(shape_a // 2, 2, shape_b // 2, 2, shape_c // 2, 2)
    return 0.5 * jnp.sum(blocks, axis=(1, 3, 5))


def prolong(values):
    shape_a, shape_b, shape_c = values.shape
    spread = jnp.broadcast_to(
        values[:, None, :, None, :, None], (shape_a, 2, shape_b, 2, shape_c, 2)
    )
    return spread.reshape(2 * shape_a, 2 * shape_b, 2 * shape_c)


def vcycle(level_num, iterate, source):
    iterate = smooth_pass(iterate, source, stencil, True)
    coarsest = None
    if level_num < LEVELS - 1:
        residue = source - stencil(iterate)
        coarse, coarsest = vcycle(level_num + 1, None, restrict(residue))
        iterate = iterate + prolong(coarse)
    result = smooth_pass(iterate, source, stencil, False)
    if level_num == LEVELS - 1:
        coarsest = result
    return (result, coarsest)


def collect(values):
    gathered = lax.all_gather(values, "gz", axis=0, tiled=True)
    gathered = lax.all_gather(gathered, "gy", axis=2, tiled=True)
    return lax.all_gather(gathered, "gx", axis=1, tiled=True)


def local_stencil(values):
    return valid_op(extended(values[None], 1)[0])


def own_block(whole, block_shape):
    start_z = lax.axis_index("gz") * block_shape[0]
    start_x = lax.axis_index("gx") * block_shape[1]
    start_y = lax.axis_index("gy") * block_shape[2]
    return lax.dynamic_slice(whole, (start_z, start_x, start_y), block_shape)


def body_cycle(level_num, iterate, source, from_zero, gather_at):
    if level_num == gather_at:
        whole_source = collect(source)
        coarse, coarsest = vcycle(level_num, None, whole_source)
        return (own_block(coarse, source.shape), coarsest)
    iterate = smooth_pass(iterate, source, local_stencil, from_zero)
    residue = source - local_stencil(iterate)
    coarse, coarsest = body_cycle(level_num + 1, None, restrict(residue), True, gather_at)
    iterate = iterate + prolong(coarse)
    return (smooth_pass(iterate, source, local_stencil, False), coarsest)


def body_levels(divergence, pressure_prev):
    pressure, coarse_correction = body_cycle(0, pressure_prev, divergence, False, 3)
    residual = divergence - local_stencil(pressure)
    return (pressure, residual, coarse_correction)


def iota(shape, dim):
    return lax.broadcasted_iota(jnp.int32, shape, dim)


def signed(index, size, extent):
    return jnp.where(index >= (size + extent) // 2, index - extent, index)


def split(values):
    terms = []
    for _ in range(3):
        term = values.astype(jnp.bfloat16)
        terms.append(term)
        values = values - term.astype(F32)
    return terms


def right_dot(values, table):
    parts = [jnp.dot(t, table, preferred_element_type=F32) for t in split(values)]
    return parts[0] + parts[1] + parts[2]


def left_dot(table, values):
    parts = [jnp.dot(table, t, preferred_element_type=F32) for t in split(values)]
    return parts[0] + parts[1] + parts[2]


def as_table(keep, value=1.0):
    return jnp.where(keep, value, 0.0).astype(jnp.bfloat16)


def lateral(v):
    rows, lanes = v.shape
    return (
        pltpu.roll(v, 1, 0) + pltpu.roll(v, rows - 1, 0)
        + pltpu.roll(v, 1, 1) + pltpu.roll(v, lanes - 1, 1)
    )


def apply_at(ref, k, lateral_of=lateral):
    centre = ref[k]
    beside = lateral_of(centre)
    if k > 0:
        beside = beside + ref[k - 1]
    if k < ref.shape[0] - 1:
        beside = beside + ref[k + 1]
    return 6.0 * centre - beside


def wrapped_mask(shape, sizes, low, high):
    keep = None
    for dim, size in sizes.items():
        at = signed(iota(shape, dim), size, shape[dim])
        good = ((at >= 0) | low[dim]) & ((at < size) | high[dim])
        keep = good if keep is None else keep & good
    return jnp.where(keep, 1.0, 0.0).astype(F32)


def side(index, flip):
    if flip == 1:
        return (index & 1) == 0, None
    return index < 2, (index == 1) | (index == 2)


def place(axis, count):
    index = lax.axis_index(axis)
    return index, index > 0, index < count - 1


def only(keep, v):
    return jnp.where(keep, v, 0.0)


def shifted(v, lanes):
    lanes = lanes % LANES
    return v if lanes == 0 else pltpu.roll(v, lanes, 1)


def lanes_of(v, first, count):
    lane = iota(v.shape, 1)
    last = first + count
    if last <= LANES:
        return (lane >= first) & (lane < last)
    return (lane >= first) | (lane < last - LANES)


def moved(v, first, count, to):
    first = first % LANES
    return shifted(only(lanes_of(v, first, count), v), to - first)


def side_pack(tile, slot):
    return moved(tile, LANES - 3, 6, 8 * slot)


def side_unpack(packed, slot):
    return moved(packed, 8 * slot, 6, LANES - 3)


SLOTS = LANES // 8


def slab_emit(r_ref, x_ref, out, at, up):
    ez, ex, _ = r_ref.shape
    start = jnp.where(up, ez - 5, 0)
    start_x = jnp.where(up, ez - 3, 1)
    lat = None
    for j in range(7):
        v = r_ref[start + j] if j < 5 else x_ref[start_x + j - 5]
        out[at + j * ex:at + (j + 1) * ex, :] = v[:, 0:LANES]
        part = side_pack(v[:, LANES:], j)
        lat = part if lat is None else lat + part
    out[at + 7 * ex:at + 8 * ex, :] = lat


def slab_add(r_ref, x_ref, slab, at, up):
    ez, ex, _ = r_ref.shape
    start = jnp.where(up, ez - 6, 1)
    start_x = jnp.where(up, ez - 5, 3)
    lat = slab[at + 7 * ex:at + 8 * ex, :]
    for j in range(7):
        ref, k = (r_ref, start + j) if j < 5 else (x_ref, start_x + j - 5)
        ref[k, :, 0:LANES] += slab[at + j * ex:at + (j + 1) * ex, :]
        ref[k, :, LANES:] += side_unpack(lat, j)


def rows_out(r, x, up):
    bx = r.shape[0] - 8
    row = iota((8, r.shape[1]), 0)
    first, last, spill = r[0:8], r[bx - 8:bx], r[bx:]
    to_high = pltpu.roll(jnp.where(row >= 6, last, spill), 2, 0)
    to_low = pltpu.roll(jnp.where(row >= 5, spill, first), 3, 0)
    out = jnp.where(up, to_high, to_low)
    if x is None:
        return only(row < 5, out)
    spill = x[bx:]
    extra = jnp.where(up, pltpu.roll(spill, 5, 0), pltpu.roll(spill, 7, 0))
    return jnp.where(row < 5, out, only(row < 7, extra))


def rows_in(r_ref, x_ref, k, rows, up):
    bx = r_ref.shape[1] - 8
    row = iota(rows.shape, 0)
    high, low = pltpu.roll(rows, 5, 0), pltpu.roll(rows, 6, 0)
    r_ref[k, 0:8] += only(jnp.logical_not(up) & (row < 3), low)
    r_ref[k, bx - 8:bx] += only(up & (row >= 5), high)
    r_ref[k, bx:] += jnp.where(up, only(row < 2, high), only(row >= 6, low))
    if x_ref is not None:
        x_ref[k, 0:8] += only(jnp.logical_not(up) & (row < 2), pltpu.roll(rows, 3, 0))
        x_ref[k, bx - 8:bx] += only(up & (row >= 6), pltpu.roll(rows, 1, 0))


def rows_emit(r_ref, x_ref, out, up):
    ez = r_ref.shape[0]
    for group in range(-(-ez // SLOTS)):
        lat = jnp.zeros((8, LANES), F32)
        for k in range(group * SLOTS, min(ez, (group + 1) * SLOTS)):
            rows = rows_out(r_ref[k], x_ref[k], up)
            out[8 * k:8 * k + 8, :] = rows[:, 0:LANES]
            lat = lat + side_pack(rows[:, LANES:], k - group * SLOTS)
        out[8 * (ez + group):8 * (ez + group) + 8, :] = lat


def rows_add(r_ref, x_ref, slab, up):
    ez = r_ref.shape[0]
    for k in range(ez):
        at = 8 * (ez + k // SLOTS)
        lat = side_unpack(slab[at:at + 8, :], k % SLOTS)
        rows = jnp.concatenate([slab[8 * k:8 * k + 8, :], lat], axis=1)
        rows_in(r_ref, x_ref, k, rows, up)


class Plan:
    def __init__(self, shape, peers):
        self.peers = peers
        self.block = bz, bx, by = shape
        self.ext = self.ez, self.ex, self.ey = bz + 6, bx + 8, by + LANES
        self.rows, self.pairs = bx // 2, bz // 4 + 2
        self.lat_at = self.pairs * (self.rows + 4)
        self.coarse = self.lat_at + 16
        self.x_groups = -(-self.ez // SLOTS)
        self.slab = max(8 * self.ex, (self.ez + self.x_groups) * 8)
        self.layers = bz + 4
        self.level1 = (peers[0] * bz // 2, peers[1] * bx // 2, LANES)
        self.level2 = (peers[0] * bz // 4, peers[1] * bx // 4, peers[2] * by // 4)
        self.inner = [0, 1] + [2] * bz + [1, 0]
        self.slots, at = [], 0
        for count in self.inner:
            self.slots.append(at)
            at += 3 + count + (2 if count == 2 else 0)
        assert at <= LANES
        self.fine_rows = self.ex
        self.edge = self.fine_rows + self.level1[0] * self.level1[1] // 8
        self.wide2 = by // 4 + 4
        self.fold = LANES // self.wide2
        self.lines2 = -(-self.level2[0] // self.fold)
        self.share = self.lines2 * self.level2[1]


def first_kernel(plan, both, r_ref, x_ref, pay, d_one, d_two, pairs, lines):
    p_ext, b_ext = both.at[0], both.at[1]
    bz, bx, by = plan.block
    ez, ex, ey = plan.ext
    peers = plan.peers
    iz, z_low, z_high = place("gz", peers[0])
    ix, x_low, x_high = place("gx", peers[1])
    _, y_low, y_high = place("gy", peers[2])
    flat = wrapped_mask((ex, ey), {0: bx, 1: by}, (x_low, y_low), (x_high, y_high))
    below = jnp.where(z_low, 1.0, 0.0).astype(F32)
    above = jnp.where(z_high, 1.0, 0.0).astype(F32)

    def masked(k, v):
        v = v * flat
        if k < 3:
            v = v * below
        if k >= 3 + bz:
            v = v * above
        return v

    zero = jnp.zeros((ex, ey), F32)
    for k in range(ez):
        if 2 <= k < ez - 2:
            r = b_ext[k] - apply_at(p_ext, k)
            r_ref[k] = r
            d_one[k] = masked(k, r * first_scale)
        else:
            d_one[k] = zero
    for k in range(ez):
        if 1 <= k < ez - 1:
            r = -apply_at(d_one, k)
            if 2 <= k < ez - 2:
                r = r + r_ref[k]
            r_ref[k] = r
            d_two[k] = masked(k, carry_coef * d_one[k] + fresh_coef * r)
        else:
            d_two[k] = zero
    for k in range(ez):
        r = -apply_at(d_two, k)
        if 1 <= k < ez - 1:
            r = r + r_ref[k]
        r_ref[k] = masked(k, r)
        x_ref[k] = p_ext[k] + d_one[k] + d_two[k]


    coarse_z, rows = 2 * plan.pairs, plan.rows
    for zc in range(coarse_z):
        low, high = 2 * zc - 1, 2 * zc
        if low < 0:
            total = r_ref[high]
        elif high >= ez:
            total = r_ref[low]
        else:
            total = r_ref[low] + r_ref[high]
        base = zc * ex
        for tile in range(ey // LANES):
            here = slice(tile * LANES, (tile + 1) * LANES)
            pairs[tile, base:base + ex, :] = total[:, here]
            even = pairs.at[tile][pl.ds(base, ex // 2, 2), :]
            odd = pairs.at[tile][pl.ds(base + 1, ex // 2, 2), :]
            sums = even + odd
            at = zc // 2 * rows
            lines[zc % 2, at:at + rows, here] = sums[0:rows]
            at = plan.pairs * rows + zc // 2 * 4
            lines[zc % 2, at:at + 4, here] = sums[rows:rows + 4]
    fine = signed(iota((ey, LANES), 0), by, ey)
    coarse = signed(iota((ey, LANES), 1), by // 2, LANES)
    table = as_table((fine >> 1) == coarse, 0.5)
    even, odd = right_dot(lines[0], table), right_dot(lines[1], table)
    lane = iota(even.shape, 1)
    at = plan.slab
    pay[at:at + plan.lat_at, :] = jnp.where(lane < LANES // 2, even, shifted(odd, LANES // 2))
    own_lat = spill_lat = None
    row = iota((8, LANES), 0)
    for zc in range(coarse_z):
        source = (even, odd)[zc % 2]
        base = zc // 2 * rows
        tile = source[base:base + rows]
        part = moved(tile, by // 2, 2, 4 * zc) + moved(tile, LANES - 2, 2, 4 * zc + 2)
        own_lat = part if own_lat is None else own_lat + part
        base = plan.pairs * rows + zc // 4 * 8
        tile = source[base:base + 8]
        if zc // 2 % 2:
            tile = pltpu.roll(tile, 4, 0)
        tile = only(row < 4, tile)
        part = moved(tile, by // 2, 2, 4 * zc) + moved(tile, LANES - 2, 2, 4 * zc + 2)
        spill_lat = part if spill_lat is None else spill_lat + part
    at = plan.slab + plan.lat_at
    pay[at:at + 8, :] = own_lat
    pay[at + 8:at + 16, :] = spill_lat
    inner = (iz == 1) | (iz == 2)

    @pl.when(inner)
    def _():
        slab_emit(r_ref, x_ref, pay, 0, side(iz, 3)[0])

    @pl.when(jnp.logical_not(inner))
    def _():
        rows_emit(r_ref, x_ref, pay, side(ix, 1)[0])


def step_kernel(plan, r_in, x_in, ours, got, r_ref, x_ref, pay):
    iz, _, _ = place("gz", plan.peers[0])
    ix, _, _ = place("gx", plan.peers[1])
    up_z, inner = side(iz, 3)
    up_x, _ = side(ix, 1)
    for k in range(plan.ez):
        r_ref[k] = r_in[k]
        x_ref[k] = x_in[k]

    @pl.when(inner)
    def _():
        slab_add(r_ref, x_ref, got, 0, up_z)
        rows_emit(r_ref, x_ref, pay, up_x)

    @pl.when(jnp.logical_not(inner))
    def _():
        rows_add(r_ref, x_ref, got, up_x)
        pay[0:plan.slab, :] = jnp.zeros((plan.slab, LANES), F32)

    for j, ref in enumerate((ours, got)):
        here = plan.slab + j * plan.coarse
        pay[here:here + plan.coarse, :] = ref[plan.slab:plan.slab + plan.coarse, :]


def core_kernel(plan, r_in, x_in, ours, got, r_ref, x_ref, pay):
    iz, _, _ = place("gz", plan.peers[0])
    ix, _, _ = place("gx", plan.peers[1])
    _, inner = side(iz, 3)
    up_x, _ = side(ix, 1)
    for k in range(plan.ez):
        r_ref[k] = r_in[k]
        x_ref[k] = x_in[k]

    @pl.when(inner)
    def _():
        rows_add(r_ref, x_ref, got, up_x)

    slab_emit(r_ref, x_ref, pay, 0, side(iz, 1)[0])
    for j, ref in enumerate((ours, got)):
        here = plan.slab + 2 * j * plan.coarse
        pay[here:here + 2 * plan.coarse, :] = ref[plan.slab:plan.slab + 2 * plan.coarse, :]


def plane_kernel(plan, r_in, x_in, ours, theirs, r_ref, x_ref, r1_ref, x1_ref, pay, later, share,
                 r_all, x_all, b1, d1, d2, pairs, lines):
    bz, bx, by = plan.block
    ez, ex, ey = plan.ext
    layers = plan.layers
    iz, _, _ = place("gz", plan.peers[0])
    ix, _, _ = place("gx", plan.peers[1])
    iy, y_low, y_high = place("gy", plan.peers[2])
    up_z, _ = side(iz, 1)
    for k in range(ez):
        r_all[k] = r_in[k]
        x_all[k] = x_in[k]
    slab_add(r_all, x_all, theirs, 0, up_z)
    for k in range(layers):
        r_ref[k] = r_all[k + 1]
    for k in range(bz):
        x_ref[k] = x_all[k + 3, 0:bx, 0:by]

    up, _ = side(iy, 1)
    up_inner, _ = side(iy, 3)
    high, low = jnp.zeros((ex, LANES), F32), jnp.zeros((ex, LANES), F32)
    for k in range(layers):
        slot, inner = plan.slots[k], plan.inner[k]
        count = 3 + inner
        v, spill = r_all[k + 1, :, 0:by], r_all[k + 1, :, by:ey]
        high = high + moved(jnp.where(lanes_of(v, 0, 3), spill, v), LANES - inner, count, slot)
        mixed = jnp.where(lanes_of(v, 0, 2), v, spill)
        low = low + moved(mixed, LANES - 3, count, slot)
        if inner == 2:
            spill = x_all[k + 1, :, by:ey]
            high = high + moved(spill, 0, 2, slot + count)
            low = low + moved(spill, LANES - 2, 2, slot + count)
    pay[0:ex, :] = jnp.where(up, high, low)
    later[0:ex, :] = jnp.where(up_inner, high, low)

    nz1, nx1, _ = plan.level1
    rows, half = plan.rows, by // 2
    for k in range(nz1):
        b1[k] = jnp.zeros((nx1, LANES), F32)
    row = iota((8, LANES), 0)
    for j in range(plan.peers[0]):
        for i in range(plan.peers[1]):
            flip = iz ^ j
            other = ((flip ^ (flip >> 1)) & 1) == 1
            along_z, along_x = flip >> 1, ix ^ i
            met_z = ((iz == 1) | (iz == 2)) ^ other
            chip = jnp.where(met_z, along_z + 2 * along_x, along_x + 2 * along_z)
            at = pl.multiple_of(plan.slab + chip * plan.coarse, 8)

            def rows_at(offset, count):
                here = pl.ds(pl.multiple_of(at + offset, 8), count)
                return jnp.where(other, theirs[here, :], ours[here, :])

            own_lat = rows_at(plan.lat_at, 8)
            spill_lat = rows_at(plan.lat_at + 8, 8)
            for zp in range(plan.pairs):
                own = rows_at(zp * rows, rows)
                if zp % 2 == 0:
                    spill_two = rows_at(plan.pairs * rows + zp * 4, 8)
                spill = spill_two if zp % 2 == 0 else pltpu.roll(spill_two, 4, 0)
                for part in range(2):
                    zc = 2 * zp + part
                    k = j * (bz // 2) + zc - 2
                    if not 0 <= k < nz1:
                        continue

                    def wide(main, lat):
                        return (
                            moved(main, part * half, half, 0)
                            + moved(lat, 4 * zc, 2, half) + moved(lat, 4 * zc + 2, 2, LANES - 2)
                        )

                    b1[k, i * rows:(i + 1) * rows, :] += wide(own, own_lat)
                    v = wide(spill, spill_lat)
                    if i + 1 < plan.peers[1]:
                        at_row = (i + 1) * rows
                        b1[k, at_row:at_row + 8, :] += only(row < 2, v)
                    if i > 0:
                        at_row = i * rows - 8
                        b1[k, at_row:at_row + 8, :] += only(row >= 6, pltpu.roll(v, 4, 0))

    lateral1 = level_lateral((nx1, LANES))
    keep = wrapped_mask((nx1, LANES), {1: half}, (None, y_low), (None, y_high))
    for k in range(nz1):
        d1[k] = b1[k] * first_scale
    for k in range(nz1):
        r = b1[k] - apply_at(d1, k, lateral1)
        r1_ref[k] = r
        d2[k] = keep * (carry_coef * d1[k] + fresh_coef * r)
    for k in range(nz1):
        r1_ref[k] = keep * (r1_ref[k] - apply_at(d2, k, lateral1))
        x1_ref[k] = d1[k] + d2[k]

    nz2, nx2, _ = plan.level2
    for zc in range(nz2):
        pairs[zc * nx1:(zc + 1) * nx1, :] = r1_ref[2 * zc] + r1_ref[2 * zc + 1]
        part, at = divmod(zc, plan.lines2)
        lines[part, at * nx2:(at + 1) * nx2, :] = (
            pairs[pl.ds(zc * nx1, nx2, 2), :] + pairs[pl.ds(zc * nx1 + 1, nx2, 2), :]
        )
    fine = signed(iota((LANES, LANES), 0), half, LANES)
    total = None
    for part in range(plan.fold):
        count = min(plan.lines2, nz2 - part * plan.lines2) * nx2
        if count < plan.share:
            lines[part, count:, :] = jnp.zeros((plan.share - count, LANES), F32)
        coarse = iota((LANES, LANES), 1) - part * plan.wide2 - 2
        near = (coarse >= -2) & (coarse < plan.wide2 - 2)
        term = right_dot(lines[part], as_table(near & ((fine >> 1) == coarse), 0.5))
        total = term if total is None else total + term
    share[...] = total
    pay[plan.edge:plan.edge + plan.share, :] = total

    per_tile = LANES // 16
    for group in range(nz1 // per_tile):
        tiles = []
        for which in range(2):
            total = jnp.zeros((nx1, LANES), F32)
            for j in range(per_tile):
                k = group * per_tile + j
                first = half - 3 if which == 0 else LANES - 4
                total = total + moved(r1_ref[k], first, 7, 16 * j)
                first = half - 2 if which == 0 else LANES - 3
                total = total + moved(x1_ref[k], first, 5, 16 * j + 7)
            tiles.append(total)
        here = slice(plan.fine_rows + group * nx1, plan.fine_rows + (group + 1) * nx1)
        pay[here, :] = jnp.where(up, tiles[0], tiles[1])
        later[here, :] = jnp.where(up_inner, tiles[0], tiles[1])


def level_lateral(shape):
    row = iota(shape, 0)
    not_first = jnp.where(row > 0, 1.0, 0.0).astype(F32)
    not_last = jnp.where(row < shape[0] - 1, 1.0, 0.0).astype(F32)

    def beside(v):
        return (
            not_first * pltpu.roll(v, 1, 0) + not_last * pltpu.roll(v, shape[0] - 1, 0)
            + pltpu.roll(v, 1, 1) + pltpu.roll(v, LANES - 1, 1)
        )

    return beside


def small_cycle(level, source):
    step = 1 << (level - 2)
    row, lane = iota((8, LANES), 0), iota((8, LANES), 1)
    count = len(source)
    shifts = []
    if step < 8:
        shifts += [(step, 0, row >= step), (8 - step, 0, row < 8 - step)]
    shifts += [(step, 1, lane >= step), (LANES - step, 1, lane < LANES - step)]

    def op(v):
        out = []
        for k in range(count):
            beside = None
            for shift, dim, keep in shifts:
                part = only(keep, pltpu.roll(v[k], shift, dim))
                beside = part if beside is None else beside + part
            if k > 0:
                beside = beside + v[k - 1]
            if k < count - 1:
                beside = beside + v[k + 1]
            out.append(6.0 * v[k] - beside)
        return out

    d = [first_scale * v for v in source]
    r = [b - t for b, t in zip(source, op(d))]
    d2 = [carry_coef * v + fresh_coef * t for v, t in zip(d, r)]
    x = [v + t for v, t in zip(d, d2)]
    r = [v - t for v, t in zip(r, op(d2))]
    coarsest = None
    if level < LEVELS - 1:
        keep = only((row % (2 * step) == 0) & (lane % (2 * step) == 0), 0.5)
        coarse = []
        for k in range(0, count, 2):
            v = r[k] + r[k + 1]
            v = v + pltpu.roll(v, 8 - step, 0)
            coarse.append(keep * (v + pltpu.roll(v, LANES - step, 1)))
        coarse, coarsest = small_cycle(level + 1, coarse)
        e = []
        for v in coarse:
            v = v + pltpu.roll(v, step, 0)
            e += [v + pltpu.roll(v, step, 1)] * 2
        x = [v + t for v, t in zip(x, e)]
        r = [v - t for v, t in zip(r, op(e))]
    d = [first_scale * v for v in r]
    r = [v - t for v, t in zip(r, op(d))]
    x = [v + (t + (carry_coef * t + fresh_coef * u)) for v, t, u in zip(x, d, r)]
    return x, (x if level == LEVELS - 1 else coarsest)


def last_kernel(plan, r_in, x_in, r1_in, x1_in, ours, from_a, from_b, from_3, from_2, p_out, res_out, last_ref, *scratch):
    shares, p_ref, res_ref, r, q1, e1, e0, d0, d1, r1, lines, wide, sem = scratch
    bz, bx, by = plan.block
    ez, ex, ey = plan.ext
    nz1, nx1, _ = plan.level1
    nz2, nx2, ny2 = plan.level2
    layers, half = plan.layers, by // 2
    iz, z_low, z_high = place("gz", plan.peers[0])
    ix, x_low, x_high = place("gx", plan.peers[1])
    iy, y_low, y_high = place("gy", plan.peers[2])

    shares[0] = ours[...]
    shares[1] = from_a[plan.edge:plan.edge + plan.share, :]
    shares[2] = from_2[...]
    shares[3] = from_3[...]
    own2 = half // 2
    source = []
    for part in range(plan.fold):
        total = None
        for j in range(plan.peers[2]):
            v = moved(shares[iy ^ j], part * plan.wide2, plan.wide2, own2 * j - 2)
            total = v if total is None else total + v
        source += [total[nx2 * k:nx2 * (k + 1)] for k in range(plan.lines2)]
    source = source[:nz2]
    e2, coarsest = small_cycle(2, source)
    for k in range(nz2):
        lines[k * nx2:(k + 1) * nx2, :] = e2[k]
    thin = as_table(iota((LANES, LANES), 0) == 8 * iota((LANES, LANES), 1))
    for k in range(last_ref.shape[0]):
        last_ref[k] = right_dot(coarsest[k], thin)[0:1, 0:last_ref.shape[2]]

    up_a, _ = side(iy, 1)
    _, near_b = side(iy, 3)

    def sent(rows):
        a, b = from_a[rows[0]:rows[1], :], only(near_b, from_b[rows[0]:rows[1], :])
        return jnp.where(up_a, a, b), jnp.where(up_a, b, a)

    fine = signed(iota((LANES, LANES), 1), half, LANES)
    coarse = iota((LANES, LANES), 0) - iy * own2
    e2 = right_dot(lines[...], as_table((fine >> 1) == coarse))
    for zc in range(nz2):
        v = e2[zc * nx2:(zc + 1) * nx2]
        for part in range(2):
            q1.at[2 * zc + part][pl.ds(0, nx2, 2), :] = v
            q1.at[2 * zc + part][pl.ds(1, nx2, 2), :] = v
    per_tile = LANES // 16
    lateral1 = level_lateral((nx1, LANES))
    keep = wrapped_mask((nx1, LANES), {1: half}, (None, y_low), (None, y_high))
    for group in range(nz1 // per_tile):
        at = plan.fine_rows + group * nx1
        high, low = sent((at, at + nx1))
        for j in range(per_tile):
            k = group * per_tile + j
            s = 16 * j
            r1[k] = (
                r1_in[k] + moved(high, s, 7, half - 4) + moved(low, s, 7, LANES - 3)
                - apply_at(q1, k, lateral1)
            )
            e1[k + 2, 8:8 + nx1, :] = (
                x1_in[k] + q1[k]
                + moved(high, s + 7, 5, half - 3) + moved(low, s + 7, 5, LANES - 2)
            )
    for k in range(nz1):
        d1[k] = keep * (r1[k] * first_scale)
    nothing = jnp.zeros((8, LANES), F32)
    for k in range(nz1 + 4):
        e1[k, 0:8, :] = nothing
        e1[k, 8 + nx1:16 + nx1, :] = nothing
        if not 2 <= k < nz1 + 2:
            e1[k, 8:8 + nx1, :] = jnp.zeros((nx1, LANES), F32)
    for k in range(nz1):
        v = r1[k] - apply_at(d1, k, lateral1)
        e1[k + 2, 8:8 + nx1, :] += d1[k] + keep * (carry_coef * d1[k] + fresh_coef * v)

    coarse = signed(iota((LANES, ey), 0), half, LANES)
    fine = signed(iota((LANES, ey), 1), by, ey)
    double = as_table((fine >> 1) == coarse)
    half_z, half_x = bz // 2, bx // 2
    for zc in range(half_z + 4):
        start = pl.multiple_of(ix * half_x, 8)
        v = e1[iz * half_z + zc, pl.ds(start, half_x + 16), :]
        own, low, high = v[8:8 + half_x], v[0:8], v[8 + half_x:16 + half_x]
        at = zc * ex
        wide[pl.ds(at, half_x, 2), :] = own
        wide[pl.ds(at + 1, half_x, 2), :] = own
        for j in range(2):
            for twin in range(2):
                row = at + bx + 2 * j + twin
                wide[row:row + 1, :] = high[j:j + 1]
                row = at + ex - 4 + 2 * j + twin
                wide[row:row + 1, :] = low[6 + j:7 + j]
    for zc in range(half_z + 4):
        v = right_dot(wide[zc * ex:(zc + 1) * ex, :], double)
        for k in (2 * zc - 1, 2 * zc):
            if 0 <= k < ez:
                e0[k] = v
    flat = wrapped_mask((ex, ey), {0: bx, 1: by}, (x_low, y_low), (x_high, y_high))
    below = jnp.where(z_low, 1.0, 0.0).astype(F32)
    above = jnp.where(z_high, 1.0, 0.0).astype(F32)

    def masked(k, v):
        v = v * flat
        if k < 3:
            v = v * below
        if k >= 3 + bz:
            v = v * above
        return v

    high, low = sent((0, ex))
    for k in range(layers):
        s, inner = plan.slots[k], plan.inner[k]
        v = r_in[k] - apply_at(e0, k + 1)
        own = v[:, 0:by] + moved(high, s, 3, LANES - 3) + moved(low, s + inner, 3, 0)
        spill = v[:, by:ey]
        if inner:
            spill = spill + moved(high, s + 3, inner, 0) + moved(low, s, inner, LANES - inner)
        r[k, :, 0:by] = own
        r[k, :, by:ey] = spill
        d0[k] = masked(k + 1, r[k] * first_scale)
        if inner == 2:
            s = s + 3 + inner
            p_ref[k - 2] = (
                x_in[k - 2] + e0[k + 1, 0:bx, 0:by]
                + (moved(high, s, 2, LANES - 2) + moved(low, s, 2, 0))[0:bx]
            )
    for k in range(1, layers - 1):
        v = r[k] - apply_at(d0, k)
        r[k] = v
        v = masked(k + 1, carry_coef * d0[k] + fresh_coef * v)
        e0[k] = v
        if 2 <= k < 2 + bz:
            p_ref[k - 2] += d0[k, 0:bx, 0:by] + v[0:bx, 0:by]
    copy = pltpu.make_async_copy(p_ref, p_out, sem.at[0])
    copy.start()
    copies = [copy]
    parts = 2
    for part in range(parts):
        here = range(part * bz // parts, (part + 1) * bz // parts)
        for j in here:
            v = r[j + 2] - apply_at(e0, j + 2)
            res_ref[j] = v[0:bx, 0:by]
        here = pl.ds(here[0], bz // parts)
        copy = pltpu.make_async_copy(res_ref.at[here], res_out.at[here], sem.at[1 + part])
        copy.start()
        copies.append(copy)
    for copy in copies:
        copy.wait()


def whole(shape):
    return jax.ShapeDtypeStruct(shape, F32)


VMEM = pl.BlockSpec(memory_space=pltpu.VMEM)
ANY = pl.BlockSpec(memory_space=pl.ANY)
VMEM_BYTES = 24 << 20


def run(kernel, plan, outs, scratch, *operands, out_specs=None, semaphores=0):
    scratch = [pltpu.VMEM(s, F32) for s in scratch]
    if semaphores:
        scratch.append(pltpu.SemaphoreType.DMA((semaphores,)))
    return pl.pallas_call(
        functools.partial(kernel, plan),
        out_shape=[whole(s) for s in outs],
        in_specs=[VMEM] * len(operands),
        out_specs=out_specs or [VMEM] * len(outs),
        scratch_shapes=scratch,
        compiler_params=pltpu.CompilerParams(vmem_limit_bytes=VMEM_BYTES),
    )(*operands)


def swap(values, partner):
    axes = ("gx", "gy", "gz")
    counts = [lax.axis_size(a) for a in axes]
    pairs = []
    for i in range(counts[0] * counts[1] * counts[2]):
        to = partner(i // (counts[1] * counts[2]), i // counts[2] % counts[1], i % counts[2])
        if to is not None:
            pairs.append((i, (to[0] * counts[1] + to[1]) * counts[2] + to[2]))
    return lax.ppermute(values, axes, pairs)


def swap_parts(values, partner):
    cut = values.shape[0] * 5 // 64 * 8
    parts = [swap(values[:cut], partner), swap(values[cut:], partner)]
    return jnp.concatenate(parts, axis=0)


def body_fast(divergence, pressure_prev):
    plan = Plan(divergence.shape, tuple(lax.axis_size(a) for a in ("gz", "gx", "gy")))
    ext, level1 = plan.ext, plan.level1
    payload = [(plan.slab + n * plan.coarse, LANES) for n in (1, 2, 4)]
    both = jnp.stack([pressure_prev, divergence])
    both = jnp.pad(both, ((0, 0), (3, 3), (0, plan.ex - plan.block[1]), (0, plan.ey - plan.block[2])))
    r, x, ours = run(
        first_kernel, plan, [ext, ext, payload[0]],
        [ext, ext, (2, 2 * plan.pairs * plan.ex, LANES), (2, plan.lat_at, plan.ey)],
        both,
    )
    got = swap_parts(ours, lambda x, y, z: (x, y, z ^ 3) if z in (1, 2) else (x ^ 1, y, z))
    r, x, ours = run(step_kernel, plan, [ext, ext, payload[1]], [], r, x, ours, got)
    got = swap_parts(ours, lambda x, y, z: (x ^ 1, y, z) if z in (1, 2) else (x, y, z ^ 3))
    r, x, ours = run(core_kernel, plan, [ext, ext, payload[2]], [], r, x, ours, got)
    got = swap(ours, lambda x, y, z: (x, y, z ^ 1))
    nz2, nx2, _ = plan.level2
    layers = (plan.layers, plan.ex, plan.ey)
    share = (plan.share, LANES)
    r, x, r1, x1, now, later, ours = run(
        plane_kernel, plan,
        [layers, plan.block, level1, level1, (plan.edge + plan.share, LANES), (plan.edge, LANES), share],
        [ext, ext, level1, level1, level1, (nz2 * level1[1], LANES), (plan.fold,) + share],
        r, x, ours, got,
    )
    from_a = swap(now, lambda x, y, z: (x, y ^ 1, z))
    from_b = swap(later, lambda x, y, z: (x, y ^ 3, z) if y in (1, 2) else None)
    from_3 = swap(ours, lambda x, y, z: (x, y ^ 3, z))
    from_2 = swap(ours, lambda x, y, z: (x, y ^ 2, z))
    return run(
        last_kernel, plan,
        [plan.block, plan.block, tuple(n >> 3 for n in plan.level2)],
        [(4,) + share, plan.block, plan.block, layers, level1,
         (level1[0] + 4, level1[1] + 16, LANES), ext, layers, level1, level1,
         (nz2 * nx2, LANES), (2 * plan.pairs * plan.ex, LANES)],
        r, x, r1, x1, ours, from_a, from_b, from_3, from_2,
        out_specs=[ANY, ANY, VMEM], semaphores=3,
    )


def fits_fast(shape, peers):
    bz, bx, by = shape
    nz, nx, ny = peers
    return (
        nz == 4 and nx == 2 and ny == 4 and bz == 16 and by == LANES
        and nx * bx == 4 * 8 and ny * by == 4 * LANES
    )


def body(divergence, pressure_prev):
    peers = tuple(lax.axis_size(a) for a in ("gz", "gx", "gy"))
    if fits_fast(divergence.shape, peers):
        return tuple(body_fast(divergence, pressure_prev))
    return body_levels(divergence, pressure_prev)


def solution(mesh):
    in_specs = (P("gz", "gx", "gy"), P("gz", "gx", "gy"))
    out_specs = (P("gz", "gx", "gy"), P("gz", "gx", "gy"), P())
    return jax.shard_map(body, mesh=mesh, in_specs=in_specs, out_specs=out_specs, check_vma=False)
```

```python
import functools

import jax
import jax.numpy as jnp
from jax import lax
from jax.experimental import pallas as pl
from jax.experimental.pallas import tpu as pltpu
from jax.sharding import PartitionSpec as P

LEVELS = 6


first_scale = 1.0 / 7.5
rho_one = 1.0 / (2.0 * (5.0 / 3.0) - 0.6)
carry_coef = 0.6 * rho_one
fresh_coef = 2.0 * rho_one / (0.75 * 6.0)

LANES = 128
F32 = jnp.float32
AXES = (("gz", 0), ("gx", 1), ("gy", 2))


def extended(x, width):
    for axis, dim in AXES:
        peers, length = (lax.axis_size(axis), x.shape[dim + 1])
        up = [(i, (i + 1) % peers) for i in range(peers - 1)]
        down = [(j, i) for i, j in up]
        last = lax.slice_in_dim(x, length - width, length, axis=dim + 1)
        first = lax.slice_in_dim(x, 0, width, axis=dim + 1)
        before = lax.ppermute(last, axis, up)
        after = lax.ppermute(first, axis, down)
        x = jnp.concatenate([before, x, after], axis=dim + 1)
    return x


def stencil(values):
    padded = jnp.pad(values, 1)
    return valid_op(padded)


def valid_op(padded):
    beside = padded[2:, 1:-1, 1:-1] + padded[:-2, 1:-1, 1:-1]
    beside = beside + padded[1:-1, 2:, 1:-1] + padded[1:-1, :-2, 1:-1]
    beside = beside + padded[1:-1, 1:-1, 2:] + padded[1:-1, 1:-1, :-2]
    return 6.0 * padded[1:-1, 1:-1, 1:-1] - beside


def smooth_pass(iterate, source, apply_op, from_zero):
    residue = source if from_zero else source - apply_op(iterate)
    update = residue * first_scale
    iterate = update if from_zero else iterate + update
    residue = source - apply_op(iterate)
    update = carry_coef * update + fresh_coef * residue
    return iterate + update


def restrict(values):
    shape_a, shape_b, shape_c = values.shape
    blocks = values.reshape(shape_a // 2, 2, shape_b // 2, 2, shape_c // 2, 2)
    return 0.5 * jnp.sum(blocks, axis=(1, 3, 5))


def prolong(values):
    shape_a, shape_b, shape_c = values.shape
    spread = jnp.broadcast_to(
        values[:, None, :, None, :, None], (shape_a, 2, shape_b, 2, shape_c, 2)
    )
    return spread.reshape(2 * shape_a, 2 * shape_b, 2 * shape_c)


def vcycle(level_num, iterate, source):
    iterate = smooth_pass(iterate, source, stencil, True)
    coarsest = None
    if level_num < LEVELS - 1:
        residue = source - stencil(iterate)
        coarse, coarsest = vcycle(level_num + 1, None, restrict(residue))
        iterate = iterate + prolong(coarse)
    result = smooth_pass(iterate, source, stencil, False)
    if level_num == LEVELS - 1:
        coarsest = result
    return (result, coarsest)


def collect(values):
    gathered = lax.all_gather(values, "gz", axis=0, tiled=True)
    gathered = lax.all_gather(gathered, "gy", axis=2, tiled=True)
    return lax.all_gather(gathered, "gx", axis=1, tiled=True)


def local_stencil(values):
    return valid_op(extended(values[None], 1)[0])


def own_block(whole, block_shape):
    start_z = lax.axis_index("gz") * block_shape[0]
    start_x = lax.axis_index("gx") * block_shape[1]
    start_y = lax.axis_index("gy") * block_shape[2]
    return lax.dynamic_slice(whole, (start_z, start_x, start_y), block_shape)


def body_cycle(level_num, iterate, source, from_zero, gather_at):
    if level_num == gather_at:
        whole_source = collect(source)
        coarse, coarsest = vcycle(level_num, None, whole_source)
        return (own_block(coarse, source.shape), coarsest)
    iterate = smooth_pass(iterate, source, local_stencil, from_zero)
    residue = source - local_stencil(iterate)
    coarse, coarsest = body_cycle(level_num + 1, None, restrict(residue), True, gather_at)
    iterate = iterate + prolong(coarse)
    return (smooth_pass(iterate, source, local_stencil, False), coarsest)


def body_levels(divergence, pressure_prev):
    pressure, coarse_correction = body_cycle(0, pressure_prev, divergence, False, 3)
    residual = divergence - local_stencil(pressure)
    return (pressure, residual, coarse_correction)


def iota(shape, dim):
    return lax.broadcasted_iota(jnp.int32, shape, dim)


def signed(index, size, extent):
    return jnp.where(index >= (size + extent) // 2, index - extent, index)


def split(values):
    terms = []
    for _ in range(3):
        term = values.astype(jnp.bfloat16)
        terms.append(term)
        values = values - term.astype(F32)
    return terms


def right_dot(values, table):
    parts = [jnp.dot(t, table, preferred_element_type=F32) for t in split(values)]
    return parts[0] + parts[1] + parts[2]


def left_dot(table, values):
    parts = [jnp.dot(table, t, preferred_element_type=F32) for t in split(values)]
    return parts[0] + parts[1] + parts[2]


def as_table(keep, value=1.0):
    return jnp.where(keep, value, 0.0).astype(jnp.bfloat16)


def lateral(v):
    rows, lanes = v.shape
    return (
        pltpu.roll(v, 1, 0) + pltpu.roll(v, rows - 1, 0)
        + pltpu.roll(v, 1, 1) + pltpu.roll(v, lanes - 1, 1)
    )


def apply_at(ref, k, lateral_of=lateral):
    centre = ref[k]
    beside = lateral_of(centre)
    if k > 0:
        beside = beside + ref[k - 1]
    if k < ref.shape[0] - 1:
        beside = beside + ref[k + 1]
    return 6.0 * centre - beside


def wrapped_mask(shape, sizes, low, high):
    keep = None
    for dim, size in sizes.items():
        at = signed(iota(shape, dim), size, shape[dim])
        good = ((at >= 0) | low[dim]) & ((at < size) | high[dim])
        keep = good if keep is None else keep & good
    return jnp.where(keep, 1.0, 0.0).astype(F32)


def side(index, flip):
    if flip == 1:
        return (index & 1) == 0, None
    return index < 2, (index == 1) | (index == 2)


def place(axis, count):
    index = lax.axis_index(axis)
    return index, index > 0, index < count - 1


def only(keep, v):
    return jnp.where(keep, v, 0.0)


def shifted(v, lanes):
    lanes = lanes % LANES
    return v if lanes == 0 else pltpu.roll(v, lanes, 1)


def lanes_of(v, first, count):
    lane = iota(v.shape, 1)
    last = first + count
    if last <= LANES:
        return (lane >= first) & (lane < last)
    return (lane >= first) | (lane < last - LANES)


def moved(v, first, count, to):
    first = first % LANES
    return shifted(only(lanes_of(v, first, count), v), to - first)


def side_pack(tile, slot):
    return moved(tile, LANES - 3, 6, 6 * slot)


def side_unpack(packed, slot):
    return moved(packed, 6 * slot, 6, LANES - 3)


def slab_layers(r_ref, x_ref, up, low, high):
    start = jnp.where(up, high[0], low[0])
    start_x = jnp.where(up, high[1], low[1])
    return [(r_ref, start + j) for j in range(5)] + [(x_ref, start_x + j) for j in range(2)]


def slab_own(r_ref, x_ref, up):
    ez = r_ref.shape[0]
    return slab_layers(r_ref, x_ref, up, (0, 1), (ez - 5, ez - 3))


def slab_there(r_ref, x_ref, up):
    ez = r_ref.shape[0]
    return slab_layers(r_ref, x_ref, up, (1, 3), (ez - 6, ez - 5))


def slab_emit(r_ref, x_ref, out, up):
    ex = r_ref.shape[1]
    lat = None
    for j, (ref, k) in enumerate(slab_own(r_ref, x_ref, up)):
        v = ref[k]
        out[j * ex:(j + 1) * ex, :] = v[:, 0:LANES]
        part = side_pack(v[:, LANES:], j)
        lat = part if lat is None else lat + part
    out[7 * ex:8 * ex, :] = lat


def slab_add(r_ref, x_ref, slab, up):
    ex = r_ref.shape[1]
    lat = slab[7 * ex:8 * ex, :]
    for j, (ref, k) in enumerate(slab_there(r_ref, x_ref, up)):
        ref[k, :, 0:LANES] += slab[j * ex:(j + 1) * ex, :]
        ref[k, :, LANES:] += side_unpack(lat, j)


BESIDE = ((2, 2, 0, 0), (1, 1, 0, 3), (3, 1, 0, 5), (5, 1, 1, 0), (6, 1, 1, 3))


def beside(tile, count):
    row = iota(tile.shape, 0)
    return only((row < count) | (row >= 8 - count), tile)


def thin_emit(r_ref, x_ref, out, up):
    bx = r_ref.shape[1] - 8
    layers = slab_own(r_ref, x_ref, up)
    lat = None
    for j, (ref, k) in enumerate(layers):
        out[j * bx:(j + 1) * bx, :] = ref[k, 0:bx, 0:LANES]
        part = side_pack(ref[k, 0:bx, LANES:], j)
        lat = part if lat is None else lat + part
    tiles = [None, None]
    for j, count, which, turn in BESIDE:
        ref, k = layers[j]
        part = beside(ref[k, bx:, 0:LANES], count)
        part = pltpu.roll(part, turn, 0) if turn else part
        tiles[which] = part if tiles[which] is None else tiles[which] + part
    at = 7 * bx
    out[at:at + 8, :] = tiles[0]
    out[at + 8:at + 16, :] = tiles[1]
    out[at + 16:at + 16 + bx, :] = lat
    for j in (1, 2, 3):
        ref, k = layers[j]
        out[at + 16:at + 24, :] += side_pack(ref[k, bx:, LANES:], 6 + j)


def thin_add(r_ref, x_ref, slab, up):
    bx = r_ref.shape[1] - 8
    layers = slab_there(r_ref, x_ref, up)
    at = 7 * bx
    lat = slab[at + 16:at + 16 + bx, :]
    for j, (ref, k) in enumerate(layers):
        ref[k, 0:bx, 0:LANES] += slab[j * bx:(j + 1) * bx, :]
        ref[k, 0:bx, LANES:] += side_unpack(lat, j)
    for j, count, which, turn in BESIDE:
        ref, k = layers[j]
        tile = slab[at + 8 * which:at + 8 * which + 8, :]
        tile = pltpu.roll(tile, 8 - turn, 0) if turn else tile
        ref[k, bx:, 0:LANES] += beside(tile, count)
    for j in (1, 2, 3):
        ref, k = layers[j]
        ref[k, bx:, LANES:] += side_unpack(lat[0:8], 6 + j)


def rows_out(r, x, up):
    bx = r.shape[0] - 8
    row = iota((8, r.shape[1]), 0)
    first, last, spill = r[0:8], r[bx - 8:bx], r[bx:]
    to_high = pltpu.roll(jnp.where(row >= 6, last, spill), 2, 0)
    to_low = pltpu.roll(jnp.where(row >= 5, spill, first), 3, 0)
    out = jnp.where(up, to_high, to_low)
    if x is None:
        return only(row < 5, out)
    spill = x[bx:]
    extra = jnp.where(up, pltpu.roll(spill, 5, 0), pltpu.roll(spill, 7, 0))
    return jnp.where(row < 5, out, only(row < 7, extra))


def rows_in(r_ref, x_ref, k, rows, up):
    bx = r_ref.shape[1] - 8
    row = iota(rows.shape, 0)
    high, low = pltpu.roll(rows, 5, 0), pltpu.roll(rows, 6, 0)
    r_ref[k, 0:8] += only(jnp.logical_not(up) & (row < 3), low)
    r_ref[k, bx - 8:bx] += only(up & (row >= 5), high)
    r_ref[k, bx:] += jnp.where(up, only(row < 2, high), only(row >= 6, low))
    if x_ref is not None:
        x_ref[k, 0:8] += only(jnp.logical_not(up) & (row < 2), pltpu.roll(rows, 3, 0))
        x_ref[k, bx - 8:bx] += only(up & (row >= 6), pltpu.roll(rows, 1, 0))


def rows_emit(r_ref, x_ref, out, up):
    ez = r_ref.shape[0]
    row = iota((8, LANES), 0)
    lat = jnp.zeros((8, LANES), F32)
    for t, k in enumerate(range(1, ez - 1)):
        far = {1: 0, ez - 2: ez - 1}.get(k)
        rows = rows_out(r_ref[k], None if far is not None else x_ref[k], up)
        tile = rows[:, 0:LANES]
        if far is not None:
            more = rows_out(r_ref[far, :, 0:LANES], None, up)
            more = jnp.where(up, pltpu.roll(more, 5, 0), pltpu.roll(more, 2, 0))
            tile = jnp.where((row == 5) | (row == 6), more, tile)
        out[8 * t:8 * t + 8, :] = tile
        lat = lat + side_pack(rows[:, LANES:], t)
    at = 8 * (ez - 2)
    out[at:at + 8, :] = lat


def rows_add(r_ref, x_ref, slab, up):
    ez = r_ref.shape[0]
    at = 8 * (ez - 2)
    lat = slab[at:at + 8, :]
    row = iota((8, LANES), 0)
    for t, k in enumerate(range(1, ez - 1)):
        far = {1: 0, ez - 2: ez - 1}.get(k)
        tile = slab[8 * t:8 * t + 8, :]
        rows = jnp.concatenate([tile, side_unpack(lat, t)], axis=1)
        rows_in(r_ref, None if far is not None else x_ref, k, rows, up)
        if far is not None:
            tile = only((row == 5) | (row == 6), tile)
            tile = jnp.where(up, pltpu.roll(tile, 6, 0), pltpu.roll(tile, 3, 0))
            rows = jnp.concatenate([tile, jnp.zeros((8, LANES), F32)], axis=1)
            rows_in(r_ref, None, far, rows, up)


class Plan:
    def first_layer(self, iz):
        start = iz * (self.block[0] // 2) - 4
        return jnp.clip(start, 0, self.level1[0] - self.window[0])

    def __init__(self, shape, peers):
        self.peers = peers
        self.block = bz, bx, by = shape
        self.ext = self.ez, self.ex, self.ey = bz + 6, bx + 8, by + LANES
        self.rows, self.pairs = bx // 2, bz // 4 + 2
        self.lat_at = self.pairs * (self.rows + 4)
        self.coarse = self.lat_at + 8
        self.slab = 8 * self.ex
        self.slab_z = 8 * bx + 16
        self.slab_x = 8 * (bz + 5)
        self.corner = 6 * 8
        self.layers = bz + 4
        self.level1 = (peers[0] * bz // 2, peers[1] * bx // 2, LANES)
        self.level2 = (peers[0] * bz // 4, peers[1] * bx // 4, peers[2] * by // 4)
        self.inner = [0, 1] + [2] * bz + [1, 0]
        self.slots, at = [], 0
        for count in self.inner:
            self.slots.append(at)
            at += 3 + count + (2 if count == 2 else 0)
        assert at <= LANES
        self.fine_rows = self.ex
        self.window = (bz // 2 + 8, self.level1[1], LANES)
        self.edge = self.fine_rows + self.window[0] * self.window[1] // 8
        self.wide2 = by // 4 + 4
        self.fold = LANES // self.wide2
        self.lines2 = -(-self.level2[0] // self.fold)
        self.share = self.lines2 * self.level2[1]


def first_kernel(plan, both, r_ref, x_ref, pay_z, pay_x, pay_d, d_one, d_two, pairs, lines):
    p_ext, b_ext = both.at[0], both.at[1]
    bz, bx, by = plan.block
    ez, ex, ey = plan.ext
    peers = plan.peers
    iz, z_low, z_high = place("gz", peers[0])
    ix, x_low, x_high = place("gx", peers[1])
    _, y_low, y_high = place("gy", peers[2])
    flat = wrapped_mask((ex, ey), {0: bx, 1: by}, (x_low, y_low), (x_high, y_high))
    below = jnp.where(z_low, 1.0, 0.0).astype(F32)
    above = jnp.where(z_high, 1.0, 0.0).astype(F32)

    def masked(k, v):
        v = v * flat
        if k < 3:
            v = v * below
        if k >= 3 + bz:
            v = v * above
        return v

    zero = jnp.zeros((ex, ey), F32)
    for k in range(ez):
        if 2 <= k < ez - 2:
            r = b_ext[k] - apply_at(p_ext, k)
            r_ref[k] = r
            d_one[k] = masked(k, r * first_scale)
        else:
            d_one[k] = zero
    for k in range(ez):
        if 1 <= k < ez - 1:
            r = -apply_at(d_one, k)
            if 2 <= k < ez - 2:
                r = r + r_ref[k]
            r_ref[k] = r
            d_two[k] = masked(k, carry_coef * d_one[k] + fresh_coef * r)
        else:
            d_two[k] = zero
    for k in range(ez):
        r = -apply_at(d_two, k)
        if 1 <= k < ez - 1:
            r = r + r_ref[k]
        r_ref[k] = masked(k, r)
        x_ref[k] = p_ext[k] + d_one[k] + d_two[k]


    coarse_z, rows = 2 * plan.pairs, plan.rows
    for zc in range(coarse_z):
        low, high = 2 * zc - 1, 2 * zc
        if low < 0:
            total = r_ref[high]
        elif high >= ez:
            total = r_ref[low]
        else:
            total = r_ref[low] + r_ref[high]
        base = zc * ex
        for tile in range(ey // LANES):
            here = slice(tile * LANES, (tile + 1) * LANES)
            pairs[tile, base:base + ex, :] = total[:, here]
            even = pairs.at[tile][pl.ds(base, ex // 2, 2), :]
            odd = pairs.at[tile][pl.ds(base + 1, ex // 2, 2), :]
            sums = even + odd
            at = zc // 2 * rows
            lines[zc % 2, at:at + rows, here] = sums[0:rows]
            at = plan.pairs * rows + zc // 2 * 4
            lines[zc % 2, at:at + 4, here] = sums[rows:rows + 4]
    fine = signed(iota((ey, LANES), 0), by, ey)
    coarse = signed(iota((ey, LANES), 1), by // 2, LANES)
    table = as_table((fine >> 1) == coarse, 0.5)
    even, odd = right_dot(lines[0], table), right_dot(lines[1], table)
    lane = iota(even.shape, 1)
    main = jnp.where(lane < LANES // 2, even, shifted(odd, LANES // 2))
    own_lat = spill_lat = None
    row = iota((8, LANES), 0)
    for zc in range(coarse_z):
        source = (even, odd)[zc % 2]
        base = zc // 2 * rows
        tile = source[base:base + rows]
        part = moved(tile, by // 2, 2, 4 * zc) + moved(tile, LANES - 2, 2, 4 * zc + 2)
        own_lat = part if own_lat is None else own_lat + part
        base = plan.pairs * rows + zc // 4 * 8
        tile = source[base:base + 8]
        if zc // 2 % 2:
            tile = pltpu.roll(tile, 4, 0)
        tile = only(row < 4, tile)
        slot = LANES // 2 + 4 * zc
        part = moved(tile, by // 2, 2, slot) + moved(tile, LANES - 2, 2, slot + 2)
        spill_lat = part if spill_lat is None else spill_lat + part
    for pay, at in ((pay_z, plan.slab_z), (pay_x, plan.slab_x), (pay_d, plan.corner)):
        pay[at:at + plan.lat_at, :] = main
        pay[at + plan.lat_at:at + plan.coarse, :] = own_lat + spill_lat

    up_z, _ = side(iz, 3)
    up_x, _ = side(ix, 1)
    thin_emit(r_ref, x_ref, pay_z, up_z)
    rows_emit(r_ref, x_ref, pay_x, up_x)
    lat = jnp.zeros((8, LANES), F32)
    start = jnp.where(up_z, ez - 5, 0)
    for j in range(5):
        out = rows_out(r_ref[start + j], x_ref[start + j] if j == 2 else None, up_x)
        pay_d[8 * j:8 * j + 8, :] = out[:, 0:LANES]
        lat = lat + side_pack(out[:, LANES:], j)
    pay_d[40:48, :] = lat


def chip_kernel(plan, r_in, x_in, from_z, from_x, from_d, r_ref, x_ref, pay):
    ez, ex, ey = plan.ext
    iz, _, _ = place("gz", plan.peers[0])
    ix, _, _ = place("gx", plan.peers[1])
    up_z, near = side(iz, 3)
    up_x, _ = side(ix, 1)
    for k in range(ez):
        r_ref[k] = r_in[k]
        x_ref[k] = x_in[k]
    rows_add(r_ref, x_ref, from_x, up_x)

    @pl.when(near)
    def _():
        thin_add(r_ref, x_ref, from_z, up_z)
        start = jnp.where(up_z, ez - 6, 1)
        lat = from_d[40:48, :]
        for j in range(5):
            rows = from_d[8 * j:8 * j + 8, :]
            rows = jnp.concatenate([rows, side_unpack(lat, j)], axis=1)
            rows_in(r_ref, x_ref if j == 2 else None, start + j, rows, up_x)

    slab_emit(r_ref, x_ref, pay, side(iz, 1)[0])


def plane_kernel(plan, r_in, x_in, ours, theirs, r_ref, x_ref, r1_ref, x1_ref, pay, later, share,
                 r_all, x_all, b1, d1, d2, r1, x1, pairs, lines):
    bz, bx, by = plan.block
    ez, ex, ey = plan.ext
    layers = plan.layers
    iz, _, _ = place("gz", plan.peers[0])
    ix, _, _ = place("gx", plan.peers[1])
    iy, y_low, y_high = place("gy", plan.peers[2])
    up_z, _ = side(iz, 1)
    for k in range(ez):
        r_all[k] = r_in[k]
        x_all[k] = x_in[k]
    slab_add(r_all, x_all, theirs, up_z)
    for k in range(layers):
        r_ref[k] = r_all[k + 1]
    for k in range(bz):
        x_ref[k] = x_all[k + 3, 0:bx, 0:by]

    up, _ = side(iy, 1)
    up_inner, _ = side(iy, 3)
    high, low = jnp.zeros((ex, LANES), F32), jnp.zeros((ex, LANES), F32)
    for k in range(layers):
        slot, inner = plan.slots[k], plan.inner[k]
        count = 3 + inner
        v, spill = r_all[k + 1, :, 0:by], r_all[k + 1, :, by:ey]
        high = high + moved(jnp.where(lanes_of(v, 0, 3), spill, v), LANES - inner, count, slot)
        mixed = jnp.where(lanes_of(v, 0, 2), v, spill)
        low = low + moved(mixed, LANES - 3, count, slot)
        if inner == 2:
            spill = x_all[k + 1, :, by:ey]
            high = high + moved(spill, 0, 2, slot + count)
            low = low + moved(spill, LANES - 2, 2, slot + count)
    pay[0:ex, :] = jnp.where(up, high, low)
    later[0:ex, :] = jnp.where(up_inner, high, low)

    nz1, nx1, _ = plan.level1
    rows, half = plan.rows, by // 2
    for k in range(nz1):
        b1[k] = jnp.zeros((nx1, LANES), F32)
    row = iota((8, LANES), 0)
    for j in range(plan.peers[0]):
        for i in range(plan.peers[1]):
            flip = iz ^ j
            other = ((flip ^ (flip >> 1)) & 1) == 1
            chip = (flip >> 1) + 2 * (ix ^ i)
            at = pl.multiple_of(plan.slab + chip * plan.coarse, 8)

            def rows_at(offset, count):
                here = pl.ds(pl.multiple_of(at + offset, 8), count)
                return jnp.where(other, theirs[here, :], ours[here, :])

            lat = rows_at(plan.lat_at, 8)
            for zp in range(plan.pairs):
                own = rows_at(zp * rows, rows)
                if zp % 2 == 0:
                    spill_two = rows_at(plan.pairs * rows + zp * 4, 8)
                spill = spill_two if zp % 2 == 0 else pltpu.roll(spill_two, 4, 0)
                for part in range(2):
                    zc = 2 * zp + part
                    k = j * (bz // 2) + zc - 2
                    if not 0 <= k < nz1:
                        continue

                    def wide(main, slot):
                        return (
                            moved(main, part * half, half, 0)
                            + moved(lat, slot, 2, half) + moved(lat, slot + 2, 2, LANES - 2)
                        )

                    b1[k, i * rows:(i + 1) * rows, :] += wide(own, 4 * zc)
                    v = wide(spill, LANES // 2 + 4 * zc)
                    if i + 1 < plan.peers[1]:
                        at_row = (i + 1) * rows
                        b1[k, at_row:at_row + 8, :] += only(row < 2, v)
                    if i > 0:
                        at_row = i * rows - 8
                        b1[k, at_row:at_row + 8, :] += only(row >= 6, pltpu.roll(v, 4, 0))

    lateral1 = level_lateral((nx1, LANES))
    keep = wrapped_mask((nx1, LANES), {1: half}, (None, y_low), (None, y_high))
    for k in range(nz1):
        d1[k] = b1[k] * first_scale
    for k in range(nz1):
        r = b1[k] - apply_at(d1, k, lateral1)
        r1[k] = r
        d2[k] = keep * (carry_coef * d1[k] + fresh_coef * r)
    for k in range(nz1):
        r1[k] = keep * (r1[k] - apply_at(d2, k, lateral1))
        x1[k] = d1[k] + d2[k]

    nz2, nx2, _ = plan.level2
    for zc in range(nz2):
        pairs[zc * nx1:(zc + 1) * nx1, :] = r1[2 * zc] + r1[2 * zc + 1]
        part, at = divmod(zc, plan.lines2)
        lines[part, at * nx2:(at + 1) * nx2, :] = (
            pairs[pl.ds(zc * nx1, nx2, 2), :] + pairs[pl.ds(zc * nx1 + 1, nx2, 2), :]
        )
    fine = signed(iota((LANES, LANES), 0), half, LANES)
    total = None
    for part in range(plan.fold):
        count = min(plan.lines2, nz2 - part * plan.lines2) * nx2
        if count < plan.share:
            lines[part, count:, :] = jnp.zeros((plan.share - count, LANES), F32)
        coarse = iota((LANES, LANES), 1) - part * plan.wide2 - 2
        near = (coarse >= -2) & (coarse < plan.wide2 - 2)
        term = right_dot(lines[part], as_table(near & ((fine >> 1) == coarse), 0.5))
        total = term if total is None else total + term
    share[...] = total
    pay[plan.edge:plan.edge + plan.share, :] = total
    later[plan.edge:plan.edge + plan.share, :] = total

    start = plan.first_layer(iz)
    for k in range(plan.window[0]):
        r1_ref[k] = r1[start + k]
        x1_ref[k] = x1[start + k]
    per_tile = LANES // 16
    for group in range(plan.window[0] // per_tile):
        tiles = []
        for which in range(2):
            total = jnp.zeros((nx1, LANES), F32)
            for j in range(per_tile):
                k = group * per_tile + j
                first = half - 3 if which == 0 else LANES - 4
                total = total + moved(r1_ref[k], first, 7, 16 * j)
                first = half - 2 if which == 0 else LANES - 3
                total = total + moved(x1_ref[k], first, 5, 16 * j + 7)
            tiles.append(total)
        here = slice(plan.fine_rows + group * nx1, plan.fine_rows + (group + 1) * nx1)
        pay[here, :] = jnp.where(up, tiles[0], tiles[1])
        later[here, :] = jnp.where(up_inner, tiles[0], tiles[1])


def level_lateral(shape):
    row = iota(shape, 0)
    not_first = jnp.where(row > 0, 1.0, 0.0).astype(F32)
    not_last = jnp.where(row < shape[0] - 1, 1.0, 0.0).astype(F32)

    def beside(v):
        return (
            not_first * pltpu.roll(v, 1, 0) + not_last * pltpu.roll(v, shape[0] - 1, 0)
            + pltpu.roll(v, 1, 1) + pltpu.roll(v, LANES - 1, 1)
        )

    return beside


def small_cycle(level, source):
    step = 1 << (level - 2)
    row, lane = iota((8, LANES), 0), iota((8, LANES), 1)
    count = len(source)
    shifts = []
    if step < 8:
        shifts += [(step, 0, row >= step), (8 - step, 0, row < 8 - step)]
    shifts += [(step, 1, lane >= step), (LANES - step, 1, lane < LANES - step)]

    def op(v):
        out = []
        for k in range(count):
            beside = None
            for shift, dim, keep in shifts:
                part = only(keep, pltpu.roll(v[k], shift, dim))
                beside = part if beside is None else beside + part
            if k > 0:
                beside = beside + v[k - 1]
            if k < count - 1:
                beside = beside + v[k + 1]
            out.append(6.0 * v[k] - beside)
        return out

    d = [first_scale * v for v in source]
    r = [b - t for b, t in zip(source, op(d))]
    d2 = [carry_coef * v + fresh_coef * t for v, t in zip(d, r)]
    x = [v + t for v, t in zip(d, d2)]
    r = [v - t for v, t in zip(r, op(d2))]
    coarsest = None
    if level < LEVELS - 1:
        keep = only((row % (2 * step) == 0) & (lane % (2 * step) == 0), 0.5)
        coarse = []
        for k in range(0, count, 2):
            v = r[k] + r[k + 1]
            v = v + pltpu.roll(v, 8 - step, 0)
            coarse.append(keep * (v + pltpu.roll(v, LANES - step, 1)))
        coarse, coarsest = small_cycle(level + 1, coarse)
        e = []
        for v in coarse:
            v = v + pltpu.roll(v, step, 0)
            e += [v + pltpu.roll(v, step, 1)] * 2
        x = [v + t for v, t in zip(x, e)]
        r = [v - t for v, t in zip(r, op(e))]
    d = [first_scale * v for v in r]
    r = [v - t for v, t in zip(r, op(d))]
    x = [v + (t + (carry_coef * t + fresh_coef * u)) for v, t, u in zip(x, d, r)]
    return x, (x if level == LEVELS - 1 else coarsest)


def last_kernel(plan, r_in, x_in, r1_in, x1_in, ours, from_a, from_b, from_c, p_out, res_out, last_ref, *scratch):
    shares, p_ref, res_ref, r, q1, e1, e0, d0, d1, r1, lines, wide, sem = scratch
    bz, bx, by = plan.block
    ez, ex, ey = plan.ext
    nz1, nx1, _ = plan.window
    nz2, nx2, _ = plan.level2
    layers, half = plan.layers, by // 2
    iz, z_low, z_high = place("gz", plan.peers[0])
    ix, x_low, x_high = place("gx", plan.peers[1])
    iy, y_low, y_high = place("gy", plan.peers[2])

    shares[0] = ours[...]
    shares[1] = from_a[plan.edge:plan.edge + plan.share, :]
    shares[3] = from_b[plan.edge:plan.edge + plan.share, :]
    shares[2] = from_c[...]
    own2 = half // 2
    source = []
    for part in range(plan.fold):
        total = None
        for j in range(plan.peers[2]):
            v = moved(shares[iy ^ j], part * plan.wide2, plan.wide2, own2 * j - 2)
            total = v if total is None else total + v
        source += [total[nx2 * k:nx2 * (k + 1)] for k in range(plan.lines2)]
    source = source[:nz2]
    e2, coarsest = small_cycle(2, source)
    for k in range(nz2):
        lines[k * nx2:(k + 1) * nx2, :] = e2[k]
    thin = as_table(iota((LANES, LANES), 0) == 8 * iota((LANES, LANES), 1))
    for k in range(last_ref.shape[0]):
        last_ref[k] = right_dot(coarsest[k], thin)[0:1, 0:last_ref.shape[2]]

    up_a, _ = side(iy, 1)
    _, near_b = side(iy, 3)

    def sent(rows):
        a, b = from_a[rows[0]:rows[1], :], only(near_b, from_b[rows[0]:rows[1], :])
        return jnp.where(up_a, a, b), jnp.where(up_a, b, a)

    fine = signed(iota((LANES, LANES), 1), half, LANES)
    coarse = iota((LANES, LANES), 0) - iy * own2
    start = plan.first_layer(iz)
    here = pl.ds(pl.multiple_of(start // 2 * nx2, 8), nz1 // 2 * nx2)
    e2 = right_dot(lines[here, :], as_table((fine >> 1) == coarse))
    for zc in range(nz1 // 2):
        v = e2[zc * nx2:(zc + 1) * nx2]
        for part in range(2):
            q1.at[2 * zc + part][pl.ds(0, nx2, 2), :] = v
            q1.at[2 * zc + part][pl.ds(1, nx2, 2), :] = v
    per_tile = LANES // 16
    lateral1 = level_lateral((nx1, LANES))
    keep = wrapped_mask((nx1, LANES), {1: half}, (None, y_low), (None, y_high))
    for group in range(nz1 // per_tile):
        at = plan.fine_rows + group * nx1
        high, low = sent((at, at + nx1))
        for j in range(per_tile):
            k = group * per_tile + j
            s = 16 * j
            r1[k] = (
                r1_in[k] + moved(high, s, 7, half - 4) + moved(low, s, 7, LANES - 3)
                - apply_at(q1, k, lateral1)
            )
            e1[k + 2, 8:8 + nx1, :] = (
                x1_in[k] + q1[k]
                + moved(high, s + 7, 5, half - 3) + moved(low, s + 7, 5, LANES - 2)
            )
    for k in range(nz1):
        d1[k] = keep * (r1[k] * first_scale)
    nothing = jnp.zeros((8, LANES), F32)
    for k in range(nz1 + 4):
        e1[k, 0:8, :] = nothing
        e1[k, 8 + nx1:16 + nx1, :] = nothing
        if not 2 <= k < nz1 + 2:
            e1[k, 8:8 + nx1, :] = jnp.zeros((nx1, LANES), F32)
    for k in range(nz1):
        v = r1[k] - apply_at(d1, k, lateral1)
        e1[k + 2, 8:8 + nx1, :] += d1[k] + keep * (carry_coef * d1[k] + fresh_coef * v)

    coarse = signed(iota((LANES, ey), 0), half, LANES)
    fine = signed(iota((LANES, ey), 1), by, ey)
    double = as_table((fine >> 1) == coarse)
    half_z, half_x = bz // 2, bx // 2
    for zc in range(half_z + 4):
        here = pl.ds(pl.multiple_of(ix * half_x, 8), half_x + 16)
        v = e1[iz * half_z - start + zc, here, :]
        own, low, high = v[8:8 + half_x], v[0:8], v[8 + half_x:16 + half_x]
        at = zc * ex
        wide[pl.ds(at, half_x, 2), :] = own
        wide[pl.ds(at + 1, half_x, 2), :] = own
        for j in range(2):
            for twin in range(2):
                row = at + bx + 2 * j + twin
                wide[row:row + 1, :] = high[j:j + 1]
                row = at + ex - 4 + 2 * j + twin
                wide[row:row + 1, :] = low[6 + j:7 + j]
    for zc in range(half_z + 4):
        v = right_dot(wide[zc * ex:(zc + 1) * ex, :], double)
        for k in (2 * zc - 1, 2 * zc):
            if 0 <= k < ez:
                e0[k] = v
    flat = wrapped_mask((ex, ey), {0: bx, 1: by}, (x_low, y_low), (x_high, y_high))
    below = jnp.where(z_low, 1.0, 0.0).astype(F32)
    above = jnp.where(z_high, 1.0, 0.0).astype(F32)

    def masked(k, v):
        v = v * flat
        if k < 3:
            v = v * below
        if k >= 3 + bz:
            v = v * above
        return v

    high, low = sent((0, ex))
    for k in range(layers):
        s, inner = plan.slots[k], plan.inner[k]
        v = r_in[k] - apply_at(e0, k + 1)
        own = v[:, 0:by] + moved(high, s, 3, LANES - 3) + moved(low, s + inner, 3, 0)
        spill = v[:, by:ey]
        if inner:
            spill = spill + moved(high, s + 3, inner, 0) + moved(low, s, inner, LANES - inner)
        r[k, :, 0:by] = own
        r[k, :, by:ey] = spill
        d0[k] = masked(k + 1, r[k] * first_scale)
        if inner == 2:
            s = s + 3 + inner
            p_ref[k - 2] = (
                x_in[k - 2] + e0[k + 1, 0:bx, 0:by]
                + (moved(high, s, 2, LANES - 2) + moved(low, s, 2, 0))[0:bx]
            )
    for k in range(1, layers - 1):
        v = r[k] - apply_at(d0, k)
        r[k] = v
        v = masked(k + 1, carry_coef * d0[k] + fresh_coef * v)
        e0[k] = v
        if 2 <= k < 2 + bz:
            p_ref[k - 2] += d0[k, 0:bx, 0:by] + v[0:bx, 0:by]
    copy = pltpu.make_async_copy(p_ref, p_out, sem.at[0])
    copy.start()
    copies = [copy]
    parts = 2
    for part in range(parts):
        here = range(part * bz // parts, (part + 1) * bz // parts)
        for j in here:
            v = r[j + 2] - apply_at(e0, j + 2)
            res_ref[j] = v[0:bx, 0:by]
        here = pl.ds(here[0], bz // parts)
        copy = pltpu.make_async_copy(res_ref.at[here], res_out.at[here], sem.at[1 + part])
        copy.start()
        copies.append(copy)
    for copy in copies:
        copy.wait()


def whole(shape):
    return jax.ShapeDtypeStruct(shape, F32)


VMEM = pl.BlockSpec(memory_space=pltpu.VMEM)
ANY = pl.BlockSpec(memory_space=pl.ANY)
VMEM_BYTES = 24 << 20


def run(kernel, plan, outs, scratch, *operands, out_specs=None, semaphores=0):
    scratch = [pltpu.VMEM(s, F32) for s in scratch]
    if semaphores:
        scratch.append(pltpu.SemaphoreType.DMA((semaphores,)))
    return pl.pallas_call(
        functools.partial(kernel, plan),
        out_shape=[whole(s) for s in outs],
        in_specs=[VMEM] * len(operands),
        out_specs=out_specs or [VMEM] * len(outs),
        scratch_shapes=scratch,
        compiler_params=pltpu.CompilerParams(vmem_limit_bytes=VMEM_BYTES),
    )(*operands)


def swap(values, partner):
    axes = ("gx", "gy", "gz")
    counts = [lax.axis_size(a) for a in axes]
    pairs = []
    for i in range(counts[0] * counts[1] * counts[2]):
        to = partner(i // (counts[1] * counts[2]), i // counts[2] % counts[1], i % counts[2])
        if to is not None:
            pairs.append((i, (to[0] * counts[1] + to[1]) * counts[2] + to[2]))
    return lax.ppermute(values, axes, pairs)


def body_fast(divergence, pressure_prev):
    plan = Plan(divergence.shape, tuple(lax.axis_size(a) for a in ("gz", "gx", "gy")))
    ext, level1 = plan.ext, plan.level1
    window, layers = plan.window, (plan.layers, plan.ex, plan.ey)
    payload = [(n + plan.coarse, LANES) for n in (plan.slab_z, plan.slab_x, plan.corner)]
    both = jnp.stack([pressure_prev, divergence])
    both = jnp.pad(both, ((0, 0), (3, 3), (0, plan.ex - plan.block[1]), (0, plan.ey - plan.block[2])))
    r, x, pay_z, pay_x, pay_d = run(
        first_kernel, plan, [ext, ext] + payload,
        [ext, ext, (2, 2 * plan.pairs * plan.ex, LANES), (2, plan.lat_at, plan.ey)],
        both,
    )
    from_z = swap(pay_z, lambda x, y, z: (x, y, z ^ 3))
    from_x = swap(pay_x, lambda x, y, z: (x ^ 1, y, z))
    from_d = swap(pay_d, lambda x, y, z: (x ^ 1, y, z ^ 3))
    r, x, slab = run(
        chip_kernel, plan, [ext, ext, (plan.slab, LANES)], [], r, x, from_z, from_x, from_d
    )
    ours = jnp.concatenate([
        slab, pay_z[plan.slab_z:], from_z[plan.slab_z:], from_x[plan.slab_x:], from_d[plan.corner:]
    ], axis=0)
    got = swap(ours, lambda x, y, z: (x, y, z ^ 1))
    nz2, nx2, _ = plan.level2
    share = (plan.share, LANES)
    r, x, r1, x1, now, later, ours = run(
        plane_kernel, plan,
        [layers, plan.block, window, window, (plan.edge + plan.share, LANES),
         (plan.edge + plan.share, LANES), share],
        [ext, ext, level1, level1, level1, level1, level1, (nz2 * level1[1], LANES),
         (plan.fold,) + share],
        r, x, ours, got,
    )
    from_a = swap(now, lambda x, y, z: (x, y ^ 1, z))
    from_b = swap(later, lambda x, y, z: (x, y ^ 3, z))
    from_c = swap(ours, lambda x, y, z: (x, y ^ 2, z))
    return run(
        last_kernel, plan,
        [plan.block, plan.block, tuple(n >> 3 for n in plan.level2)],
        [(4,) + share, plan.block, plan.block, layers, window,
         (window[0] + 4, window[1] + 16, LANES), ext, layers, window, window,
         (nz2 * nx2, LANES), (2 * plan.pairs * plan.ex, LANES)],
        r, x, r1, x1, ours, from_a, from_b, from_c,
        out_specs=[ANY, ANY, VMEM], semaphores=3,
    )


def fits_fast(shape, peers):
    bz, bx, by = shape
    nz, nx, ny = peers
    return (
        nz == 4 and nx == 2 and ny == 4 and bz == 16 and by == LANES
        and nx * bx == 4 * 8 and ny * by == 4 * LANES
    )


def body(divergence, pressure_prev):
    peers = tuple(lax.axis_size(a) for a in ("gz", "gx", "gy"))
    if fits_fast(divergence.shape, peers):
        return tuple(body_fast(divergence, pressure_prev))
    return body_levels(divergence, pressure_prev)


def solution(mesh):
    in_specs = (P("gz", "gx", "gy"), P("gz", "gx", "gy"))
    out_specs = (P("gz", "gx", "gy"), P("gz", "gx", "gy"), P())
    return jax.shard_map(body, mesh=mesh, in_specs=in_specs, out_specs=out_specs, check_vma=False)
```

```python
import functools
import math

import jax
import jax.numpy as jnp
from jax import lax
from jax.experimental import pallas as pl
from jax.experimental.pallas import tpu as pltpu
from jax.sharding import PartitionSpec as P

LEVELS = 6


first_scale = 1.0 / 7.5
rho_one = 1.0 / (2.0 * (5.0 / 3.0) - 0.6)
carry_coef = 0.6 * rho_one
fresh_coef = 2.0 * rho_one / (0.75 * 6.0)

LANES = 128
F32 = jnp.float32
AXES = (("gz", 0), ("gx", 1), ("gy", 2))


def extended(x, width):
    for axis, dim in AXES:
        peers, length = (lax.axis_size(axis), x.shape[dim + 1])
        up = [(i, (i + 1) % peers) for i in range(peers - 1)]
        down = [(j, i) for i, j in up]
        last = lax.slice_in_dim(x, length - width, length, axis=dim + 1)
        first = lax.slice_in_dim(x, 0, width, axis=dim + 1)
        before = lax.ppermute(last, axis, up)
        after = lax.ppermute(first, axis, down)
        x = jnp.concatenate([before, x, after], axis=dim + 1)
    return x


def stencil(values):
    padded = jnp.pad(values, 1)
    return valid_op(padded)


def valid_op(padded):
    beside = padded[2:, 1:-1, 1:-1] + padded[:-2, 1:-1, 1:-1]
    beside = beside + padded[1:-1, 2:, 1:-1] + padded[1:-1, :-2, 1:-1]
    beside = beside + padded[1:-1, 1:-1, 2:] + padded[1:-1, 1:-1, :-2]
    return 6.0 * padded[1:-1, 1:-1, 1:-1] - beside


def smooth_pass(iterate, source, apply_op, from_zero):
    residue = source if from_zero else source - apply_op(iterate)
    update = residue * first_scale
    iterate = update if from_zero else iterate + update
    residue = source - apply_op(iterate)
    update = carry_coef * update + fresh_coef * residue
    return iterate + update


def restrict(values):
    shape_a, shape_b, shape_c = values.shape
    blocks = values.reshape(shape_a // 2, 2, shape_b // 2, 2, shape_c // 2, 2)
    return 0.5 * jnp.sum(blocks, axis=(1, 3, 5))


def prolong(values):
    shape_a, shape_b, shape_c = values.shape
    spread = jnp.broadcast_to(
        values[:, None, :, None, :, None], (shape_a, 2, shape_b, 2, shape_c, 2)
    )
    return spread.reshape(2 * shape_a, 2 * shape_b, 2 * shape_c)


def vcycle(level_num, iterate, source):
    iterate = smooth_pass(iterate, source, stencil, True)
    coarsest = None
    if level_num < LEVELS - 1:
        residue = source - stencil(iterate)
        coarse, coarsest = vcycle(level_num + 1, None, restrict(residue))
        iterate = iterate + prolong(coarse)
    result = smooth_pass(iterate, source, stencil, False)
    if level_num == LEVELS - 1:
        coarsest = result
    return (result, coarsest)


def collect(values):
    gathered = lax.all_gather(values, "gz", axis=0, tiled=True)
    gathered = lax.all_gather(gathered, "gy", axis=2, tiled=True)
    return lax.all_gather(gathered, "gx", axis=1, tiled=True)


def local_stencil(values):
    return valid_op(extended(values[None], 1)[0])


def own_block(whole, block_shape):
    start_z = lax.axis_index("gz") * block_shape[0]
    start_x = lax.axis_index("gx") * block_shape[1]
    start_y = lax.axis_index("gy") * block_shape[2]
    return lax.dynamic_slice(whole, (start_z, start_x, start_y), block_shape)


def body_cycle(level_num, iterate, source, from_zero, gather_at):
    if level_num == gather_at:
        whole_source = collect(source)
        coarse, coarsest = vcycle(level_num, None, whole_source)
        return (own_block(coarse, source.shape), coarsest)
    iterate = smooth_pass(iterate, source, local_stencil, from_zero)
    residue = source - local_stencil(iterate)
    coarse, coarsest = body_cycle(level_num + 1, None, restrict(residue), True, gather_at)
    iterate = iterate + prolong(coarse)
    return (smooth_pass(iterate, source, local_stencil, False), coarsest)


def body_levels(divergence, pressure_prev):
    pressure, coarse_correction = body_cycle(0, pressure_prev, divergence, False, 3)
    residual = divergence - local_stencil(pressure)
    return (pressure, residual, coarse_correction)


def iota(shape, dim):
    return lax.broadcasted_iota(jnp.int32, shape, dim)


def signed(index, size, extent):
    return jnp.where(index >= (size + extent) // 2, index - extent, index)


def split(values):
    terms = []
    for _ in range(3):
        term = values.astype(jnp.bfloat16)
        terms.append(term)
        values = values - term.astype(F32)
    return terms


def right_dot(values, table):
    parts = [jnp.dot(t, table, preferred_element_type=F32) for t in split(values)]
    return parts[0] + parts[1] + parts[2]


def left_dot(table, values):
    parts = [jnp.dot(table, t, preferred_element_type=F32) for t in split(values)]
    return parts[0] + parts[1] + parts[2]


def as_table(keep, value=1.0):
    return jnp.where(keep, value, 0.0).astype(jnp.bfloat16)


def lateral(v):
    rows, lanes = v.shape
    return (
        pltpu.roll(v, 1, 0) + pltpu.roll(v, rows - 1, 0)
        + pltpu.roll(v, 1, 1) + pltpu.roll(v, lanes - 1, 1)
    )


def apply_at(ref, k, lateral_of=lateral):
    centre = ref[k]
    beside = lateral_of(centre)
    if k > 0:
        beside = beside + ref[k - 1]
    if k < ref.shape[0] - 1:
        beside = beside + ref[k + 1]
    return 6.0 * centre - beside


def wrapped_mask(shape, sizes, low, high):
    keep = None
    for dim, size in sizes.items():
        at = signed(iota(shape, dim), size, shape[dim])
        good = ((at >= 0) | low[dim]) & ((at < size) | high[dim])
        keep = good if keep is None else keep & good
    return jnp.where(keep, 1.0, 0.0).astype(F32)


def side(index, flip):
    if flip == 1:
        return (index & 1) == 0, None
    return index < 2, (index == 1) | (index == 2)


def place(axis, count):
    index = lax.axis_index(axis)
    return index, index > 0, index < count - 1


def only(keep, v):
    return jnp.where(keep, v, 0.0)


def shifted(v, lanes):
    lanes = lanes % LANES
    return v if lanes == 0 else pltpu.roll(v, lanes, 1)


def lanes_of(v, first, count):
    lane = iota(v.shape, 1)
    last = first + count
    if last <= LANES:
        return (lane >= first) & (lane < last)
    return (lane >= first) | (lane < last - LANES)


def moved(v, first, count, to):
    first = first % LANES
    return shifted(only(lanes_of(v, first, count), v), to - first)


def side_pack(tile, slot):
    return moved(tile, LANES - 3, 6, 6 * slot)


def side_unpack(packed, slot):
    return moved(packed, 6 * slot, 6, LANES - 3)


def slab_layers(r_ref, x_ref, up, low, high):
    start = jnp.where(up, high[0], low[0])
    start_x = jnp.where(up, high[1], low[1])
    return [(r_ref, start + j) for j in range(5)] + [(x_ref, start_x + j) for j in range(2)]


def slab_own(r_ref, x_ref, up):
    ez = r_ref.shape[0]
    return slab_layers(r_ref, x_ref, up, (0, 1), (ez - 5, ez - 3))


def slab_there(r_ref, x_ref, up):
    ez = r_ref.shape[0]
    return slab_layers(r_ref, x_ref, up, (1, 3), (ez - 6, ez - 5))


def slab_emit(r_ref, x_ref, out, up):
    ex = r_ref.shape[1]
    lat = None
    for j, (ref, k) in enumerate(slab_own(r_ref, x_ref, up)):
        v = ref[k]
        out[j * ex:(j + 1) * ex, :] = v[:, 0:LANES]
        part = side_pack(v[:, LANES:], j)
        lat = part if lat is None else lat + part
    out[7 * ex:8 * ex, :] = lat


def slab_add(r_ref, x_ref, slab, up):
    ex = r_ref.shape[1]
    lat = slab[7 * ex:8 * ex, :]
    for j, (ref, k) in enumerate(slab_there(r_ref, x_ref, up)):
        ref[k, :, 0:LANES] += slab[j * ex:(j + 1) * ex, :]
        ref[k, :, LANES:] += side_unpack(lat, j)


BESIDE = ((2, 2, 0, 0), (1, 1, 0, 3), (3, 1, 0, 5), (5, 1, 1, 0), (6, 1, 1, 3))


def beside(tile, count):
    row = iota(tile.shape, 0)
    return only((row < count) | (row >= 8 - count), tile)


def thin_emit(r_ref, x_ref, out, up):
    bx = r_ref.shape[1] - 8
    layers = slab_own(r_ref, x_ref, up)
    lat = None
    for j, (ref, k) in enumerate(layers):
        out[j * bx:(j + 1) * bx, :] = ref[k, 0:bx, 0:LANES]
        part = side_pack(ref[k, 0:bx, LANES:], j)
        lat = part if lat is None else lat + part
    tiles = [None, None]
    for j, count, which, turn in BESIDE:
        ref, k = layers[j]
        part = beside(ref[k, bx:, 0:LANES], count)
        part = pltpu.roll(part, turn, 0) if turn else part
        tiles[which] = part if tiles[which] is None else tiles[which] + part
    at = 7 * bx
    out[at:at + 8, :] = tiles[0]
    out[at + 8:at + 16, :] = tiles[1]
    out[at + 16:at + 16 + bx, :] = lat
    for j in (1, 2, 3):
        ref, k = layers[j]
        out[at + 16:at + 24, :] += side_pack(ref[k, bx:, LANES:], 6 + j)


def thin_add(r_ref, x_ref, slab, up):
    bx = r_ref.shape[1] - 8
    layers = slab_there(r_ref, x_ref, up)
    at = 7 * bx
    lat = slab[at + 16:at + 16 + bx, :]
    for j, (ref, k) in enumerate(layers):
        ref[k, 0:bx, 0:LANES] += slab[j * bx:(j + 1) * bx, :]
        ref[k, 0:bx, LANES:] += side_unpack(lat, j)
    for j, count, which, turn in BESIDE:
        ref, k = layers[j]
        tile = slab[at + 8 * which:at + 8 * which + 8, :]
        tile = pltpu.roll(tile, 8 - turn, 0) if turn else tile
        ref[k, bx:, 0:LANES] += beside(tile, count)
    for j in (1, 2, 3):
        ref, k = layers[j]
        ref[k, bx:, LANES:] += side_unpack(lat[0:8], 6 + j)


def rows_out(r, x, up):
    bx = r.shape[0] - 8
    row = iota((8, r.shape[1]), 0)
    first, last, spill = r[0:8], r[bx - 8:bx], r[bx:]
    to_high = pltpu.roll(jnp.where(row >= 6, last, spill), 2, 0)
    to_low = pltpu.roll(jnp.where(row >= 5, spill, first), 3, 0)
    out = jnp.where(up, to_high, to_low)
    if x is None:
        return only(row < 5, out)
    spill = x[bx:]
    extra = jnp.where(up, pltpu.roll(spill, 5, 0), pltpu.roll(spill, 7, 0))
    return jnp.where(row < 5, out, only(row < 7, extra))


def rows_in(r_ref, x_ref, k, rows, up):
    bx = r_ref.shape[1] - 8
    row = iota(rows.shape, 0)
    high, low = pltpu.roll(rows, 5, 0), pltpu.roll(rows, 6, 0)
    r_ref[k, 0:8] += only(jnp.logical_not(up) & (row < 3), low)
    r_ref[k, bx - 8:bx] += only(up & (row >= 5), high)
    r_ref[k, bx:] += jnp.where(up, only(row < 2, high), only(row >= 6, low))
    if x_ref is not None:
        x_ref[k, 0:8] += only(jnp.logical_not(up) & (row < 2), pltpu.roll(rows, 3, 0))
        x_ref[k, bx - 8:bx] += only(up & (row >= 6), pltpu.roll(rows, 1, 0))


def rows_emit(r_ref, x_ref, out, up):
    ez = r_ref.shape[0]
    row = iota((8, LANES), 0)
    lat = jnp.zeros((8, LANES), F32)
    for t, k in enumerate(range(1, ez - 1)):
        far = {1: 0, ez - 2: ez - 1}.get(k)
        rows = rows_out(r_ref[k], None if far is not None else x_ref[k], up)
        tile = rows[:, 0:LANES]
        if far is not None:
            more = rows_out(r_ref[far, :, 0:LANES], None, up)
            more = jnp.where(up, pltpu.roll(more, 5, 0), pltpu.roll(more, 2, 0))
            tile = jnp.where((row == 5) | (row == 6), more, tile)
        out[8 * t:8 * t + 8, :] = tile
        lat = lat + side_pack(rows[:, LANES:], t)
    at = 8 * (ez - 2)
    out[at:at + 8, :] = lat


def rows_add(r_ref, x_ref, slab, up):
    ez = r_ref.shape[0]
    at = 8 * (ez - 2)
    lat = slab[at:at + 8, :]
    row = iota((8, LANES), 0)
    for t, k in enumerate(range(1, ez - 1)):
        far = {1: 0, ez - 2: ez - 1}.get(k)
        tile = slab[8 * t:8 * t + 8, :]
        rows = jnp.concatenate([tile, side_unpack(lat, t)], axis=1)
        rows_in(r_ref, None if far is not None else x_ref, k, rows, up)
        if far is not None:
            tile = only((row == 5) | (row == 6), tile)
            tile = jnp.where(up, pltpu.roll(tile, 6, 0), pltpu.roll(tile, 3, 0))
            rows = jnp.concatenate([tile, jnp.zeros((8, LANES), F32)], axis=1)
            rows_in(r_ref, None, far, rows, up)


class Plan:
    def first_layer(self, iz):
        start = iz * (self.block[0] // 2) - 4
        return jnp.clip(start, 0, self.level1[0] - self.window[0])

    def __init__(self, shape, peers):
        self.peers = peers
        self.block = bz, bx, by = shape
        self.ext = self.ez, self.ex, self.ey = bz + 6, bx + 8, by + LANES
        self.rows, self.pairs = bx // 2, bz // 4 + 2
        self.lat_at = self.pairs * (self.rows + 4)
        self.coarse = self.lat_at + 8
        self.slab = 8 * self.ex
        self.slab_z = 8 * bx + 16
        self.slab_x = 8 * (bz + 5)
        self.corner = 6 * 8
        self.layers = bz + 4
        self.level1 = (peers[0] * bz // 2, peers[1] * bx // 2, LANES)
        self.level2 = (peers[0] * bz // 4, peers[1] * bx // 4, peers[2] * by // 4)
        self.inner = [0, 1] + [2] * bz + [1, 0]
        self.slots, at = [], 0
        for count in self.inner:
            self.slots.append(at)
            at += 3 + count + (2 if count == 2 else 0)
        assert at <= LANES
        self.fine_rows = self.ex
        self.window = (bz // 2 + 8, self.level1[1], LANES)
        self.edge = self.fine_rows + self.window[0] * self.window[1] // 8
        self.wide2 = by // 4 + 4
        self.fold = LANES // self.wide2
        self.lines2 = -(-self.level2[0] // self.fold)
        self.share = self.lines2 * self.level2[1]


def first_kernel(plan, both, r_ref, x_ref, pay_z, pay_x, pay_d, d_one, d_two, pairs, lines):
    p_ext, b_ext = both.at[0], both.at[1]
    bz, bx, by = plan.block
    ez, ex, ey = plan.ext
    peers = plan.peers
    iz, z_low, z_high = place("gz", peers[0])
    ix, x_low, x_high = place("gx", peers[1])
    _, y_low, y_high = place("gy", peers[2])
    flat = wrapped_mask((ex, ey), {0: bx, 1: by}, (x_low, y_low), (x_high, y_high))
    below = jnp.where(z_low, 1.0, 0.0).astype(F32)
    above = jnp.where(z_high, 1.0, 0.0).astype(F32)

    def masked(k, v):
        v = v * flat
        if k < 3:
            v = v * below
        if k >= 3 + bz:
            v = v * above
        return v

    zero = jnp.zeros((ex, ey), F32)
    for k in range(ez):
        if 2 <= k < ez - 2:
            r = b_ext[k] - apply_at(p_ext, k)
            r_ref[k] = r
            d_one[k] = masked(k, r * first_scale)
        else:
            d_one[k] = zero
    for k in range(ez):
        if 1 <= k < ez - 1:
            r = -apply_at(d_one, k)
            if 2 <= k < ez - 2:
                r = r + r_ref[k]
            r_ref[k] = r
            d_two[k] = masked(k, carry_coef * d_one[k] + fresh_coef * r)
        else:
            d_two[k] = zero
    for k in range(ez):
        r = -apply_at(d_two, k)
        if 1 <= k < ez - 1:
            r = r + r_ref[k]
        r_ref[k] = masked(k, r)
        x_ref[k] = p_ext[k] + d_one[k] + d_two[k]


    coarse_z, rows = 2 * plan.pairs, plan.rows
    for zc in range(coarse_z):
        low, high = 2 * zc - 1, 2 * zc
        if low < 0:
            total = r_ref[high]
        elif high >= ez:
            total = r_ref[low]
        else:
            total = r_ref[low] + r_ref[high]
        base = zc * ex
        for tile in range(ey // LANES):
            here = slice(tile * LANES, (tile + 1) * LANES)
            pairs[tile, base:base + ex, :] = total[:, here]
            even = pairs.at[tile][pl.ds(base, ex // 2, 2), :]
            odd = pairs.at[tile][pl.ds(base + 1, ex // 2, 2), :]
            sums = even + odd
            at = zc // 2 * rows
            lines[zc % 2, at:at + rows, here] = sums[0:rows]
            at = plan.pairs * rows + zc // 2 * 4
            lines[zc % 2, at:at + 4, here] = sums[rows:rows + 4]
    fine = signed(iota((ey, LANES), 0), by, ey)
    coarse = signed(iota((ey, LANES), 1), by // 2, LANES)
    table = as_table((fine >> 1) == coarse, 0.5)
    even, odd = right_dot(lines[0], table), right_dot(lines[1], table)
    lane = iota(even.shape, 1)
    main = jnp.where(lane < LANES // 2, even, shifted(odd, LANES // 2))
    own_lat = spill_lat = None
    row = iota((8, LANES), 0)
    for zc in range(coarse_z):
        source = (even, odd)[zc % 2]
        base = zc // 2 * rows
        tile = source[base:base + rows]
        part = moved(tile, by // 2, 2, 4 * zc) + moved(tile, LANES - 2, 2, 4 * zc + 2)
        own_lat = part if own_lat is None else own_lat + part
        base = plan.pairs * rows + zc // 4 * 8
        tile = source[base:base + 8]
        if zc // 2 % 2:
            tile = pltpu.roll(tile, 4, 0)
        tile = only(row < 4, tile)
        slot = LANES // 2 + 4 * zc
        part = moved(tile, by // 2, 2, slot) + moved(tile, LANES - 2, 2, slot + 2)
        spill_lat = part if spill_lat is None else spill_lat + part
    for pay, at in ((pay_z, plan.slab_z), (pay_x, plan.slab_x), (pay_d, plan.corner)):
        pay[at:at + plan.lat_at, :] = main
        pay[at + plan.lat_at:at + plan.coarse, :] = own_lat + spill_lat

    up_z, _ = side(iz, 3)
    up_x, _ = side(ix, 1)
    thin_emit(r_ref, x_ref, pay_z, up_z)
    rows_emit(r_ref, x_ref, pay_x, up_x)
    lat = jnp.zeros((8, LANES), F32)
    start = jnp.where(up_z, ez - 5, 0)
    for j in range(5):
        out = rows_out(r_ref[start + j], x_ref[start + j] if j == 2 else None, up_x)
        pay_d[8 * j:8 * j + 8, :] = out[:, 0:LANES]
        lat = lat + side_pack(out[:, LANES:], j)
    pay_d[40:48, :] = lat


def chip_kernel(plan, r_in, x_in, from_z, from_x, from_d, r_ref, x_ref, pay):
    ez, ex, ey = plan.ext
    iz, _, _ = place("gz", plan.peers[0])
    ix, _, _ = place("gx", plan.peers[1])
    up_z, near = side(iz, 3)
    up_x, _ = side(ix, 1)
    for k in range(ez):
        r_ref[k] = r_in[k]
        x_ref[k] = x_in[k]
    rows_add(r_ref, x_ref, from_x, up_x)

    @pl.when(near)
    def _():
        thin_add(r_ref, x_ref, from_z, up_z)
        start = jnp.where(up_z, ez - 6, 1)
        lat = from_d[40:48, :]
        for j in range(5):
            rows = from_d[8 * j:8 * j + 8, :]
            rows = jnp.concatenate([rows, side_unpack(lat, j)], axis=1)
            rows_in(r_ref, x_ref if j == 2 else None, start + j, rows, up_x)

    slab_emit(r_ref, x_ref, pay, side(iz, 1)[0])


def plane_kernel(plan, ours, theirs, r1_ref, x1_ref, share, b1, d1, d2, r1, x1, pairs, lines):
    bz, bx, by = plan.block
    iz, _, _ = place("gz", plan.peers[0])
    ix, _, _ = place("gx", plan.peers[1])
    iy, y_low, y_high = place("gy", plan.peers[2])

    nz1, nx1, _ = plan.level1
    rows, half = plan.rows, by // 2
    for k in range(nz1):
        b1[k] = jnp.zeros((nx1, LANES), F32)
    row = iota((8, LANES), 0)
    for j in range(plan.peers[0]):
        for i in range(plan.peers[1]):
            flip = iz ^ j
            other = ((flip ^ (flip >> 1)) & 1) == 1
            chip = (flip >> 1) + 2 * (ix ^ i)
            at = pl.multiple_of(plan.slab + chip * plan.coarse, 8)

            def rows_at(offset, count):
                here = pl.ds(pl.multiple_of(at + offset, 8), count)
                return jnp.where(other, theirs[here, :], ours[here, :])

            lat = rows_at(plan.lat_at, 8)
            for zp in range(plan.pairs):
                own = rows_at(zp * rows, rows)
                if zp % 2 == 0:
                    spill_two = rows_at(plan.pairs * rows + zp * 4, 8)
                spill = spill_two if zp % 2 == 0 else pltpu.roll(spill_two, 4, 0)
                for part in range(2):
                    zc = 2 * zp + part
                    k = j * (bz // 2) + zc - 2
                    if not 0 <= k < nz1:
                        continue

                    def wide(main, slot):
                        return (
                            moved(main, part * half, half, 0)
                            + moved(lat, slot, 2, half) + moved(lat, slot + 2, 2, LANES - 2)
                        )

                    b1[k, i * rows:(i + 1) * rows, :] += wide(own, 4 * zc)
                    v = wide(spill, LANES // 2 + 4 * zc)
                    if i + 1 < plan.peers[1]:
                        at_row = (i + 1) * rows
                        b1[k, at_row:at_row + 8, :] += only(row < 2, v)
                    if i > 0:
                        at_row = i * rows - 8
                        b1[k, at_row:at_row + 8, :] += only(row >= 6, pltpu.roll(v, 4, 0))

    lateral1 = level_lateral((nx1, LANES))
    keep = wrapped_mask((nx1, LANES), {1: half}, (None, y_low), (None, y_high))
    for k in range(nz1):
        d1[k] = b1[k] * first_scale
    for k in range(nz1):
        r = b1[k] - apply_at(d1, k, lateral1)
        r1[k] = r
        d2[k] = keep * (carry_coef * d1[k] + fresh_coef * r)
    for k in range(nz1):
        r1[k] = keep * (r1[k] - apply_at(d2, k, lateral1))
        x1[k] = d1[k] + d2[k]

    nz2, nx2, _ = plan.level2
    for zc in range(nz2):
        pairs[zc * nx1:(zc + 1) * nx1, :] = r1[2 * zc] + r1[2 * zc + 1]
        part, at = divmod(zc, plan.lines2)
        lines[part, at * nx2:(at + 1) * nx2, :] = (
            pairs[pl.ds(zc * nx1, nx2, 2), :] + pairs[pl.ds(zc * nx1 + 1, nx2, 2), :]
        )
    fine = signed(iota((LANES, LANES), 0), half, LANES)
    total = None
    for part in range(plan.fold):
        count = min(plan.lines2, nz2 - part * plan.lines2) * nx2
        if count < plan.share:
            lines[part, count:, :] = jnp.zeros((plan.share - count, LANES), F32)
        coarse = iota((LANES, LANES), 1) - part * plan.wide2 - 2
        near = (coarse >= -2) & (coarse < plan.wide2 - 2)
        term = right_dot(lines[part], as_table(near & ((fine >> 1) == coarse), 0.5))
        total = term if total is None else total + term
    share[...] = total

    start = plan.first_layer(iz)
    for k in range(plan.window[0]):
        r1_ref[k] = r1[start + k]
        x1_ref[k] = x1[start + k]


def border_kernel(plan, r_in, x_in, theirs, r1_ref, x1_ref, r_ref, x_ref, pay, later, r_all, x_all):
    bz, bx, by = plan.block
    ez, ex, ey = plan.ext
    layers, half = plan.layers, by // 2
    iz, _, _ = place("gz", plan.peers[0])
    iy, _, _ = place("gy", plan.peers[2])
    nx1 = plan.window[1]
    up_z, _ = side(iz, 1)
    for k in range(ez):
        r_all[k] = r_in[k]
        x_all[k] = x_in[k]
    slab_add(r_all, x_all, theirs, up_z)
    for k in range(layers):
        r_ref[k] = r_all[k + 1]
    for k in range(bz):
        x_ref[k] = x_all[k + 3, 0:bx, 0:by]

    up, _ = side(iy, 1)
    up_inner, _ = side(iy, 3)
    high, low = jnp.zeros((ex, LANES), F32), jnp.zeros((ex, LANES), F32)
    for k in range(layers):
        slot, inner = plan.slots[k], plan.inner[k]
        count = 3 + inner
        v, spill = r_all[k + 1, :, 0:by], r_all[k + 1, :, by:ey]
        high = high + moved(jnp.where(lanes_of(v, 0, 3), spill, v), LANES - inner, count, slot)
        mixed = jnp.where(lanes_of(v, 0, 2), v, spill)
        low = low + moved(mixed, LANES - 3, count, slot)
        if inner == 2:
            spill = x_all[k + 1, :, by:ey]
            high = high + moved(spill, 0, 2, slot + count)
            low = low + moved(spill, LANES - 2, 2, slot + count)
    pay[0:ex, :] = jnp.where(up, high, low)
    later[0:ex, :] = jnp.where(up_inner, high, low)

    per_tile = LANES // 16
    for group in range(plan.window[0] // per_tile):
        tiles = []
        for which in range(2):
            total = jnp.zeros((nx1, LANES), F32)
            for j in range(per_tile):
                k = group * per_tile + j
                first = half - 3 if which == 0 else LANES - 4
                total = total + moved(r1_ref[k], first, 7, 16 * j)
                first = half - 2 if which == 0 else LANES - 3
                total = total + moved(x1_ref[k], first, 5, 16 * j + 7)
            tiles.append(total)
        here = slice(plan.fine_rows + group * nx1, plan.fine_rows + (group + 1) * nx1)
        pay[here, :] = jnp.where(up, tiles[0], tiles[1])
        later[here, :] = jnp.where(up_inner, tiles[0], tiles[1])


def level_lateral(shape):
    row = iota(shape, 0)
    not_first = jnp.where(row > 0, 1.0, 0.0).astype(F32)
    not_last = jnp.where(row < shape[0] - 1, 1.0, 0.0).astype(F32)

    def beside(v):
        return (
            not_first * pltpu.roll(v, 1, 0) + not_last * pltpu.roll(v, shape[0] - 1, 0)
            + pltpu.roll(v, 1, 1) + pltpu.roll(v, LANES - 1, 1)
        )

    return beside


def small_cycle(level, source):
    step = 1 << (level - 2)
    row, lane = iota((8, LANES), 0), iota((8, LANES), 1)
    count = len(source)
    shifts = []
    if step < 8:
        shifts += [(step, 0, row >= step), (8 - step, 0, row < 8 - step)]
    shifts += [(step, 1, lane >= step), (LANES - step, 1, lane < LANES - step)]

    def op(v):
        out = []
        for k in range(count):
            beside = None
            for shift, dim, keep in shifts:
                part = only(keep, pltpu.roll(v[k], shift, dim))
                beside = part if beside is None else beside + part
            if k > 0:
                beside = beside + v[k - 1]
            if k < count - 1:
                beside = beside + v[k + 1]
            out.append(6.0 * v[k] - beside)
        return out

    d = [first_scale * v for v in source]
    r = [b - t for b, t in zip(source, op(d))]
    d2 = [carry_coef * v + fresh_coef * t for v, t in zip(d, r)]
    x = [v + t for v, t in zip(d, d2)]
    r = [v - t for v, t in zip(r, op(d2))]
    coarsest = None
    if level < LEVELS - 1:
        keep = only((row % (2 * step) == 0) & (lane % (2 * step) == 0), 0.5)
        coarse = []
        for k in range(0, count, 2):
            v = r[k] + r[k + 1]
            v = v + pltpu.roll(v, 8 - step, 0)
            coarse.append(keep * (v + pltpu.roll(v, LANES - step, 1)))
        coarse, coarsest = small_cycle(level + 1, coarse)
        e = []
        for v in coarse:
            v = v + pltpu.roll(v, step, 0)
            e += [v + pltpu.roll(v, step, 1)] * 2
        x = [v + t for v, t in zip(x, e)]
        r = [v - t for v, t in zip(r, op(e))]
    d = [first_scale * v for v in r]
    r = [v - t for v, t in zip(r, op(d))]
    x = [v + (t + (carry_coef * t + fresh_coef * u)) for v, t, u in zip(x, d, r)]
    return x, (x if level == LEVELS - 1 else coarsest)


def last_kernel(plan, r_in, x_in, r1_in, x1_in, ours, from_a, from_b, p_out, res_out, last_ref, *scratch):
    shares, p_ref, res_ref, r, q1, e1, e0, d0, d1, r1, lines, wide, sem = scratch
    bz, bx, by = plan.block
    ez, ex, ey = plan.ext
    nz1, nx1, _ = plan.window
    nz2, nx2, _ = plan.level2
    layers, half = plan.layers, by // 2
    iz, z_low, z_high = place("gz", plan.peers[0])
    ix, x_low, x_high = place("gx", plan.peers[1])
    iy, y_low, y_high = place("gy", plan.peers[2])

    for j, ref in enumerate((ours, from_a)):
        for k in range(2):
            here = plan.edge + k * plan.share
            shares[j + 2 * k] = ref[here:here + plan.share, :]
    own2 = half // 2
    source = []
    for part in range(plan.fold):
        total = None
        for j in range(plan.peers[2]):
            v = moved(shares[iy ^ j], part * plan.wide2, plan.wide2, own2 * j - 2)
            total = v if total is None else total + v
        source += [total[nx2 * k:nx2 * (k + 1)] for k in range(plan.lines2)]
    source = source[:nz2]
    e2, coarsest = small_cycle(2, source)
    for k in range(nz2):
        lines[k * nx2:(k + 1) * nx2, :] = e2[k]
    thin = as_table(iota((LANES, LANES), 0) == 8 * iota((LANES, LANES), 1))
    for k in range(last_ref.shape[0]):
        last_ref[k] = right_dot(coarsest[k], thin)[0:1, 0:last_ref.shape[2]]

    up_a, _ = side(iy, 1)
    _, near_b = side(iy, 3)

    def sent(rows):
        a, b = from_a[rows[0]:rows[1], :], only(near_b, from_b[rows[0]:rows[1], :])
        return jnp.where(up_a, a, b), jnp.where(up_a, b, a)

    fine = signed(iota((LANES, LANES), 1), half, LANES)
    coarse = iota((LANES, LANES), 0) - iy * own2
    start = plan.first_layer(iz)
    here = pl.ds(pl.multiple_of(start // 2 * nx2, 8), nz1 // 2 * nx2)
    e2 = right_dot(lines[here, :], as_table((fine >> 1) == coarse))
    for zc in range(nz1 // 2):
        v = e2[zc * nx2:(zc + 1) * nx2]
        for part in range(2):
            q1.at[2 * zc + part][pl.ds(0, nx2, 2), :] = v
            q1.at[2 * zc + part][pl.ds(1, nx2, 2), :] = v
    per_tile = LANES // 16
    lateral1 = level_lateral((nx1, LANES))
    keep = wrapped_mask((nx1, LANES), {1: half}, (None, y_low), (None, y_high))
    for group in range(nz1 // per_tile):
        at = plan.fine_rows + group * nx1
        high, low = sent((at, at + nx1))
        for j in range(per_tile):
            k = group * per_tile + j
            s = 16 * j
            r1[k] = (
                r1_in[k] + moved(high, s, 7, half - 4) + moved(low, s, 7, LANES - 3)
                - apply_at(q1, k, lateral1)
            )
            e1[k + 2, 8:8 + nx1, :] = (
                x1_in[k] + q1[k]
                + moved(high, s + 7, 5, half - 3) + moved(low, s + 7, 5, LANES - 2)
            )
    for k in range(nz1):
        d1[k] = keep * (r1[k] * first_scale)
    nothing = jnp.zeros((8, LANES), F32)
    for k in range(nz1 + 4):
        e1[k, 0:8, :] = nothing
        e1[k, 8 + nx1:16 + nx1, :] = nothing
        if not 2 <= k < nz1 + 2:
            e1[k, 8:8 + nx1, :] = jnp.zeros((nx1, LANES), F32)
    for k in range(nz1):
        v = r1[k] - apply_at(d1, k, lateral1)
        e1[k + 2, 8:8 + nx1, :] += d1[k] + keep * (carry_coef * d1[k] + fresh_coef * v)

    coarse = signed(iota((LANES, ey), 0), half, LANES)
    fine = signed(iota((LANES, ey), 1), by, ey)
    double = as_table((fine >> 1) == coarse)
    half_z, half_x = bz // 2, bx // 2
    for zc in range(half_z + 4):
        here = pl.ds(pl.multiple_of(ix * half_x, 8), half_x + 16)
        v = e1[iz * half_z - start + zc, here, :]
        own, low, high = v[8:8 + half_x], v[0:8], v[8 + half_x:16 + half_x]
        at = zc * ex
        wide[pl.ds(at, half_x, 2), :] = own
        wide[pl.ds(at + 1, half_x, 2), :] = own
        for j in range(2):
            for twin in range(2):
                row = at + bx + 2 * j + twin
                wide[row:row + 1, :] = high[j:j + 1]
                row = at + ex - 4 + 2 * j + twin
                wide[row:row + 1, :] = low[6 + j:7 + j]
    for zc in range(half_z + 4):
        v = right_dot(wide[zc * ex:(zc + 1) * ex, :], double)
        for k in (2 * zc - 1, 2 * zc):
            if 0 <= k < ez:
                e0[k] = v
    flat = wrapped_mask((ex, ey), {0: bx, 1: by}, (x_low, y_low), (x_high, y_high))
    below = jnp.where(z_low, 1.0, 0.0).astype(F32)
    above = jnp.where(z_high, 1.0, 0.0).astype(F32)

    def masked(k, v):
        v = v * flat
        if k < 3:
            v = v * below
        if k >= 3 + bz:
            v = v * above
        return v

    high, low = sent((0, ex))
    for k in range(layers):
        s, inner = plan.slots[k], plan.inner[k]
        v = r_in[k] - apply_at(e0, k + 1)
        own = v[:, 0:by] + moved(high, s, 3, LANES - 3) + moved(low, s + inner, 3, 0)
        spill = v[:, by:ey]
        if inner:
            spill = spill + moved(high, s + 3, inner, 0) + moved(low, s, inner, LANES - inner)
        r[k, :, 0:by] = own
        r[k, :, by:ey] = spill
        d0[k] = masked(k + 1, r[k] * first_scale)
        if inner == 2:
            s = s + 3 + inner
            p_ref[k - 2] = (
                x_in[k - 2] + e0[k + 1, 0:bx, 0:by]
                + (moved(high, s, 2, LANES - 2) + moved(low, s, 2, 0))[0:bx]
            )
    for k in range(1, layers - 1):
        v = r[k] - apply_at(d0, k)
        r[k] = v
        v = masked(k + 1, carry_coef * d0[k] + fresh_coef * v)
        e0[k] = v
        if 2 <= k < 2 + bz:
            p_ref[k - 2] += d0[k, 0:bx, 0:by] + v[0:bx, 0:by]
    copy = pltpu.make_async_copy(p_ref, p_out, sem.at[0])
    copy.start()
    copies = [copy]
    parts = 2
    for part in range(parts):
        here = range(part * bz // parts, (part + 1) * bz // parts)
        for j in here:
            v = r[j + 2] - apply_at(e0, j + 2)
            res_ref[j] = v[0:bx, 0:by]
        here = pl.ds(here[0], bz // parts)
        copy = pltpu.make_async_copy(res_ref.at[here], res_out.at[here], sem.at[1 + part])
        copy.start()
        copies.append(copy)
    for copy in copies:
        copy.wait()


def whole(shape):
    return jax.ShapeDtypeStruct(shape, F32)


VMEM = pl.BlockSpec(memory_space=pltpu.VMEM)
ANY = pl.BlockSpec(memory_space=pl.ANY)
VMEM_BYTES = 24 << 20


def run(kernel, plan, outs, scratch, *operands, out_specs=None, semaphores=0):
    scratch = [pltpu.VMEM(s, F32) for s in scratch]
    if semaphores:
        scratch.append(pltpu.SemaphoreType.DMA((semaphores,)))
    moved_bytes = 4 * sum(math.prod(s) for s in [v.shape for v in operands] + list(outs))
    return pl.pallas_call(
        functools.partial(kernel, plan),
        out_shape=[whole(s) for s in outs],
        in_specs=[VMEM] * len(operands),
        out_specs=out_specs or [VMEM] * len(outs),
        scratch_shapes=scratch,
        compiler_params=pltpu.CompilerParams(vmem_limit_bytes=VMEM_BYTES),
        cost_estimate=pl.CostEstimate(
            flops=8 * moved_bytes, bytes_accessed=moved_bytes, transcendentals=0
        ),
    )(*operands)


def swap(values, partner):
    axes = ("gx", "gy", "gz")
    counts = [lax.axis_size(a) for a in axes]
    pairs = []
    for i in range(counts[0] * counts[1] * counts[2]):
        to = partner(i // (counts[1] * counts[2]), i // counts[2] % counts[1], i % counts[2])
        if to is not None:
            pairs.append((i, (to[0] * counts[1] + to[1]) * counts[2] + to[2]))
    return lax.ppermute(values, axes, pairs)


def body_fast(divergence, pressure_prev):
    plan = Plan(divergence.shape, tuple(lax.axis_size(a) for a in ("gz", "gx", "gy")))
    ext, level1 = plan.ext, plan.level1
    window, layers = plan.window, (plan.layers, plan.ex, plan.ey)
    payload = [(n + plan.coarse, LANES) for n in (plan.slab_z, plan.slab_x, plan.corner)]
    both = jnp.stack([pressure_prev, divergence])
    both = jnp.pad(both, ((0, 0), (3, 3), (0, plan.ex - plan.block[1]), (0, plan.ey - plan.block[2])))
    r, x, pay_z, pay_x, pay_d = run(
        first_kernel, plan, [ext, ext] + payload,
        [ext, ext, (2, 2 * plan.pairs * plan.ex, LANES), (2, plan.lat_at, plan.ey)],
        both,
    )
    from_z = swap(pay_z, lambda x, y, z: (x, y, z ^ 3))
    from_x = swap(pay_x, lambda x, y, z: (x ^ 1, y, z))
    from_d = swap(pay_d, lambda x, y, z: (x ^ 1, y, z ^ 3))
    r, x, slab = run(
        chip_kernel, plan, [ext, ext, (plan.slab, LANES)], [], r, x, from_z, from_x, from_d
    )
    ours = jnp.concatenate([
        slab, pay_z[plan.slab_z:], from_z[plan.slab_z:], from_x[plan.slab_x:], from_d[plan.corner:]
    ], axis=0)
    got = swap(ours, lambda x, y, z: (x, y, z ^ 1))
    nz2, nx2, _ = plan.level2
    share = (plan.share, LANES)
    r1, x1, ours = run(
        plane_kernel, plan, [window, window, share],
        [level1, level1, level1, level1, level1, (nz2 * level1[1], LANES), (plan.fold,) + share],
        ours, got,
    )
    there = swap(ours, lambda x, y, z: (x, y ^ 2, z))
    edge = (plan.edge, LANES)
    r, x, now, later = run(
        border_kernel, plan, [layers, plan.block, edge, edge], [ext, ext], r, x, got, r1, x1
    )
    ours = jnp.concatenate([now, ours, there], axis=0)
    from_a = swap(ours, lambda x, y, z: (x, y ^ 1, z))
    from_b = swap(later, lambda x, y, z: (x, y ^ 3, z) if y in (1, 2) else None)
    return run(
        last_kernel, plan,
        [plan.block, plan.block, tuple(n >> 3 for n in plan.level2)],
        [(4,) + share, plan.block, plan.block, layers, window,
         (window[0] + 4, window[1] + 16, LANES), ext, layers, window, window,
         (nz2 * nx2, LANES), (2 * plan.pairs * plan.ex, LANES)],
        r, x, r1, x1, ours, from_a, from_b,
        out_specs=[ANY, ANY, VMEM], semaphores=3,
    )


def fits_fast(shape, peers):
    bz, bx, by = shape
    nz, nx, ny = peers
    return (
        nz == 4 and nx == 2 and ny == 4 and bz == 16 and by == LANES
        and nx * bx == 4 * 8 and ny * by == 4 * LANES
    )


def body(divergence, pressure_prev):
    peers = tuple(lax.axis_size(a) for a in ("gz", "gx", "gy"))
    if fits_fast(divergence.shape, peers):
        return tuple(body_fast(divergence, pressure_prev))
    return body_levels(divergence, pressure_prev)


def solution(mesh):
    in_specs = (P("gz", "gx", "gy"), P("gz", "gx", "gy"))
    out_specs = (P("gz", "gx", "gy"), P("gz", "gx", "gy"), P())
    return jax.shard_map(body, mesh=mesh, in_specs=in_specs, out_specs=out_specs, check_vma=False)
```

```python
import functools

import jax
import jax.numpy as jnp
from jax import lax
from jax.experimental import pallas as pl
from jax.experimental.pallas import tpu as pltpu
from jax.sharding import PartitionSpec as P

LEVELS = 6


first_scale = 1.0 / 7.5
rho_one = 1.0 / (2.0 * (5.0 / 3.0) - 0.6)
carry_coef = 0.6 * rho_one
fresh_coef = 2.0 * rho_one / (0.75 * 6.0)

LANES = 128
F32 = jnp.float32
AXES = (("gz", 0), ("gx", 1), ("gy", 2))


def extended(x, width):
    for axis, dim in AXES:
        peers, length = (lax.axis_size(axis), x.shape[dim + 1])
        up = [(i, (i + 1) % peers) for i in range(peers - 1)]
        down = [(j, i) for i, j in up]
        last = lax.slice_in_dim(x, length - width, length, axis=dim + 1)
        first = lax.slice_in_dim(x, 0, width, axis=dim + 1)
        before = lax.ppermute(last, axis, up)
        after = lax.ppermute(first, axis, down)
        x = jnp.concatenate([before, x, after], axis=dim + 1)
    return x


def stencil(values):
    padded = jnp.pad(values, 1)
    return valid_op(padded)


def valid_op(padded):
    beside = padded[2:, 1:-1, 1:-1] + padded[:-2, 1:-1, 1:-1]
    beside = beside + padded[1:-1, 2:, 1:-1] + padded[1:-1, :-2, 1:-1]
    beside = beside + padded[1:-1, 1:-1, 2:] + padded[1:-1, 1:-1, :-2]
    return 6.0 * padded[1:-1, 1:-1, 1:-1] - beside


def smooth_pass(iterate, source, apply_op, from_zero):
    residue = source if from_zero else source - apply_op(iterate)
    update = residue * first_scale
    iterate = update if from_zero else iterate + update
    residue = source - apply_op(iterate)
    update = carry_coef * update + fresh_coef * residue
    return iterate + update


def restrict(values):
    shape_a, shape_b, shape_c = values.shape
    blocks = values.reshape(shape_a // 2, 2, shape_b // 2, 2, shape_c // 2, 2)
    return 0.5 * jnp.sum(blocks, axis=(1, 3, 5))


def prolong(values):
    shape_a, shape_b, shape_c = values.shape
    spread = jnp.broadcast_to(
        values[:, None, :, None, :, None], (shape_a, 2, shape_b, 2, shape_c, 2)
    )
    return spread.reshape(2 * shape_a, 2 * shape_b, 2 * shape_c)


def vcycle(level_num, iterate, source):
    iterate = smooth_pass(iterate, source, stencil, True)
    coarsest = None
    if level_num < LEVELS - 1:
        residue = source - stencil(iterate)
        coarse, coarsest = vcycle(level_num + 1, None, restrict(residue))
        iterate = iterate + prolong(coarse)
    result = smooth_pass(iterate, source, stencil, False)
    if level_num == LEVELS - 1:
        coarsest = result
    return (result, coarsest)


def collect(values):
    gathered = lax.all_gather(values, "gz", axis=0, tiled=True)
    gathered = lax.all_gather(gathered, "gy", axis=2, tiled=True)
    return lax.all_gather(gathered, "gx", axis=1, tiled=True)


def local_stencil(values):
    return valid_op(extended(values[None], 1)[0])


def own_block(whole, block_shape):
    start_z = lax.axis_index("gz") * block_shape[0]
    start_x = lax.axis_index("gx") * block_shape[1]
    start_y = lax.axis_index("gy") * block_shape[2]
    return lax.dynamic_slice(whole, (start_z, start_x, start_y), block_shape)


def body_cycle(level_num, iterate, source, from_zero, gather_at):
    if level_num == gather_at:
        whole_source = collect(source)
        coarse, coarsest = vcycle(level_num, None, whole_source)
        return (own_block(coarse, source.shape), coarsest)
    iterate = smooth_pass(iterate, source, local_stencil, from_zero)
    residue = source - local_stencil(iterate)
    coarse, coarsest = body_cycle(level_num + 1, None, restrict(residue), True, gather_at)
    iterate = iterate + prolong(coarse)
    return (smooth_pass(iterate, source, local_stencil, False), coarsest)


def body_levels(divergence, pressure_prev):
    pressure, coarse_correction = body_cycle(0, pressure_prev, divergence, False, 3)
    residual = divergence - local_stencil(pressure)
    return (pressure, residual, coarse_correction)


def iota(shape, dim):
    return lax.broadcasted_iota(jnp.int32, shape, dim)


def signed(index, size, extent):
    return jnp.where(index >= (size + extent) // 2, index - extent, index)


def right_dot(values, table):
    rows = values.shape[0]
    terms = []
    for _ in range(3):
        term = values.astype(jnp.bfloat16)
        terms.append(term)
        values = values - term.astype(F32)
    out = jnp.dot(jnp.concatenate(terms, axis=0), table, preferred_element_type=F32)
    return out[0:rows] + out[rows:2 * rows] + out[2 * rows:3 * rows]


def as_table(keep, value=1.0):
    return jnp.where(keep, value, 0.0).astype(jnp.bfloat16)


def lateral(v):
    rows, lanes = v.shape
    return (
        pltpu.roll(v, 1, 0) + pltpu.roll(v, rows - 1, 0)
        + pltpu.roll(v, 1, 1) + pltpu.roll(v, lanes - 1, 1)
    )


def apply_at(ref, k, lateral_of=lateral):
    centre = ref[k]
    beside = lateral_of(centre)
    if k > 0:
        beside = beside + ref[k - 1]
    if k < ref.shape[0] - 1:
        beside = beside + ref[k + 1]
    return 6.0 * centre - beside


def wrapped_mask(shape, sizes, low, high):
    keep = None
    for dim, size in sizes.items():
        at = signed(iota(shape, dim), size, shape[dim])
        good = ((at >= 0) | low[dim]) & ((at < size) | high[dim])
        keep = good if keep is None else keep & good
    return jnp.where(keep, 1.0, 0.0).astype(F32)


def side(index, flip):
    if flip == 1:
        return (index & 1) == 0, None
    return index < 2, (index == 1) | (index == 2)


def place(axis, count):
    index = lax.axis_index(axis)
    return index, index > 0, index < count - 1


def only(keep, v):
    return jnp.where(keep, v, 0.0)


def shifted(v, lanes):
    lanes = lanes % LANES
    return v if lanes == 0 else pltpu.roll(v, lanes, 1)


def lanes_of(v, first, count):
    lane = iota(v.shape, 1)
    last = first + count
    if last <= LANES:
        return (lane >= first) & (lane < last)
    return (lane >= first) | (lane < last - LANES)


def moved(v, first, count, to):
    first = first % LANES
    return shifted(only(lanes_of(v, first, count), v), to - first)


def landed(v, first, count, to):
    to = to % LANES
    v = shifted(v, to - first)
    return only(lanes_of(v, to, count), v)


def side_pack(tile, slot):
    return moved(tile, LANES - 3, 6, 6 * slot)


def side_unpack(packed, slot):
    return landed(packed, 6 * slot, 6, LANES - 3)


def slab_layers(r_ref, x_ref, up, low, high):
    start = jnp.where(up, high[0], low[0])
    start_x = jnp.where(up, high[1], low[1])
    return [(r_ref, start + j) for j in range(5)] + [(x_ref, start_x + j) for j in range(2)]


def slab_own(r_ref, x_ref, up):
    ez = r_ref.shape[0]
    return slab_layers(r_ref, x_ref, up, (0, 1), (ez - 5, ez - 3))


def slab_there(r_ref, x_ref, up):
    ez = r_ref.shape[0]
    return slab_layers(r_ref, x_ref, up, (1, 3), (ez - 6, ez - 5))


def slab_emit(r_ref, x_ref, out, up):
    ex = r_ref.shape[1]
    lat = None
    for j, (ref, k) in enumerate(slab_own(r_ref, x_ref, up)):
        v = ref[k]
        out[j * ex:(j + 1) * ex, :] = v[:, 0:LANES]
        part = side_pack(v[:, LANES:], j)
        lat = part if lat is None else lat + part
    out[7 * ex:8 * ex, :] = lat


def slab_add(r_ref, x_ref, slab, up):
    ex = r_ref.shape[1]
    lat = slab[7 * ex:8 * ex, :]
    for j, (ref, k) in enumerate(slab_there(r_ref, x_ref, up)):
        ref[k, :, 0:LANES] += slab[j * ex:(j + 1) * ex, :]
        ref[k, :, LANES:] += side_unpack(lat, j)


BESIDE = ((2, 2, 0, 0), (1, 1, 0, 3), (3, 1, 0, 5), (5, 1, 1, 0), (6, 1, 1, 3))


def beside(tile, count):
    row = iota(tile.shape, 0)
    return only((row < count) | (row >= 8 - count), tile)


def thin_emit(r_ref, x_ref, out, up):
    bx = r_ref.shape[1] - 8
    layers = slab_own(r_ref, x_ref, up)
    lat = None
    for j, (ref, k) in enumerate(layers):
        out[j * bx:(j + 1) * bx, :] = ref[k, 0:bx, 0:LANES]
        part = side_pack(ref[k, 0:bx, LANES:], j)
        lat = part if lat is None else lat + part
    tiles = [None, None]
    for j, count, which, turn in BESIDE:
        ref, k = layers[j]
        part = beside(ref[k, bx:, 0:LANES], count)
        part = pltpu.roll(part, turn, 0) if turn else part
        tiles[which] = part if tiles[which] is None else tiles[which] + part
    at = 7 * bx
    out[at:at + 8, :] = tiles[0]
    out[at + 8:at + 16, :] = tiles[1]
    out[at + 16:at + 16 + bx, :] = lat
    for j in (1, 2, 3):
        ref, k = layers[j]
        out[at + 16:at + 24, :] += side_pack(ref[k, bx:, LANES:], 6 + j)


def thin_add(r_ref, x_ref, slab, up):
    bx = r_ref.shape[1] - 8
    layers = slab_there(r_ref, x_ref, up)
    at = 7 * bx
    lat = slab[at + 16:at + 16 + bx, :]
    for j, (ref, k) in enumerate(layers):
        ref[k, 0:bx, 0:LANES] += slab[j * bx:(j + 1) * bx, :]
        ref[k, 0:bx, LANES:] += side_unpack(lat, j)
    for j, count, which, turn in BESIDE:
        ref, k = layers[j]
        tile = slab[at + 8 * which:at + 8 * which + 8, :]
        tile = pltpu.roll(tile, 8 - turn, 0) if turn else tile
        ref[k, bx:, 0:LANES] += beside(tile, count)
    for j in (1, 2, 3):
        ref, k = layers[j]
        ref[k, bx:, LANES:] += side_unpack(lat[0:8], 6 + j)


def rows_out(r, x, up):
    bx = r.shape[0] - 8
    row = iota((8, r.shape[1]), 0)
    first, last, spill = r[0:8], r[bx - 8:bx], r[bx:]
    to_high = pltpu.roll(jnp.where(row >= 6, last, spill), 2, 0)
    to_low = pltpu.roll(jnp.where(row >= 5, spill, first), 3, 0)
    out = jnp.where(up, to_high, to_low)
    if x is None:
        return only(row < 5, out)
    spill = x[bx:]
    extra = jnp.where(up, pltpu.roll(spill, 5, 0), pltpu.roll(spill, 7, 0))
    return jnp.where(row < 5, out, only(row < 7, extra))


def rows_in(r_ref, x_ref, k, rows, up):
    bx = r_ref.shape[1] - 8
    row = iota(rows.shape, 0)
    high, low = pltpu.roll(rows, 5, 0), pltpu.roll(rows, 6, 0)
    r_ref[k, 0:8] += only(jnp.logical_not(up) & (row < 3), low)
    r_ref[k, bx - 8:bx] += only(up & (row >= 5), high)
    r_ref[k, bx:] += jnp.where(up, only(row < 2, high), only(row >= 6, low))
    if x_ref is not None:
        x_ref[k, 0:8] += only(jnp.logical_not(up) & (row < 2), pltpu.roll(rows, 3, 0))
        x_ref[k, bx - 8:bx] += only(up & (row >= 6), pltpu.roll(rows, 1, 0))


def rows_emit(r_ref, x_ref, out, up):
    ez = r_ref.shape[0]
    row = iota((8, LANES), 0)
    lat = jnp.zeros((8, LANES), F32)
    for t, k in enumerate(range(1, ez - 1)):
        far = {1: 0, ez - 2: ez - 1}.get(k)
        rows = rows_out(r_ref[k], None if far is not None else x_ref[k], up)
        tile = rows[:, 0:LANES]
        if far is not None:
            more = rows_out(r_ref[far, :, 0:LANES], None, up)
            more = jnp.where(up, pltpu.roll(more, 5, 0), pltpu.roll(more, 2, 0))
            tile = jnp.where((row == 5) | (row == 6), more, tile)
        out[8 * t:8 * t + 8, :] = tile
        lat = lat + side_pack(rows[:, LANES:], t)
    at = 8 * (ez - 2)
    out[at:at + 8, :] = lat


def rows_add(r_ref, x_ref, slab, up):
    ez = r_ref.shape[0]
    at = 8 * (ez - 2)
    lat = slab[at:at + 8, :]
    row = iota((8, LANES), 0)
    for t, k in enumerate(range(1, ez - 1)):
        far = {1: 0, ez - 2: ez - 1}.get(k)
        tile = slab[8 * t:8 * t + 8, :]
        rows = jnp.concatenate([tile, side_unpack(lat, t)], axis=1)
        rows_in(r_ref, None if far is not None else x_ref, k, rows, up)
        if far is not None:
            tile = only((row == 5) | (row == 6), tile)
            tile = jnp.where(up, pltpu.roll(tile, 6, 0), pltpu.roll(tile, 3, 0))
            rows = jnp.concatenate([tile, jnp.zeros((8, LANES), F32)], axis=1)
            rows_in(r_ref, None, far, rows, up)


class Plan:
    def first_layer(self, iz):
        start = iz * (self.block[0] // 2) - 4
        return jnp.clip(start, 0, self.level1[0] - self.window[0])

    def __init__(self, shape, peers):
        self.peers = peers
        self.block = bz, bx, by = shape
        self.ext = self.ez, self.ex, self.ey = bz + 6, bx + 8, by + LANES
        self.rows, self.pairs = bx // 2, bz // 4 + 2
        self.lat_at = self.pairs * (self.rows + 4)
        self.coarse = self.lat_at + 8
        self.slab = 8 * self.ex
        self.slab_z = 8 * bx + 16
        self.slab_x = 8 * (bz + 5)
        self.corner = 6 * 8
        self.layers = bz + 4
        self.level1 = (peers[0] * bz // 2, peers[1] * bx // 2, LANES)
        self.level2 = (peers[0] * bz // 4, peers[1] * bx // 4, peers[2] * by // 4)
        self.inner = [0, 1] + [2] * bz + [1, 0]
        self.slots, at = [], 0
        for count in self.inner:
            self.slots.append(at)
            at += 3 + count + (2 if count == 2 else 0)
        assert at <= LANES
        self.fine_rows = self.ex
        self.window = (bz // 2 + 8, self.level1[1], LANES)
        self.edge = self.fine_rows + self.window[0] * self.window[1] // 8
        self.wide2 = by // 4 + 4
        self.fold = LANES // self.wide2
        self.lines2 = -(-self.level2[0] // self.fold)
        self.share = self.lines2 * self.level2[1]


def first_kernel(plan, both, r_ref, x_ref, pay_z, pay_x, pay_d, d_one, d_two, pairs, lines):
    p_ext, b_ext = both.at[0], both.at[1]
    bz, bx, by = plan.block
    ez, ex, ey = plan.ext
    peers = plan.peers
    iz, z_low, z_high = place("gz", peers[0])
    ix, x_low, x_high = place("gx", peers[1])
    _, y_low, y_high = place("gy", peers[2])
    flat = wrapped_mask((ex, ey), {0: bx, 1: by}, (x_low, y_low), (x_high, y_high))
    below = jnp.where(z_low, 1.0, 0.0).astype(F32)
    above = jnp.where(z_high, 1.0, 0.0).astype(F32)

    def masked(k, v):
        v = v * flat
        if k < 3:
            v = v * below
        if k >= 3 + bz:
            v = v * above
        return v

    zero = jnp.zeros((ex, ey), F32)
    for k in range(ez):
        if 2 <= k < ez - 2:
            r = b_ext[k] - apply_at(p_ext, k)
            r_ref[k] = r
            d_one[k] = masked(k, r * first_scale)
        else:
            d_one[k] = zero
    for k in range(ez):
        if 1 <= k < ez - 1:
            r = -apply_at(d_one, k)
            if 2 <= k < ez - 2:
                r = r + r_ref[k]
            r_ref[k] = r
            d_two[k] = masked(k, carry_coef * d_one[k] + fresh_coef * r)
        else:
            d_two[k] = zero
    for k in range(ez):
        r = -apply_at(d_two, k)
        if 1 <= k < ez - 1:
            r = r + r_ref[k]
        r_ref[k] = masked(k, r)
        x_ref[k] = p_ext[k] + d_one[k] + d_two[k]


    coarse_z, rows = 2 * plan.pairs, plan.rows
    for zc in range(coarse_z):
        low, high = 2 * zc - 1, 2 * zc
        if low < 0:
            total = r_ref[high]
        elif high >= ez:
            total = r_ref[low]
        else:
            total = r_ref[low] + r_ref[high]
        base = zc * ex
        for tile in range(ey // LANES):
            here = slice(tile * LANES, (tile + 1) * LANES)
            pairs[tile, base:base + ex, :] = total[:, here]
            even = pairs.at[tile][pl.ds(base, ex // 2, 2), :]
            odd = pairs.at[tile][pl.ds(base + 1, ex // 2, 2), :]
            sums = even + odd
            at = zc // 2 * rows
            at += zc % 2 * plan.lat_at
            lines[at:at + rows, here] = sums[0:rows]
            at = plan.pairs * rows + zc // 2 * 4 + zc % 2 * plan.lat_at
            lines[at:at + 4, here] = sums[rows:rows + 4]
    fine = signed(iota((ey, LANES), 0), by, ey)
    coarse = signed(iota((ey, LANES), 1), by // 2, LANES)
    table = as_table((fine >> 1) == coarse, 0.5)
    out = right_dot(lines[...], table)
    even, odd = out[0:plan.lat_at], out[plan.lat_at:]
    lane = iota(even.shape, 1)
    main = jnp.where(lane < LANES // 2, even, shifted(odd, LANES // 2))
    own_lat = spill_lat = None
    row = iota((8, LANES), 0)
    for zc in range(coarse_z):
        source = (even, odd)[zc % 2]
        base = zc // 2 * rows
        tile = source[base:base + rows]
        part = moved(tile, by // 2, 2, 4 * zc) + moved(tile, LANES - 2, 2, 4 * zc + 2)
        own_lat = part if own_lat is None else own_lat + part
        base = plan.pairs * rows + zc // 4 * 8
        tile = source[base:base + 8]
        if zc // 2 % 2:
            tile = pltpu.roll(tile, 4, 0)
        tile = only(row < 4, tile)
        slot = LANES // 2 + 4 * zc
        part = moved(tile, by // 2, 2, slot) + moved(tile, LANES - 2, 2, slot + 2)
        spill_lat = part if spill_lat is None else spill_lat + part
    for pay, at in ((pay_z, plan.slab_z), (pay_x, plan.slab_x), (pay_d, plan.corner)):
        pay[at:at + plan.lat_at, :] = main
        pay[at + plan.lat_at:at + plan.coarse, :] = own_lat + spill_lat

    up_z, _ = side(iz, 3)
    up_x, _ = side(ix, 1)
    thin_emit(r_ref, x_ref, pay_z, up_z)
    rows_emit(r_ref, x_ref, pay_x, up_x)
    lat = jnp.zeros((8, LANES), F32)
    start = jnp.where(up_z, ez - 5, 0)
    for j in range(5):
        out = rows_out(r_ref[start + j], x_ref[start + j] if j == 2 else None, up_x)
        pay_d[8 * j:8 * j + 8, :] = out[:, 0:LANES]
        lat = lat + side_pack(out[:, LANES:], j)
    pay_d[40:48, :] = lat


def chip_kernel(plan, r_in, x_in, from_z, from_x, from_d, r_ref, x_ref, pay):
    ez, ex, ey = plan.ext
    iz, _, _ = place("gz", plan.peers[0])
    ix, _, _ = place("gx", plan.peers[1])
    up_z, near = side(iz, 3)
    up_x, _ = side(ix, 1)
    for k in range(ez):
        r_ref[k] = r_in[k]
        x_ref[k] = x_in[k]
    rows_add(r_ref, x_ref, from_x, up_x)

    @pl.when(near)
    def _():
        thin_add(r_ref, x_ref, from_z, up_z)
        start = jnp.where(up_z, ez - 6, 1)
        lat = from_d[40:48, :]
        for j in range(5):
            rows = from_d[8 * j:8 * j + 8, :]
            rows = jnp.concatenate([rows, side_unpack(lat, j)], axis=1)
            rows_in(r_ref, x_ref if j == 2 else None, start + j, rows, up_x)

    slab_emit(r_ref, x_ref, pay, side(iz, 1)[0])


def plane_kernel(plan, r_in, x_in, ours, theirs, r_ref, x_ref, r1_ref, x1_ref, pay, later, share,
                 r_all, x_all, b1, d1, d2, r1, x1, pairs, lines):
    bz, bx, by = plan.block
    ez, ex, ey = plan.ext
    layers = plan.layers
    iz, _, _ = place("gz", plan.peers[0])
    ix, _, _ = place("gx", plan.peers[1])
    iy, y_low, y_high = place("gy", plan.peers[2])
    up_z, _ = side(iz, 1)
    for k in range(ez):
        r_all[k] = r_in[k]
        x_all[k] = x_in[k]
    slab_add(r_all, x_all, theirs, up_z)
    for k in range(layers):
        r_ref[k] = r_all[k + 1]
    for k in range(bz):
        x_ref[k] = x_all[k + 3, 0:bx, 0:by]

    up, _ = side(iy, 1)
    up_inner, _ = side(iy, 3)
    high, low = jnp.zeros((ex, LANES), F32), jnp.zeros((ex, LANES), F32)
    for k in range(layers):
        slot, inner = plan.slots[k], plan.inner[k]
        count = 3 + inner
        v, spill = r_all[k + 1, :, 0:by], r_all[k + 1, :, by:ey]
        high = high + moved(jnp.where(lanes_of(v, 0, 3), spill, v), LANES - inner, count, slot)
        mixed = jnp.where(lanes_of(v, 0, 2), v, spill)
        low = low + moved(mixed, LANES - 3, count, slot)
        if inner == 2:
            spill = x_all[k + 1, :, by:ey]
            high = high + moved(spill, 0, 2, slot + count)
            low = low + moved(spill, LANES - 2, 2, slot + count)
    pay[0:ex, :] = jnp.where(up, high, low)
    later[0:ex, :] = jnp.where(up_inner, high, low)

    nz1, nx1, _ = plan.level1
    rows, half = plan.rows, by // 2
    for k in range(nz1):
        b1[k] = jnp.zeros((nx1, LANES), F32)
    row = iota((8, LANES), 0)
    for j in range(plan.peers[0]):
        for i in range(plan.peers[1]):
            flip = iz ^ j
            other = ((flip ^ (flip >> 1)) & 1) == 1
            chip = (flip >> 1) + 2 * (ix ^ i)
            at = pl.multiple_of(plan.slab + chip * plan.coarse, 8)

            def rows_at(offset, count):
                here = pl.ds(pl.multiple_of(at + offset, 8), count)
                return jnp.where(other, theirs[here, :], ours[here, :])

            lat = rows_at(plan.lat_at, 8)
            for zp in range(plan.pairs):
                own = rows_at(zp * rows, rows)
                if zp % 2 == 0:
                    spill_two = rows_at(plan.pairs * rows + zp * 4, 8)
                spill = spill_two if zp % 2 == 0 else pltpu.roll(spill_two, 4, 0)
                for part in range(2):
                    zc = 2 * zp + part
                    k = j * (bz // 2) + zc - 2
                    if not 0 <= k < nz1:
                        continue

                    def wide(main, slot):
                        return (
                            landed(main, part * half, half, 0)
                            + landed(lat, slot, 2, half) + landed(lat, slot + 2, 2, LANES - 2)
                        )

                    b1[k, i * rows:(i + 1) * rows, :] += wide(own, 4 * zc)
                    v = wide(spill, LANES // 2 + 4 * zc)
                    if i + 1 < plan.peers[1]:
                        at_row = (i + 1) * rows
                        b1[k, at_row:at_row + 8, :] += only(row < 2, v)
                    if i > 0:
                        at_row = i * rows - 8
                        b1[k, at_row:at_row + 8, :] += only(row >= 6, pltpu.roll(v, 4, 0))

    lateral1 = level_lateral((nx1, LANES))
    keep = wrapped_mask((nx1, LANES), {1: half}, (None, y_low), (None, y_high))
    for k in range(nz1):
        d1[k] = b1[k] * first_scale
    for k in range(nz1):
        r = b1[k] - apply_at(d1, k, lateral1)
        r1[k] = r
        d2[k] = keep * (carry_coef * d1[k] + fresh_coef * r)
    for k in range(nz1):
        r1[k] = keep * (r1[k] - apply_at(d2, k, lateral1))
        x1[k] = d1[k] + d2[k]

    nz2, nx2, _ = plan.level2
    for zc in range(nz2):
        pairs[zc * nx1:(zc + 1) * nx1, :] = r1[2 * zc] + r1[2 * zc + 1]
        part, at = divmod(zc, plan.lines2)
        lines[at * nx2:(at + 1) * nx2, part * LANES:(part + 1) * LANES] = (
            pairs[pl.ds(zc * nx1, nx2, 2), :] + pairs[pl.ds(zc * nx1 + 1, nx2, 2), :]
        )
    shape = (plan.fold * LANES, LANES)
    fine, coarse = iota(shape, 0), iota(shape, 1)
    part, fine = fine // LANES, signed(fine % LANES, half, LANES)
    coarse = coarse - part * plan.wide2 - 2
    near = (coarse >= -2) & (coarse < plan.wide2 - 2)
    for part in range(plan.fold):
        count = min(plan.lines2, nz2 - part * plan.lines2) * nx2
        if count < plan.share:
            here = slice(part * LANES, (part + 1) * LANES)
            lines[count:, here] = jnp.zeros((plan.share - count, LANES), F32)
    total = right_dot(lines[...], as_table(near & ((fine >> 1) == coarse), 0.5))
    share[...] = total
    pay[plan.edge:plan.edge + plan.share, :] = total
    later[plan.edge:plan.edge + plan.share, :] = total

    start = plan.first_layer(iz)
    for k in range(plan.window[0]):
        r1_ref[k] = r1[start + k]
        x1_ref[k] = x1[start + k]
    per_tile = LANES // 16
    for group in range(plan.window[0] // per_tile):
        tiles = []
        for which in range(2):
            total = jnp.zeros((nx1, LANES), F32)
            for j in range(per_tile):
                k = group * per_tile + j
                first = half - 3 if which == 0 else LANES - 4
                total = total + moved(r1_ref[k], first, 7, 16 * j)
                first = half - 2 if which == 0 else LANES - 3
                total = total + moved(x1_ref[k], first, 5, 16 * j + 7)
            tiles.append(total)
        here = slice(plan.fine_rows + group * nx1, plan.fine_rows + (group + 1) * nx1)
        pay[here, :] = jnp.where(up, tiles[0], tiles[1])
        later[here, :] = jnp.where(up_inner, tiles[0], tiles[1])


def level_lateral(shape):
    row = iota(shape, 0)
    not_first = jnp.where(row > 0, 1.0, 0.0).astype(F32)
    not_last = jnp.where(row < shape[0] - 1, 1.0, 0.0).astype(F32)

    def beside(v):
        return (
            not_first * pltpu.roll(v, 1, 0) + not_last * pltpu.roll(v, shape[0] - 1, 0)
            + pltpu.roll(v, 1, 1) + pltpu.roll(v, LANES - 1, 1)
        )

    return beside


def small_cycle(level, source):
    step = 1 << (level - 2)
    row, lane = iota((8, LANES), 0), iota((8, LANES), 1)
    count = len(source)
    shifts = []
    if step < 8:
        shifts += [(step, 0, row >= step), (8 - step, 0, row < 8 - step)]
    shifts += [(step, 1, lane >= step), (LANES - step, 1, lane < LANES - step)]

    def op(v):
        out = []
        for k in range(count):
            beside = None
            for shift, dim, keep in shifts:
                part = only(keep, pltpu.roll(v[k], shift, dim))
                beside = part if beside is None else beside + part
            if k > 0:
                beside = beside + v[k - 1]
            if k < count - 1:
                beside = beside + v[k + 1]
            out.append(6.0 * v[k] - beside)
        return out

    d = [first_scale * v for v in source]
    r = [b - t for b, t in zip(source, op(d))]
    d2 = [carry_coef * v + fresh_coef * t for v, t in zip(d, r)]
    x = [v + t for v, t in zip(d, d2)]
    r = [v - t for v, t in zip(r, op(d2))]
    coarsest = None
    if level < LEVELS - 1:
        keep = only((row % (2 * step) == 0) & (lane % (2 * step) == 0), 0.5)
        coarse = []
        for k in range(0, count, 2):
            v = r[k] + r[k + 1]
            v = v + pltpu.roll(v, 8 - step, 0)
            coarse.append(keep * (v + pltpu.roll(v, LANES - step, 1)))
        coarse, coarsest = small_cycle(level + 1, coarse)
        e = []
        for v in coarse:
            v = v + pltpu.roll(v, step, 0)
            e += [v + pltpu.roll(v, step, 1)] * 2
        x = [v + t for v, t in zip(x, e)]
        r = [v - t for v, t in zip(r, op(e))]
    d = [first_scale * v for v in r]
    r = [v - t for v, t in zip(r, op(d))]
    x = [v + (t + (carry_coef * t + fresh_coef * u)) for v, t, u in zip(x, d, r)]
    return x, (x if level == LEVELS - 1 else coarsest)


def last_kernel(plan, r_in, x_in, r1_in, x1_in, ours, from_a, from_b, from_c, p_out, res_out, last_ref, *scratch):
    shares, p_ref, res_ref, r, q1, e1, e0, d0, d1, r1, lines, wide, sem = scratch
    bz, bx, by = plan.block
    ez, ex, ey = plan.ext
    nz1, nx1, _ = plan.window
    nz2, nx2, _ = plan.level2
    layers, half = plan.layers, by // 2
    iz, z_low, z_high = place("gz", plan.peers[0])
    ix, x_low, x_high = place("gx", plan.peers[1])
    iy, y_low, y_high = place("gy", plan.peers[2])

    shares[0] = ours[...]
    shares[1] = from_a[plan.edge:plan.edge + plan.share, :]
    shares[3] = from_b[plan.edge:plan.edge + plan.share, :]
    shares[2] = from_c[...]
    own2 = half // 2
    source = []
    for part in range(plan.fold):
        total = None
        for j in range(plan.peers[2]):
            v = moved(shares[iy ^ j], part * plan.wide2, plan.wide2, own2 * j - 2)
            total = v if total is None else total + v
        source += [total[nx2 * k:nx2 * (k + 1)] for k in range(plan.lines2)]
    source = source[:nz2]
    e2, coarsest = small_cycle(2, source)
    for k in range(nz2):
        lines[k * nx2:(k + 1) * nx2, :] = e2[k]
    thin = as_table(iota((LANES, LANES), 0) == 8 * iota((LANES, LANES), 1))
    for k in range(last_ref.shape[0]):
        last_ref[k] = right_dot(coarsest[k], thin)[0:1, 0:last_ref.shape[2]]

    up_a, _ = side(iy, 1)
    _, near_b = side(iy, 3)

    def sent(rows):
        a, b = from_a[rows[0]:rows[1], :], only(near_b, from_b[rows[0]:rows[1], :])
        return jnp.where(up_a, a, b), jnp.where(up_a, b, a)

    fine = signed(iota((LANES, LANES), 1), half, LANES)
    coarse = iota((LANES, LANES), 0) - iy * own2
    start = plan.first_layer(iz)
    here = pl.ds(pl.multiple_of(start // 2 * nx2, 8), nz1 // 2 * nx2)
    e2 = right_dot(lines[here, :], as_table((fine >> 1) == coarse))
    for zc in range(nz1 // 2):
        v = e2[zc * nx2:(zc + 1) * nx2]
        for part in range(2):
            q1.at[2 * zc + part][pl.ds(0, nx2, 2), :] = v
            q1.at[2 * zc + part][pl.ds(1, nx2, 2), :] = v
    per_tile = LANES // 16
    lateral1 = level_lateral((nx1, LANES))
    keep = wrapped_mask((nx1, LANES), {1: half}, (None, y_low), (None, y_high))
    for group in range(nz1 // per_tile):
        at = plan.fine_rows + group * nx1
        high, low = sent((at, at + nx1))
        for j in range(per_tile):
            k = group * per_tile + j
            s = 16 * j
            r1[k] = (
                r1_in[k] + landed(high, s, 7, half - 4) + landed(low, s, 7, LANES - 3)
                - apply_at(q1, k, lateral1)
            )
            e1[k + 2, 8:8 + nx1, :] = (
                x1_in[k] + q1[k]
                + landed(high, s + 7, 5, half - 3) + landed(low, s + 7, 5, LANES - 2)
            )
    for k in range(nz1):
        d1[k] = keep * (r1[k] * first_scale)
    nothing = jnp.zeros((8, LANES), F32)
    for k in range(nz1 + 4):
        e1[k, 0:8, :] = nothing
        e1[k, 8 + nx1:16 + nx1, :] = nothing
        if not 2 <= k < nz1 + 2:
            e1[k, 8:8 + nx1, :] = jnp.zeros((nx1, LANES), F32)
    for k in range(nz1):
        v = r1[k] - apply_at(d1, k, lateral1)
        e1[k + 2, 8:8 + nx1, :] += d1[k] + keep * (carry_coef * d1[k] + fresh_coef * v)

    coarse = signed(iota((LANES, ey), 0), half, LANES)
    fine = signed(iota((LANES, ey), 1), by, ey)
    double = as_table((fine >> 1) == coarse)
    half_z, half_x = bz // 2, bx // 2
    for zc in range(half_z + 4):
        here = pl.ds(pl.multiple_of(ix * half_x, 8), half_x + 16)
        v = e1[iz * half_z - start + zc, here, :]
        own, low, high = v[8:8 + half_x], v[0:8], v[8 + half_x:16 + half_x]
        at = zc * ex
        wide[pl.ds(at, half_x, 2), :] = own
        wide[pl.ds(at + 1, half_x, 2), :] = own
        for j in range(2):
            for twin in range(2):
                row = at + bx + 2 * j + twin
                wide[row:row + 1, :] = high[j:j + 1]
                row = at + ex - 4 + 2 * j + twin
                wide[row:row + 1, :] = low[6 + j:7 + j]
    out = right_dot(wide[...], double)
    for zc in range(half_z + 4):
        for k in (2 * zc - 1, 2 * zc):
            if 0 <= k < ez:
                e0[k] = out[zc * ex:(zc + 1) * ex]
    flat = wrapped_mask((ex, ey), {0: bx, 1: by}, (x_low, y_low), (x_high, y_high))
    below = jnp.where(z_low, 1.0, 0.0).astype(F32)
    above = jnp.where(z_high, 1.0, 0.0).astype(F32)

    def masked(k, v):
        v = v * flat
        if k < 3:
            v = v * below
        if k >= 3 + bz:
            v = v * above
        return v

    high, low = sent((0, ex))
    for k in range(layers):
        s, inner = plan.slots[k], plan.inner[k]
        v = r_in[k] - apply_at(e0, k + 1)
        own = v[:, 0:by] + landed(high, s, 3, LANES - 3) + landed(low, s + inner, 3, 0)
        spill = v[:, by:ey]
        if inner:
            spill = spill + landed(high, s + 3, inner, 0) + landed(low, s, inner, LANES - inner)
        r[k, :, 0:by] = own
        r[k, :, by:ey] = spill
        d0[k] = masked(k + 1, r[k] * first_scale)
        if inner == 2:
            s = s + 3 + inner
            p_ref[k - 2] = (
                x_in[k - 2] + e0[k + 1, 0:bx, 0:by]
                + (landed(high, s, 2, LANES - 2) + landed(low, s, 2, 0))[0:bx]
            )
    for k in range(1, layers - 1):
        v = r[k] - apply_at(d0, k)
        r[k] = v
        v = masked(k + 1, carry_coef * d0[k] + fresh_coef * v)
        e0[k] = v
        if 2 <= k < 2 + bz:
            p_ref[k - 2] += d0[k, 0:bx, 0:by] + v[0:bx, 0:by]
    copy = pltpu.make_async_copy(p_ref, p_out, sem.at[0])
    copy.start()
    copies = [copy]
    parts = 2
    for part in range(parts):
        here = range(part * bz // parts, (part + 1) * bz // parts)
        for j in here:
            v = r[j + 2] - apply_at(e0, j + 2)
            res_ref[j] = v[0:bx, 0:by]
        here = pl.ds(here[0], bz // parts)
        copy = pltpu.make_async_copy(res_ref.at[here], res_out.at[here], sem.at[1 + part])
        copy.start()
        copies.append(copy)
    for copy in copies:
        copy.wait()


def whole(shape):
    return jax.ShapeDtypeStruct(shape, F32)


VMEM = pl.BlockSpec(memory_space=pltpu.VMEM)
ANY = pl.BlockSpec(memory_space=pl.ANY)
VMEM_BYTES = 24 << 20


def run(kernel, plan, outs, scratch, *operands, out_specs=None, semaphores=0):
    scratch = [pltpu.VMEM(s, F32) for s in scratch]
    if semaphores:
        scratch.append(pltpu.SemaphoreType.DMA((semaphores,)))
    return pl.pallas_call(
        functools.partial(kernel, plan),
        out_shape=[whole(s) for s in outs],
        in_specs=[VMEM] * len(operands),
        out_specs=out_specs or [VMEM] * len(outs),
        scratch_shapes=scratch,
        compiler_params=pltpu.CompilerParams(vmem_limit_bytes=VMEM_BYTES),
    )(*operands)


def swap(values, partner):
    axes = ("gx", "gy", "gz")
    counts = [lax.axis_size(a) for a in axes]
    pairs = []
    for i in range(counts[0] * counts[1] * counts[2]):
        to = partner(i // (counts[1] * counts[2]), i // counts[2] % counts[1], i % counts[2])
        if to is not None:
            pairs.append((i, (to[0] * counts[1] + to[1]) * counts[2] + to[2]))
    return lax.ppermute(values, axes, pairs)


def body_fast(divergence, pressure_prev):
    plan = Plan(divergence.shape, tuple(lax.axis_size(a) for a in ("gz", "gx", "gy")))
    ext, level1 = plan.ext, plan.level1
    window, layers = plan.window, (plan.layers, plan.ex, plan.ey)
    payload = [(n + plan.coarse, LANES) for n in (plan.slab_z, plan.slab_x, plan.corner)]
    both = jnp.stack([pressure_prev, divergence])
    both = jnp.pad(both, ((0, 0), (3, 3), (0, plan.ex - plan.block[1]), (0, plan.ey - plan.block[2])))
    r, x, pay_z, pay_x, pay_d = run(
        first_kernel, plan, [ext, ext] + payload,
        [ext, ext, (2, 2 * plan.pairs * plan.ex, LANES), (2 * plan.lat_at, plan.ey)],
        both,
    )
    from_z = swap(pay_z, lambda x, y, z: (x, y, z ^ 3))
    from_x = swap(pay_x, lambda x, y, z: (x ^ 1, y, z))
    from_d = swap(pay_d, lambda x, y, z: (x ^ 1, y, z ^ 3))
    r, x, slab = run(
        chip_kernel, plan, [ext, ext, (plan.slab, LANES)], [], r, x, from_z, from_x, from_d
    )
    ours = jnp.concatenate([
        slab, pay_z[plan.slab_z:], from_z[plan.slab_z:], from_x[plan.slab_x:], from_d[plan.corner:]
    ], axis=0)
    got = swap(ours, lambda x, y, z: (x, y, z ^ 1))
    nz2, nx2, _ = plan.level2
    share = (plan.share, LANES)
    r, x, r1, x1, now, later, ours = run(
        plane_kernel, plan,
        [layers, plan.block, window, window, (plan.edge + plan.share, LANES),
         (plan.edge + plan.share, LANES), share],
        [ext, ext, level1, level1, level1, level1, level1, (nz2 * level1[1], LANES),
         (plan.share, plan.fold * LANES)],
        r, x, ours, got,
    )
    from_a = swap(now, lambda x, y, z: (x, y ^ 1, z))
    from_b = swap(later, lambda x, y, z: (x, y ^ 3, z))
    from_c = swap(ours, lambda x, y, z: (x, y ^ 2, z))
    return run(
        last_kernel, plan,
        [plan.block, plan.block, tuple(n >> 3 for n in plan.level2)],
        [(4,) + share, plan.block, plan.block, layers, window,
         (window[0] + 4, window[1] + 16, LANES), ext, layers, window, window,
         (nz2 * nx2, LANES), (2 * plan.pairs * plan.ex, LANES)],
        r, x, r1, x1, ours, from_a, from_b, from_c,
        out_specs=[ANY, ANY, VMEM], semaphores=3,
    )


def fits_fast(shape, peers):
    bz, bx, by = shape
    nz, nx, ny = peers
    return (
        nz == 4 and nx == 2 and ny == 4 and bz == 16 and by == LANES
        and nx * bx == 4 * 8 and ny * by == 4 * LANES
    )


def body(divergence, pressure_prev):
    peers = tuple(lax.axis_size(a) for a in ("gz", "gx", "gy"))
    if fits_fast(divergence.shape, peers):
        return tuple(body_fast(divergence, pressure_prev))
    return body_levels(divergence, pressure_prev)


def solution(mesh):
    in_specs = (P("gz", "gx", "gy"), P("gz", "gx", "gy"))
    out_specs = (P("gz", "gx", "gy"), P("gz", "gx", "gy"), P())
    return jax.shard_map(body, mesh=mesh, in_specs=in_specs, out_specs=out_specs, check_vma=False)
```

```python
import functools

import jax
import jax.numpy as jnp
from jax import lax
from jax.experimental import pallas as pl
from jax.experimental.pallas import tpu as pltpu
from jax.sharding import PartitionSpec as P

LEVELS = 6


first_scale = 1.0 / 7.5
rho_one = 1.0 / (2.0 * (5.0 / 3.0) - 0.6)
carry_coef = 0.6 * rho_one
fresh_coef = 2.0 * rho_one / (0.75 * 6.0)

LANES = 128
F32 = jnp.float32
AXES = (("gz", 0), ("gx", 1), ("gy", 2))


def extended(x, width):
    for axis, dim in AXES:
        peers, length = (lax.axis_size(axis), x.shape[dim + 1])
        up = [(i, (i + 1) % peers) for i in range(peers - 1)]
        down = [(j, i) for i, j in up]
        last = lax.slice_in_dim(x, length - width, length, axis=dim + 1)
        first = lax.slice_in_dim(x, 0, width, axis=dim + 1)
        before = lax.ppermute(last, axis, up)
        after = lax.ppermute(first, axis, down)
        x = jnp.concatenate([before, x, after], axis=dim + 1)
    return x


def stencil(values):
    padded = jnp.pad(values, 1)
    return valid_op(padded)


def valid_op(padded):
    beside = padded[2:, 1:-1, 1:-1] + padded[:-2, 1:-1, 1:-1]
    beside = beside + padded[1:-1, 2:, 1:-1] + padded[1:-1, :-2, 1:-1]
    beside = beside + padded[1:-1, 1:-1, 2:] + padded[1:-1, 1:-1, :-2]
    return 6.0 * padded[1:-1, 1:-1, 1:-1] - beside


def smooth_pass(iterate, source, apply_op, from_zero):
    residue = source if from_zero else source - apply_op(iterate)
    update = residue * first_scale
    iterate = update if from_zero else iterate + update
    residue = source - apply_op(iterate)
    update = carry_coef * update + fresh_coef * residue
    return iterate + update


def restrict(values):
    shape_a, shape_b, shape_c = values.shape
    blocks = values.reshape(shape_a // 2, 2, shape_b // 2, 2, shape_c // 2, 2)
    return 0.5 * jnp.sum(blocks, axis=(1, 3, 5))


def prolong(values):
    shape_a, shape_b, shape_c = values.shape
    spread = jnp.broadcast_to(
        values[:, None, :, None, :, None], (shape_a, 2, shape_b, 2, shape_c, 2)
    )
    return spread.reshape(2 * shape_a, 2 * shape_b, 2 * shape_c)


def vcycle(level_num, iterate, source):
    iterate = smooth_pass(iterate, source, stencil, True)
    coarsest = None
    if level_num < LEVELS - 1:
        residue = source - stencil(iterate)
        coarse, coarsest = vcycle(level_num + 1, None, restrict(residue))
        iterate = iterate + prolong(coarse)
    result = smooth_pass(iterate, source, stencil, False)
    if level_num == LEVELS - 1:
        coarsest = result
    return (result, coarsest)


def collect(values):
    gathered = lax.all_gather(values, "gz", axis=0, tiled=True)
    gathered = lax.all_gather(gathered, "gy", axis=2, tiled=True)
    return lax.all_gather(gathered, "gx", axis=1, tiled=True)


def local_stencil(values):
    return valid_op(extended(values[None], 1)[0])


def own_block(whole, block_shape):
    start_z = lax.axis_index("gz") * block_shape[0]
    start_x = lax.axis_index("gx") * block_shape[1]
    start_y = lax.axis_index("gy") * block_shape[2]
    return lax.dynamic_slice(whole, (start_z, start_x, start_y), block_shape)


def body_cycle(level_num, iterate, source, from_zero, gather_at):
    if level_num == gather_at:
        whole_source = collect(source)
        coarse, coarsest = vcycle(level_num, None, whole_source)
        return (own_block(coarse, source.shape), coarsest)
    iterate = smooth_pass(iterate, source, local_stencil, from_zero)
    residue = source - local_stencil(iterate)
    coarse, coarsest = body_cycle(level_num + 1, None, restrict(residue), True, gather_at)
    iterate = iterate + prolong(coarse)
    return (smooth_pass(iterate, source, local_stencil, False), coarsest)


def body_levels(divergence, pressure_prev):
    pressure, coarse_correction = body_cycle(0, pressure_prev, divergence, False, 3)
    residual = divergence - local_stencil(pressure)
    return (pressure, residual, coarse_correction)


def iota(shape, dim):
    return lax.broadcasted_iota(jnp.int32, shape, dim)


def signed(index, size, extent):
    return jnp.where(index >= (size + extent) // 2, index - extent, index)


def right_dot(values, table):
    rows = values.shape[0]
    terms = []
    for _ in range(3):
        term = values.astype(jnp.bfloat16)
        terms.append(term)
        values = values - term.astype(F32)
    out = jnp.dot(jnp.concatenate(terms, axis=0), table, preferred_element_type=F32)
    return out[0:rows] + out[rows:2 * rows] + out[2 * rows:3 * rows]


def right_dots(values, table):
    total = None
    for _ in range(3):
        term = values.astype(jnp.bfloat16)
        part = jnp.dot(term, table, preferred_element_type=F32)
        total = part if total is None else total + part
        values = values - term.astype(F32)
    return total


def as_table(keep, value=1.0):
    return jnp.where(keep, value, 0.0).astype(jnp.bfloat16)


def lateral(v):
    rows, lanes = v.shape
    return (
        pltpu.roll(v, 1, 0) + pltpu.roll(v, rows - 1, 0)
        + pltpu.roll(v, 1, 1) + pltpu.roll(v, lanes - 1, 1)
    )


def apply_at(ref, k, lateral_of=lateral):
    centre = ref[k]
    beside = lateral_of(centre)
    if k > 0:
        beside = beside + ref[k - 1]
    if k < ref.shape[0] - 1:
        beside = beside + ref[k + 1]
    return 6.0 * centre - beside


def padded(plan):
    return (plan.ey // LANES, plan.ez, plan.ex + 16, LANES)


def put(ref, k, v):
    rows = v.shape[0]
    for tile in range(ref.shape[0]):
        part = v[:, tile * LANES:(tile + 1) * LANES]
        ref[tile, k, 8:8 + rows, :] = part
        ref[tile, k, 7:8, :] = part[rows - 1:rows]
        ref[tile, k, 8 + rows:9 + rows, :] = part[0:1]


def rows_of(ref, k, first):
    here = pl.ds(first, ref.shape[2] - 16)
    return jnp.concatenate([ref[tile, k, here, :] for tile in range(ref.shape[0])], axis=1)


def apply_padded(ref, k, origin):
    centre = rows_of(ref, k, 8)
    lanes = centre.shape[1]
    beside = rows_of(ref, k, origin - 1) + rows_of(ref, k, origin + 1)
    beside = beside + (pltpu.roll(centre, 1, 1) + pltpu.roll(centre, lanes - 1, 1))
    if k > 0:
        beside = beside + rows_of(ref, k - 1, 8)
    if k < ref.shape[1] - 1:
        beside = beside + rows_of(ref, k + 1, 8)
    return 6.0 * centre - beside


def wrapped_mask(shape, sizes, low, high):
    keep = None
    for dim, size in sizes.items():
        at = signed(iota(shape, dim), size, shape[dim])
        good = ((at >= 0) | low[dim]) & ((at < size) | high[dim])
        keep = good if keep is None else keep & good
    return jnp.where(keep, 1.0, 0.0).astype(F32)


def side(index, flip):
    if flip == 1:
        return (index & 1) == 0, None
    return index < 2, (index == 1) | (index == 2)


def place(axis, count):
    index = lax.axis_index(axis)
    return index, index > 0, index < count - 1


def only(keep, v):
    return jnp.where(keep, v, 0.0)


def shifted(v, lanes):
    lanes = lanes % LANES
    return v if lanes == 0 else pltpu.roll(v, lanes, 1)


def lanes_of(v, first, count):
    lane = iota(v.shape, 1)
    last = first + count
    if last <= LANES:
        return (lane >= first) & (lane < last)
    return (lane >= first) | (lane < last - LANES)


def moved(v, first, count, to):
    first = first % LANES
    return shifted(only(lanes_of(v, first, count), v), to - first)


def landed(v, first, count, to):
    to = to % LANES
    v = shifted(v, to - first)
    return only(lanes_of(v, to, count), v)


def side_pack(tile, slot):
    return moved(tile, LANES - 3, 6, 6 * slot)


def side_unpack(packed, slot):
    return landed(packed, 6 * slot, 6, LANES - 3)


def slab_layers(r_ref, x_ref, up, low, high):
    start = jnp.where(up, high[0], low[0])
    start_x = jnp.where(up, high[1], low[1])
    return [(r_ref, start + j) for j in range(5)] + [(x_ref, start_x + j) for j in range(2)]


def slab_own(r_ref, x_ref, up):
    ez = r_ref.shape[0]
    return slab_layers(r_ref, x_ref, up, (0, 1), (ez - 5, ez - 3))


def slab_there(r_ref, x_ref, up):
    ez = r_ref.shape[0]
    return slab_layers(r_ref, x_ref, up, (1, 3), (ez - 6, ez - 5))


def slab_emit(r_ref, x_ref, out, up):
    ex = r_ref.shape[1]
    lat = None
    for j, (ref, k) in enumerate(slab_own(r_ref, x_ref, up)):
        v = ref[k]
        out[j * ex:(j + 1) * ex, :] = v[:, 0:LANES]
        part = side_pack(v[:, LANES:], j)
        lat = part if lat is None else lat + part
    out[7 * ex:8 * ex, :] = lat


def slab_add(r_ref, x_ref, slab, up):
    ex = r_ref.shape[1]
    lat = slab[7 * ex:8 * ex, :]
    for j, (ref, k) in enumerate(slab_there(r_ref, x_ref, up)):
        ref[k, :, 0:LANES] += slab[j * ex:(j + 1) * ex, :]
        ref[k, :, LANES:] += side_unpack(lat, j)


BESIDE = ((2, 2, 0, 0), (1, 1, 0, 3), (3, 1, 0, 5), (5, 1, 1, 0), (6, 1, 1, 3))


def beside(tile, count):
    row = iota(tile.shape, 0)
    return only((row < count) | (row >= 8 - count), tile)


def thin_emit(r_ref, x_ref, out, up):
    bx = r_ref.shape[1] - 8
    layers = slab_own(r_ref, x_ref, up)
    lat = None
    for j, (ref, k) in enumerate(layers):
        out[j * bx:(j + 1) * bx, :] = ref[k, 0:bx, 0:LANES]
        part = side_pack(ref[k, 0:bx, LANES:], j)
        lat = part if lat is None else lat + part
    tiles = [None, None]
    for j, count, which, turn in BESIDE:
        ref, k = layers[j]
        part = beside(ref[k, bx:, 0:LANES], count)
        part = pltpu.roll(part, turn, 0) if turn else part
        tiles[which] = part if tiles[which] is None else tiles[which] + part
    at = 7 * bx
    out[at:at + 8, :] = tiles[0]
    out[at + 8:at + 16, :] = tiles[1]
    out[at + 16:at + 16 + bx, :] = lat
    for j in (1, 2, 3):
        ref, k = layers[j]
        out[at + 16:at + 24, :] += side_pack(ref[k, bx:, LANES:], 6 + j)


def thin_add(r_ref, x_ref, slab, up):
    bx = r_ref.shape[1] - 8
    layers = slab_there(r_ref, x_ref, up)
    at = 7 * bx
    lat = slab[at + 16:at + 16 + bx, :]
    for j, (ref, k) in enumerate(layers):
        ref[k, 0:bx, 0:LANES] += slab[j * bx:(j + 1) * bx, :]
        ref[k, 0:bx, LANES:] += side_unpack(lat, j)
    for j, count, which, turn in BESIDE:
        ref, k = layers[j]
        tile = slab[at + 8 * which:at + 8 * which + 8, :]
        tile = pltpu.roll(tile, 8 - turn, 0) if turn else tile
        ref[k, bx:, 0:LANES] += beside(tile, count)
    for j in (1, 2, 3):
        ref, k = layers[j]
        ref[k, bx:, LANES:] += side_unpack(lat[0:8], 6 + j)


def rows_out(r, x, up):
    bx = r.shape[0] - 8
    row = iota((8, r.shape[1]), 0)
    first, last, spill = r[0:8], r[bx - 8:bx], r[bx:]
    to_high = pltpu.roll(jnp.where(row >= 6, last, spill), 2, 0)
    to_low = pltpu.roll(jnp.where(row >= 5, spill, first), 3, 0)
    out = jnp.where(up, to_high, to_low)
    if x is None:
        return only(row < 5, out)
    spill = x[bx:]
    extra = jnp.where(up, pltpu.roll(spill, 5, 0), pltpu.roll(spill, 7, 0))
    return jnp.where(row < 5, out, only(row < 7, extra))


def rows_in(r_ref, x_ref, k, rows, up):
    bx = r_ref.shape[1] - 8
    row = iota(rows.shape, 0)
    high, low = pltpu.roll(rows, 5, 0), pltpu.roll(rows, 6, 0)
    r_ref[k, 0:8] += only(jnp.logical_not(up) & (row < 3), low)
    r_ref[k, bx - 8:bx] += only(up & (row >= 5), high)
    r_ref[k, bx:] += jnp.where(up, only(row < 2, high), only(row >= 6, low))
    if x_ref is not None:
        x_ref[k, 0:8] += only(jnp.logical_not(up) & (row < 2), pltpu.roll(rows, 3, 0))
        x_ref[k, bx - 8:bx] += only(up & (row >= 6), pltpu.roll(rows, 1, 0))


def rows_emit(r_ref, x_ref, out, up):
    ez = r_ref.shape[0]
    row = iota((8, LANES), 0)
    lat = jnp.zeros((8, LANES), F32)
    for t, k in enumerate(range(1, ez - 1)):
        far = {1: 0, ez - 2: ez - 1}.get(k)
        rows = rows_out(r_ref[k], None if far is not None else x_ref[k], up)
        tile = rows[:, 0:LANES]
        if far is not None:
            more = rows_out(r_ref[far, :, 0:LANES], None, up)
            more = jnp.where(up, pltpu.roll(more, 5, 0), pltpu.roll(more, 2, 0))
            tile = jnp.where((row == 5) | (row == 6), more, tile)
        out[8 * t:8 * t + 8, :] = tile
        lat = lat + side_pack(rows[:, LANES:], t)
    at = 8 * (ez - 2)
    out[at:at + 8, :] = lat


def rows_add(r_ref, x_ref, slab, up):
    ez = r_ref.shape[0]
    at = 8 * (ez - 2)
    lat = slab[at:at + 8, :]
    row = iota((8, LANES), 0)
    for t, k in enumerate(range(1, ez - 1)):
        far = {1: 0, ez - 2: ez - 1}.get(k)
        tile = slab[8 * t:8 * t + 8, :]
        rows = jnp.concatenate([tile, side_unpack(lat, t)], axis=1)
        rows_in(r_ref, None if far is not None else x_ref, k, rows, up)
        if far is not None:
            tile = only((row == 5) | (row == 6), tile)
            tile = jnp.where(up, pltpu.roll(tile, 6, 0), pltpu.roll(tile, 3, 0))
            rows = jnp.concatenate([tile, jnp.zeros((8, LANES), F32)], axis=1)
            rows_in(r_ref, None, far, rows, up)


class Plan:
    def first_layer(self, iz):
        start = iz * (self.block[0] // 2) - 4
        return jnp.clip(start, 0, self.level1[0] - self.window[0])

    def __init__(self, shape, peers):
        self.peers = peers
        self.block = bz, bx, by = shape
        self.ext = self.ez, self.ex, self.ey = bz + 6, bx + 8, by + LANES
        self.rows, self.pairs = bx // 2, bz // 4 + 2
        self.lat_at = self.pairs * (self.rows + 4)
        self.coarse = self.lat_at + 8
        self.slab = 8 * self.ex
        self.slab_z = 8 * bx + 16
        self.slab_x = 8 * (bz + 5)
        self.corner = 6 * 8
        self.layers = bz + 4
        self.level1 = (peers[0] * bz // 2, peers[1] * bx // 2, LANES)
        self.level2 = (peers[0] * bz // 4, peers[1] * bx // 4, peers[2] * by // 4)
        self.inner = [0, 1] + [2] * bz + [1, 0]
        self.slots, at = [], 0
        for count in self.inner:
            self.slots.append(at)
            at += 3 + count + (2 if count == 2 else 0)
        assert at <= LANES
        self.fine_rows = self.ex
        self.window = (bz // 2 + 8, self.level1[1], LANES)
        self.edge = self.fine_rows + self.window[0] * self.window[1] // 8
        self.wide2 = by // 4 + 4
        self.fold = LANES // self.wide2
        self.lines2 = -(-self.level2[0] // self.fold)
        self.share = self.lines2 * self.level2[1]


def first_kernel(plan, both, r_ref, x_ref, pay_z, pay_x, pay_d, d_one, d_two, pairs, lines):
    p_ext, b_ext = both.at[0], both.at[1]
    bz, bx, by = plan.block
    ez, ex, ey = plan.ext
    peers = plan.peers
    iz, z_low, z_high = place("gz", peers[0])
    ix, x_low, x_high = place("gx", peers[1])
    _, y_low, y_high = place("gy", peers[2])
    flat = wrapped_mask((ex, ey), {0: bx, 1: by}, (x_low, y_low), (x_high, y_high))
    below = jnp.where(z_low, 1.0, 0.0).astype(F32)
    above = jnp.where(z_high, 1.0, 0.0).astype(F32)

    def masked(k, v):
        v = v * flat
        if k < 3:
            v = v * below
        if k >= 3 + bz:
            v = v * above
        return v

    zero = jnp.zeros((ex, ey), F32)
    origin = 8 + (iz >> 8)
    for k in range(ez):
        if 2 <= k < ez - 2:
            r = b_ext[k] - apply_at(p_ext, k)
            r_ref[k] = r
            put(d_one, k, masked(k, r * first_scale))
        elif 1 <= k < ez - 1:
            put(d_one, k, zero)
    for k in range(ez):
        if 1 <= k < ez - 1:
            if 2 <= k < ez - 2:
                r = r_ref[k] - apply_padded(d_one, k, origin)
                d = carry_coef * rows_of(d_one, k, 8) + fresh_coef * r
            else:
                inward = k + 1 if k == 1 else k - 1
                r = rows_of(d_one, inward, 8)
                d = fresh_coef * r
            r_ref[k] = r
            put(d_two, k, masked(k, d))
    for k in range(ez):
        if 1 <= k < ez - 1:
            part = rows_of(d_two, k, 8)
            beside = rows_of(d_two, k, origin - 1) + rows_of(d_two, k, origin + 1)
            beside = beside + (pltpu.roll(part, 1, 1) + pltpu.roll(part, ey - 1, 1))
            if k > 1:
                beside = beside + rows_of(d_two, k - 1, 8)
            if k < ez - 2:
                beside = beside + rows_of(d_two, k + 1, 8)
            r_ref[k] = masked(k, r_ref[k] - (6.0 * part - beside))
            x_ref[k] = p_ext[k] + (rows_of(d_one, k, 8) + part)
        else:
            r_ref[k] = masked(k, rows_of(d_two, 1 if k == 0 else ez - 2, 8))
            x_ref[k] = zero

    coarse_z, rows = 2 * plan.pairs, plan.rows
    for zc in range(coarse_z):
        low, high = 2 * zc - 1, 2 * zc
        if low < 0:
            total = r_ref[high]
        elif high >= ez:
            total = r_ref[low]
        else:
            total = r_ref[low] + r_ref[high]
        base = zc * ex
        for tile in range(ey // LANES):
            here = slice(tile * LANES, (tile + 1) * LANES)
            pairs[tile, base:base + ex, :] = total[:, here]
            even = pairs.at[tile][pl.ds(base, ex // 2, 2), :]
            odd = pairs.at[tile][pl.ds(base + 1, ex // 2, 2), :]
            sums = even + odd
            at = zc // 2 * rows
            at += zc % 2 * plan.lat_at
            lines[at:at + rows, here] = sums[0:rows]
            at = plan.pairs * rows + zc // 2 * 4 + zc % 2 * plan.lat_at
            lines[at:at + 4, here] = sums[rows:rows + 4]
    fine = signed(iota((ey, LANES), 0), by, ey)
    coarse = signed(iota((ey, LANES), 1), by // 2, LANES)
    table = as_table((fine >> 1) == coarse, 0.5)
    out = right_dot(lines[...], table)
    even, odd = out[0:plan.lat_at], out[plan.lat_at:]
    lane = iota(even.shape, 1)
    main = jnp.where(lane < LANES // 2, even, shifted(odd, LANES // 2))
    own_lat = spill_lat = None
    row = iota((8, LANES), 0)
    for zc in range(coarse_z):
        source = (even, odd)[zc % 2]
        base = zc // 2 * rows
        tile = source[base:base + rows]
        part = moved(tile, by // 2, 2, 4 * zc) + moved(tile, LANES - 2, 2, 4 * zc + 2)
        own_lat = part if own_lat is None else own_lat + part
        base = plan.pairs * rows + zc // 4 * 8
        tile = source[base:base + 8]
        if zc // 2 % 2:
            tile = pltpu.roll(tile, 4, 0)
        tile = only(row < 4, tile)
        slot = LANES // 2 + 4 * zc
        part = moved(tile, by // 2, 2, slot) + moved(tile, LANES - 2, 2, slot + 2)
        spill_lat = part if spill_lat is None else spill_lat + part
    for pay, at in ((pay_z, plan.slab_z), (pay_x, plan.slab_x), (pay_d, plan.corner)):
        pay[at:at + plan.lat_at, :] = main
        pay[at + plan.lat_at:at + plan.coarse, :] = own_lat + spill_lat

    up_z, _ = side(iz, 3)
    up_x, _ = side(ix, 1)
    thin_emit(r_ref, x_ref, pay_z, up_z)
    rows_emit(r_ref, x_ref, pay_x, up_x)
    lat = jnp.zeros((8, LANES), F32)
    start = jnp.where(up_z, ez - 5, 0)
    for j in range(5):
        out = rows_out(r_ref[start + j], x_ref[start + j] if j == 2 else None, up_x)
        pay_d[8 * j:8 * j + 8, :] = out[:, 0:LANES]
        lat = lat + side_pack(out[:, LANES:], j)
    pay_d[40:48, :] = lat


def chip_kernel(plan, r_in, x_in, from_z, from_x, from_d, r_ref, x_ref, pay):
    ez, ex, ey = plan.ext
    iz, _, _ = place("gz", plan.peers[0])
    ix, _, _ = place("gx", plan.peers[1])
    up_z, near = side(iz, 3)
    up_x, _ = side(ix, 1)
    for k in range(ez):
        r_ref[k] = r_in[k]
        x_ref[k] = x_in[k]
    rows_add(r_ref, x_ref, from_x, up_x)

    @pl.when(near)
    def _():
        thin_add(r_ref, x_ref, from_z, up_z)
        start = jnp.where(up_z, ez - 6, 1)
        lat = from_d[40:48, :]
        for j in range(5):
            rows = from_d[8 * j:8 * j + 8, :]
            rows = jnp.concatenate([rows, side_unpack(lat, j)], axis=1)
            rows_in(r_ref, x_ref if j == 2 else None, start + j, rows, up_x)

    slab_emit(r_ref, x_ref, pay, side(iz, 1)[0])


def plane_kernel(plan, r_in, x_in, ours, theirs, r_ref, x_ref, r1_ref, x1_ref, pay, later, share,
                 r_all, x_all, b1, d1, d2, r1, x1, pairs, lines):
    bz, bx, by = plan.block
    ez, ex, ey = plan.ext
    layers = plan.layers
    iz, _, _ = place("gz", plan.peers[0])
    ix, _, _ = place("gx", plan.peers[1])
    iy, y_low, y_high = place("gy", plan.peers[2])
    up_z, _ = side(iz, 1)
    for k in range(ez):
        r_all[k] = r_in[k]
        x_all[k] = x_in[k]
    slab_add(r_all, x_all, theirs, up_z)
    for k in range(layers):
        r_ref[k] = r_all[k + 1]
    for k in range(bz):
        x_ref[k] = x_all[k + 3, 0:bx, 0:by]

    up, _ = side(iy, 1)
    up_inner, _ = side(iy, 3)
    high, low = jnp.zeros((ex, LANES), F32), jnp.zeros((ex, LANES), F32)
    for k in range(layers):
        slot, inner = plan.slots[k], plan.inner[k]
        count = 3 + inner
        v, spill = r_all[k + 1, :, 0:by], r_all[k + 1, :, by:ey]
        high = high + moved(jnp.where(lanes_of(v, 0, 3), spill, v), LANES - inner, count, slot)
        mixed = jnp.where(lanes_of(v, 0, 2), v, spill)
        low = low + moved(mixed, LANES - 3, count, slot)
        if inner == 2:
            spill = x_all[k + 1, :, by:ey]
            high = high + moved(spill, 0, 2, slot + count)
            low = low + moved(spill, LANES - 2, 2, slot + count)
    pay[0:ex, :] = jnp.where(up, high, low)
    later[0:ex, :] = jnp.where(up_inner, high, low)

    nz1, nx1, _ = plan.level1
    rows, half = plan.rows, by // 2
    for k in range(nz1):
        b1[k] = jnp.zeros((nx1, LANES), F32)
    row = iota((8, LANES), 0)
    for j in range(plan.peers[0]):
        for i in range(plan.peers[1]):
            flip = iz ^ j
            other = ((flip ^ (flip >> 1)) & 1) == 1
            chip = (flip >> 1) + 2 * (ix ^ i)
            at = pl.multiple_of(plan.slab + chip * plan.coarse, 8)

            def rows_at(offset, count):
                here = pl.ds(pl.multiple_of(at + offset, 8), count)
                return jnp.where(other, theirs[here, :], ours[here, :])

            lat = rows_at(plan.lat_at, 8)
            for zp in range(plan.pairs):
                own = rows_at(zp * rows, rows)
                if zp % 2 == 0:
                    spill_two = rows_at(plan.pairs * rows + zp * 4, 8)
                spill = spill_two if zp % 2 == 0 else pltpu.roll(spill_two, 4, 0)
                for part in range(2):
                    zc = 2 * zp + part
                    k = j * (bz // 2) + zc - 2
                    if not 0 <= k < nz1:
                        continue

                    def wide(main, slot):
                        return (
                            landed(main, part * half, half, 0)
                            + landed(lat, slot, 2, half) + landed(lat, slot + 2, 2, LANES - 2)
                        )

                    b1[k, i * rows:(i + 1) * rows, :] += wide(own, 4 * zc)
                    v = wide(spill, LANES // 2 + 4 * zc)
                    if i + 1 < plan.peers[1]:
                        at_row = (i + 1) * rows
                        b1[k, at_row:at_row + 8, :] += only(row < 2, v)
                    if i > 0:
                        at_row = i * rows - 8
                        b1[k, at_row:at_row + 8, :] += only(row >= 6, pltpu.roll(v, 4, 0))

    lateral1 = level_lateral((nx1, LANES))
    keep = wrapped_mask((nx1, LANES), {1: half}, (None, y_low), (None, y_high))
    for k in range(nz1):
        d1[k] = b1[k] * first_scale
    for k in range(nz1):
        r = b1[k] - apply_at(d1, k, lateral1)
        r1[k] = r
        d2[k] = keep * (carry_coef * d1[k] + fresh_coef * r)
    for k in range(nz1):
        r1[k] = keep * (r1[k] - apply_at(d2, k, lateral1))
        x1[k] = d1[k] + d2[k]

    nz2, nx2, _ = plan.level2
    for zc in range(nz2):
        pairs[zc * nx1:(zc + 1) * nx1, :] = r1[2 * zc] + r1[2 * zc + 1]
        part, at = divmod(zc, plan.lines2)
        lines[at * nx2:(at + 1) * nx2, part * LANES:(part + 1) * LANES] = (
            pairs[pl.ds(zc * nx1, nx2, 2), :] + pairs[pl.ds(zc * nx1 + 1, nx2, 2), :]
        )
    shape = (plan.fold * LANES, LANES)
    fine, coarse = iota(shape, 0), iota(shape, 1)
    part, fine = fine // LANES, signed(fine % LANES, half, LANES)
    coarse = coarse - part * plan.wide2 - 2
    near = (coarse >= -2) & (coarse < plan.wide2 - 2)
    for part in range(plan.fold):
        count = min(plan.lines2, nz2 - part * plan.lines2) * nx2
        if count < plan.share:
            here = slice(part * LANES, (part + 1) * LANES)
            lines[count:, here] = jnp.zeros((plan.share - count, LANES), F32)
    total = right_dot(lines[...], as_table(near & ((fine >> 1) == coarse), 0.5))
    share[...] = total
    pay[plan.edge:plan.edge + plan.share, :] = total
    later[plan.edge:plan.edge + plan.share, :] = total

    start = plan.first_layer(iz)
    for k in range(plan.window[0]):
        r1_ref[k] = r1[start + k]
        x1_ref[k] = x1[start + k]
    per_tile = LANES // 16
    for group in range(plan.window[0] // per_tile):
        tiles = []
        for which in range(2):
            total = jnp.zeros((nx1, LANES), F32)
            for j in range(per_tile):
                k = group * per_tile + j
                first = half - 3 if which == 0 else LANES - 4
                total = total + moved(r1_ref[k], first, 7, 16 * j)
                first = half - 2 if which == 0 else LANES - 3
                total = total + moved(x1_ref[k], first, 5, 16 * j + 7)
            tiles.append(total)
        here = slice(plan.fine_rows + group * nx1, plan.fine_rows + (group + 1) * nx1)
        pay[here, :] = jnp.where(up, tiles[0], tiles[1])
        later[here, :] = jnp.where(up_inner, tiles[0], tiles[1])


def level_lateral(shape):
    row = iota(shape, 0)
    not_first = jnp.where(row > 0, 1.0, 0.0).astype(F32)
    not_last = jnp.where(row < shape[0] - 1, 1.0, 0.0).astype(F32)

    def beside(v):
        return (
            not_first * pltpu.roll(v, 1, 0) + not_last * pltpu.roll(v, shape[0] - 1, 0)
            + pltpu.roll(v, 1, 1) + pltpu.roll(v, LANES - 1, 1)
        )

    return beside


def small_cycle(level, source):
    step = 1 << (level - 2)
    row, lane = iota((8, LANES), 0), iota((8, LANES), 1)
    count = len(source)
    shifts = []
    if step < 8:
        shifts += [(step, 0, row >= step), (8 - step, 0, row < 8 - step)]
    shifts += [(step, 1, lane >= step), (LANES - step, 1, lane < LANES - step)]

    def op(v):
        out = []
        for k in range(count):
            beside = None
            for shift, dim, keep in shifts:
                part = only(keep, pltpu.roll(v[k], shift, dim))
                beside = part if beside is None else beside + part
            if k > 0:
                beside = beside + v[k - 1]
            if k < count - 1:
                beside = beside + v[k + 1]
            out.append(6.0 * v[k] - beside)
        return out

    d = [first_scale * v for v in source]
    r = [b - t for b, t in zip(source, op(d))]
    d2 = [carry_coef * v + fresh_coef * t for v, t in zip(d, r)]
    x = [v + t for v, t in zip(d, d2)]
    r = [v - t for v, t in zip(r, op(d2))]
    coarsest = None
    if level < LEVELS - 1:
        keep = only((row % (2 * step) == 0) & (lane % (2 * step) == 0), 0.5)
        coarse = []
        for k in range(0, count, 2):
            v = r[k] + r[k + 1]
            v = v + pltpu.roll(v, 8 - step, 0)
            coarse.append(keep * (v + pltpu.roll(v, LANES - step, 1)))
        coarse, coarsest = small_cycle(level + 1, coarse)
        e = []
        for v in coarse:
            v = v + pltpu.roll(v, step, 0)
            e += [v + pltpu.roll(v, step, 1)] * 2
        x = [v + t for v, t in zip(x, e)]
        r = [v - t for v, t in zip(r, op(e))]
    d = [first_scale * v for v in r]
    r = [v - t for v, t in zip(r, op(d))]
    x = [v + (t + (carry_coef * t + fresh_coef * u)) for v, t, u in zip(x, d, r)]
    return x, (x if level == LEVELS - 1 else coarsest)


def last_kernel(plan, r_in, x_in, r1_in, x1_in, ours, from_a, from_b, from_c, p_out, res_out, last_ref, *scratch):
    shares, p_ref, res_ref, r, q1, e1, e0, d0, d1, r1, lines, wide, sem = scratch
    bz, bx, by = plan.block
    ez, ex, ey = plan.ext
    nz1, nx1, _ = plan.window
    nz2, nx2, _ = plan.level2
    layers, half = plan.layers, by // 2
    iz, z_low, z_high = place("gz", plan.peers[0])
    ix, x_low, x_high = place("gx", plan.peers[1])
    iy, y_low, y_high = place("gy", plan.peers[2])

    shares[0] = ours[...]
    shares[1] = from_a[plan.edge:plan.edge + plan.share, :]
    shares[3] = from_b[plan.edge:plan.edge + plan.share, :]
    shares[2] = from_c[...]
    own2 = half // 2
    source = []
    for part in range(plan.fold):
        total = None
        for j in range(plan.peers[2]):
            v = moved(shares[iy ^ j], part * plan.wide2, plan.wide2, own2 * j - 2)
            total = v if total is None else total + v
        source += [total[nx2 * k:nx2 * (k + 1)] for k in range(plan.lines2)]
    source = source[:nz2]
    e2, coarsest = small_cycle(2, source)
    for k in range(nz2):
        lines[k * nx2:(k + 1) * nx2, :] = e2[k]
    thin = as_table(iota((LANES, LANES), 0) == 8 * iota((LANES, LANES), 1))
    for k in range(last_ref.shape[0]):
        last_ref[k] = right_dot(coarsest[k], thin)[0:1, 0:last_ref.shape[2]]

    up_a, _ = side(iy, 1)
    _, near_b = side(iy, 3)

    def sent(rows):
        a, b = from_a[rows[0]:rows[1], :], only(near_b, from_b[rows[0]:rows[1], :])
        return jnp.where(up_a, a, b), jnp.where(up_a, b, a)

    fine = signed(iota((LANES, LANES), 1), half, LANES)
    coarse = iota((LANES, LANES), 0) - iy * own2
    start = plan.first_layer(iz)
    here = pl.ds(pl.multiple_of(start // 2 * nx2, 8), nz1 // 2 * nx2)
    e2 = right_dot(lines[here, :], as_table((fine >> 1) == coarse))
    for zc in range(nz1 // 2):
        v = e2[zc * nx2:(zc + 1) * nx2]
        for part in range(2):
            q1.at[2 * zc + part][pl.ds(0, nx2, 2), :] = v
            q1.at[2 * zc + part][pl.ds(1, nx2, 2), :] = v
    per_tile = LANES // 16
    lateral1 = level_lateral((nx1, LANES))
    keep = wrapped_mask((nx1, LANES), {1: half}, (None, y_low), (None, y_high))
    for group in range(nz1 // per_tile):
        at = plan.fine_rows + group * nx1
        high, low = sent((at, at + nx1))
        for j in range(per_tile):
            k = group * per_tile + j
            s = 16 * j
            r1[k] = (
                r1_in[k] + landed(high, s, 7, half - 4) + landed(low, s, 7, LANES - 3)
                - apply_at(q1, k, lateral1)
            )
            e1[k + 2, 8:8 + nx1, :] = (
                x1_in[k] + q1[k]
                + landed(high, s + 7, 5, half - 3) + landed(low, s + 7, 5, LANES - 2)
            )
    for k in range(nz1):
        d1[k] = keep * (r1[k] * first_scale)
    nothing = jnp.zeros((8, LANES), F32)
    for k in range(nz1 + 4):
        e1[k, 0:8, :] = nothing
        e1[k, 8 + nx1:16 + nx1, :] = nothing
        if not 2 <= k < nz1 + 2:
            e1[k, 8:8 + nx1, :] = jnp.zeros((nx1, LANES), F32)
    for k in range(nz1):
        v = r1[k] - apply_at(d1, k, lateral1)
        e1[k + 2, 8:8 + nx1, :] += d1[k] + keep * (carry_coef * d1[k] + fresh_coef * v)

    coarse = signed(iota((LANES, ey), 0), half, LANES)
    fine = signed(iota((LANES, ey), 1), by, ey)
    double = as_table((fine >> 1) == coarse)
    half_z, half_x = bz // 2, bx // 2
    for zc in range(half_z + 4):
        here = pl.ds(pl.multiple_of(ix * half_x, 8), half_x + 16)
        v = e1[iz * half_z - start + zc, here, :]
        own, low, high = v[8:8 + half_x], v[0:8], v[8 + half_x:16 + half_x]
        at = zc * ex
        wide[pl.ds(at, half_x, 2), :] = own
        wide[pl.ds(at + 1, half_x, 2), :] = own
        for j in range(2):
            for twin in range(2):
                row = at + bx + 2 * j + twin
                wide[row:row + 1, :] = high[j:j + 1]
                row = at + ex - 4 + 2 * j + twin
                wide[row:row + 1, :] = low[6 + j:7 + j]
    origin = 8 + (iz >> 8)
    for zc in range(half_z + 4):
        v = right_dots(wide[zc * ex:(zc + 1) * ex, :], double)
        for k in (2 * zc - 1, 2 * zc):
            if 0 <= k < ez:
                put(e0, k, v)
    flat = wrapped_mask((ex, ey), {0: bx, 1: by}, (x_low, y_low), (x_high, y_high))
    below = jnp.where(z_low, 1.0, 0.0).astype(F32)
    above = jnp.where(z_high, 1.0, 0.0).astype(F32)

    def masked(k, v):
        v = v * flat
        if k < 3:
            v = v * below
        if k >= 3 + bz:
            v = v * above
        return v

    high, low = sent((0, ex))
    for k in range(layers):
        s, inner = plan.slots[k], plan.inner[k]
        v = r_in[k] - apply_padded(e0, k + 1, origin)
        own = v[:, 0:by] + landed(high, s, 3, LANES - 3) + landed(low, s + inner, 3, 0)
        spill = v[:, by:ey]
        if inner:
            spill = spill + landed(high, s + 3, inner, 0) + landed(low, s, inner, LANES - inner)
        r[k, :, 0:by] = own
        r[k, :, by:ey] = spill
        put(d0, k, masked(k + 1, r[k] * first_scale))
        if inner == 2:
            s = s + 3 + inner
            p_ref[k - 2] = (
                x_in[k - 2] + e0[0, k + 1, 8:8 + bx, :]
                + (landed(high, s, 2, LANES - 2) + landed(low, s, 2, 0))[0:bx]
            )
    for k in range(1, layers - 1):
        v = r[k] - apply_padded(d0, k, origin)
        r[k] = v
        d = rows_of(d0, k, 8)
        v = masked(k + 1, carry_coef * d + fresh_coef * v)
        put(e0, k, v)
        if 2 <= k < 2 + bz:
            p_ref[k - 2] += d[0:bx, 0:by] + v[0:bx, 0:by]
    copy = pltpu.make_async_copy(p_ref, p_out, sem.at[0])
    copy.start()
    copies = [copy]
    parts = 2
    for part in range(parts):
        here = range(part * bz // parts, (part + 1) * bz // parts)
        for j in here:
            v = r[j + 2] - apply_padded(e0, j + 2, origin)
            res_ref[j] = v[0:bx, 0:by]
        here = pl.ds(here[0], bz // parts)
        copy = pltpu.make_async_copy(res_ref.at[here], res_out.at[here], sem.at[1 + part])
        copy.start()
        copies.append(copy)
    for copy in copies:
        copy.wait()


def whole(shape):
    return jax.ShapeDtypeStruct(shape, F32)


VMEM = pl.BlockSpec(memory_space=pltpu.VMEM)
ANY = pl.BlockSpec(memory_space=pl.ANY)
VMEM_BYTES = 24 << 20


def run(kernel, plan, outs, scratch, *operands, out_specs=None, semaphores=0):
    scratch = [pltpu.VMEM(s, F32) for s in scratch]
    if semaphores:
        scratch.append(pltpu.SemaphoreType.DMA((semaphores,)))
    return pl.pallas_call(
        functools.partial(kernel, plan),
        out_shape=[whole(s) for s in outs],
        in_specs=[VMEM] * len(operands),
        out_specs=out_specs or [VMEM] * len(outs),
        scratch_shapes=scratch,
        compiler_params=pltpu.CompilerParams(vmem_limit_bytes=VMEM_BYTES),
    )(*operands)


def swap(values, partner):
    axes = ("gx", "gy", "gz")
    counts = [lax.axis_size(a) for a in axes]
    pairs = []
    for i in range(counts[0] * counts[1] * counts[2]):
        to = partner(i // (counts[1] * counts[2]), i // counts[2] % counts[1], i % counts[2])
        if to is not None:
            pairs.append((i, (to[0] * counts[1] + to[1]) * counts[2] + to[2]))
    return lax.ppermute(values, axes, pairs)


def body_fast(divergence, pressure_prev):
    plan = Plan(divergence.shape, tuple(lax.axis_size(a) for a in ("gz", "gx", "gy")))
    ext, level1 = plan.ext, plan.level1
    window, layers = plan.window, (plan.layers, plan.ex, plan.ey)
    payload = [(n + plan.coarse, LANES) for n in (plan.slab_z, plan.slab_x, plan.corner)]
    both = jnp.stack([pressure_prev, divergence])
    both = jnp.pad(both, ((0, 0), (3, 3), (0, plan.ex - plan.block[1]), (0, plan.ey - plan.block[2])))
    r, x, pay_z, pay_x, pay_d = run(
        first_kernel, plan, [ext, ext] + payload,
        [padded(plan), padded(plan), (2, 2 * plan.pairs * plan.ex, LANES),
         (2 * plan.lat_at, plan.ey)],
        both,
    )
    from_z = swap(pay_z, lambda x, y, z: (x, y, z ^ 3))
    from_x = swap(pay_x, lambda x, y, z: (x ^ 1, y, z))
    from_d = swap(pay_d, lambda x, y, z: (x ^ 1, y, z ^ 3))
    r, x, slab = run(
        chip_kernel, plan, [ext, ext, (plan.slab, LANES)], [], r, x, from_z, from_x, from_d
    )
    ours = jnp.concatenate([
        slab, pay_z[plan.slab_z:], from_z[plan.slab_z:], from_x[plan.slab_x:], from_d[plan.corner:]
    ], axis=0)
    got = swap(ours, lambda x, y, z: (x, y, z ^ 1))
    nz2, nx2, _ = plan.level2
    share = (plan.share, LANES)
    r, x, r1, x1, now, later, ours = run(
        plane_kernel, plan,
        [layers, plan.block, window, window, (plan.edge + plan.share, LANES),
         (plan.edge + plan.share, LANES), share],
        [ext, ext, level1, level1, level1, level1, level1, (nz2 * level1[1], LANES),
         (plan.share, plan.fold * LANES)],
        r, x, ours, got,
    )
    from_a = swap(now, lambda x, y, z: (x, y ^ 1, z))
    from_b = swap(later, lambda x, y, z: (x, y ^ 3, z))
    from_c = swap(ours, lambda x, y, z: (x, y ^ 2, z))
    return run(
        last_kernel, plan,
        [plan.block, plan.block, tuple(n >> 3 for n in plan.level2)],
        [(4,) + share, plan.block, plan.block, layers, window,
         (window[0] + 4, window[1] + 16, LANES), padded(plan), padded(plan), window, window,
         (nz2 * nx2, LANES), (2 * plan.pairs * plan.ex, LANES)],
        r, x, r1, x1, ours, from_a, from_b, from_c,
        out_specs=[ANY, ANY, VMEM], semaphores=3,
    )


def fits_fast(shape, peers):
    bz, bx, by = shape
    nz, nx, ny = peers
    return (
        nz == 4 and nx == 2 and ny == 4 and bz == 16 and by == LANES
        and nx * bx == 4 * 8 and ny * by == 4 * LANES
    )


def body(divergence, pressure_prev):
    peers = tuple(lax.axis_size(a) for a in ("gz", "gx", "gy"))
    if fits_fast(divergence.shape, peers):
        return tuple(body_fast(divergence, pressure_prev))
    return body_levels(divergence, pressure_prev)


def solution(mesh):
    in_specs = (P("gz", "gx", "gy"), P("gz", "gx", "gy"))
    out_specs = (P("gz", "gx", "gy"), P("gz", "gx", "gy"), P())
    return jax.shard_map(body, mesh=mesh, in_specs=in_specs, out_specs=out_specs, check_vma=False)
```

```python
import functools

import jax
import jax.numpy as jnp
from jax import lax
from jax.experimental import pallas as pl
from jax.experimental.pallas import tpu as pltpu
from jax.sharding import PartitionSpec as P

LEVELS = 6


first_scale = 1.0 / 7.5
rho_one = 1.0 / (2.0 * (5.0 / 3.0) - 0.6)
carry_coef = 0.6 * rho_one
fresh_coef = 2.0 * rho_one / (0.75 * 6.0)

LANES = 128
F32 = jnp.float32
AXES = (("gz", 0), ("gx", 1), ("gy", 2))


def extended(x, width):
    for axis, dim in AXES:
        peers, length = (lax.axis_size(axis), x.shape[dim + 1])
        up = [(i, (i + 1) % peers) for i in range(peers - 1)]
        down = [(j, i) for i, j in up]
        last = lax.slice_in_dim(x, length - width, length, axis=dim + 1)
        first = lax.slice_in_dim(x, 0, width, axis=dim + 1)
        before = lax.ppermute(last, axis, up)
        after = lax.ppermute(first, axis, down)
        x = jnp.concatenate([before, x, after], axis=dim + 1)
    return x


def stencil(values):
    padded = jnp.pad(values, 1)
    return valid_op(padded)


def valid_op(padded):
    beside = padded[2:, 1:-1, 1:-1] + padded[:-2, 1:-1, 1:-1]
    beside = beside + padded[1:-1, 2:, 1:-1] + padded[1:-1, :-2, 1:-1]
    beside = beside + padded[1:-1, 1:-1, 2:] + padded[1:-1, 1:-1, :-2]
    return 6.0 * padded[1:-1, 1:-1, 1:-1] - beside


def smooth_pass(iterate, source, apply_op, from_zero):
    residue = source if from_zero else source - apply_op(iterate)
    update = residue * first_scale
    iterate = update if from_zero else iterate + update
    residue = source - apply_op(iterate)
    update = carry_coef * update + fresh_coef * residue
    return iterate + update


def restrict(values):
    shape_a, shape_b, shape_c = values.shape
    blocks = values.reshape(shape_a // 2, 2, shape_b // 2, 2, shape_c // 2, 2)
    return 0.5 * jnp.sum(blocks, axis=(1, 3, 5))


def prolong(values):
    shape_a, shape_b, shape_c = values.shape
    spread = jnp.broadcast_to(
        values[:, None, :, None, :, None], (shape_a, 2, shape_b, 2, shape_c, 2)
    )
    return spread.reshape(2 * shape_a, 2 * shape_b, 2 * shape_c)


def vcycle(level_num, iterate, source):
    iterate = smooth_pass(iterate, source, stencil, True)
    coarsest = None
    if level_num < LEVELS - 1:
        residue = source - stencil(iterate)
        coarse, coarsest = vcycle(level_num + 1, None, restrict(residue))
        iterate = iterate + prolong(coarse)
    result = smooth_pass(iterate, source, stencil, False)
    if level_num == LEVELS - 1:
        coarsest = result
    return (result, coarsest)


def collect(values):
    gathered = lax.all_gather(values, "gz", axis=0, tiled=True)
    gathered = lax.all_gather(gathered, "gy", axis=2, tiled=True)
    return lax.all_gather(gathered, "gx", axis=1, tiled=True)


def local_stencil(values):
    return valid_op(extended(values[None], 1)[0])


def own_block(whole, block_shape):
    start_z = lax.axis_index("gz") * block_shape[0]
    start_x = lax.axis_index("gx") * block_shape[1]
    start_y = lax.axis_index("gy") * block_shape[2]
    return lax.dynamic_slice(whole, (start_z, start_x, start_y), block_shape)


def body_cycle(level_num, iterate, source, from_zero, gather_at):
    if level_num == gather_at:
        whole_source = collect(source)
        coarse, coarsest = vcycle(level_num, None, whole_source)
        return (own_block(coarse, source.shape), coarsest)
    iterate = smooth_pass(iterate, source, local_stencil, from_zero)
    residue = source - local_stencil(iterate)
    coarse, coarsest = body_cycle(level_num + 1, None, restrict(residue), True, gather_at)
    iterate = iterate + prolong(coarse)
    return (smooth_pass(iterate, source, local_stencil, False), coarsest)


def body_levels(divergence, pressure_prev):
    pressure, coarse_correction = body_cycle(0, pressure_prev, divergence, False, 3)
    residual = divergence - local_stencil(pressure)
    return (pressure, residual, coarse_correction)


def iota(shape, dim):
    return lax.broadcasted_iota(jnp.int32, shape, dim)


def signed(index, size, extent):
    return jnp.where(index >= (size + extent) // 2, index - extent, index)


def right_dot(values, table):
    rows = values.shape[0]
    terms = []
    for _ in range(3):
        term = values.astype(jnp.bfloat16)
        terms.append(term)
        values = values - term.astype(F32)
    out = jnp.dot(jnp.concatenate(terms, axis=0), table, preferred_element_type=F32)
    return out[0:rows] + out[rows:2 * rows] + out[2 * rows:3 * rows]


def right_dots(values, table):
    total = None
    for _ in range(3):
        term = values.astype(jnp.bfloat16)
        part = jnp.dot(term, table, preferred_element_type=F32)
        total = part if total is None else total + part
        values = values - term.astype(F32)
    return total


def as_table(keep, value=1.0):
    return jnp.where(keep, value, 0.0).astype(jnp.bfloat16)


def lateral(v):
    rows, lanes = v.shape
    return (
        pltpu.roll(v, 1, 0) + pltpu.roll(v, rows - 1, 0)
        + pltpu.roll(v, 1, 1) + pltpu.roll(v, lanes - 1, 1)
    )


def apply_at(ref, k, lateral_of=lateral):
    centre = ref[k]
    beside = lateral_of(centre)
    if k > 0:
        beside = beside + ref[k - 1]
    if k < ref.shape[0] - 1:
        beside = beside + ref[k + 1]
    return 6.0 * centre - beside


def padded(plan):
    return (plan.ey // LANES, plan.ez, plan.ex + 16, LANES)


def put(ref, k, v):
    rows = v.shape[0]
    for tile in range(ref.shape[0]):
        part = v[:, tile * LANES:(tile + 1) * LANES]
        ref[tile, k, 8:8 + rows, :] = part
        ref[tile, k, 7:8, :] = part[rows - 1:rows]
        ref[tile, k, 8 + rows:9 + rows, :] = part[0:1]


def rows_of(ref, k, first):
    here = pl.ds(first, ref.shape[2] - 16)
    return jnp.concatenate([ref[tile, k, here, :] for tile in range(ref.shape[0])], axis=1)


def apply_padded(ref, k, origin):
    centre = rows_of(ref, k, 8)
    lanes = centre.shape[1]
    beside = rows_of(ref, k, origin - 1) + rows_of(ref, k, origin + 1)
    beside = beside + (pltpu.roll(centre, 1, 1) + pltpu.roll(centre, lanes - 1, 1))
    if k > 0:
        beside = beside + rows_of(ref, k - 1, 8)
    if k < ref.shape[1] - 1:
        beside = beside + rows_of(ref, k + 1, 8)
    return 6.0 * centre - beside


def wrapped_mask(shape, sizes, low, high):
    keep = None
    for dim, size in sizes.items():
        at = signed(iota(shape, dim), size, shape[dim])
        good = ((at >= 0) | low[dim]) & ((at < size) | high[dim])
        keep = good if keep is None else keep & good
    return jnp.where(keep, 1.0, 0.0).astype(F32)


def side(index, flip):
    if flip == 1:
        return (index & 1) == 0, None
    return index < 2, (index == 1) | (index == 2)


def place(axis, count):
    index = lax.axis_index(axis)
    return index, index > 0, index < count - 1


def only(keep, v):
    return jnp.where(keep, v, 0.0)


def shifted(v, lanes):
    lanes = lanes % LANES
    return v if lanes == 0 else pltpu.roll(v, lanes, 1)


def lanes_of(v, first, count):
    lane = iota(v.shape, 1)
    last = first + count
    if last <= LANES:
        return (lane >= first) & (lane < last)
    return (lane >= first) | (lane < last - LANES)


def moved(v, first, count, to):
    first = first % LANES
    return shifted(only(lanes_of(v, first, count), v), to - first)


def landed(v, first, count, to):
    to = to % LANES
    v = shifted(v, to - first)
    return only(lanes_of(v, to, count), v)


def side_pack(tile, slot):
    return moved(tile, LANES - 3, 6, 6 * slot)


def side_unpack(packed, slot):
    return landed(packed, 6 * slot, 6, LANES - 3)


def slab_layers(r_ref, x_ref, up, low, high):
    start = jnp.where(up, high[0], low[0])
    start_x = jnp.where(up, high[1], low[1])
    return [(r_ref, start + j) for j in range(5)] + [(x_ref, start_x + j) for j in range(2)]


def slab_own(r_ref, x_ref, up):
    ez = r_ref.shape[0]
    return slab_layers(r_ref, x_ref, up, (0, 1), (ez - 5, ez - 3))


def slab_there(r_ref, x_ref, up):
    ez = r_ref.shape[0]
    return slab_layers(r_ref, x_ref, up, (1, 3), (ez - 6, ez - 5))


def slab_emit(r_ref, x_ref, out, up):
    ex = r_ref.shape[1]
    lat = None
    for j, (ref, k) in enumerate(slab_own(r_ref, x_ref, up)):
        v = ref[k]
        out[j * ex:(j + 1) * ex, :] = v[:, 0:LANES]
        part = side_pack(v[:, LANES:], j)
        lat = part if lat is None else lat + part
    out[7 * ex:8 * ex, :] = lat


def slab_add(r_ref, x_ref, slab, up):
    ex = r_ref.shape[1]
    lat = slab[7 * ex:8 * ex, :]
    for j, (ref, k) in enumerate(slab_there(r_ref, x_ref, up)):
        ref[k, :, 0:LANES] += slab[j * ex:(j + 1) * ex, :]
        ref[k, :, LANES:] += side_unpack(lat, j)


BESIDE = ((2, 2, 0, 0), (1, 1, 0, 3), (3, 1, 0, 5), (5, 1, 1, 0), (6, 1, 1, 3))


def beside(tile, count):
    row = iota(tile.shape, 0)
    return only((row < count) | (row >= 8 - count), tile)


def thin_emit(r_ref, x_ref, out, up):
    bx = r_ref.shape[1] - 8
    layers = slab_own(r_ref, x_ref, up)
    lat = None
    for j, (ref, k) in enumerate(layers):
        out[j * bx:(j + 1) * bx, :] = ref[k, 0:bx, 0:LANES]
        part = side_pack(ref[k, 0:bx, LANES:], j)
        lat = part if lat is None else lat + part
    tiles = [None, None]
    for j, count, which, turn in BESIDE:
        ref, k = layers[j]
        part = beside(ref[k, bx:, 0:LANES], count)
        part = pltpu.roll(part, turn, 0) if turn else part
        tiles[which] = part if tiles[which] is None else tiles[which] + part
    at = 7 * bx
    out[at:at + 8, :] = tiles[0]
    out[at + 8:at + 16, :] = tiles[1]
    out[at + 16:at + 16 + bx, :] = lat
    for j in (1, 2, 3):
        ref, k = layers[j]
        out[at + 16:at + 24, :] += side_pack(ref[k, bx:, LANES:], 6 + j)


def thin_add(r_ref, x_ref, slab, up):
    bx = r_ref.shape[1] - 8
    layers = slab_there(r_ref, x_ref, up)
    at = 7 * bx
    lat = slab[at + 16:at + 16 + bx, :]
    for j, (ref, k) in enumerate(layers):
        ref[k, 0:bx, 0:LANES] += slab[j * bx:(j + 1) * bx, :]
        ref[k, 0:bx, LANES:] += side_unpack(lat, j)
    for j, count, which, turn in BESIDE:
        ref, k = layers[j]
        tile = slab[at + 8 * which:at + 8 * which + 8, :]
        tile = pltpu.roll(tile, 8 - turn, 0) if turn else tile
        ref[k, bx:, 0:LANES] += beside(tile, count)
    for j in (1, 2, 3):
        ref, k = layers[j]
        ref[k, bx:, LANES:] += side_unpack(lat[0:8], 6 + j)


def rows_out(r, x, up):
    bx = r.shape[0] - 8
    row = iota((8, r.shape[1]), 0)
    first, last, spill = r[0:8], r[bx - 8:bx], r[bx:]
    to_high = pltpu.roll(jnp.where(row >= 6, last, spill), 2, 0)
    to_low = pltpu.roll(jnp.where(row >= 5, spill, first), 3, 0)
    out = jnp.where(up, to_high, to_low)
    if x is None:
        return only(row < 5, out)
    spill = x[bx:]
    extra = jnp.where(up, pltpu.roll(spill, 5, 0), pltpu.roll(spill, 7, 0))
    return jnp.where(row < 5, out, only(row < 7, extra))


def rows_in(r_ref, x_ref, k, rows, up):
    bx = r_ref.shape[1] - 8
    row = iota(rows.shape, 0)
    high, low = pltpu.roll(rows, 5, 0), pltpu.roll(rows, 6, 0)
    r_ref[k, 0:8] += only(jnp.logical_not(up) & (row < 3), low)
    r_ref[k, bx - 8:bx] += only(up & (row >= 5), high)
    r_ref[k, bx:] += jnp.where(up, only(row < 2, high), only(row >= 6, low))
    if x_ref is not None:
        x_ref[k, 0:8] += only(jnp.logical_not(up) & (row < 2), pltpu.roll(rows, 3, 0))
        x_ref[k, bx - 8:bx] += only(up & (row >= 6), pltpu.roll(rows, 1, 0))


def rows_emit(r_ref, x_ref, out, up):
    ez = r_ref.shape[0]
    row = iota((8, LANES), 0)
    lat = jnp.zeros((8, LANES), F32)
    for t, k in enumerate(range(1, ez - 1)):
        far = {1: 0, ez - 2: ez - 1}.get(k)
        rows = rows_out(r_ref[k], None if far is not None else x_ref[k], up)
        tile = rows[:, 0:LANES]
        if far is not None:
            more = rows_out(r_ref[far, :, 0:LANES], None, up)
            more = jnp.where(up, pltpu.roll(more, 5, 0), pltpu.roll(more, 2, 0))
            tile = jnp.where((row == 5) | (row == 6), more, tile)
        out[8 * t:8 * t + 8, :] = tile
        lat = lat + side_pack(rows[:, LANES:], t)
    at = 8 * (ez - 2)
    out[at:at + 8, :] = lat


def rows_add(r_ref, x_ref, slab, up):
    ez = r_ref.shape[0]
    at = 8 * (ez - 2)
    lat = slab[at:at + 8, :]
    row = iota((8, LANES), 0)
    for t, k in enumerate(range(1, ez - 1)):
        far = {1: 0, ez - 2: ez - 1}.get(k)
        tile = slab[8 * t:8 * t + 8, :]
        rows = jnp.concatenate([tile, side_unpack(lat, t)], axis=1)
        rows_in(r_ref, None if far is not None else x_ref, k, rows, up)
        if far is not None:
            tile = only((row == 5) | (row == 6), tile)
            tile = jnp.where(up, pltpu.roll(tile, 6, 0), pltpu.roll(tile, 3, 0))
            rows = jnp.concatenate([tile, jnp.zeros((8, LANES), F32)], axis=1)
            rows_in(r_ref, None, far, rows, up)


class Plan:
    def first_layer(self, iz):
        start = iz * (self.block[0] // 2) - 4
        return jnp.clip(start, 0, self.level1[0] - self.window[0])

    def __init__(self, shape, peers):
        self.peers = peers
        self.block = bz, bx, by = shape
        self.ext = self.ez, self.ex, self.ey = bz + 6, bx + 8, by + LANES
        self.rows, self.pairs = bx // 2, bz // 4 + 2
        self.lat_at = self.pairs * (self.rows + 4)
        self.coarse = self.lat_at + 8
        self.slab = 8 * self.ex
        self.slab_z = 8 * bx + 16
        self.slab_x = 8 * (bz + 5)
        self.corner = 6 * 8
        self.layers = bz + 4
        self.level1 = (peers[0] * bz // 2, peers[1] * bx // 2, LANES)
        self.level2 = (peers[0] * bz // 4, peers[1] * bx // 4, peers[2] * by // 4)
        self.inner = [0, 1] + [2] * bz + [1, 0]
        self.slots, at = [], 0
        for count in self.inner:
            self.slots.append(at)
            at += 3 + count + (2 if count == 2 else 0)
        assert at <= LANES
        self.fine_rows = self.ex
        self.window = (bz // 2 + 8, self.level1[1], LANES)
        self.edge = self.fine_rows + self.window[0] * self.window[1] // 8
        self.wide2 = by // 4 + 4
        self.fold = LANES // self.wide2
        self.lines2 = -(-self.level2[0] // self.fold)
        self.share = self.lines2 * self.level2[1]


def first_kernel(plan, both, r_ref, x_ref, pay_z, pay_x, pay_d, d_one, d_two, pairs, lines):
    p_ext, b_ext = both.at[0], both.at[1]
    bz, bx, by = plan.block
    ez, ex, ey = plan.ext
    peers = plan.peers
    iz, z_low, z_high = place("gz", peers[0])
    ix, x_low, x_high = place("gx", peers[1])
    _, y_low, y_high = place("gy", peers[2])
    flat = wrapped_mask((ex, ey), {0: bx, 1: by}, (x_low, y_low), (x_high, y_high))
    below = jnp.where(z_low, 1.0, 0.0).astype(F32)
    above = jnp.where(z_high, 1.0, 0.0).astype(F32)

    def masked(k, v):
        v = v * flat
        if k < 3:
            v = v * below
        if k >= 3 + bz:
            v = v * above
        return v

    zero = jnp.zeros((ex, ey), F32)
    origin = 8 + (iz >> 8)
    for k in range(ez):
        if 2 <= k < ez - 2:
            r = b_ext[k] - apply_at(p_ext, k)
            r_ref[k] = r
            put(d_one, k, masked(k, r * first_scale))
        elif 1 <= k < ez - 1:
            put(d_one, k, zero)
    for k in range(ez):
        if 1 <= k < ez - 1:
            if 2 <= k < ez - 2:
                r = r_ref[k] - apply_padded(d_one, k, origin)
                d = carry_coef * rows_of(d_one, k, 8) + fresh_coef * r
            else:
                inward = k + 1 if k == 1 else k - 1
                r = rows_of(d_one, inward, 8)
                d = fresh_coef * r
            r_ref[k] = r
            put(d_two, k, masked(k, d))
    for k in range(ez):
        if 1 <= k < ez - 1:
            part = rows_of(d_two, k, 8)
            beside = rows_of(d_two, k, origin - 1) + rows_of(d_two, k, origin + 1)
            beside = beside + (pltpu.roll(part, 1, 1) + pltpu.roll(part, ey - 1, 1))
            if k > 1:
                beside = beside + rows_of(d_two, k - 1, 8)
            if k < ez - 2:
                beside = beside + rows_of(d_two, k + 1, 8)
            r_ref[k] = masked(k, r_ref[k] - (6.0 * part - beside))
            x_ref[k] = p_ext[k] + (rows_of(d_one, k, 8) + part)
        else:
            r_ref[k] = masked(k, rows_of(d_two, 1 if k == 0 else ez - 2, 8))
            x_ref[k] = zero

    coarse_z, rows = 2 * plan.pairs, plan.rows
    for zc in range(coarse_z):
        low, high = 2 * zc - 1, 2 * zc
        if low < 0:
            total = r_ref[high]
        elif high >= ez:
            total = r_ref[low]
        else:
            total = r_ref[low] + r_ref[high]
        base = zc * ex
        for tile in range(ey // LANES):
            here = slice(tile * LANES, (tile + 1) * LANES)
            pairs[tile, base:base + ex, :] = total[:, here]
            even = pairs.at[tile][pl.ds(base, ex // 2, 2), :]
            odd = pairs.at[tile][pl.ds(base + 1, ex // 2, 2), :]
            sums = even + odd
            at = zc // 2 * rows
            at += zc % 2 * plan.lat_at
            lines[at:at + rows, here] = sums[0:rows]
            at = plan.pairs * rows + zc // 2 * 4 + zc % 2 * plan.lat_at
            lines[at:at + 4, here] = sums[rows:rows + 4]
    fine = signed(iota((ey, LANES), 0), by, ey)
    coarse = signed(iota((ey, LANES), 1), by // 2, LANES)
    table = as_table((fine >> 1) == coarse, 0.5)
    out = right_dot(lines[...], table)
    even, odd = out[0:plan.lat_at], out[plan.lat_at:]
    lane = iota(even.shape, 1)
    main = jnp.where(lane < LANES // 2, even, shifted(odd, LANES // 2))
    own_lat = spill_lat = None
    row = iota((8, LANES), 0)
    for zc in range(coarse_z):
        source = (even, odd)[zc % 2]
        base = zc // 2 * rows
        tile = source[base:base + rows]
        part = moved(tile, by // 2, 2, 4 * zc) + moved(tile, LANES - 2, 2, 4 * zc + 2)
        own_lat = part if own_lat is None else own_lat + part
        base = plan.pairs * rows + zc // 4 * 8
        tile = source[base:base + 8]
        if zc // 2 % 2:
            tile = pltpu.roll(tile, 4, 0)
        tile = only(row < 4, tile)
        slot = LANES // 2 + 4 * zc
        part = moved(tile, by // 2, 2, slot) + moved(tile, LANES - 2, 2, slot + 2)
        spill_lat = part if spill_lat is None else spill_lat + part
    for pay, at in ((pay_z, plan.slab_z), (pay_x, plan.slab_x), (pay_d, plan.corner)):
        pay[at:at + plan.lat_at, :] = main
        pay[at + plan.lat_at:at + plan.coarse, :] = own_lat + spill_lat

    up_z, _ = side(iz, 3)
    up_x, _ = side(ix, 1)
    thin_emit(r_ref, x_ref, pay_z, up_z)
    rows_emit(r_ref, x_ref, pay_x, up_x)
    lat = jnp.zeros((8, LANES), F32)
    start = jnp.where(up_z, ez - 5, 0)
    for j in range(5):
        out = rows_out(r_ref[start + j], x_ref[start + j] if j == 2 else None, up_x)
        pay_d[8 * j:8 * j + 8, :] = out[:, 0:LANES]
        lat = lat + side_pack(out[:, LANES:], j)
    pay_d[40:48, :] = lat


def chip_kernel(plan, r_in, x_in, from_z, from_x, from_d, r_ref, x_ref, pay):
    ez, ex, ey = plan.ext
    iz, _, _ = place("gz", plan.peers[0])
    ix, _, _ = place("gx", plan.peers[1])
    up_z, near = side(iz, 3)
    up_x, _ = side(ix, 1)
    for k in range(ez):
        r_ref[k] = r_in[k]
        x_ref[k] = x_in[k]
    rows_add(r_ref, x_ref, from_x, up_x)

    @pl.when(near)
    def _():
        thin_add(r_ref, x_ref, from_z, up_z)
        start = jnp.where(up_z, ez - 6, 1)
        lat = from_d[40:48, :]
        for j in range(5):
            rows = from_d[8 * j:8 * j + 8, :]
            rows = jnp.concatenate([rows, side_unpack(lat, j)], axis=1)
            rows_in(r_ref, x_ref if j == 2 else None, start + j, rows, up_x)

    slab_emit(r_ref, x_ref, pay, side(iz, 1)[0])


def plane_kernel(plan, r_in, x_in, ours, theirs, r_ref, x_ref, r1_ref, x1_ref, pay, later, share,
                 r_all, x_all, b1, d1, d2, r1, x1, pairs, lines):
    bz, bx, by = plan.block
    ez, ex, ey = plan.ext
    layers = plan.layers
    iz, _, _ = place("gz", plan.peers[0])
    ix, _, _ = place("gx", plan.peers[1])
    iy, y_low, y_high = place("gy", plan.peers[2])
    up_z, _ = side(iz, 1)
    for k in range(ez):
        r_all[k] = r_in[k]
        x_all[k] = x_in[k]
    slab_add(r_all, x_all, theirs, up_z)
    for k in range(layers):
        r_ref[k] = r_all[k + 1]
    for k in range(bz):
        x_ref[k] = x_all[k + 3, 0:bx, 0:by]

    up, _ = side(iy, 1)
    up_inner, _ = side(iy, 3)
    high, low = jnp.zeros((ex, LANES), F32), jnp.zeros((ex, LANES), F32)
    for k in range(layers):
        slot, inner = plan.slots[k], plan.inner[k]
        count = 3 + inner
        v, spill = r_all[k + 1, :, 0:by], r_all[k + 1, :, by:ey]
        high = high + moved(jnp.where(lanes_of(v, 0, 3), spill, v), LANES - inner, count, slot)
        mixed = jnp.where(lanes_of(v, 0, 2), v, spill)
        low = low + moved(mixed, LANES - 3, count, slot)
        if inner == 2:
            spill = x_all[k + 1, :, by:ey]
            high = high + moved(spill, 0, 2, slot + count)
            low = low + moved(spill, LANES - 2, 2, slot + count)
    pay[0:ex, :] = jnp.where(up, high, low)
    later[0:ex, :] = jnp.where(up_inner, high, low)

    nz1, nx1, _ = plan.level1
    rows, half = plan.rows, by // 2
    for k in range(nz1):
        b1[k] = jnp.zeros((nx1, LANES), F32)
    row = iota((8, LANES), 0)
    for j in range(plan.peers[0]):
        for i in range(plan.peers[1]):
            flip = iz ^ j
            other = ((flip ^ (flip >> 1)) & 1) == 1
            chip = (flip >> 1) + 2 * (ix ^ i)
            at = pl.multiple_of(plan.slab + chip * plan.coarse, 8)

            def rows_at(offset, count):
                here = pl.ds(pl.multiple_of(at + offset, 8), count)
                return jnp.where(other, theirs[here, :], ours[here, :])

            lat = rows_at(plan.lat_at, 8)
            for zp in range(plan.pairs):
                own = rows_at(zp * rows, rows)
                if zp % 2 == 0:
                    spill_two = rows_at(plan.pairs * rows + zp * 4, 8)
                spill = spill_two if zp % 2 == 0 else pltpu.roll(spill_two, 4, 0)
                for part in range(2):
                    zc = 2 * zp + part
                    k = j * (bz // 2) + zc - 2
                    if not 0 <= k < nz1:
                        continue

                    def wide(main, slot):
                        return (
                            landed(main, part * half, half, 0)
                            + landed(lat, slot, 2, half) + landed(lat, slot + 2, 2, LANES - 2)
                        )

                    b1[k, i * rows:(i + 1) * rows, :] += wide(own, 4 * zc)
                    v = wide(spill, LANES // 2 + 4 * zc)
                    if i + 1 < plan.peers[1]:
                        at_row = (i + 1) * rows
                        b1[k, at_row:at_row + 8, :] += only(row < 2, v)
                    if i > 0:
                        at_row = i * rows - 8
                        b1[k, at_row:at_row + 8, :] += only(row >= 6, pltpu.roll(v, 4, 0))

    lateral1 = level_lateral((nx1, LANES))
    keep = wrapped_mask((nx1, LANES), {1: half}, (None, y_low), (None, y_high))
    for k in range(nz1):
        d1[k] = b1[k] * first_scale
    for k in range(nz1):
        r = b1[k] - apply_at(d1, k, lateral1)
        r1[k] = r
        d2[k] = keep * (carry_coef * d1[k] + fresh_coef * r)
    for k in range(nz1):
        r1[k] = keep * (r1[k] - apply_at(d2, k, lateral1))
        x1[k] = d1[k] + d2[k]

    nz2, nx2, _ = plan.level2
    for zc in range(nz2):
        pairs[zc * nx1:(zc + 1) * nx1, :] = r1[2 * zc] + r1[2 * zc + 1]
        part, at = divmod(zc, plan.lines2)
        lines[at * nx2:(at + 1) * nx2, part * LANES:(part + 1) * LANES] = (
            pairs[pl.ds(zc * nx1, nx2, 2), :] + pairs[pl.ds(zc * nx1 + 1, nx2, 2), :]
        )
    shape = (plan.fold * LANES, LANES)
    fine, coarse = iota(shape, 0), iota(shape, 1)
    part, fine = fine // LANES, signed(fine % LANES, half, LANES)
    coarse = coarse - part * plan.wide2 - 2
    near = (coarse >= -2) & (coarse < plan.wide2 - 2)
    for part in range(plan.fold):
        count = min(plan.lines2, nz2 - part * plan.lines2) * nx2
        if count < plan.share:
            here = slice(part * LANES, (part + 1) * LANES)
            lines[count:, here] = jnp.zeros((plan.share - count, LANES), F32)
    total = right_dot(lines[...], as_table(near & ((fine >> 1) == coarse), 0.5))
    share[...] = total
    pay[plan.edge:plan.edge + plan.share, :] = total
    later[plan.edge:plan.edge + plan.share, :] = total

    start = plan.first_layer(iz)
    for k in range(plan.window[0]):
        r1_ref[k] = r1[start + k]
        x1_ref[k] = x1[start + k]
    per_tile = LANES // 16
    for group in range(plan.window[0] // per_tile):
        tiles = []
        for which in range(2):
            total = jnp.zeros((nx1, LANES), F32)
            for j in range(per_tile):
                k = group * per_tile + j
                first = half - 3 if which == 0 else LANES - 4
                total = total + moved(r1_ref[k], first, 7, 16 * j)
                first = half - 2 if which == 0 else LANES - 3
                total = total + moved(x1_ref[k], first, 5, 16 * j + 7)
            tiles.append(total)
        here = slice(plan.fine_rows + group * nx1, plan.fine_rows + (group + 1) * nx1)
        pay[here, :] = jnp.where(up, tiles[0], tiles[1])
        later[here, :] = jnp.where(up_inner, tiles[0], tiles[1])


def level_lateral(shape):
    row = iota(shape, 0)
    not_first = jnp.where(row > 0, 1.0, 0.0).astype(F32)
    not_last = jnp.where(row < shape[0] - 1, 1.0, 0.0).astype(F32)

    def beside(v):
        return (
            not_first * pltpu.roll(v, 1, 0) + not_last * pltpu.roll(v, shape[0] - 1, 0)
            + pltpu.roll(v, 1, 1) + pltpu.roll(v, LANES - 1, 1)
        )

    return beside


def small_cycle(level, source):
    step = 1 << (level - 2)
    row, lane = iota((8, LANES), 0), iota((8, LANES), 1)
    count = len(source)
    shifts = []
    if step < 8:
        shifts += [(step, 0, row >= step), (8 - step, 0, row < 8 - step)]
    shifts += [(step, 1, lane >= step), (LANES - step, 1, lane < LANES - step)]

    def op(v):
        out = []
        for k in range(count):
            beside = None
            for shift, dim, keep in shifts:
                part = only(keep, pltpu.roll(v[k], shift, dim))
                beside = part if beside is None else beside + part
            if k > 0:
                beside = beside + v[k - 1]
            if k < count - 1:
                beside = beside + v[k + 1]
            out.append(6.0 * v[k] - beside)
        return out

    d = [first_scale * v for v in source]
    r = [b - t for b, t in zip(source, op(d))]
    d2 = [carry_coef * v + fresh_coef * t for v, t in zip(d, r)]
    x = [v + t for v, t in zip(d, d2)]
    r = [v - t for v, t in zip(r, op(d2))]
    coarsest = None
    if level < LEVELS - 1:
        keep = only((row % (2 * step) == 0) & (lane % (2 * step) == 0), 0.5)
        coarse = []
        for k in range(0, count, 2):
            v = r[k] + r[k + 1]
            v = v + pltpu.roll(v, 8 - step, 0)
            coarse.append(keep * (v + pltpu.roll(v, LANES - step, 1)))
        coarse, coarsest = small_cycle(level + 1, coarse)
        e = []
        for v in coarse:
            v = v + pltpu.roll(v, step, 0)
            e += [v + pltpu.roll(v, step, 1)] * 2
        x = [v + t for v, t in zip(x, e)]
        r = [v - t for v, t in zip(r, op(e))]
    d = [first_scale * v for v in r]
    r = [v - t for v, t in zip(r, op(d))]
    x = [v + (t + (carry_coef * t + fresh_coef * u)) for v, t, u in zip(x, d, r)]
    return x, (x if level == LEVELS - 1 else coarsest)


def last_kernel(plan, r_in, x_in, r1_in, x1_in, ours, from_a, from_b, from_2, from_3, p_out, res_out, last_ref, *scratch):
    shares, p_ref, res_ref, r, q1, e1, e0, d0, d1, r1, lines, wide, sem = scratch
    bz, bx, by = plan.block
    ez, ex, ey = plan.ext
    nz1, nx1, _ = plan.window
    nz2, nx2, _ = plan.level2
    layers, half = plan.layers, by // 2
    iz, z_low, z_high = place("gz", plan.peers[0])
    ix, x_low, x_high = place("gx", plan.peers[1])
    iy, y_low, y_high = place("gy", plan.peers[2])

    shares[0] = ours[...]
    shares[1] = from_a[plan.edge:plan.edge + plan.share, :]
    inner = side(iy, 3)[1]
    shares[3] = jnp.where(inner, from_b[plan.edge:plan.edge + plan.share, :], from_3[...])
    shares[2] = from_2[...]
    own2 = half // 2
    source = []
    for part in range(plan.fold):
        total = None
        for j in range(plan.peers[2]):
            v = moved(shares[iy ^ j], part * plan.wide2, plan.wide2, own2 * j - 2)
            total = v if total is None else total + v
        source += [total[nx2 * k:nx2 * (k + 1)] for k in range(plan.lines2)]
    source = source[:nz2]
    e2, coarsest = small_cycle(2, source)
    for k in range(nz2):
        lines[k * nx2:(k + 1) * nx2, :] = e2[k]
    thin = as_table(iota((LANES, LANES), 0) == 8 * iota((LANES, LANES), 1))
    for k in range(last_ref.shape[0]):
        last_ref[k] = right_dot(coarsest[k], thin)[0:1, 0:last_ref.shape[2]]

    up_a, _ = side(iy, 1)
    _, near_b = side(iy, 3)

    def sent(rows):
        a, b = from_a[rows[0]:rows[1], :], only(near_b, from_b[rows[0]:rows[1], :])
        return jnp.where(up_a, a, b), jnp.where(up_a, b, a)

    fine = signed(iota((LANES, LANES), 1), half, LANES)
    coarse = iota((LANES, LANES), 0) - iy * own2
    start = plan.first_layer(iz)
    here = pl.ds(pl.multiple_of(start // 2 * nx2, 8), nz1 // 2 * nx2)
    e2 = right_dot(lines[here, :], as_table((fine >> 1) == coarse))
    for zc in range(nz1 // 2):
        v = e2[zc * nx2:(zc + 1) * nx2]
        for part in range(2):
            q1.at[2 * zc + part][pl.ds(0, nx2, 2), :] = v
            q1.at[2 * zc + part][pl.ds(1, nx2, 2), :] = v
    per_tile = LANES // 16
    lateral1 = level_lateral((nx1, LANES))
    keep = wrapped_mask((nx1, LANES), {1: half}, (None, y_low), (None, y_high))
    for group in range(nz1 // per_tile):
        at = plan.fine_rows + group * nx1
        high, low = sent((at, at + nx1))
        for j in range(per_tile):
            k = group * per_tile + j
            s = 16 * j
            r1[k] = (
                r1_in[k] + landed(high, s, 7, half - 4) + landed(low, s, 7, LANES - 3)
                - apply_at(q1, k, lateral1)
            )
            e1[k + 2, 8:8 + nx1, :] = (
                x1_in[k] + q1[k]
                + landed(high, s + 7, 5, half - 3) + landed(low, s + 7, 5, LANES - 2)
            )
    for k in range(nz1):
        d1[k] = keep * (r1[k] * first_scale)
    nothing = jnp.zeros((8, LANES), F32)
    for k in range(nz1 + 4):
        e1[k, 0:8, :] = nothing
        e1[k, 8 + nx1:16 + nx1, :] = nothing
        if not 2 <= k < nz1 + 2:
            e1[k, 8:8 + nx1, :] = jnp.zeros((nx1, LANES), F32)
    for k in range(nz1):
        v = r1[k] - apply_at(d1, k, lateral1)
        e1[k + 2, 8:8 + nx1, :] += d1[k] + keep * (carry_coef * d1[k] + fresh_coef * v)

    coarse = signed(iota((LANES, ey), 0), half, LANES)
    fine = signed(iota((LANES, ey), 1), by, ey)
    double = as_table((fine >> 1) == coarse)
    half_z, half_x = bz // 2, bx // 2
    for zc in range(half_z + 4):
        here = pl.ds(pl.multiple_of(ix * half_x, 8), half_x + 16)
        v = e1[iz * half_z - start + zc, here, :]
        own, low, high = v[8:8 + half_x], v[0:8], v[8 + half_x:16 + half_x]
        at = zc * ex
        wide[pl.ds(at, half_x, 2), :] = own
        wide[pl.ds(at + 1, half_x, 2), :] = own
        for j in range(2):
            for twin in range(2):
                row = at + bx + 2 * j + twin
                wide[row:row + 1, :] = high[j:j + 1]
                row = at + ex - 4 + 2 * j + twin
                wide[row:row + 1, :] = low[6 + j:7 + j]
    origin = 8 + (iz >> 8)
    for zc in range(half_z + 4):
        v = right_dots(wide[zc * ex:(zc + 1) * ex, :], double)
        for k in (2 * zc - 1, 2 * zc):
            if 0 <= k < ez:
                put(e0, k, v)
    flat = wrapped_mask((ex, ey), {0: bx, 1: by}, (x_low, y_low), (x_high, y_high))
    below = jnp.where(z_low, 1.0, 0.0).astype(F32)
    above = jnp.where(z_high, 1.0, 0.0).astype(F32)

    def masked(k, v):
        v = v * flat
        if k < 3:
            v = v * below
        if k >= 3 + bz:
            v = v * above
        return v

    high, low = sent((0, ex))
    for k in range(layers):
        s, inner = plan.slots[k], plan.inner[k]
        v = r_in[k] - apply_padded(e0, k + 1, origin)
        own = v[:, 0:by] + landed(high, s, 3, LANES - 3) + landed(low, s + inner, 3, 0)
        spill = v[:, by:ey]
        if inner:
            spill = spill + landed(high, s + 3, inner, 0) + landed(low, s, inner, LANES - inner)
        r[k, :, 0:by] = own
        r[k, :, by:ey] = spill
        put(d0, k, masked(k + 1, r[k] * first_scale))
        if inner == 2:
            s = s + 3 + inner
            p_ref[k - 2] = (
                x_in[k - 2] + e0[0, k + 1, 8:8 + bx, :]
                + (landed(high, s, 2, LANES - 2) + landed(low, s, 2, 0))[0:bx]
            )
    for k in range(1, layers - 1):
        v = r[k] - apply_padded(d0, k, origin)
        r[k] = v
        d = rows_of(d0, k, 8)
        v = masked(k + 1, carry_coef * d + fresh_coef * v)
        put(e0, k, v)
        if 2 <= k < 2 + bz:
            p_ref[k - 2] += d[0:bx, 0:by] + v[0:bx, 0:by]
    copy = pltpu.make_async_copy(p_ref, p_out, sem.at[0])
    copy.start()
    copies = [copy]
    parts = 2
    for part in range(parts):
        here = range(part * bz // parts, (part + 1) * bz // parts)
        for j in here:
            v = r[j + 2] - apply_padded(e0, j + 2, origin)
            res_ref[j] = v[0:bx, 0:by]
        here = pl.ds(here[0], bz // parts)
        copy = pltpu.make_async_copy(res_ref.at[here], res_out.at[here], sem.at[1 + part])
        copy.start()
        copies.append(copy)
    for copy in copies:
        copy.wait()


def whole(shape):
    return jax.ShapeDtypeStruct(shape, F32)


VMEM = pl.BlockSpec(memory_space=pltpu.VMEM)
ANY = pl.BlockSpec(memory_space=pl.ANY)
VMEM_BYTES = 24 << 20


def run(kernel, plan, outs, scratch, *operands, out_specs=None, semaphores=0):
    scratch = [pltpu.VMEM(s, F32) for s in scratch]
    if semaphores:
        scratch.append(pltpu.SemaphoreType.DMA((semaphores,)))
    return pl.pallas_call(
        functools.partial(kernel, plan),
        out_shape=[whole(s) for s in outs],
        in_specs=[VMEM] * len(operands),
        out_specs=out_specs or [VMEM] * len(outs),
        scratch_shapes=scratch,
        compiler_params=pltpu.CompilerParams(vmem_limit_bytes=VMEM_BYTES),
    )(*operands)


def swap(values, partner):
    axes = ("gx", "gy", "gz")
    counts = [lax.axis_size(a) for a in axes]
    pairs = []
    for i in range(counts[0] * counts[1] * counts[2]):
        to = partner(i // (counts[1] * counts[2]), i // counts[2] % counts[1], i % counts[2])
        if to is not None:
            pairs.append((i, (to[0] * counts[1] + to[1]) * counts[2] + to[2]))
    return lax.ppermute(values, axes, pairs)


def body_fast(divergence, pressure_prev):
    plan = Plan(divergence.shape, tuple(lax.axis_size(a) for a in ("gz", "gx", "gy")))
    ext, level1 = plan.ext, plan.level1
    window, layers = plan.window, (plan.layers, plan.ex, plan.ey)
    payload = [(n + plan.coarse, LANES) for n in (plan.slab_z, plan.slab_x, plan.corner)]
    both = jnp.stack([pressure_prev, divergence])
    both = jnp.pad(both, ((0, 0), (3, 3), (0, plan.ex - plan.block[1]), (0, plan.ey - plan.block[2])))
    r, x, pay_z, pay_x, pay_d = run(
        first_kernel, plan, [ext, ext] + payload,
        [padded(plan), padded(plan), (2, 2 * plan.pairs * plan.ex, LANES),
         (2 * plan.lat_at, plan.ey)],
        both,
    )
    from_z = swap(pay_z, lambda x, y, z: (x, y, z ^ 3))
    from_x = swap(pay_x, lambda x, y, z: (x ^ 1, y, z))
    from_d = swap(pay_d, lambda x, y, z: (x ^ 1, y, z ^ 3))
    r, x, slab = run(
        chip_kernel, plan, [ext, ext, (plan.slab, LANES)], [], r, x, from_z, from_x, from_d
    )
    ours = jnp.concatenate([
        slab, pay_z[plan.slab_z:], from_z[plan.slab_z:], from_x[plan.slab_x:], from_d[plan.corner:]
    ], axis=0)
    got = swap(ours, lambda x, y, z: (x, y, z ^ 1))
    nz2, nx2, _ = plan.level2
    share = (plan.share, LANES)
    r, x, r1, x1, now, later, ours = run(
        plane_kernel, plan,
        [layers, plan.block, window, window, (plan.edge + plan.share, LANES),
         (plan.edge + plan.share, LANES), share],
        [ext, ext, level1, level1, level1, level1, level1, (nz2 * level1[1], LANES),
         (plan.share, plan.fold * LANES)],
        r, x, ours, got,
    )
    from_a = swap(now, lambda x, y, z: (x, y ^ 1, z))
    from_b = swap(later, lambda x, y, z: (x, y ^ 3, z) if y in (1, 2) else None)
    from_3 = swap(ours, lambda x, y, z: (x, y ^ 3, z) if y in (0, 3) else None)
    from_2 = swap(ours, lambda x, y, z: (x, y ^ 2, z))
    return run(
        last_kernel, plan,
        [plan.block, plan.block, tuple(n >> 3 for n in plan.level2)],
        [(4,) + share, plan.block, plan.block, layers, window,
         (window[0] + 4, window[1] + 16, LANES), padded(plan), padded(plan), window, window,
         (nz2 * nx2, LANES), (2 * plan.pairs * plan.ex, LANES)],
        r, x, r1, x1, ours, from_a, from_b, from_2, from_3,
        out_specs=[ANY, ANY, VMEM], semaphores=3,
    )


def fits_fast(shape, peers):
    bz, bx, by = shape
    nz, nx, ny = peers
    return (
        nz == 4 and nx == 2 and ny == 4 and bz == 16 and by == LANES
        and nx * bx == 4 * 8 and ny * by == 4 * LANES
    )


def body(divergence, pressure_prev):
    peers = tuple(lax.axis_size(a) for a in ("gz", "gx", "gy"))
    if fits_fast(divergence.shape, peers):
        return tuple(body_fast(divergence, pressure_prev))
    return body_levels(divergence, pressure_prev)


def solution(mesh):
    in_specs = (P("gz", "gx", "gy"), P("gz", "gx", "gy"))
    out_specs = (P("gz", "gx", "gy"), P("gz", "gx", "gy"), P())
    return jax.shard_map(body, mesh=mesh, in_specs=in_specs, out_specs=out_specs, check_vma=False)
```

```python
import functools

import jax
import jax.numpy as jnp
from jax import lax
from jax.experimental import pallas as pl
from jax.experimental.pallas import tpu as pltpu
from jax.sharding import PartitionSpec as P

LEVELS = 6


first_scale = 1.0 / 7.5
rho_one = 1.0 / (2.0 * (5.0 / 3.0) - 0.6)
carry_coef = 0.6 * rho_one
fresh_coef = 2.0 * rho_one / (0.75 * 6.0)

LANES = 128
F32 = jnp.float32
AXES = (("gz", 0), ("gx", 1), ("gy", 2))


def extended(x, width):
    for axis, dim in AXES:
        peers, length = (lax.axis_size(axis), x.shape[dim + 1])
        up = [(i, (i + 1) % peers) for i in range(peers - 1)]
        down = [(j, i) for i, j in up]
        last = lax.slice_in_dim(x, length - width, length, axis=dim + 1)
        first = lax.slice_in_dim(x, 0, width, axis=dim + 1)
        before = lax.ppermute(last, axis, up)
        after = lax.ppermute(first, axis, down)
        x = jnp.concatenate([before, x, after], axis=dim + 1)
    return x


def stencil(values):
    padded = jnp.pad(values, 1)
    return valid_op(padded)


def valid_op(padded):
    beside = padded[2:, 1:-1, 1:-1] + padded[:-2, 1:-1, 1:-1]
    beside = beside + padded[1:-1, 2:, 1:-1] + padded[1:-1, :-2, 1:-1]
    beside = beside + padded[1:-1, 1:-1, 2:] + padded[1:-1, 1:-1, :-2]
    return 6.0 * padded[1:-1, 1:-1, 1:-1] - beside


def smooth_pass(iterate, source, apply_op, from_zero):
    residue = source if from_zero else source - apply_op(iterate)
    update = residue * first_scale
    iterate = update if from_zero else iterate + update
    residue = source - apply_op(iterate)
    update = carry_coef * update + fresh_coef * residue
    return iterate + update


def restrict(values):
    shape_a, shape_b, shape_c = values.shape
    blocks = values.reshape(shape_a // 2, 2, shape_b // 2, 2, shape_c // 2, 2)
    return 0.5 * jnp.sum(blocks, axis=(1, 3, 5))


def prolong(values):
    shape_a, shape_b, shape_c = values.shape
    spread = jnp.broadcast_to(
        values[:, None, :, None, :, None], (shape_a, 2, shape_b, 2, shape_c, 2)
    )
    return spread.reshape(2 * shape_a, 2 * shape_b, 2 * shape_c)


def vcycle(level_num, iterate, source):
    iterate = smooth_pass(iterate, source, stencil, True)
    coarsest = None
    if level_num < LEVELS - 1:
        residue = source - stencil(iterate)
        coarse, coarsest = vcycle(level_num + 1, None, restrict(residue))
        iterate = iterate + prolong(coarse)
    result = smooth_pass(iterate, source, stencil, False)
    if level_num == LEVELS - 1:
        coarsest = result
    return (result, coarsest)


def collect(values):
    gathered = lax.all_gather(values, "gz", axis=0, tiled=True)
    gathered = lax.all_gather(gathered, "gy", axis=2, tiled=True)
    return lax.all_gather(gathered, "gx", axis=1, tiled=True)


def local_stencil(values):
    return valid_op(extended(values[None], 1)[0])


def own_block(whole, block_shape):
    start_z = lax.axis_index("gz") * block_shape[0]
    start_x = lax.axis_index("gx") * block_shape[1]
    start_y = lax.axis_index("gy") * block_shape[2]
    return lax.dynamic_slice(whole, (start_z, start_x, start_y), block_shape)


def body_cycle(level_num, iterate, source, from_zero, gather_at):
    if level_num == gather_at:
        whole_source = collect(source)
        coarse, coarsest = vcycle(level_num, None, whole_source)
        return (own_block(coarse, source.shape), coarsest)
    iterate = smooth_pass(iterate, source, local_stencil, from_zero)
    residue = source - local_stencil(iterate)
    coarse, coarsest = body_cycle(level_num + 1, None, restrict(residue), True, gather_at)
    iterate = iterate + prolong(coarse)
    return (smooth_pass(iterate, source, local_stencil, False), coarsest)


def body_levels(divergence, pressure_prev):
    pressure, coarse_correction = body_cycle(0, pressure_prev, divergence, False, 3)
    residual = divergence - local_stencil(pressure)
    return (pressure, residual, coarse_correction)


def iota(shape, dim):
    return lax.broadcasted_iota(jnp.int32, shape, dim)


def signed(index, size, extent):
    return jnp.where(index >= (size + extent) // 2, index - extent, index)


def right_dot(values, table):
    rows = values.shape[0]
    terms = []
    for _ in range(3):
        term = values.astype(jnp.bfloat16)
        terms.append(term)
        values = values - term.astype(F32)
    out = jnp.dot(jnp.concatenate(terms, axis=0), table, preferred_element_type=F32)
    return out[0:rows] + out[rows:2 * rows] + out[2 * rows:3 * rows]


def right_dots(values, table):
    total = None
    for _ in range(3):
        term = values.astype(jnp.bfloat16)
        part = jnp.dot(term, table, preferred_element_type=F32)
        total = part if total is None else total + part
        values = values - term.astype(F32)
    return total


def as_table(keep, value=1.0):
    return jnp.where(keep, value, 0.0).astype(jnp.bfloat16)


def lateral(v):
    rows, lanes = v.shape
    return (
        pltpu.roll(v, 1, 0) + pltpu.roll(v, rows - 1, 0)
        + pltpu.roll(v, 1, 1) + pltpu.roll(v, lanes - 1, 1)
    )


def apply_at(ref, k, lateral_of=lateral):
    centre = ref[k]
    beside = lateral_of(centre)
    if k > 0:
        beside = beside + ref[k - 1]
    if k < ref.shape[0] - 1:
        beside = beside + ref[k + 1]
    return 6.0 * centre - beside


def padded(plan):
    return (plan.ey // LANES, plan.ez, plan.ex + 16, LANES)


def put(ref, k, v):
    rows = v.shape[0]
    for tile in range(ref.shape[0]):
        part = v[:, tile * LANES:(tile + 1) * LANES]
        ref[tile, k, 8:8 + rows, :] = part
        ref[tile, k, 7:8, :] = part[rows - 1:rows]
        ref[tile, k, 8 + rows:9 + rows, :] = part[0:1]


def rows_of(ref, k, first):
    here = pl.ds(first, ref.shape[2] - 16)
    return jnp.concatenate([ref[tile, k, here, :] for tile in range(ref.shape[0])], axis=1)


def apply_padded(ref, k, origin):
    centre = rows_of(ref, k, 8)
    lanes = centre.shape[1]
    beside = rows_of(ref, k, origin - 1) + rows_of(ref, k, origin + 1)
    beside = beside + (pltpu.roll(centre, 1, 1) + pltpu.roll(centre, lanes - 1, 1))
    if k > 0:
        beside = beside + rows_of(ref, k - 1, 8)
    if k < ref.shape[1] - 1:
        beside = beside + rows_of(ref, k + 1, 8)
    return 6.0 * centre - beside


def wrapped_mask(shape, sizes, low, high):
    keep = None
    for dim, size in sizes.items():
        at = signed(iota(shape, dim), size, shape[dim])
        good = ((at >= 0) | low[dim]) & ((at < size) | high[dim])
        keep = good if keep is None else keep & good
    return jnp.where(keep, 1.0, 0.0).astype(F32)


def side(index, flip):
    if flip == 1:
        return (index & 1) == 0, None
    return index < 2, (index == 1) | (index == 2)


def place(axis, count):
    index = lax.axis_index(axis)
    return index, index > 0, index < count - 1


def only(keep, v):
    return jnp.where(keep, v, 0.0)


def shifted(v, lanes):
    lanes = lanes % LANES
    return v if lanes == 0 else pltpu.roll(v, lanes, 1)


def lanes_of(v, first, count):
    lane = iota(v.shape, 1)
    last = first + count
    if last <= LANES:
        return (lane >= first) & (lane < last)
    return (lane >= first) | (lane < last - LANES)


def moved(v, first, count, to):
    first = first % LANES
    return shifted(only(lanes_of(v, first, count), v), to - first)


def landed(v, first, count, to):
    to = to % LANES
    v = shifted(v, to - first)
    return only(lanes_of(v, to, count), v)


def side_pack(tile, slot):
    return moved(tile, LANES - 3, 6, 6 * slot)


def side_unpack(packed, slot):
    return landed(packed, 6 * slot, 6, LANES - 3)


def slab_layers(r_ref, x_ref, up, low, high):
    start = jnp.where(up, high[0], low[0])
    start_x = jnp.where(up, high[1], low[1])
    return [(r_ref, start + j) for j in range(5)] + [(x_ref, start_x + j) for j in range(2)]


def slab_own(r_ref, x_ref, up):
    ez = r_ref.shape[0]
    return slab_layers(r_ref, x_ref, up, (0, 1), (ez - 5, ez - 3))


def slab_there(r_ref, x_ref, up):
    ez = r_ref.shape[0]
    return slab_layers(r_ref, x_ref, up, (1, 3), (ez - 6, ez - 5))


def slab_emit(r_ref, x_ref, out, up):
    ex = r_ref.shape[1]
    lat = None
    for j, (ref, k) in enumerate(slab_own(r_ref, x_ref, up)):
        v = ref[k]
        out[j * ex:(j + 1) * ex, :] = v[:, 0:LANES]
        part = side_pack(v[:, LANES:], j)
        lat = part if lat is None else lat + part
    out[7 * ex:8 * ex, :] = lat


def slab_add(r_ref, x_ref, slab, up):
    ex = r_ref.shape[1]
    lat = slab[7 * ex:8 * ex, :]
    for j, (ref, k) in enumerate(slab_there(r_ref, x_ref, up)):
        ref[k, :, 0:LANES] += slab[j * ex:(j + 1) * ex, :]
        ref[k, :, LANES:] += side_unpack(lat, j)


BESIDE = ((2, 2, 0, 0), (1, 1, 0, 3), (3, 1, 0, 5), (5, 1, 1, 0), (6, 1, 1, 3))


def beside(tile, count):
    row = iota(tile.shape, 0)
    return only((row < count) | (row >= 8 - count), tile)


def thin_emit(r_ref, x_ref, out, up):
    bx = r_ref.shape[1] - 8
    layers = slab_own(r_ref, x_ref, up)
    lat = None
    for j, (ref, k) in enumerate(layers):
        out[j * bx:(j + 1) * bx, :] = ref[k, 0:bx, 0:LANES]
        part = side_pack(ref[k, 0:bx, LANES:], j)
        lat = part if lat is None else lat + part
    tiles = [None, None]
    for j, count, which, turn in BESIDE:
        ref, k = layers[j]
        part = beside(ref[k, bx:, 0:LANES], count)
        part = pltpu.roll(part, turn, 0) if turn else part
        tiles[which] = part if tiles[which] is None else tiles[which] + part
    at = 7 * bx
    out[at:at + 8, :] = tiles[0]
    out[at + 8:at + 16, :] = tiles[1]
    out[at + 16:at + 16 + bx, :] = lat
    for j in (1, 2, 3):
        ref, k = layers[j]
        out[at + 16:at + 24, :] += side_pack(ref[k, bx:, LANES:], 6 + j)


def thin_add(r_ref, x_ref, slab, up):
    bx = r_ref.shape[1] - 8
    layers = slab_there(r_ref, x_ref, up)
    at = 7 * bx
    lat = slab[at + 16:at + 16 + bx, :]
    for j, (ref, k) in enumerate(layers):
        ref[k, 0:bx, 0:LANES] += slab[j * bx:(j + 1) * bx, :]
        ref[k, 0:bx, LANES:] += side_unpack(lat, j)
    for j, count, which, turn in BESIDE:
        ref, k = layers[j]
        tile = slab[at + 8 * which:at + 8 * which + 8, :]
        tile = pltpu.roll(tile, 8 - turn, 0) if turn else tile
        ref[k, bx:, 0:LANES] += beside(tile, count)
    for j in (1, 2, 3):
        ref, k = layers[j]
        ref[k, bx:, LANES:] += side_unpack(lat[0:8], 6 + j)


def rows_out(r, x, up):
    bx = r.shape[0] - 8
    row = iota((8, r.shape[1]), 0)
    first, last, spill = r[0:8], r[bx - 8:bx], r[bx:]
    to_high = pltpu.roll(jnp.where(row >= 6, last, spill), 2, 0)
    to_low = pltpu.roll(jnp.where(row >= 5, spill, first), 3, 0)
    out = jnp.where(up, to_high, to_low)
    if x is None:
        return only(row < 5, out)
    spill = x[bx:]
    extra = jnp.where(up, pltpu.roll(spill, 5, 0), pltpu.roll(spill, 7, 0))
    return jnp.where(row < 5, out, only(row < 7, extra))


def rows_in(r_ref, x_ref, k, rows, up):
    bx = r_ref.shape[1] - 8
    row = iota(rows.shape, 0)
    high, low = pltpu.roll(rows, 5, 0), pltpu.roll(rows, 6, 0)
    r_ref[k, 0:8] += only(jnp.logical_not(up) & (row < 3), low)
    r_ref[k, bx - 8:bx] += only(up & (row >= 5), high)
    r_ref[k, bx:] += jnp.where(up, only(row < 2, high), only(row >= 6, low))
    if x_ref is not None:
        x_ref[k, 0:8] += only(jnp.logical_not(up) & (row < 2), pltpu.roll(rows, 3, 0))
        x_ref[k, bx - 8:bx] += only(up & (row >= 6), pltpu.roll(rows, 1, 0))


def rows_emit(r_ref, x_ref, out, up):
    ez = r_ref.shape[0]
    row = iota((8, LANES), 0)
    lat = jnp.zeros((8, LANES), F32)
    for t, k in enumerate(range(1, ez - 1)):
        far = {1: 0, ez - 2: ez - 1}.get(k)
        rows = rows_out(r_ref[k], None if far is not None else x_ref[k], up)
        tile = rows[:, 0:LANES]
        if far is not None:
            more = rows_out(r_ref[far, :, 0:LANES], None, up)
            more = jnp.where(up, pltpu.roll(more, 5, 0), pltpu.roll(more, 2, 0))
            tile = jnp.where((row == 5) | (row == 6), more, tile)
        out[8 * t:8 * t + 8, :] = tile
        lat = lat + side_pack(rows[:, LANES:], t)
    at = 8 * (ez - 2)
    out[at:at + 8, :] = lat


def rows_add(r_ref, x_ref, slab, up):
    ez = r_ref.shape[0]
    at = 8 * (ez - 2)
    lat = slab[at:at + 8, :]
    row = iota((8, LANES), 0)
    for t, k in enumerate(range(1, ez - 1)):
        far = {1: 0, ez - 2: ez - 1}.get(k)
        tile = slab[8 * t:8 * t + 8, :]
        rows = jnp.concatenate([tile, side_unpack(lat, t)], axis=1)
        rows_in(r_ref, None if far is not None else x_ref, k, rows, up)
        if far is not None:
            tile = only((row == 5) | (row == 6), tile)
            tile = jnp.where(up, pltpu.roll(tile, 6, 0), pltpu.roll(tile, 3, 0))
            rows = jnp.concatenate([tile, jnp.zeros((8, LANES), F32)], axis=1)
            rows_in(r_ref, None, far, rows, up)


class Plan:
    def first_layer(self, iz):
        start = iz * (self.block[0] // 2) - 4
        return jnp.clip(start, 0, self.level1[0] - self.window[0])

    def __init__(self, shape, peers):
        self.peers = peers
        self.block = bz, bx, by = shape
        self.ext = self.ez, self.ex, self.ey = bz + 6, bx + 8, by + LANES
        self.rows, self.pairs = bx // 2, bz // 4 + 2
        self.lat_at = self.pairs * (self.rows + 4)
        self.coarse = self.lat_at + 8
        self.slab = 8 * self.ex
        self.slab_z = 8 * bx + 16
        self.slab_x = 8 * (bz + 5)
        self.corner = 6 * 8
        self.layers = bz + 4
        self.level1 = (peers[0] * bz // 2, peers[1] * bx // 2, LANES)
        self.level2 = (peers[0] * bz // 4, peers[1] * bx // 4, peers[2] * by // 4)
        self.inner = [0, 1] + [2] * bz + [1, 0]
        self.slots, at = [], 0
        for count in self.inner:
            self.slots.append(at)
            at += 3 + count + (2 if count == 2 else 0)
        assert at <= LANES
        self.fine_rows = self.ex
        self.window = (bz // 2 + 8, self.level1[1], LANES)
        self.edge = self.fine_rows + self.window[0] * self.window[1] // 8
        self.wide2 = by // 4 + 4
        self.fold = LANES // self.wide2
        self.lines2 = -(-self.level2[0] // self.fold)
        self.share = self.lines2 * self.level2[1]


def first_kernel(plan, both, r_ref, x_ref, pay_z, pay_x, pay_d, d_one, d_two, pairs, lines):
    p_ext, b_ext = both.at[0], both.at[1]
    bz, bx, by = plan.block
    ez, ex, ey = plan.ext
    peers = plan.peers
    iz, z_low, z_high = place("gz", peers[0])
    ix, x_low, x_high = place("gx", peers[1])
    _, y_low, y_high = place("gy", peers[2])
    flat = wrapped_mask((ex, ey), {0: bx, 1: by}, (x_low, y_low), (x_high, y_high))
    below = jnp.where(z_low, 1.0, 0.0).astype(F32)
    above = jnp.where(z_high, 1.0, 0.0).astype(F32)

    def masked(k, v):
        v = v * flat
        if k < 3:
            v = v * below
        if k >= 3 + bz:
            v = v * above
        return v

    zero = jnp.zeros((ex, ey), F32)
    origin = 8 + (iz >> 8)
    for k in range(ez):
        if 2 <= k < ez - 2:
            r = b_ext[k] - apply_at(p_ext, k)
            r_ref[k] = r
            put(d_one, k, masked(k, r * first_scale))
        elif 1 <= k < ez - 1:
            put(d_one, k, zero)
    for k in range(ez):
        if 1 <= k < ez - 1:
            if 2 <= k < ez - 2:
                r = r_ref[k] - apply_padded(d_one, k, origin)
                d = carry_coef * rows_of(d_one, k, 8) + fresh_coef * r
            else:
                inward = k + 1 if k == 1 else k - 1
                r = rows_of(d_one, inward, 8)
                d = fresh_coef * r
            r_ref[k] = r
            put(d_two, k, masked(k, d))
    for k in range(ez):
        if 1 <= k < ez - 1:
            part = rows_of(d_two, k, 8)
            beside = rows_of(d_two, k, origin - 1) + rows_of(d_two, k, origin + 1)
            beside = beside + (pltpu.roll(part, 1, 1) + pltpu.roll(part, ey - 1, 1))
            if k > 1:
                beside = beside + rows_of(d_two, k - 1, 8)
            if k < ez - 2:
                beside = beside + rows_of(d_two, k + 1, 8)
            r_ref[k] = masked(k, r_ref[k] - (6.0 * part - beside))
            x_ref[k] = p_ext[k] + (rows_of(d_one, k, 8) + part)
        else:
            r_ref[k] = masked(k, rows_of(d_two, 1 if k == 0 else ez - 2, 8))
            x_ref[k] = zero

    coarse_z, rows = 2 * plan.pairs, plan.rows
    for zc in range(coarse_z):
        low, high = 2 * zc - 1, 2 * zc
        if low < 0:
            total = r_ref[high]
        elif high >= ez:
            total = r_ref[low]
        else:
            total = r_ref[low] + r_ref[high]
        base = zc * ex
        for tile in range(ey // LANES):
            here = slice(tile * LANES, (tile + 1) * LANES)
            pairs[tile, base:base + ex, :] = total[:, here]
            even = pairs.at[tile][pl.ds(base, ex // 2, 2), :]
            odd = pairs.at[tile][pl.ds(base + 1, ex // 2, 2), :]
            sums = even + odd
            at = zc // 2 * rows
            at += zc % 2 * plan.lat_at
            lines[at:at + rows, here] = sums[0:rows]
            at = plan.pairs * rows + zc // 2 * 4 + zc % 2 * plan.lat_at
            lines[at:at + 4, here] = sums[rows:rows + 4]
    fine = signed(iota((ey, LANES), 0), by, ey)
    coarse = signed(iota((ey, LANES), 1), by // 2, LANES)
    table = as_table((fine >> 1) == coarse, 0.5)
    out = right_dot(lines[...], table)
    even, odd = out[0:plan.lat_at], out[plan.lat_at:]
    lane = iota(even.shape, 1)
    main = jnp.where(lane < LANES // 2, even, shifted(odd, LANES // 2))
    own_lat = spill_lat = None
    row = iota((8, LANES), 0)
    for zc in range(coarse_z):
        source = (even, odd)[zc % 2]
        base = zc // 2 * rows
        tile = source[base:base + rows]
        part = moved(tile, by // 2, 2, 4 * zc) + moved(tile, LANES - 2, 2, 4 * zc + 2)
        own_lat = part if own_lat is None else own_lat + part
        base = plan.pairs * rows + zc // 4 * 8
        tile = source[base:base + 8]
        if zc // 2 % 2:
            tile = pltpu.roll(tile, 4, 0)
        tile = only(row < 4, tile)
        slot = LANES // 2 + 4 * zc
        part = moved(tile, by // 2, 2, slot) + moved(tile, LANES - 2, 2, slot + 2)
        spill_lat = part if spill_lat is None else spill_lat + part
    for pay, at in ((pay_z, plan.slab_z), (pay_x, plan.slab_x), (pay_d, plan.corner)):
        pay[at:at + plan.lat_at, :] = main
        pay[at + plan.lat_at:at + plan.coarse, :] = own_lat + spill_lat

    up_z, _ = side(iz, 3)
    up_x, _ = side(ix, 1)
    thin_emit(r_ref, x_ref, pay_z, up_z)
    rows_emit(r_ref, x_ref, pay_x, up_x)
    lat = jnp.zeros((8, LANES), F32)
    start = jnp.where(up_z, ez - 5, 0)
    for j in range(5):
        out = rows_out(r_ref[start + j], x_ref[start + j] if j == 2 else None, up_x)
        pay_d[8 * j:8 * j + 8, :] = out[:, 0:LANES]
        lat = lat + side_pack(out[:, LANES:], j)
    pay_d[40:48, :] = lat


def chip_kernel(plan, r_in, x_in, from_z, from_x, from_d, r_ref, x_ref, pay):
    ez, ex, ey = plan.ext
    iz, _, _ = place("gz", plan.peers[0])
    ix, _, _ = place("gx", plan.peers[1])
    up_z, near = side(iz, 3)
    up_x, _ = side(ix, 1)
    for k in range(ez):
        r_ref[k] = r_in[k]
        x_ref[k] = x_in[k]
    rows_add(r_ref, x_ref, from_x, up_x)

    @pl.when(near)
    def _():
        thin_add(r_ref, x_ref, from_z, up_z)
        start = jnp.where(up_z, ez - 6, 1)
        lat = from_d[40:48, :]
        for j in range(5):
            rows = from_d[8 * j:8 * j + 8, :]
            rows = jnp.concatenate([rows, side_unpack(lat, j)], axis=1)
            rows_in(r_ref, x_ref if j == 2 else None, start + j, rows, up_x)

    slab_emit(r_ref, x_ref, pay, side(iz, 1)[0])


def plane_kernel(plan, r_in, x_in, ours, theirs, r_ref, x_ref, r1_ref, x1_ref, pay, later, share,
                 r_all, x_all, b1, d1, d2, r1, x1, pairs, lines):
    bz, bx, by = plan.block
    ez, ex, ey = plan.ext
    layers = plan.layers
    iz, _, _ = place("gz", plan.peers[0])
    ix, _, _ = place("gx", plan.peers[1])
    iy, y_low, y_high = place("gy", plan.peers[2])
    up_z, _ = side(iz, 1)
    for k in range(ez):
        r_all[k] = r_in[k]
        x_all[k] = x_in[k]
    slab_add(r_all, x_all, theirs, up_z)
    for k in range(layers):
        r_ref[k] = r_all[k + 1]
    for k in range(bz):
        x_ref[k] = x_all[k + 3, 0:bx, 0:by]

    up, _ = side(iy, 1)
    up_inner, _ = side(iy, 3)
    high, low = jnp.zeros((ex, LANES), F32), jnp.zeros((ex, LANES), F32)
    for k in range(layers):
        slot, inner = plan.slots[k], plan.inner[k]
        count = 3 + inner
        v, spill = r_all[k + 1, :, 0:by], r_all[k + 1, :, by:ey]
        high = high + moved(jnp.where(lanes_of(v, 0, 3), spill, v), LANES - inner, count, slot)
        mixed = jnp.where(lanes_of(v, 0, 2), v, spill)
        low = low + moved(mixed, LANES - 3, count, slot)
        if inner == 2:
            spill = x_all[k + 1, :, by:ey]
            high = high + moved(spill, 0, 2, slot + count)
            low = low + moved(spill, LANES - 2, 2, slot + count)
    pay[0:ex, :] = jnp.where(up, high, low)
    later[0:ex, :] = jnp.where(up_inner, high, low)

    nz1, nx1, _ = plan.level1
    rows, half = plan.rows, by // 2
    for k in range(nz1):
        b1[k] = jnp.zeros((nx1, LANES), F32)
    row = iota((8, LANES), 0)
    for j in range(plan.peers[0]):
        for i in range(plan.peers[1]):
            flip = iz ^ j
            other = ((flip ^ (flip >> 1)) & 1) == 1
            chip = (flip >> 1) + 2 * (ix ^ i)
            at = pl.multiple_of(plan.slab + chip * plan.coarse, 8)

            def rows_at(offset, count):
                here = pl.ds(pl.multiple_of(at + offset, 8), count)
                return jnp.where(other, theirs[here, :], ours[here, :])

            lat = rows_at(plan.lat_at, 8)
            for zp in range(plan.pairs):
                own = rows_at(zp * rows, rows)
                if zp % 2 == 0:
                    spill_two = rows_at(plan.pairs * rows + zp * 4, 8)
                spill = spill_two if zp % 2 == 0 else pltpu.roll(spill_two, 4, 0)
                for part in range(2):
                    zc = 2 * zp + part
                    k = j * (bz // 2) + zc - 2
                    if not 0 <= k < nz1:
                        continue

                    def wide(main, slot):
                        return (
                            landed(main, part * half, half, 0)
                            + landed(lat, slot, 2, half) + landed(lat, slot + 2, 2, LANES - 2)
                        )

                    b1[k, i * rows:(i + 1) * rows, :] += wide(own, 4 * zc)
                    v = wide(spill, LANES // 2 + 4 * zc)
                    if i + 1 < plan.peers[1]:
                        at_row = (i + 1) * rows
                        b1[k, at_row:at_row + 8, :] += only(row < 2, v)
                    if i > 0:
                        at_row = i * rows - 8
                        b1[k, at_row:at_row + 8, :] += only(row >= 6, pltpu.roll(v, 4, 0))

    lateral1 = level_lateral((nx1, LANES))
    keep = wrapped_mask((nx1, LANES), {1: half}, (None, y_low), (None, y_high))
    for k in range(nz1):
        d1[k] = b1[k] * first_scale
    for k in range(nz1):
        r = b1[k] - apply_at(d1, k, lateral1)
        r1[k] = r
        d2[k] = keep * (carry_coef * d1[k] + fresh_coef * r)
    for k in range(nz1):
        r1[k] = keep * (r1[k] - apply_at(d2, k, lateral1))
        x1[k] = d1[k] + d2[k]

    nz2, nx2, _ = plan.level2
    for zc in range(nz2):
        pairs[zc * nx1:(zc + 1) * nx1, :] = r1[2 * zc] + r1[2 * zc + 1]
        part, at = divmod(zc, plan.lines2)
        lines[at * nx2:(at + 1) * nx2, part * LANES:(part + 1) * LANES] = (
            pairs[pl.ds(zc * nx1, nx2, 2), :] + pairs[pl.ds(zc * nx1 + 1, nx2, 2), :]
        )
    shape = (plan.fold * LANES, LANES)
    fine, coarse = iota(shape, 0), iota(shape, 1)
    part, fine = fine // LANES, signed(fine % LANES, half, LANES)
    coarse = coarse - part * plan.wide2 - 2
    near = (coarse >= -2) & (coarse < plan.wide2 - 2)
    for part in range(plan.fold):
        count = min(plan.lines2, nz2 - part * plan.lines2) * nx2
        if count < plan.share:
            here = slice(part * LANES, (part + 1) * LANES)
            lines[count:, here] = jnp.zeros((plan.share - count, LANES), F32)
    total = right_dot(lines[...], as_table(near & ((fine >> 1) == coarse), 0.5))
    share[...] = total
    pay[plan.edge:plan.edge + plan.share, :] = total
    later[plan.edge:plan.edge + plan.share, :] = total

    start = plan.first_layer(iz)
    for k in range(plan.window[0]):
        r1_ref[k] = r1[start + k]
        x1_ref[k] = x1[start + k]
    per_tile = LANES // 16
    for group in range(plan.window[0] // per_tile):
        tiles = []
        for which in range(2):
            total = jnp.zeros((nx1, LANES), F32)
            for j in range(per_tile):
                k = group * per_tile + j
                first = half - 3 if which == 0 else LANES - 4
                total = total + moved(r1_ref[k], first, 7, 16 * j)
                first = half - 2 if which == 0 else LANES - 3
                total = total + moved(x1_ref[k], first, 5, 16 * j + 7)
            tiles.append(total)
        here = slice(plan.fine_rows + group * nx1, plan.fine_rows + (group + 1) * nx1)
        pay[here, :] = jnp.where(up, tiles[0], tiles[1])
        later[here, :] = jnp.where(up_inner, tiles[0], tiles[1])


def level_lateral(shape):
    row = iota(shape, 0)
    not_first = jnp.where(row > 0, 1.0, 0.0).astype(F32)
    not_last = jnp.where(row < shape[0] - 1, 1.0, 0.0).astype(F32)

    def beside(v):
        return (
            not_first * pltpu.roll(v, 1, 0) + not_last * pltpu.roll(v, shape[0] - 1, 0)
            + pltpu.roll(v, 1, 1) + pltpu.roll(v, LANES - 1, 1)
        )

    return beside


def small_cycle(level, source):
    step = 1 << (level - 2)
    row, lane = iota((8, LANES), 0), iota((8, LANES), 1)
    count = len(source)
    shifts = []
    if step < 8:
        shifts += [(step, 0, row >= step), (8 - step, 0, row < 8 - step)]
    shifts += [(step, 1, lane >= step), (LANES - step, 1, lane < LANES - step)]

    def op(v):
        out = []
        for k in range(count):
            beside = None
            for shift, dim, keep in shifts:
                part = only(keep, pltpu.roll(v[k], shift, dim))
                beside = part if beside is None else beside + part
            if k > 0:
                beside = beside + v[k - 1]
            if k < count - 1:
                beside = beside + v[k + 1]
            out.append(6.0 * v[k] - beside)
        return out

    def moves(v, dim, places):
        size, shift = v.shape[dim], places * step
        if abs(shift) >= size:
            return jnp.zeros_like(v)
        index = row if dim == 0 else lane
        keep = index < size - shift if shift > 0 else index >= -shift
        return only(keep, pltpu.roll(v, -shift % size, dim))

    def at(values, k):
        return values[k] if 0 <= k < len(values) else None

    def added(*terms):
        total = None
        for term in terms:
            if term is not None:
                total = term if total is None else total + term
        return total

    d = [first_scale * v for v in source]
    before = [b - t for b, t in zip(source, op(d))]
    d2 = [carry_coef * v + fresh_coef * t for v, t in zip(d, before)]
    x = [v + t for v, t in zip(d, d2)]
    r = [v - t for v, t in zip(before, op(d2))]
    coarsest = None
    if level < LEVELS - 1:
        keep = only((row % (2 * step) == 0) & (lane % (2 * step) == 0), 0.5)
        coarse = []
        for k in range(0, count, 2):
            v = d2[k] + d2[k + 1]
            beyond = added(at(d2, k - 1), at(d2, k + 2))
            rest = before[k] + before[k + 1] - 5.0 * v
            rest = rest if beyond is None else rest + beyond
            along = [
                v + moves(v, dim, 1) + (moves(v, dim, -1) + moves(v, dim, 2)) for dim in range(2)
            ]
            first = rest + moves(rest, 0, 1) + along[0]
            coarse.append(keep * (
                first + moves(first, 1, 1) + (along[1] + moves(along[1], 0, 1))
            ))
        coarse, coarsest = small_cycle(level + 1, coarse)
        e, beside = [], []
        for v in coarse:
            back = [moves(v, dim, -1) for dim in range(2)]
            wide = v + back[0]
            e.append(wide + moves(wide, 1, -1))
            along = [
                v + back[dim] + (moves(v, dim, 1) + moves(v, dim, -2)) for dim in range(2)
            ]
            beside.append(
                along[0] + moves(along[0], 1, -1) + (along[1] + moves(along[1], 0, -1))
            )
        for k in range(count):
            own = e[k // 2]
            change = 5.0 * own - beside[k // 2]
            beyond = at(e, k // 2 + (1 if k % 2 else -1))
            if beyond is not None:
                change = change - beyond
            x[k] = x[k] + own
            r[k] = r[k] - change
    d = [first_scale * v for v in r]
    r = [v - t for v, t in zip(r, op(d))]
    x = [v + (t + (carry_coef * t + fresh_coef * u)) for v, t, u in zip(x, d, r)]
    return x, (x if level == LEVELS - 1 else coarsest)


def last_kernel(plan, r_in, x_in, r1_in, x1_in, ours, from_a, from_b, from_c, p_out, res_out, last_ref, *scratch):
    shares, p_ref, res_ref, r, q1, e1, e0, d0, d1, r1, lines, wide, sem = scratch
    bz, bx, by = plan.block
    ez, ex, ey = plan.ext
    nz1, nx1, _ = plan.window
    nz2, nx2, _ = plan.level2
    layers, half = plan.layers, by // 2
    iz, z_low, z_high = place("gz", plan.peers[0])
    ix, x_low, x_high = place("gx", plan.peers[1])
    iy, y_low, y_high = place("gy", plan.peers[2])

    shares[0] = ours[...]
    shares[1] = from_a[plan.edge:plan.edge + plan.share, :]
    shares[3] = from_b[plan.edge:plan.edge + plan.share, :]
    shares[2] = from_c[...]
    own2 = half // 2
    source = []
    for part in range(plan.fold):
        total = None
        for j in range(plan.peers[2]):
            v = moved(shares[iy ^ j], part * plan.wide2, plan.wide2, own2 * j - 2)
            total = v if total is None else total + v
        source += [total[nx2 * k:nx2 * (k + 1)] for k in range(plan.lines2)]
    source = source[:nz2]
    e2, coarsest = small_cycle(2, source)
    for k in range(nz2):
        lines[k * nx2:(k + 1) * nx2, :] = e2[k]
    thin = as_table(iota((LANES, LANES), 0) == 8 * iota((LANES, LANES), 1))
    for k in range(last_ref.shape[0]):
        last_ref[k] = right_dot(coarsest[k], thin)[0:1, 0:last_ref.shape[2]]

    up_a, _ = side(iy, 1)
    _, near_b = side(iy, 3)

    def sent(rows):
        a, b = from_a[rows[0]:rows[1], :], only(near_b, from_b[rows[0]:rows[1], :])
        return jnp.where(up_a, a, b), jnp.where(up_a, b, a)

    fine = signed(iota((LANES, LANES), 1), half, LANES)
    coarse = iota((LANES, LANES), 0) - iy * own2
    start = plan.first_layer(iz)
    here = pl.ds(pl.multiple_of(start // 2 * nx2, 8), nz1 // 2 * nx2)
    e2 = right_dot(lines[here, :], as_table((fine >> 1) == coarse))
    for zc in range(nz1 // 2):
        v = e2[zc * nx2:(zc + 1) * nx2]
        for part in range(2):
            q1.at[2 * zc + part][pl.ds(0, nx2, 2), :] = v
            q1.at[2 * zc + part][pl.ds(1, nx2, 2), :] = v
    per_tile = LANES // 16
    lateral1 = level_lateral((nx1, LANES))
    keep = wrapped_mask((nx1, LANES), {1: half}, (None, y_low), (None, y_high))
    for group in range(nz1 // per_tile):
        at = plan.fine_rows + group * nx1
        high, low = sent((at, at + nx1))
        for j in range(per_tile):
            k = group * per_tile + j
            s = 16 * j
            r1[k] = (
                r1_in[k] + landed(high, s, 7, half - 4) + landed(low, s, 7, LANES - 3)
                - apply_at(q1, k, lateral1)
            )
            e1[k + 2, 8:8 + nx1, :] = (
                x1_in[k] + q1[k]
                + landed(high, s + 7, 5, half - 3) + landed(low, s + 7, 5, LANES - 2)
            )
    for k in range(nz1):
        d1[k] = keep * (r1[k] * first_scale)
    nothing = jnp.zeros((8, LANES), F32)
    for k in range(nz1 + 4):
        e1[k, 0:8, :] = nothing
        e1[k, 8 + nx1:16 + nx1, :] = nothing
        if not 2 <= k < nz1 + 2:
            e1[k, 8:8 + nx1, :] = jnp.zeros((nx1, LANES), F32)
    for k in range(nz1):
        v = r1[k] - apply_at(d1, k, lateral1)
        e1[k + 2, 8:8 + nx1, :] += d1[k] + keep * (carry_coef * d1[k] + fresh_coef * v)

    coarse = signed(iota((LANES, ey), 0), half, LANES)
    fine = signed(iota((LANES, ey), 1), by, ey)
    double = as_table((fine >> 1) == coarse)
    half_z, half_x = bz // 2, bx // 2
    for zc in range(half_z + 4):
        here = pl.ds(pl.multiple_of(ix * half_x, 8), half_x + 16)
        v = e1[iz * half_z - start + zc, here, :]
        own, low, high = v[8:8 + half_x], v[0:8], v[8 + half_x:16 + half_x]
        at = zc * ex
        wide[pl.ds(at, half_x, 2), :] = own
        wide[pl.ds(at + 1, half_x, 2), :] = own
        for j in range(2):
            for twin in range(2):
                row = at + bx + 2 * j + twin
                wide[row:row + 1, :] = high[j:j + 1]
                row = at + ex - 4 + 2 * j + twin
                wide[row:row + 1, :] = low[6 + j:7 + j]
    origin = 8 + (iz >> 8)
    for zc in range(half_z + 4):
        v = right_dots(wide[zc * ex:(zc + 1) * ex, :], double)
        for k in (2 * zc - 1, 2 * zc):
            if 0 <= k < ez:
                put(e0, k, v)
    flat = wrapped_mask((ex, ey), {0: bx, 1: by}, (x_low, y_low), (x_high, y_high))
    below = jnp.where(z_low, 1.0, 0.0).astype(F32)
    above = jnp.where(z_high, 1.0, 0.0).astype(F32)

    def masked(k, v):
        v = v * flat
        if k < 3:
            v = v * below
        if k >= 3 + bz:
            v = v * above
        return v

    high, low = sent((0, ex))
    for k in range(layers):
        s, inner = plan.slots[k], plan.inner[k]
        v = r_in[k] - apply_padded(e0, k + 1, origin)
        own = v[:, 0:by] + landed(high, s, 3, LANES - 3) + landed(low, s + inner, 3, 0)
        spill = v[:, by:ey]
        if inner:
            spill = spill + landed(high, s + 3, inner, 0) + landed(low, s, inner, LANES - inner)
        r[k, :, 0:by] = own
        r[k, :, by:ey] = spill
        put(d0, k, masked(k + 1, r[k] * first_scale))
        if inner == 2:
            s = s + 3 + inner
            p_ref[k - 2] = (
                x_in[k - 2] + e0[0, k + 1, 8:8 + bx, :]
                + (landed(high, s, 2, LANES - 2) + landed(low, s, 2, 0))[0:bx]
            )
    for k in range(1, layers - 1):
        v = r[k] - apply_padded(d0, k, origin)
        r[k] = v
        d = rows_of(d0, k, 8)
        v = masked(k + 1, carry_coef * d + fresh_coef * v)
        put(e0, k, v)
        if 2 <= k < 2 + bz:
            p_ref[k - 2] += d[0:bx, 0:by] + v[0:bx, 0:by]
    copy = pltpu.make_async_copy(p_ref, p_out, sem.at[0])
    copy.start()
    copies = [copy]
    parts = 2
    for part in range(parts):
        here = range(part * bz // parts, (part + 1) * bz // parts)
        for j in here:
            v = r[j + 2] - apply_padded(e0, j + 2, origin)
            res_ref[j] = v[0:bx, 0:by]
        here = pl.ds(here[0], bz // parts)
        copy = pltpu.make_async_copy(res_ref.at[here], res_out.at[here], sem.at[1 + part])
        copy.start()
        copies.append(copy)
    for copy in copies:
        copy.wait()


def whole(shape):
    return jax.ShapeDtypeStruct(shape, F32)


VMEM = pl.BlockSpec(memory_space=pltpu.VMEM)
ANY = pl.BlockSpec(memory_space=pl.ANY)
VMEM_BYTES = 24 << 20


def run(kernel, plan, outs, scratch, *operands, out_specs=None, semaphores=0):
    scratch = [pltpu.VMEM(s, F32) for s in scratch]
    if semaphores:
        scratch.append(pltpu.SemaphoreType.DMA((semaphores,)))
    return pl.pallas_call(
        functools.partial(kernel, plan),
        out_shape=[whole(s) for s in outs],
        in_specs=[VMEM] * len(operands),
        out_specs=out_specs or [VMEM] * len(outs),
        scratch_shapes=scratch,
        compiler_params=pltpu.CompilerParams(vmem_limit_bytes=VMEM_BYTES),
    )(*operands)


def swap(values, partner):
    axes = ("gx", "gy", "gz")
    counts = [lax.axis_size(a) for a in axes]
    pairs = []
    for i in range(counts[0] * counts[1] * counts[2]):
        to = partner(i // (counts[1] * counts[2]), i // counts[2] % counts[1], i % counts[2])
        if to is not None:
            pairs.append((i, (to[0] * counts[1] + to[1]) * counts[2] + to[2]))
    return lax.ppermute(values, axes, pairs)


def body_fast(divergence, pressure_prev):
    plan = Plan(divergence.shape, tuple(lax.axis_size(a) for a in ("gz", "gx", "gy")))
    ext, level1 = plan.ext, plan.level1
    window, layers = plan.window, (plan.layers, plan.ex, plan.ey)
    payload = [(n + plan.coarse, LANES) for n in (plan.slab_z, plan.slab_x, plan.corner)]
    both = jnp.stack([pressure_prev, divergence])
    both = jnp.pad(both, ((0, 0), (3, 3), (0, plan.ex - plan.block[1]), (0, plan.ey - plan.block[2])))
    r, x, pay_z, pay_x, pay_d = run(
        first_kernel, plan, [ext, ext] + payload,
        [padded(plan), padded(plan), (2, 2 * plan.pairs * plan.ex, LANES),
         (2 * plan.lat_at, plan.ey)],
        both,
    )
    from_z = swap(pay_z, lambda x, y, z: (x, y, z ^ 3))
    from_x = swap(pay_x, lambda x, y, z: (x ^ 1, y, z))
    from_d = swap(pay_d, lambda x, y, z: (x ^ 1, y, z ^ 3))
    r, x, slab = run(
        chip_kernel, plan, [ext, ext, (plan.slab, LANES)], [], r, x, from_z, from_x, from_d
    )
    ours = jnp.concatenate([
        slab, pay_z[plan.slab_z:], from_z[plan.slab_z:], from_x[plan.slab_x:], from_d[plan.corner:]
    ], axis=0)
    got = swap(ours, lambda x, y, z: (x, y, z ^ 1))
    nz2, nx2, _ = plan.level2
    share = (plan.share, LANES)
    r, x, r1, x1, now, later, ours = run(
        plane_kernel, plan,
        [layers, plan.block, window, window, (plan.edge + plan.share, LANES),
         (plan.edge + plan.share, LANES), share],
        [ext, ext, level1, level1, level1, level1, level1, (nz2 * level1[1], LANES),
         (plan.share, plan.fold * LANES)],
        r, x, ours, got,
    )
    from_a = swap(now, lambda x, y, z: (x, y ^ 1, z))
    from_b = swap(later, lambda x, y, z: (x, y ^ 3, z))
    from_c = swap(ours, lambda x, y, z: (x, y ^ 2, z))
    return run(
        last_kernel, plan,
        [plan.block, plan.block, tuple(n >> 3 for n in plan.level2)],
        [(4,) + share, plan.block, plan.block, layers, window,
         (window[0] + 4, window[1] + 16, LANES), padded(plan), padded(plan), window, window,
         (nz2 * nx2, LANES), (2 * plan.pairs * plan.ex, LANES)],
        r, x, r1, x1, ours, from_a, from_b, from_c,
        out_specs=[ANY, ANY, VMEM], semaphores=3,
    )


def fits_fast(shape, peers):
    bz, bx, by = shape
    nz, nx, ny = peers
    return (
        nz == 4 and nx == 2 and ny == 4 and bz == 16 and by == LANES
        and nx * bx == 4 * 8 and ny * by == 4 * LANES
    )


def body(divergence, pressure_prev):
    peers = tuple(lax.axis_size(a) for a in ("gz", "gx", "gy"))
    if fits_fast(divergence.shape, peers):
        return tuple(body_fast(divergence, pressure_prev))
    return body_levels(divergence, pressure_prev)


def solution(mesh):
    in_specs = (P("gz", "gx", "gy"), P("gz", "gx", "gy"))
    out_specs = (P("gz", "gx", "gy"), P("gz", "gx", "gy"), P())
    return jax.shard_map(body, mesh=mesh, in_specs=in_specs, out_specs=out_specs, check_vma=False)
```

```python
import functools

import jax
import jax.numpy as jnp
from jax import lax
from jax.experimental import pallas as pl
from jax.experimental.pallas import tpu as pltpu
from jax.sharding import PartitionSpec as P

LEVELS = 6


first_scale = 1.0 / 7.5
rho_one = 1.0 / (2.0 * (5.0 / 3.0) - 0.6)
carry_coef = 0.6 * rho_one
fresh_coef = 2.0 * rho_one / (0.75 * 6.0)

LANES = 128
F32 = jnp.float32
AXES = (("gz", 0), ("gx", 1), ("gy", 2))


def extended(x, width):
    for axis, dim in AXES:
        peers, length = (lax.axis_size(axis), x.shape[dim + 1])
        up = [(i, (i + 1) % peers) for i in range(peers - 1)]
        down = [(j, i) for i, j in up]
        last = lax.slice_in_dim(x, length - width, length, axis=dim + 1)
        first = lax.slice_in_dim(x, 0, width, axis=dim + 1)
        before = lax.ppermute(last, axis, up)
        after = lax.ppermute(first, axis, down)
        x = jnp.concatenate([before, x, after], axis=dim + 1)
    return x


def stencil(values):
    padded = jnp.pad(values, 1)
    return valid_op(padded)


def valid_op(padded):
    beside = padded[2:, 1:-1, 1:-1] + padded[:-2, 1:-1, 1:-1]
    beside = beside + padded[1:-1, 2:, 1:-1] + padded[1:-1, :-2, 1:-1]
    beside = beside + padded[1:-1, 1:-1, 2:] + padded[1:-1, 1:-1, :-2]
    return 6.0 * padded[1:-1, 1:-1, 1:-1] - beside


def smooth_pass(iterate, source, apply_op, from_zero):
    residue = source if from_zero else source - apply_op(iterate)
    update = residue * first_scale
    iterate = update if from_zero else iterate + update
    residue = source - apply_op(iterate)
    update = carry_coef * update + fresh_coef * residue
    return iterate + update


def restrict(values):
    shape_a, shape_b, shape_c = values.shape
    blocks = values.reshape(shape_a // 2, 2, shape_b // 2, 2, shape_c // 2, 2)
    return 0.5 * jnp.sum(blocks, axis=(1, 3, 5))


def prolong(values):
    shape_a, shape_b, shape_c = values.shape
    spread = jnp.broadcast_to(
        values[:, None, :, None, :, None], (shape_a, 2, shape_b, 2, shape_c, 2)
    )
    return spread.reshape(2 * shape_a, 2 * shape_b, 2 * shape_c)


def vcycle(level_num, iterate, source):
    iterate = smooth_pass(iterate, source, stencil, True)
    coarsest = None
    if level_num < LEVELS - 1:
        residue = source - stencil(iterate)
        coarse, coarsest = vcycle(level_num + 1, None, restrict(residue))
        iterate = iterate + prolong(coarse)
    result = smooth_pass(iterate, source, stencil, False)
    if level_num == LEVELS - 1:
        coarsest = result
    return (result, coarsest)


def collect(values):
    gathered = lax.all_gather(values, "gz", axis=0, tiled=True)
    gathered = lax.all_gather(gathered, "gy", axis=2, tiled=True)
    return lax.all_gather(gathered, "gx", axis=1, tiled=True)


def local_stencil(values):
    return valid_op(extended(values[None], 1)[0])


def own_block(whole, block_shape):
    start_z = lax.axis_index("gz") * block_shape[0]
    start_x = lax.axis_index("gx") * block_shape[1]
    start_y = lax.axis_index("gy") * block_shape[2]
    return lax.dynamic_slice(whole, (start_z, start_x, start_y), block_shape)


def body_cycle(level_num, iterate, source, from_zero, gather_at):
    if level_num == gather_at:
        whole_source = collect(source)
        coarse, coarsest = vcycle(level_num, None, whole_source)
        return (own_block(coarse, source.shape), coarsest)
    iterate = smooth_pass(iterate, source, local_stencil, from_zero)
    residue = source - local_stencil(iterate)
    coarse, coarsest = body_cycle(level_num + 1, None, restrict(residue), True, gather_at)
    iterate = iterate + prolong(coarse)
    return (smooth_pass(iterate, source, local_stencil, False), coarsest)


def body_levels(divergence, pressure_prev):
    pressure, coarse_correction = body_cycle(0, pressure_prev, divergence, False, 3)
    residual = divergence - local_stencil(pressure)
    return (pressure, residual, coarse_correction)


def iota(shape, dim):
    return lax.broadcasted_iota(jnp.int32, shape, dim)


def signed(index, size, extent):
    return jnp.where(index >= (size + extent) // 2, index - extent, index)


def right_dot(values, table):
    rows = values.shape[0]
    terms = []
    for _ in range(3):
        term = values.astype(jnp.bfloat16)
        terms.append(term)
        values = values - term.astype(F32)
    out = jnp.dot(jnp.concatenate(terms, axis=0), table, preferred_element_type=F32)
    return out[0:rows] + out[rows:2 * rows] + out[2 * rows:3 * rows]


def right_dots(values, table):
    total = None
    for _ in range(3):
        term = values.astype(jnp.bfloat16)
        part = jnp.dot(term, table, preferred_element_type=F32)
        total = part if total is None else total + part
        values = values - term.astype(F32)
    return total


def as_table(keep, value=1.0):
    return jnp.where(keep, value, 0.0).astype(jnp.bfloat16)


def lateral(v):
    rows, lanes = v.shape
    return (
        pltpu.roll(v, 1, 0) + pltpu.roll(v, rows - 1, 0)
        + pltpu.roll(v, 1, 1) + pltpu.roll(v, lanes - 1, 1)
    )


def apply_at(ref, k, lateral_of=lateral):
    centre = ref[k]
    beside = lateral_of(centre)
    if k > 0:
        beside = beside + ref[k - 1]
    if k < ref.shape[0] - 1:
        beside = beside + ref[k + 1]
    return 6.0 * centre - beside


def padded(plan):
    return (plan.ey // LANES, plan.ez, plan.ex + 16, LANES)


def put(ref, k, v):
    rows = v.shape[0]
    for tile in range(ref.shape[0]):
        part = v[:, tile * LANES:(tile + 1) * LANES]
        ref[tile, k, 8:8 + rows, :] = part
        ref[tile, k, 7:8, :] = part[rows - 1:rows]
        ref[tile, k, 8 + rows:9 + rows, :] = part[0:1]


def rows_of(ref, k, first):
    here = pl.ds(first, ref.shape[2] - 16)
    return jnp.concatenate([ref[tile, k, here, :] for tile in range(ref.shape[0])], axis=1)


def apply_padded(ref, k, origin):
    centre = rows_of(ref, k, 8)
    lanes = centre.shape[1]
    beside = rows_of(ref, k, origin - 1) + rows_of(ref, k, origin + 1)
    beside = beside + (pltpu.roll(centre, 1, 1) + pltpu.roll(centre, lanes - 1, 1))
    if k > 0:
        beside = beside + rows_of(ref, k - 1, 8)
    if k < ref.shape[1] - 1:
        beside = beside + rows_of(ref, k + 1, 8)
    return 6.0 * centre - beside


def wrapped_mask(shape, sizes, low, high):
    keep = None
    for dim, size in sizes.items():
        at = signed(iota(shape, dim), size, shape[dim])
        good = ((at >= 0) | low[dim]) & ((at < size) | high[dim])
        keep = good if keep is None else keep & good
    return jnp.where(keep, 1.0, 0.0).astype(F32)


def side(index, flip):
    if flip == 1:
        return (index & 1) == 0, None
    return index < 2, (index == 1) | (index == 2)


def place(axis, count):
    index = lax.axis_index(axis)
    return index, index > 0, index < count - 1


def only(keep, v):
    return jnp.where(keep, v, 0.0)


def shifted(v, lanes):
    lanes = lanes % LANES
    return v if lanes == 0 else pltpu.roll(v, lanes, 1)


def lanes_of(v, first, count):
    lane = iota(v.shape, 1)
    last = first + count
    if last <= LANES:
        return (lane >= first) & (lane < last)
    return (lane >= first) | (lane < last - LANES)


def moved(v, first, count, to):
    first = first % LANES
    return shifted(only(lanes_of(v, first, count), v), to - first)


def landed(v, first, count, to):
    to = to % LANES
    v = shifted(v, to - first)
    return only(lanes_of(v, to, count), v)


def side_pack(tile, slot):
    return moved(tile, LANES - 3, 6, 6 * slot)


def side_unpack(packed, slot):
    return landed(packed, 6 * slot, 6, LANES - 3)


def slab_layers(r_ref, x_ref, up, low, high):
    start = jnp.where(up, high[0], low[0])
    start_x = jnp.where(up, high[1], low[1])
    return [(r_ref, start + j) for j in range(5)] + [(x_ref, start_x + j) for j in range(2)]


def slab_own(r_ref, x_ref, up):
    ez = r_ref.shape[0]
    return slab_layers(r_ref, x_ref, up, (0, 1), (ez - 5, ez - 3))


def slab_there(r_ref, x_ref, up):
    ez = r_ref.shape[0]
    return slab_layers(r_ref, x_ref, up, (1, 3), (ez - 6, ez - 5))


def slab_emit(r_ref, x_ref, out, up):
    ex = r_ref.shape[1]
    lat = None
    for j, (ref, k) in enumerate(slab_own(r_ref, x_ref, up)):
        v = ref[k]
        out[j * ex:(j + 1) * ex, :] = v[:, 0:LANES]
        part = side_pack(v[:, LANES:], j)
        lat = part if lat is None else lat + part
    out[7 * ex:8 * ex, :] = lat


def slab_add(r_ref, x_ref, slab, up):
    ex = r_ref.shape[1]
    lat = slab[7 * ex:8 * ex, :]
    for j, (ref, k) in enumerate(slab_there(r_ref, x_ref, up)):
        ref[k, :, 0:LANES] += slab[j * ex:(j + 1) * ex, :]
        ref[k, :, LANES:] += side_unpack(lat, j)


BESIDE = ((2, 2, 0, 0), (1, 1, 0, 3), (3, 1, 0, 5), (5, 1, 1, 0), (6, 1, 1, 3))


def beside(tile, count):
    row = iota(tile.shape, 0)
    return only((row < count) | (row >= 8 - count), tile)


def thin_emit(r_ref, x_ref, out, up):
    bx = r_ref.shape[1] - 8
    layers = slab_own(r_ref, x_ref, up)
    lat = None
    for j, (ref, k) in enumerate(layers):
        out[j * bx:(j + 1) * bx, :] = ref[k, 0:bx, 0:LANES]
        part = side_pack(ref[k, 0:bx, LANES:], j)
        lat = part if lat is None else lat + part
    tiles = [None, None]
    for j, count, which, turn in BESIDE:
        ref, k = layers[j]
        part = beside(ref[k, bx:, 0:LANES], count)
        part = pltpu.roll(part, turn, 0) if turn else part
        tiles[which] = part if tiles[which] is None else tiles[which] + part
    at = 7 * bx
    out[at:at + 8, :] = tiles[0]
    out[at + 8:at + 16, :] = tiles[1]
    out[at + 16:at + 16 + bx, :] = lat
    for j in (1, 2, 3):
        ref, k = layers[j]
        out[at + 16:at + 24, :] += side_pack(ref[k, bx:, LANES:], 6 + j)


def thin_add(r_ref, x_ref, slab, up):
    bx = r_ref.shape[1] - 8
    layers = slab_there(r_ref, x_ref, up)
    at = 7 * bx
    lat = slab[at + 16:at + 16 + bx, :]
    for j, (ref, k) in enumerate(layers):
        ref[k, 0:bx, 0:LANES] += slab[j * bx:(j + 1) * bx, :]
        ref[k, 0:bx, LANES:] += side_unpack(lat, j)
    for j, count, which, turn in BESIDE:
        ref, k = layers[j]
        tile = slab[at + 8 * which:at + 8 * which + 8, :]
        tile = pltpu.roll(tile, 8 - turn, 0) if turn else tile
        ref[k, bx:, 0:LANES] += beside(tile, count)
    for j in (1, 2, 3):
        ref, k = layers[j]
        ref[k, bx:, LANES:] += side_unpack(lat[0:8], 6 + j)


def rows_out(r, x, up):
    bx = r.shape[0] - 8
    row = iota((8, r.shape[1]), 0)
    first, last, spill = r[0:8], r[bx - 8:bx], r[bx:]
    to_high = pltpu.roll(jnp.where(row >= 6, last, spill), 2, 0)
    to_low = pltpu.roll(jnp.where(row >= 5, spill, first), 3, 0)
    out = jnp.where(up, to_high, to_low)
    if x is None:
        return only(row < 5, out)
    spill = x[bx:]
    extra = jnp.where(up, pltpu.roll(spill, 5, 0), pltpu.roll(spill, 7, 0))
    return jnp.where(row < 5, out, only(row < 7, extra))


def rows_in(r_ref, x_ref, k, rows, up):
    bx = r_ref.shape[1] - 8
    row = iota(rows.shape, 0)
    high, low = pltpu.roll(rows, 5, 0), pltpu.roll(rows, 6, 0)
    r_ref[k, 0:8] += only(jnp.logical_not(up) & (row < 3), low)
    r_ref[k, bx - 8:bx] += only(up & (row >= 5), high)
    r_ref[k, bx:] += jnp.where(up, only(row < 2, high), only(row >= 6, low))
    if x_ref is not None:
        x_ref[k, 0:8] += only(jnp.logical_not(up) & (row < 2), pltpu.roll(rows, 3, 0))
        x_ref[k, bx - 8:bx] += only(up & (row >= 6), pltpu.roll(rows, 1, 0))


def rows_emit(r_ref, x_ref, out, up):
    ez = r_ref.shape[0]
    row = iota((8, LANES), 0)
    lat = jnp.zeros((8, LANES), F32)
    for t, k in enumerate(range(1, ez - 1)):
        far = {1: 0, ez - 2: ez - 1}.get(k)
        rows = rows_out(r_ref[k], None if far is not None else x_ref[k], up)
        tile = rows[:, 0:LANES]
        if far is not None:
            more = rows_out(r_ref[far, :, 0:LANES], None, up)
            more = jnp.where(up, pltpu.roll(more, 5, 0), pltpu.roll(more, 2, 0))
            tile = jnp.where((row == 5) | (row == 6), more, tile)
        out[8 * t:8 * t + 8, :] = tile
        lat = lat + side_pack(rows[:, LANES:], t)
    at = 8 * (ez - 2)
    out[at:at + 8, :] = lat


def rows_add(r_ref, x_ref, slab, up):
    ez = r_ref.shape[0]
    at = 8 * (ez - 2)
    lat = slab[at:at + 8, :]
    row = iota((8, LANES), 0)
    for t, k in enumerate(range(1, ez - 1)):
        far = {1: 0, ez - 2: ez - 1}.get(k)
        tile = slab[8 * t:8 * t + 8, :]
        rows = jnp.concatenate([tile, side_unpack(lat, t)], axis=1)
        rows_in(r_ref, None if far is not None else x_ref, k, rows, up)
        if far is not None:
            tile = only((row == 5) | (row == 6), tile)
            tile = jnp.where(up, pltpu.roll(tile, 6, 0), pltpu.roll(tile, 3, 0))
            rows = jnp.concatenate([tile, jnp.zeros((8, LANES), F32)], axis=1)
            rows_in(r_ref, None, far, rows, up)


class Plan:
    def first_layer(self, iz):
        start = iz * (self.block[0] // 2) - 4
        return jnp.clip(start, 0, self.level1[0] - self.window[0])

    def __init__(self, shape, peers):
        self.peers = peers
        self.block = bz, bx, by = shape
        self.ext = self.ez, self.ex, self.ey = bz + 6, bx + 8, by + LANES
        self.rows, self.pairs = bx // 2, bz // 4 + 2
        self.lat_at = self.pairs * (self.rows + 4)
        self.coarse = self.lat_at + 8
        self.slab = 8 * self.ex
        self.slab_z = 8 * bx + 16
        self.slab_x = 8 * (bz + 5)
        self.corner = 6 * 8
        self.layers = bz + 4
        self.level1 = (peers[0] * bz // 2, peers[1] * bx // 2, LANES)
        self.level2 = (peers[0] * bz // 4, peers[1] * bx // 4, peers[2] * by // 4)
        self.inner = [0, 1] + [2] * bz + [1, 0]
        self.slots, at = [], 0
        for count in self.inner:
            self.slots.append(at)
            at += 3 + count + (2 if count == 2 else 0)
        assert at <= LANES
        self.fine_rows = self.ex
        self.window = (bz // 2 + 8, self.level1[1], LANES)
        self.edge = self.fine_rows + self.window[0] * self.window[1] // 8
        self.wide2 = by // 4 + 4
        self.fold = LANES // self.wide2
        self.lines2 = -(-self.level2[0] // self.fold)
        self.share = self.lines2 * self.level2[1]


def first_kernel(plan, both, r_ref, x_ref, pay_z, pay_x, pay_d, d_one, d_two, pairs, lines):
    p_ext, b_ext = both.at[0], both.at[1]
    bz, bx, by = plan.block
    ez, ex, ey = plan.ext
    peers = plan.peers
    iz, z_low, z_high = place("gz", peers[0])
    ix, x_low, x_high = place("gx", peers[1])
    _, y_low, y_high = place("gy", peers[2])
    flat = wrapped_mask((ex, ey), {0: bx, 1: by}, (x_low, y_low), (x_high, y_high))
    below = jnp.where(z_low, 1.0, 0.0).astype(F32)
    above = jnp.where(z_high, 1.0, 0.0).astype(F32)

    def masked(k, v):
        v = v * flat
        if k < 3:
            v = v * below
        if k >= 3 + bz:
            v = v * above
        return v

    zero = jnp.zeros((ex, ey), F32)
    origin = 8 + (iz >> 8)
    for k in range(ez):
        if 2 <= k < ez - 2:
            r = b_ext[k] - apply_at(p_ext, k)
            r_ref[k] = r
            put(d_one, k, masked(k, r * first_scale))
        elif 1 <= k < ez - 1:
            put(d_one, k, zero)
    for k in range(ez):
        if 1 <= k < ez - 1:
            if 2 <= k < ez - 2:
                r = r_ref[k] - apply_padded(d_one, k, origin)
                d = carry_coef * rows_of(d_one, k, 8) + fresh_coef * r
            else:
                inward = k + 1 if k == 1 else k - 1
                r = rows_of(d_one, inward, 8)
                d = fresh_coef * r
            r_ref[k] = r
            put(d_two, k, masked(k, d))
    for k in range(ez):
        if 1 <= k < ez - 1:
            part = rows_of(d_two, k, 8)
            beside = rows_of(d_two, k, origin - 1) + rows_of(d_two, k, origin + 1)
            beside = beside + (pltpu.roll(part, 1, 1) + pltpu.roll(part, ey - 1, 1))
            if k > 1:
                beside = beside + rows_of(d_two, k - 1, 8)
            if k < ez - 2:
                beside = beside + rows_of(d_two, k + 1, 8)
            r_ref[k] = masked(k, r_ref[k] - (6.0 * part - beside))
            x_ref[k] = p_ext[k] + (rows_of(d_one, k, 8) + part)
        else:
            r_ref[k] = masked(k, rows_of(d_two, 1 if k == 0 else ez - 2, 8))
            x_ref[k] = zero

    coarse_z, rows = 2 * plan.pairs, plan.rows
    for zc in range(coarse_z):
        low, high = 2 * zc - 1, 2 * zc
        if low < 0:
            total = r_ref[high]
        elif high >= ez:
            total = r_ref[low]
        else:
            total = r_ref[low] + r_ref[high]
        base = zc * ex
        for tile in range(ey // LANES):
            here = slice(tile * LANES, (tile + 1) * LANES)
            pairs[tile, base:base + ex, :] = total[:, here]
            even = pairs.at[tile][pl.ds(base, ex // 2, 2), :]
            odd = pairs.at[tile][pl.ds(base + 1, ex // 2, 2), :]
            sums = even + odd
            at = zc // 2 * rows
            at += zc % 2 * plan.lat_at
            lines[at:at + rows, here] = sums[0:rows]
            at = plan.pairs * rows + zc // 2 * 4 + zc % 2 * plan.lat_at
            lines[at:at + 4, here] = sums[rows:rows + 4]
    fine = signed(iota((ey, LANES), 0), by, ey)
    coarse = signed(iota((ey, LANES), 1), by // 2, LANES)
    table = as_table((fine >> 1) == coarse, 0.5)
    out = right_dot(lines[...], table)
    even, odd = out[0:plan.lat_at], out[plan.lat_at:]
    lane = iota(even.shape, 1)
    main = jnp.where(lane < LANES // 2, even, shifted(odd, LANES // 2))
    own_lat = spill_lat = None
    row = iota((8, LANES), 0)
    for zc in range(coarse_z):
        source = (even, odd)[zc % 2]
        base = zc // 2 * rows
        tile = source[base:base + rows]
        part = moved(tile, by // 2, 2, 4 * zc) + moved(tile, LANES - 2, 2, 4 * zc + 2)
        own_lat = part if own_lat is None else own_lat + part
        base = plan.pairs * rows + zc // 4 * 8
        tile = source[base:base + 8]
        if zc // 2 % 2:
            tile = pltpu.roll(tile, 4, 0)
        tile = only(row < 4, tile)
        slot = LANES // 2 + 4 * zc
        part = moved(tile, by // 2, 2, slot) + moved(tile, LANES - 2, 2, slot + 2)
        spill_lat = part if spill_lat is None else spill_lat + part
    for pay, at in ((pay_z, plan.slab_z), (pay_x, plan.slab_x), (pay_d, plan.corner)):
        pay[at:at + plan.lat_at, :] = main
        pay[at + plan.lat_at:at + plan.coarse, :] = own_lat + spill_lat

    up_z, _ = side(iz, 3)
    up_x, _ = side(ix, 1)
    thin_emit(r_ref, x_ref, pay_z, up_z)
    rows_emit(r_ref, x_ref, pay_x, up_x)
    lat = jnp.zeros((8, LANES), F32)
    start = jnp.where(up_z, ez - 5, 0)
    for j in range(5):
        out = rows_out(r_ref[start + j], x_ref[start + j] if j == 2 else None, up_x)
        pay_d[8 * j:8 * j + 8, :] = out[:, 0:LANES]
        lat = lat + side_pack(out[:, LANES:], j)
    pay_d[40:48, :] = lat


def chip_kernel(plan, r_in, x_in, from_z, from_x, from_d, r_ref, x_ref, pay):
    ez, ex, ey = plan.ext
    iz, _, _ = place("gz", plan.peers[0])
    ix, _, _ = place("gx", plan.peers[1])
    up_z, near = side(iz, 3)
    up_x, _ = side(ix, 1)
    for k in range(ez):
        r_ref[k] = r_in[k]
        x_ref[k] = x_in[k]
    rows_add(r_ref, x_ref, from_x, up_x)

    @pl.when(near)
    def _():
        thin_add(r_ref, x_ref, from_z, up_z)
        start = jnp.where(up_z, ez - 6, 1)
        lat = from_d[40:48, :]
        for j in range(5):
            rows = from_d[8 * j:8 * j + 8, :]
            rows = jnp.concatenate([rows, side_unpack(lat, j)], axis=1)
            rows_in(r_ref, x_ref if j == 2 else None, start + j, rows, up_x)

    slab_emit(r_ref, x_ref, pay, side(iz, 1)[0])


def plane_kernel(plan, r_in, x_in, ours, theirs, r_ref, x_ref, r1_ref, x1_ref, pay, later, share,
                 r_all, x_all, b1, d1, d2, r1, x1, pairs, lines):
    bz, bx, by = plan.block
    ez, ex, ey = plan.ext
    layers = plan.layers
    iz, _, _ = place("gz", plan.peers[0])
    ix, _, _ = place("gx", plan.peers[1])
    iy, y_low, y_high = place("gy", plan.peers[2])
    up_z, _ = side(iz, 1)
    for k in range(ez):
        r_all[k] = r_in[k]
        x_all[k] = x_in[k]
    slab_add(r_all, x_all, theirs, up_z)
    for k in range(layers):
        r_ref[k] = r_all[k + 1]
    for k in range(bz):
        x_ref[k] = x_all[k + 3, 0:bx, 0:by]

    up, _ = side(iy, 1)
    up_inner, _ = side(iy, 3)
    high, low = jnp.zeros((ex, LANES), F32), jnp.zeros((ex, LANES), F32)
    for k in range(layers):
        slot, inner = plan.slots[k], plan.inner[k]
        count = 3 + inner
        v, spill = r_all[k + 1, :, 0:by], r_all[k + 1, :, by:ey]
        high = high + moved(jnp.where(lanes_of(v, 0, 3), spill, v), LANES - inner, count, slot)
        mixed = jnp.where(lanes_of(v, 0, 2), v, spill)
        low = low + moved(mixed, LANES - 3, count, slot)
        if inner == 2:
            spill = x_all[k + 1, :, by:ey]
            high = high + moved(spill, 0, 2, slot + count)
            low = low + moved(spill, LANES - 2, 2, slot + count)
    pay[0:ex, :] = jnp.where(up, high, low)
    later[0:ex, :] = jnp.where(up_inner, high, low)

    nz1, nx1, _ = plan.level1
    rows, half = plan.rows, by // 2
    for k in range(nz1):
        b1[k] = jnp.zeros((nx1, LANES), F32)
    row = iota((8, LANES), 0)
    for j in range(plan.peers[0]):
        for i in range(plan.peers[1]):
            flip = iz ^ j
            other = ((flip ^ (flip >> 1)) & 1) == 1
            chip = (flip >> 1) + 2 * (ix ^ i)
            at = pl.multiple_of(plan.slab + chip * plan.coarse, 8)

            def rows_at(offset, count):
                here = pl.ds(pl.multiple_of(at + offset, 8), count)
                return jnp.where(other, theirs[here, :], ours[here, :])

            lat = rows_at(plan.lat_at, 8)
            for zp in range(plan.pairs):
                own = rows_at(zp * rows, rows)
                if zp % 2 == 0:
                    spill_two = rows_at(plan.pairs * rows + zp * 4, 8)
                spill = spill_two if zp % 2 == 0 else pltpu.roll(spill_two, 4, 0)
                for part in range(2):
                    zc = 2 * zp + part
                    k = j * (bz // 2) + zc - 2
                    if not 0 <= k < nz1:
                        continue

                    def wide(main, slot):
                        return (
                            landed(main, part * half, half, 0)
                            + landed(lat, slot, 2, half) + landed(lat, slot + 2, 2, LANES - 2)
                        )

                    b1[k, i * rows:(i + 1) * rows, :] += wide(own, 4 * zc)
                    v = wide(spill, LANES // 2 + 4 * zc)
                    if i + 1 < plan.peers[1]:
                        at_row = (i + 1) * rows
                        b1[k, at_row:at_row + 8, :] += only(row < 2, v)
                    if i > 0:
                        at_row = i * rows - 8
                        b1[k, at_row:at_row + 8, :] += only(row >= 6, pltpu.roll(v, 4, 0))

    lateral1 = level_lateral((nx1, LANES))
    keep = wrapped_mask((nx1, LANES), {1: half}, (None, y_low), (None, y_high))
    for k in range(nz1):
        d1[k] = b1[k] * first_scale
    for k in range(nz1):
        r = b1[k] - apply_at(d1, k, lateral1)
        r1[k] = r
        d2[k] = keep * (carry_coef * d1[k] + fresh_coef * r)
    for k in range(nz1):
        r1[k] = keep * (r1[k] - apply_at(d2, k, lateral1))
        x1[k] = d1[k] + d2[k]

    nz2, nx2, _ = plan.level2
    for zc in range(nz2):
        pairs[zc * nx1:(zc + 1) * nx1, :] = r1[2 * zc] + r1[2 * zc + 1]
        part, at = divmod(zc, plan.lines2)
        lines[at * nx2:(at + 1) * nx2, part * LANES:(part + 1) * LANES] = (
            pairs[pl.ds(zc * nx1, nx2, 2), :] + pairs[pl.ds(zc * nx1 + 1, nx2, 2), :]
        )
    shape = (plan.fold * LANES, LANES)
    fine, coarse = iota(shape, 0), iota(shape, 1)
    part, fine = fine // LANES, signed(fine % LANES, half, LANES)
    coarse = coarse - part * plan.wide2 - 2
    near = (coarse >= -2) & (coarse < plan.wide2 - 2)
    for part in range(plan.fold):
        count = min(plan.lines2, nz2 - part * plan.lines2) * nx2
        if count < plan.share:
            here = slice(part * LANES, (part + 1) * LANES)
            lines[count:, here] = jnp.zeros((plan.share - count, LANES), F32)
    total = right_dot(lines[...], as_table(near & ((fine >> 1) == coarse), 0.5))
    share[...] = total
    pay[plan.edge:plan.edge + plan.share, :] = total
    later[plan.edge:plan.edge + plan.share, :] = total

    start = plan.first_layer(iz)
    for k in range(plan.window[0]):
        r1_ref[k] = r1[start + k]
        x1_ref[k] = x1[start + k]
    per_tile = LANES // 16
    for group in range(plan.window[0] // per_tile):
        tiles = []
        for which in range(2):
            total = jnp.zeros((nx1, LANES), F32)
            for j in range(per_tile):
                k = group * per_tile + j
                first = half - 3 if which == 0 else LANES - 4
                total = total + moved(r1_ref[k], first, 7, 16 * j)
                first = half - 2 if which == 0 else LANES - 3
                total = total + moved(x1_ref[k], first, 5, 16 * j + 7)
            tiles.append(total)
        here = slice(plan.fine_rows + group * nx1, plan.fine_rows + (group + 1) * nx1)
        pay[here, :] = jnp.where(up, tiles[0], tiles[1])
        later[here, :] = jnp.where(up_inner, tiles[0], tiles[1])


def level_lateral(shape):
    row = iota(shape, 0)
    not_first = jnp.where(row > 0, 1.0, 0.0).astype(F32)
    not_last = jnp.where(row < shape[0] - 1, 1.0, 0.0).astype(F32)

    def beside(v):
        return (
            not_first * pltpu.roll(v, 1, 0) + not_last * pltpu.roll(v, shape[0] - 1, 0)
            + pltpu.roll(v, 1, 1) + pltpu.roll(v, LANES - 1, 1)
        )

    return beside


def line_cycle(source, step):
    lane = iota((8, LANES), 1)
    count = len(source)

    def inside(s, v):
        if s == 0:
            return v
        return only(lane < LANES - s * step if s > 0 else lane >= -s * step, v)

    def op(v, width):
        out = {}
        for s in range(-width, width + 1):
            out[s] = []
            for k in range(count):
                beside = v[s - 1][k] + v[s + 1][k]
                if k > 0:
                    beside = beside + v[s][k - 1]
                if k < count - 1:
                    beside = beside + v[s][k + 1]
                out[s].append(inside(s, 6.0 * v[s][k] - beside))
        return out

    def mix(width, *terms):
        return {
            s: [sum(c * v[s][k] for c, v in terms) for k in range(count)]
            for s in range(-width, width + 1)
        }

    b = {s: [inside(s, shifted(v, -s * step)) for v in source] for s in range(-3, 4)}
    d = mix(3, (first_scale, b))
    r = mix(2, (1.0, b), (-1.0, op(d, 2)))
    d2 = mix(2, (carry_coef, d), (fresh_coef, r))
    x = mix(0, (1.0, d), (1.0, d2))
    r = mix(1, (1.0, r), (-1.0, op(d2, 1)))
    d = mix(1, (first_scale, r))
    r = mix(0, (1.0, r), (-1.0, op(d, 0)))
    x = mix(0, (1.0, x), (1.0 + carry_coef, d), (fresh_coef, r))[0]
    return x, x


def small_cycle(level, source):
    step = 1 << (level - 2)
    row, lane = iota((8, LANES), 0), iota((8, LANES), 1)
    count = len(source)
    if level == LEVELS - 1 and step >= 8:
        return line_cycle(source, step)
    shifts = []
    if step < 8:
        shifts += [(step, 0, row >= step), (8 - step, 0, row < 8 - step)]
    shifts += [(step, 1, lane >= step), (LANES - step, 1, lane < LANES - step)]

    def op(v):
        out = []
        for k in range(count):
            beside = None
            for shift, dim, keep in shifts:
                part = only(keep, pltpu.roll(v[k], shift, dim))
                beside = part if beside is None else beside + part
            if k > 0:
                beside = beside + v[k - 1]
            if k < count - 1:
                beside = beside + v[k + 1]
            out.append(6.0 * v[k] - beside)
        return out

    def moves(v, dim, places):
        size, shift = v.shape[dim], places * step
        if abs(shift) >= size:
            return jnp.zeros_like(v)
        index = row if dim == 0 else lane
        keep = index < size - shift if shift > 0 else index >= -shift
        return only(keep, pltpu.roll(v, -shift % size, dim))

    def at(values, k):
        return values[k] if 0 <= k < len(values) else None

    def added(*terms):
        total = None
        for term in terms:
            if term is not None:
                total = term if total is None else total + term
        return total

    d = [first_scale * v for v in source]
    before = [b - t for b, t in zip(source, op(d))]
    d2 = [carry_coef * v + fresh_coef * t for v, t in zip(d, before)]
    x = [v + t for v, t in zip(d, d2)]
    r = [v - t for v, t in zip(before, op(d2))]
    coarsest = None
    if level < LEVELS - 1:
        keep = only((row % (2 * step) == 0) & (lane % (2 * step) == 0), 0.5)
        coarse = []
        for k in range(0, count, 2):
            v = d2[k] + d2[k + 1]
            beyond = added(at(d2, k - 1), at(d2, k + 2))
            rest = before[k] + before[k + 1] - 5.0 * v
            rest = rest if beyond is None else rest + beyond
            along = [
                v + moves(v, dim, 1) + (moves(v, dim, -1) + moves(v, dim, 2)) for dim in range(2)
            ]
            first = rest + moves(rest, 0, 1) + along[0]
            coarse.append(keep * (
                first + moves(first, 1, 1) + (along[1] + moves(along[1], 0, 1))
            ))
        coarse, coarsest = small_cycle(level + 1, coarse)
        e, beside = [], []
        for v in coarse:
            back = [moves(v, dim, -1) for dim in range(2)]
            wide = v + back[0]
            e.append(wide + moves(wide, 1, -1))
            along = [
                v + back[dim] + (moves(v, dim, 1) + moves(v, dim, -2)) for dim in range(2)
            ]
            beside.append(
                along[0] + moves(along[0], 1, -1) + (along[1] + moves(along[1], 0, -1))
            )
        for k in range(count):
            own = e[k // 2]
            change = 5.0 * own - beside[k // 2]
            beyond = at(e, k // 2 + (1 if k % 2 else -1))
            if beyond is not None:
                change = change - beyond
            x[k] = x[k] + own
            r[k] = r[k] - change
    d = [first_scale * v for v in r]
    r = [v - t for v, t in zip(r, op(d))]
    x = [v + (t + (carry_coef * t + fresh_coef * u)) for v, t, u in zip(x, d, r)]
    return x, (x if level == LEVELS - 1 else coarsest)


def last_kernel(plan, r_in, x_in, r1_in, x1_in, ours, from_a, from_b, from_c, p_out, res_out, last_ref, *scratch):
    shares, p_ref, res_ref, r, q1, e1, e0, d0, d1, r1, lines, wide, sem = scratch
    bz, bx, by = plan.block
    ez, ex, ey = plan.ext
    nz1, nx1, _ = plan.window
    nz2, nx2, _ = plan.level2
    layers, half = plan.layers, by // 2
    iz, z_low, z_high = place("gz", plan.peers[0])
    ix, x_low, x_high = place("gx", plan.peers[1])
    iy, y_low, y_high = place("gy", plan.peers[2])

    shares[0] = ours[...]
    shares[1] = from_a[plan.edge:plan.edge + plan.share, :]
    shares[3] = from_b[plan.edge:plan.edge + plan.share, :]
    shares[2] = from_c[...]
    own2 = half // 2
    source = []
    for part in range(plan.fold):
        total = None
        for j in range(plan.peers[2]):
            v = moved(shares[iy ^ j], part * plan.wide2, plan.wide2, own2 * j - 2)
            total = v if total is None else total + v
        source += [total[nx2 * k:nx2 * (k + 1)] for k in range(plan.lines2)]
    source = source[:nz2]
    e2, coarsest = small_cycle(2, source)
    for k in range(nz2):
        lines[k * nx2:(k + 1) * nx2, :] = e2[k]
    thin = as_table(iota((LANES, LANES), 0) == 8 * iota((LANES, LANES), 1))
    for k in range(last_ref.shape[0]):
        last_ref[k] = right_dot(coarsest[k], thin)[0:1, 0:last_ref.shape[2]]

    up_a, _ = side(iy, 1)
    _, near_b = side(iy, 3)

    def sent(rows):
        a, b = from_a[rows[0]:rows[1], :], only(near_b, from_b[rows[0]:rows[1], :])
        return jnp.where(up_a, a, b), jnp.where(up_a, b, a)

    fine = signed(iota((LANES, LANES), 1), half, LANES)
    coarse = iota((LANES, LANES), 0) - iy * own2
    start = plan.first_layer(iz)
    here = pl.ds(pl.multiple_of(start // 2 * nx2, 8), nz1 // 2 * nx2)
    e2 = right_dot(lines[here, :], as_table((fine >> 1) == coarse))
    for zc in range(nz1 // 2):
        v = e2[zc * nx2:(zc + 1) * nx2]
        for part in range(2):
            q1.at[2 * zc + part][pl.ds(0, nx2, 2), :] = v
            q1.at[2 * zc + part][pl.ds(1, nx2, 2), :] = v
    per_tile = LANES // 16
    lateral1 = level_lateral((nx1, LANES))
    keep = wrapped_mask((nx1, LANES), {1: half}, (None, y_low), (None, y_high))
    for group in range(nz1 // per_tile):
        at = plan.fine_rows + group * nx1
        high, low = sent((at, at + nx1))
        for j in range(per_tile):
            k = group * per_tile + j
            s = 16 * j
            r1[k] = (
                r1_in[k] + landed(high, s, 7, half - 4) + landed(low, s, 7, LANES - 3)
                - apply_at(q1, k, lateral1)
            )
            e1[k + 2, 8:8 + nx1, :] = (
                x1_in[k] + q1[k]
                + landed(high, s + 7, 5, half - 3) + landed(low, s + 7, 5, LANES - 2)
            )
    for k in range(nz1):
        d1[k] = keep * (r1[k] * first_scale)
    nothing = jnp.zeros((8, LANES), F32)
    for k in range(nz1 + 4):
        e1[k, 0:8, :] = nothing
        e1[k, 8 + nx1:16 + nx1, :] = nothing
        if not 2 <= k < nz1 + 2:
            e1[k, 8:8 + nx1, :] = jnp.zeros((nx1, LANES), F32)
    for k in range(nz1):
        v = r1[k] - apply_at(d1, k, lateral1)
        e1[k + 2, 8:8 + nx1, :] += d1[k] + keep * (carry_coef * d1[k] + fresh_coef * v)

    coarse = signed(iota((LANES, ey), 0), half, LANES)
    fine = signed(iota((LANES, ey), 1), by, ey)
    double = as_table((fine >> 1) == coarse)
    half_z, half_x = bz // 2, bx // 2
    for zc in range(half_z + 4):
        here = pl.ds(pl.multiple_of(ix * half_x, 8), half_x + 16)
        v = e1[iz * half_z - start + zc, here, :]
        own, low, high = v[8:8 + half_x], v[0:8], v[8 + half_x:16 + half_x]
        at = zc * ex
        wide[pl.ds(at, half_x, 2), :] = own
        wide[pl.ds(at + 1, half_x, 2), :] = own
        for j in range(2):
            for twin in range(2):
                row = at + bx + 2 * j + twin
                wide[row:row + 1, :] = high[j:j + 1]
                row = at + ex - 4 + 2 * j + twin
                wide[row:row + 1, :] = low[6 + j:7 + j]
    origin = 8 + (iz >> 8)
    for zc in range(half_z + 4):
        v = right_dots(wide[zc * ex:(zc + 1) * ex, :], double)
        for k in (2 * zc - 1, 2 * zc):
            if 0 <= k < ez:
                put(e0, k, v)
    flat = wrapped_mask((ex, ey), {0: bx, 1: by}, (x_low, y_low), (x_high, y_high))
    below = jnp.where(z_low, 1.0, 0.0).astype(F32)
    above = jnp.where(z_high, 1.0, 0.0).astype(F32)

    def masked(k, v):
        v = v * flat
        if k < 3:
            v = v * below
        if k >= 3 + bz:
            v = v * above
        return v

    high, low = sent((0, ex))
    for k in range(layers):
        s, inner = plan.slots[k], plan.inner[k]
        v = r_in[k] - apply_padded(e0, k + 1, origin)
        own = v[:, 0:by] + landed(high, s, 3, LANES - 3) + landed(low, s + inner, 3, 0)
        spill = v[:, by:ey]
        if inner:
            spill = spill + landed(high, s + 3, inner, 0) + landed(low, s, inner, LANES - inner)
        r[k, :, 0:by] = own
        r[k, :, by:ey] = spill
        put(d0, k, masked(k + 1, r[k] * first_scale))
        if inner == 2:
            s = s + 3 + inner
            p_ref[k - 2] = (
                x_in[k - 2] + e0[0, k + 1, 8:8 + bx, :]
                + (landed(high, s, 2, LANES - 2) + landed(low, s, 2, 0))[0:bx]
            )
    for k in range(1, layers - 1):
        v = r[k] - apply_padded(d0, k, origin)
        r[k] = v
        d = rows_of(d0, k, 8)
        v = masked(k + 1, carry_coef * d + fresh_coef * v)
        put(e0, k, v)
        if 2 <= k < 2 + bz:
            p_ref[k - 2] += d[0:bx, 0:by] + v[0:bx, 0:by]
    copy = pltpu.make_async_copy(p_ref, p_out, sem.at[0])
    copy.start()
    copies = [copy]
    parts = 2
    for part in range(parts):
        here = range(part * bz // parts, (part + 1) * bz // parts)
        for j in here:
            v = r[j + 2] - apply_padded(e0, j + 2, origin)
            res_ref[j] = v[0:bx, 0:by]
        here = pl.ds(here[0], bz // parts)
        copy = pltpu.make_async_copy(res_ref.at[here], res_out.at[here], sem.at[1 + part])
        copy.start()
        copies.append(copy)
    for copy in copies:
        copy.wait()


def whole(shape):
    return jax.ShapeDtypeStruct(shape, F32)


VMEM = pl.BlockSpec(memory_space=pltpu.VMEM)
ANY = pl.BlockSpec(memory_space=pl.ANY)
VMEM_BYTES = 24 << 20


def run(kernel, plan, outs, scratch, *operands, out_specs=None, semaphores=0):
    scratch = [pltpu.VMEM(s, F32) for s in scratch]
    if semaphores:
        scratch.append(pltpu.SemaphoreType.DMA((semaphores,)))
    return pl.pallas_call(
        functools.partial(kernel, plan),
        out_shape=[whole(s) for s in outs],
        in_specs=[VMEM] * len(operands),
        out_specs=out_specs or [VMEM] * len(outs),
        scratch_shapes=scratch,
        compiler_params=pltpu.CompilerParams(vmem_limit_bytes=VMEM_BYTES),
    )(*operands)


def swap(values, partner):
    axes = ("gx", "gy", "gz")
    counts = [lax.axis_size(a) for a in axes]
    pairs = []
    for i in range(counts[0] * counts[1] * counts[2]):
        to = partner(i // (counts[1] * counts[2]), i // counts[2] % counts[1], i % counts[2])
        if to is not None:
            pairs.append((i, (to[0] * counts[1] + to[1]) * counts[2] + to[2]))
    return lax.ppermute(values, axes, pairs)


def body_fast(divergence, pressure_prev):
    plan = Plan(divergence.shape, tuple(lax.axis_size(a) for a in ("gz", "gx", "gy")))
    ext, level1 = plan.ext, plan.level1
    window, layers = plan.window, (plan.layers, plan.ex, plan.ey)
    payload = [(n + plan.coarse, LANES) for n in (plan.slab_z, plan.slab_x, plan.corner)]
    both = jnp.stack([pressure_prev, divergence])
    both = jnp.pad(both, ((0, 0), (3, 3), (0, plan.ex - plan.block[1]), (0, plan.ey - plan.block[2])))
    r, x, pay_z, pay_x, pay_d = run(
        first_kernel, plan, [ext, ext] + payload,
        [padded(plan), padded(plan), (2, 2 * plan.pairs * plan.ex, LANES),
         (2 * plan.lat_at, plan.ey)],
        both,
    )
    from_z = swap(pay_z, lambda x, y, z: (x, y, z ^ 3))
    from_x = swap(pay_x, lambda x, y, z: (x ^ 1, y, z))
    from_d = swap(pay_d, lambda x, y, z: (x ^ 1, y, z ^ 3))
    r, x, slab = run(
        chip_kernel, plan, [ext, ext, (plan.slab, LANES)], [], r, x, from_z, from_x, from_d
    )
    ours = jnp.concatenate([
        slab, pay_z[plan.slab_z:], from_z[plan.slab_z:], from_x[plan.slab_x:], from_d[plan.corner:]
    ], axis=0)
    got = swap(ours, lambda x, y, z: (x, y, z ^ 1))
    nz2, nx2, _ = plan.level2
    share = (plan.share, LANES)
    r, x, r1, x1, now, later, ours = run(
        plane_kernel, plan,
        [layers, plan.block, window, window, (plan.edge + plan.share, LANES),
         (plan.edge + plan.share, LANES), share],
        [ext, ext, level1, level1, level1, level1, level1, (nz2 * level1[1], LANES),
         (plan.share, plan.fold * LANES)],
        r, x, ours, got,
    )
    from_a = swap(now, lambda x, y, z: (x, y ^ 1, z))
    from_b = swap(later, lambda x, y, z: (x, y ^ 3, z))
    from_c = swap(ours, lambda x, y, z: (x, y ^ 2, z))
    return run(
        last_kernel, plan,
        [plan.block, plan.block, tuple(n >> 3 for n in plan.level2)],
        [(4,) + share, plan.block, plan.block, layers, window,
         (window[0] + 4, window[1] + 16, LANES), padded(plan), padded(plan), window, window,
         (nz2 * nx2, LANES), (2 * plan.pairs * plan.ex, LANES)],
        r, x, r1, x1, ours, from_a, from_b, from_c,
        out_specs=[ANY, ANY, VMEM], semaphores=3,
    )


def fits_fast(shape, peers):
    bz, bx, by = shape
    nz, nx, ny = peers
    return (
        nz == 4 and nx == 2 and ny == 4 and bz == 16 and by == LANES
        and nx * bx == 4 * 8 and ny * by == 4 * LANES
    )


def body(divergence, pressure_prev):
    peers = tuple(lax.axis_size(a) for a in ("gz", "gx", "gy"))
    if fits_fast(divergence.shape, peers):
        return tuple(body_fast(divergence, pressure_prev))
    return body_levels(divergence, pressure_prev)


def solution(mesh):
    in_specs = (P("gz", "gx", "gy"), P("gz", "gx", "gy"))
    out_specs = (P("gz", "gx", "gy"), P("gz", "gx", "gy"), P())
    return jax.shard_map(body, mesh=mesh, in_specs=in_specs, out_specs=out_specs, check_vma=False)
```

```python
import functools

import jax
import jax.numpy as jnp
from jax import lax
from jax.experimental import pallas as pl
from jax.experimental.pallas import tpu as pltpu
from jax.sharding import PartitionSpec as P

LEVELS = 6


first_scale = 1.0 / 7.5
rho_one = 1.0 / (2.0 * (5.0 / 3.0) - 0.6)
carry_coef = 0.6 * rho_one
fresh_coef = 2.0 * rho_one / (0.75 * 6.0)

LANES = 128
F32 = jnp.float32
AXES = (("gz", 0), ("gx", 1), ("gy", 2))


def extended(x, width):
    for axis, dim in AXES:
        peers, length = (lax.axis_size(axis), x.shape[dim + 1])
        up = [(i, (i + 1) % peers) for i in range(peers - 1)]
        down = [(j, i) for i, j in up]
        last = lax.slice_in_dim(x, length - width, length, axis=dim + 1)
        first = lax.slice_in_dim(x, 0, width, axis=dim + 1)
        before = lax.ppermute(last, axis, up)
        after = lax.ppermute(first, axis, down)
        x = jnp.concatenate([before, x, after], axis=dim + 1)
    return x


def stencil(values):
    padded = jnp.pad(values, 1)
    return valid_op(padded)


def valid_op(padded):
    beside = padded[2:, 1:-1, 1:-1] + padded[:-2, 1:-1, 1:-1]
    beside = beside + padded[1:-1, 2:, 1:-1] + padded[1:-1, :-2, 1:-1]
    beside = beside + padded[1:-1, 1:-1, 2:] + padded[1:-1, 1:-1, :-2]
    return 6.0 * padded[1:-1, 1:-1, 1:-1] - beside


def smooth_pass(iterate, source, apply_op, from_zero):
    residue = source if from_zero else source - apply_op(iterate)
    update = residue * first_scale
    iterate = update if from_zero else iterate + update
    residue = source - apply_op(iterate)
    update = carry_coef * update + fresh_coef * residue
    return iterate + update


def restrict(values):
    shape_a, shape_b, shape_c = values.shape
    blocks = values.reshape(shape_a // 2, 2, shape_b // 2, 2, shape_c // 2, 2)
    return 0.5 * jnp.sum(blocks, axis=(1, 3, 5))


def prolong(values):
    shape_a, shape_b, shape_c = values.shape
    spread = jnp.broadcast_to(
        values[:, None, :, None, :, None], (shape_a, 2, shape_b, 2, shape_c, 2)
    )
    return spread.reshape(2 * shape_a, 2 * shape_b, 2 * shape_c)


def vcycle(level_num, iterate, source):
    iterate = smooth_pass(iterate, source, stencil, True)
    coarsest = None
    if level_num < LEVELS - 1:
        residue = source - stencil(iterate)
        coarse, coarsest = vcycle(level_num + 1, None, restrict(residue))
        iterate = iterate + prolong(coarse)
    result = smooth_pass(iterate, source, stencil, False)
    if level_num == LEVELS - 1:
        coarsest = result
    return (result, coarsest)


def collect(values):
    gathered = lax.all_gather(values, "gz", axis=0, tiled=True)
    gathered = lax.all_gather(gathered, "gy", axis=2, tiled=True)
    return lax.all_gather(gathered, "gx", axis=1, tiled=True)


def local_stencil(values):
    return valid_op(extended(values[None], 1)[0])


def own_block(whole, block_shape):
    start_z = lax.axis_index("gz") * block_shape[0]
    start_x = lax.axis_index("gx") * block_shape[1]
    start_y = lax.axis_index("gy") * block_shape[2]
    return lax.dynamic_slice(whole, (start_z, start_x, start_y), block_shape)


def body_cycle(level_num, iterate, source, from_zero, gather_at):
    if level_num == gather_at:
        whole_source = collect(source)
        coarse, coarsest = vcycle(level_num, None, whole_source)
        return (own_block(coarse, source.shape), coarsest)
    iterate = smooth_pass(iterate, source, local_stencil, from_zero)
    residue = source - local_stencil(iterate)
    coarse, coarsest = body_cycle(level_num + 1, None, restrict(residue), True, gather_at)
    iterate = iterate + prolong(coarse)
    return (smooth_pass(iterate, source, local_stencil, False), coarsest)


def body_levels(divergence, pressure_prev):
    pressure, coarse_correction = body_cycle(0, pressure_prev, divergence, False, 3)
    residual = divergence - local_stencil(pressure)
    return (pressure, residual, coarse_correction)


def iota(shape, dim):
    return lax.broadcasted_iota(jnp.int32, shape, dim)


def signed(index, size, extent):
    return jnp.where(index >= (size + extent) // 2, index - extent, index)


def right_dot(values, table):
    rows = values.shape[0]
    terms = []
    for _ in range(3):
        term = values.astype(jnp.bfloat16)
        terms.append(term)
        values = values - term.astype(F32)
    out = jnp.dot(jnp.concatenate(terms, axis=0), table, preferred_element_type=F32)
    return out[0:rows] + out[rows:2 * rows] + out[2 * rows:3 * rows]


def right_dots(values, table):
    total = None
    for _ in range(3):
        term = values.astype(jnp.bfloat16)
        part = jnp.dot(term, table, preferred_element_type=F32)
        total = part if total is None else total + part
        values = values - term.astype(F32)
    return total


def as_table(keep, value=1.0):
    return jnp.where(keep, value, 0.0).astype(jnp.bfloat16)


def lateral(v):
    rows, lanes = v.shape
    return (
        pltpu.roll(v, 1, 0) + pltpu.roll(v, rows - 1, 0)
        + pltpu.roll(v, 1, 1) + pltpu.roll(v, lanes - 1, 1)
    )


def apply_at(ref, k, lateral_of=lateral):
    centre = ref[k]
    beside = lateral_of(centre)
    if k > 0:
        beside = beside + ref[k - 1]
    if k < ref.shape[0] - 1:
        beside = beside + ref[k + 1]
    return 6.0 * centre - beside


def padded(plan):
    return (plan.ey // LANES, plan.ez, plan.ex + 16, LANES)


def put(ref, k, v):
    rows = v.shape[0]
    for tile in range(ref.shape[0]):
        part = v[:, tile * LANES:(tile + 1) * LANES]
        ref[tile, k, 8:8 + rows, :] = part
        ref[tile, k, 7:8, :] = part[rows - 1:rows]
        ref[tile, k, 8 + rows:9 + rows, :] = part[0:1]


def rows_of(ref, k, first):
    here = pl.ds(first, ref.shape[2] - 16)
    return jnp.concatenate([ref[tile, k, here, :] for tile in range(ref.shape[0])], axis=1)


def apply_padded(ref, k, origin):
    centre = rows_of(ref, k, 8)
    lanes = centre.shape[1]
    beside = rows_of(ref, k, origin - 1) + rows_of(ref, k, origin + 1)
    beside = beside + (pltpu.roll(centre, 1, 1) + pltpu.roll(centre, lanes - 1, 1))
    if k > 0:
        beside = beside + rows_of(ref, k - 1, 8)
    if k < ref.shape[1] - 1:
        beside = beside + rows_of(ref, k + 1, 8)
    return 6.0 * centre - beside


def wrapped_mask(shape, sizes, low, high):
    keep = None
    for dim, size in sizes.items():
        at = signed(iota(shape, dim), size, shape[dim])
        good = ((at >= 0) | low[dim]) & ((at < size) | high[dim])
        keep = good if keep is None else keep & good
    return jnp.where(keep, 1.0, 0.0).astype(F32)


def side(index, flip):
    if flip == 1:
        return (index & 1) == 0, None
    return index < 2, (index == 1) | (index == 2)


def place(axis, count):
    index = lax.axis_index(axis)
    return index, index > 0, index < count - 1


def only(keep, v):
    return jnp.where(keep, v, 0.0)


def shifted(v, lanes):
    lanes = lanes % LANES
    return v if lanes == 0 else pltpu.roll(v, lanes, 1)


def lanes_of(v, first, count):
    lane = iota(v.shape, 1)
    last = first + count
    if last <= LANES:
        return (lane >= first) & (lane < last)
    return (lane >= first) | (lane < last - LANES)


def moved(v, first, count, to):
    first = first % LANES
    return shifted(only(lanes_of(v, first, count), v), to - first)


def landed(v, first, count, to):
    to = to % LANES
    v = shifted(v, to - first)
    return only(lanes_of(v, to, count), v)


def side_pack(tile, slot):
    return moved(tile, LANES - 3, 6, 6 * slot)


def side_unpack(packed, slot):
    return landed(packed, 6 * slot, 6, LANES - 3)


def slab_layers(r_ref, x_ref, up, low, high):
    start = jnp.where(up, high[0], low[0])
    start_x = jnp.where(up, high[1], low[1])
    return [(r_ref, start + j) for j in range(5)] + [(x_ref, start_x + j) for j in range(2)]


def slab_own(r_ref, x_ref, up):
    ez = r_ref.shape[0]
    return slab_layers(r_ref, x_ref, up, (0, 1), (ez - 5, ez - 3))


def slab_there(r_ref, x_ref, up):
    ez = r_ref.shape[0]
    return slab_layers(r_ref, x_ref, up, (1, 3), (ez - 6, ez - 5))


def slab_emit(r_ref, x_ref, out, up):
    ex = r_ref.shape[1]
    lat = None
    for j, (ref, k) in enumerate(slab_own(r_ref, x_ref, up)):
        v = ref[k]
        out[j * ex:(j + 1) * ex, :] = v[:, 0:LANES]
        part = side_pack(v[:, LANES:], j)
        lat = part if lat is None else lat + part
    out[7 * ex:8 * ex, :] = lat


def slab_add(r_ref, x_ref, slab, up):
    ex = r_ref.shape[1]
    lat = slab[7 * ex:8 * ex, :]
    for j, (ref, k) in enumerate(slab_there(r_ref, x_ref, up)):
        ref[k, :, 0:LANES] += slab[j * ex:(j + 1) * ex, :]
        ref[k, :, LANES:] += side_unpack(lat, j)


BESIDE = ((2, 2, 0, 0), (1, 1, 0, 3), (3, 1, 0, 5), (5, 1, 1, 0), (6, 1, 1, 3))


def beside(tile, count):
    row = iota(tile.shape, 0)
    return only((row < count) | (row >= 8 - count), tile)


def thin_emit(r_ref, x_ref, out, up):
    bx = r_ref.shape[1] - 8
    layers = slab_own(r_ref, x_ref, up)
    lat = None
    for j, (ref, k) in enumerate(layers):
        out[j * bx:(j + 1) * bx, :] = ref[k, 0:bx, 0:LANES]
        part = side_pack(ref[k, 0:bx, LANES:], j)
        lat = part if lat is None else lat + part
    tiles = [None, None]
    for j, count, which, turn in BESIDE:
        ref, k = layers[j]
        part = beside(ref[k, bx:, 0:LANES], count)
        part = pltpu.roll(part, turn, 0) if turn else part
        tiles[which] = part if tiles[which] is None else tiles[which] + part
    at = 7 * bx
    out[at:at + 8, :] = tiles[0]
    out[at + 8:at + 16, :] = tiles[1]
    out[at + 16:at + 24, :] = lat[0:8] + shifted(lat[8:16], LANES // 2)
    for j in (1, 2, 3):
        ref, k = layers[j]
        out[at + 16:at + 24, :] += side_pack(ref[k, bx:, LANES:], 6 + j)


def thin_add(r_ref, x_ref, slab, up):
    bx = r_ref.shape[1] - 8
    layers = slab_there(r_ref, x_ref, up)
    at = 7 * bx
    lat = slab[at + 16:at + 24, :]
    lat = jnp.concatenate([lat, shifted(lat, LANES // 2)], axis=0)
    for j, (ref, k) in enumerate(layers):
        ref[k, 0:bx, 0:LANES] += slab[j * bx:(j + 1) * bx, :]
        ref[k, 0:bx, LANES:] += side_unpack(lat, j)
    for j, count, which, turn in BESIDE:
        ref, k = layers[j]
        tile = slab[at + 8 * which:at + 8 * which + 8, :]
        tile = pltpu.roll(tile, 8 - turn, 0) if turn else tile
        ref[k, bx:, 0:LANES] += beside(tile, count)
    for j in (1, 2, 3):
        ref, k = layers[j]
        ref[k, bx:, LANES:] += side_unpack(lat[0:8], 6 + j)


def rows_out(r, x, up):
    bx = r.shape[0] - 8
    row = iota((8, r.shape[1]), 0)
    first, last, spill = r[0:8], r[bx - 8:bx], r[bx:]
    to_high = pltpu.roll(jnp.where(row >= 6, last, spill), 2, 0)
    to_low = pltpu.roll(jnp.where(row >= 5, spill, first), 3, 0)
    out = jnp.where(up, to_high, to_low)
    if x is None:
        return only(row < 5, out)
    spill = x[bx:]
    extra = jnp.where(up, pltpu.roll(spill, 5, 0), pltpu.roll(spill, 7, 0))
    return jnp.where(row < 5, out, only(row < 7, extra))


def rows_in(r_ref, x_ref, k, rows, up):
    bx = r_ref.shape[1] - 8
    row = iota(rows.shape, 0)
    high, low = pltpu.roll(rows, 5, 0), pltpu.roll(rows, 6, 0)
    r_ref[k, 0:8] += only(jnp.logical_not(up) & (row < 3), low)
    r_ref[k, bx - 8:bx] += only(up & (row >= 5), high)
    r_ref[k, bx:] += jnp.where(up, only(row < 2, high), only(row >= 6, low))
    if x_ref is not None:
        x_ref[k, 0:8] += only(jnp.logical_not(up) & (row < 2), pltpu.roll(rows, 3, 0))
        x_ref[k, bx - 8:bx] += only(up & (row >= 6), pltpu.roll(rows, 1, 0))


def rows_emit(r_ref, x_ref, out, up):
    ez = r_ref.shape[0]
    row = iota((8, LANES), 0)
    lat = jnp.zeros((8, LANES), F32)
    for t, k in enumerate(range(1, ez - 1)):
        far = {1: 0, ez - 2: ez - 1}.get(k)
        rows = rows_out(r_ref[k], None if far is not None else x_ref[k], up)
        tile = rows[:, 0:LANES]
        if far is not None:
            more = rows_out(r_ref[far, :, 0:LANES], None, up)
            more = jnp.where(up, pltpu.roll(more, 5, 0), pltpu.roll(more, 2, 0))
            tile = jnp.where((row == 5) | (row == 6), more, tile)
        out[8 * t:8 * t + 8, :] = tile
        lat = lat + side_pack(rows[:, LANES:], t)
    at = 8 * (ez - 2)
    out[at:at + 8, :] = lat


def rows_add(r_ref, x_ref, slab, up):
    ez = r_ref.shape[0]
    at = 8 * (ez - 2)
    lat = slab[at:at + 8, :]
    row = iota((8, LANES), 0)
    for t, k in enumerate(range(1, ez - 1)):
        far = {1: 0, ez - 2: ez - 1}.get(k)
        tile = slab[8 * t:8 * t + 8, :]
        rows = jnp.concatenate([tile, side_unpack(lat, t)], axis=1)
        rows_in(r_ref, None if far is not None else x_ref, k, rows, up)
        if far is not None:
            tile = only((row == 5) | (row == 6), tile)
            tile = jnp.where(up, pltpu.roll(tile, 6, 0), pltpu.roll(tile, 3, 0))
            rows = jnp.concatenate([tile, jnp.zeros((8, LANES), F32)], axis=1)
            rows_in(r_ref, None, far, rows, up)


class Plan:
    def first_layer(self, iz):
        start = iz * (self.block[0] // 2) - 4
        return jnp.clip(start, 0, self.level1[0] - self.window[0])

    def __init__(self, shape, peers):
        self.peers = peers
        self.block = bz, bx, by = shape
        self.ext = self.ez, self.ex, self.ey = bz + 6, bx + 8, by + LANES
        self.rows, self.pairs = bx // 2, bz // 4 + 2
        self.lat_at = self.pairs * (self.rows + 4)
        self.coarse = self.lat_at + 8
        self.slab = 8 * self.ex
        self.slab_z = 7 * bx + 24
        self.slab_x = 8 * (bz + 5)
        self.corner = 6 * 8
        self.layers = bz + 4
        self.level1 = (peers[0] * bz // 2, peers[1] * bx // 2, LANES)
        self.level2 = (peers[0] * bz // 4, peers[1] * bx // 4, peers[2] * by // 4)
        self.inner = [0, 1] + [2] * bz + [1, 0]
        self.slots, at = [], 0
        for count in self.inner:
            self.slots.append(at)
            at += 3 + count + (2 if count == 2 else 0)
        assert at <= LANES
        self.fine_rows = self.ex
        self.window = (bz // 2 + 8, self.level1[1], LANES)
        self.edge = self.fine_rows + self.window[0] * self.window[1] // 8
        self.wide2 = by // 4 + 4
        self.fold = LANES // self.wide2
        self.lines2 = -(-self.level2[0] // self.fold)
        self.share = self.lines2 * self.level2[1]


def first_kernel(plan, both, r_ref, x_ref, pay_z, pay_x, pay_d, d_one, d_two, pairs, lines):
    p_ext, b_ext = both.at[0], both.at[1]
    bz, bx, by = plan.block
    ez, ex, ey = plan.ext
    peers = plan.peers
    iz, z_low, z_high = place("gz", peers[0])
    ix, x_low, x_high = place("gx", peers[1])
    _, y_low, y_high = place("gy", peers[2])
    flat = wrapped_mask((ex, ey), {0: bx, 1: by}, (x_low, y_low), (x_high, y_high))
    below = jnp.where(z_low, 1.0, 0.0).astype(F32)
    above = jnp.where(z_high, 1.0, 0.0).astype(F32)

    def masked(k, v):
        v = v * flat
        if k < 3:
            v = v * below
        if k >= 3 + bz:
            v = v * above
        return v

    zero = jnp.zeros((ex, ey), F32)
    origin = 8 + (iz >> 8)
    for k in range(ez):
        if 2 <= k < ez - 2:
            r = b_ext[k] - apply_at(p_ext, k)
            r_ref[k] = r
            put(d_one, k, masked(k, r * first_scale))
        elif 1 <= k < ez - 1:
            put(d_one, k, zero)
    for k in range(ez):
        if 1 <= k < ez - 1:
            if 2 <= k < ez - 2:
                r = r_ref[k] - apply_padded(d_one, k, origin)
                d = carry_coef * rows_of(d_one, k, 8) + fresh_coef * r
            else:
                inward = k + 1 if k == 1 else k - 1
                r = rows_of(d_one, inward, 8)
                d = fresh_coef * r
            r_ref[k] = r
            put(d_two, k, masked(k, d))
    for k in range(ez):
        if 1 <= k < ez - 1:
            part = rows_of(d_two, k, 8)
            beside = rows_of(d_two, k, origin - 1) + rows_of(d_two, k, origin + 1)
            beside = beside + (pltpu.roll(part, 1, 1) + pltpu.roll(part, ey - 1, 1))
            if k > 1:
                beside = beside + rows_of(d_two, k - 1, 8)
            if k < ez - 2:
                beside = beside + rows_of(d_two, k + 1, 8)
            r_ref[k] = masked(k, r_ref[k] - (6.0 * part - beside))
            x_ref[k] = p_ext[k] + (rows_of(d_one, k, 8) + part)
        else:
            r_ref[k] = masked(k, rows_of(d_two, 1 if k == 0 else ez - 2, 8))
            x_ref[k] = zero

    coarse_z, rows = 2 * plan.pairs, plan.rows
    for zc in range(coarse_z):
        low, high = 2 * zc - 1, 2 * zc
        if low < 0:
            total = r_ref[high]
        elif high >= ez:
            total = r_ref[low]
        else:
            total = r_ref[low] + r_ref[high]
        base = zc * ex
        for tile in range(ey // LANES):
            here = slice(tile * LANES, (tile + 1) * LANES)
            pairs[tile, base:base + ex, :] = total[:, here]
            even = pairs.at[tile][pl.ds(base, ex // 2, 2), :]
            odd = pairs.at[tile][pl.ds(base + 1, ex // 2, 2), :]
            sums = even + odd
            at = zc // 2 * rows
            at += zc % 2 * plan.lat_at
            lines[at:at + rows, here] = sums[0:rows]
            at = plan.pairs * rows + zc // 2 * 4 + zc % 2 * plan.lat_at
            lines[at:at + 4, here] = sums[rows:rows + 4]
    fine = signed(iota((ey, LANES), 0), by, ey)
    coarse = signed(iota((ey, LANES), 1), by // 2, LANES)
    table = as_table((fine >> 1) == coarse, 0.5)
    out = right_dot(lines[...], table)
    even, odd = out[0:plan.lat_at], out[plan.lat_at:]
    lane = iota(even.shape, 1)
    main = jnp.where(lane < LANES // 2, even, shifted(odd, LANES // 2))
    own_lat = spill_lat = None
    row = iota((8, LANES), 0)
    for zc in range(coarse_z):
        source = (even, odd)[zc % 2]
        base = zc // 2 * rows
        tile = source[base:base + rows]
        part = moved(tile, by // 2, 2, 4 * zc) + moved(tile, LANES - 2, 2, 4 * zc + 2)
        own_lat = part if own_lat is None else own_lat + part
        base = plan.pairs * rows + zc // 4 * 8
        tile = source[base:base + 8]
        if zc // 2 % 2:
            tile = pltpu.roll(tile, 4, 0)
        tile = only(row < 4, tile)
        slot = LANES // 2 + 4 * zc
        part = moved(tile, by // 2, 2, slot) + moved(tile, LANES - 2, 2, slot + 2)
        spill_lat = part if spill_lat is None else spill_lat + part
    for pay, at in ((pay_z, plan.slab_z), (pay_x, plan.slab_x), (pay_d, plan.corner)):
        pay[at:at + plan.lat_at, :] = main
        pay[at + plan.lat_at:at + plan.coarse, :] = own_lat + spill_lat

    up_z, _ = side(iz, 3)
    up_x, _ = side(ix, 1)
    thin_emit(r_ref, x_ref, pay_z, up_z)
    rows_emit(r_ref, x_ref, pay_x, up_x)
    lat = jnp.zeros((8, LANES), F32)
    start = jnp.where(up_z, ez - 5, 0)
    for j in range(5):
        out = rows_out(r_ref[start + j], x_ref[start + j] if j == 2 else None, up_x)
        pay_d[8 * j:8 * j + 8, :] = out[:, 0:LANES]
        lat = lat + side_pack(out[:, LANES:], j)
    pay_d[40:48, :] = lat


def chip_kernel(plan, r_in, x_in, from_z, from_x, from_d, r_ref, x_ref, pay):
    ez, ex, ey = plan.ext
    iz, _, _ = place("gz", plan.peers[0])
    ix, _, _ = place("gx", plan.peers[1])
    up_z, near = side(iz, 3)
    up_x, _ = side(ix, 1)
    for k in range(ez):
        r_ref[k] = r_in[k]
        x_ref[k] = x_in[k]
    rows_add(r_ref, x_ref, from_x, up_x)

    @pl.when(near)
    def _():
        thin_add(r_ref, x_ref, from_z, up_z)
        start = jnp.where(up_z, ez - 6, 1)
        lat = from_d[40:48, :]
        for j in range(5):
            rows = from_d[8 * j:8 * j + 8, :]
            rows = jnp.concatenate([rows, side_unpack(lat, j)], axis=1)
            rows_in(r_ref, x_ref if j == 2 else None, start + j, rows, up_x)

    slab_emit(r_ref, x_ref, pay, side(iz, 1)[0])


def plane_kernel(plan, r_in, x_in, ours, theirs, r_ref, x_ref, r1_ref, x1_ref, pay, later, share,
                 r_all, x_all, b1, d1, d2, r1, x1, pairs, lines):
    bz, bx, by = plan.block
    ez, ex, ey = plan.ext
    layers = plan.layers
    iz, _, _ = place("gz", plan.peers[0])
    ix, _, _ = place("gx", plan.peers[1])
    iy, y_low, y_high = place("gy", plan.peers[2])
    up_z, _ = side(iz, 1)
    for k in range(ez):
        r_all[k] = r_in[k]
        x_all[k] = x_in[k]
    slab_add(r_all, x_all, theirs, up_z)
    for k in range(layers):
        r_ref[k] = r_all[k + 1]
    for k in range(bz):
        x_ref[k] = x_all[k + 3, 0:bx, 0:by]

    up, _ = side(iy, 1)
    up_inner, _ = side(iy, 3)
    high, low = jnp.zeros((ex, LANES), F32), jnp.zeros((ex, LANES), F32)
    for k in range(layers):
        slot, inner = plan.slots[k], plan.inner[k]
        count = 3 + inner
        v, spill = r_all[k + 1, :, 0:by], r_all[k + 1, :, by:ey]
        high = high + moved(jnp.where(lanes_of(v, 0, 3), spill, v), LANES - inner, count, slot)
        mixed = jnp.where(lanes_of(v, 0, 2), v, spill)
        low = low + moved(mixed, LANES - 3, count, slot)
        if inner == 2:
            spill = x_all[k + 1, :, by:ey]
            high = high + moved(spill, 0, 2, slot + count)
            low = low + moved(spill, LANES - 2, 2, slot + count)
    pay[0:ex, :] = jnp.where(up, high, low)
    later[0:ex, :] = jnp.where(up_inner, high, low)

    nz1, nx1, _ = plan.level1
    rows, half = plan.rows, by // 2
    for k in range(nz1):
        b1[k] = jnp.zeros((nx1, LANES), F32)
    row = iota((8, LANES), 0)
    for j in range(plan.peers[0]):
        for i in range(plan.peers[1]):
            flip = iz ^ j
            other = ((flip ^ (flip >> 1)) & 1) == 1
            chip = (flip >> 1) + 2 * (ix ^ i)
            at = pl.multiple_of(plan.slab + chip * plan.coarse, 8)

            def rows_at(offset, count):
                here = pl.ds(pl.multiple_of(at + offset, 8), count)
                return jnp.where(other, theirs[here, :], ours[here, :])

            lat = rows_at(plan.lat_at, 8)
            for zp in range(plan.pairs):
                own = rows_at(zp * rows, rows)
                if zp % 2 == 0:
                    spill_two = rows_at(plan.pairs * rows + zp * 4, 8)
                spill = spill_two if zp % 2 == 0 else pltpu.roll(spill_two, 4, 0)
                for part in range(2):
                    zc = 2 * zp + part
                    k = j * (bz // 2) + zc - 2
                    if not 0 <= k < nz1:
                        continue

                    def wide(main, slot):
                        return (
                            landed(main, part * half, half, 0)
                            + landed(lat, slot, 2, half) + landed(lat, slot + 2, 2, LANES - 2)
                        )

                    b1[k, i * rows:(i + 1) * rows, :] += wide(own, 4 * zc)
                    v = wide(spill, LANES // 2 + 4 * zc)
                    if i + 1 < plan.peers[1]:
                        at_row = (i + 1) * rows
                        b1[k, at_row:at_row + 8, :] += only(row < 2, v)
                    if i > 0:
                        at_row = i * rows - 8
                        b1[k, at_row:at_row + 8, :] += only(row >= 6, pltpu.roll(v, 4, 0))

    lateral1 = level_lateral((nx1, LANES))
    keep = wrapped_mask((nx1, LANES), {1: half}, (None, y_low), (None, y_high))
    for k in range(nz1):
        d1[k] = b1[k] * first_scale
    for k in range(nz1):
        r = b1[k] - apply_at(d1, k, lateral1)
        r1[k] = r
        d2[k] = keep * (carry_coef * d1[k] + fresh_coef * r)
    for k in range(nz1):
        r1[k] = keep * (r1[k] - apply_at(d2, k, lateral1))
        x1[k] = d1[k] + d2[k]

    nz2, nx2, _ = plan.level2
    for zc in range(nz2):
        pairs[zc * nx1:(zc + 1) * nx1, :] = r1[2 * zc] + r1[2 * zc + 1]
        part, at = divmod(zc, plan.lines2)
        lines[at * nx2:(at + 1) * nx2, part * LANES:(part + 1) * LANES] = (
            pairs[pl.ds(zc * nx1, nx2, 2), :] + pairs[pl.ds(zc * nx1 + 1, nx2, 2), :]
        )
    shape = (plan.fold * LANES, LANES)
    fine, coarse = iota(shape, 0), iota(shape, 1)
    part, fine = fine // LANES, signed(fine % LANES, half, LANES)
    coarse = coarse - part * plan.wide2 - 2
    near = (coarse >= -2) & (coarse < plan.wide2 - 2)
    for part in range(plan.fold):
        count = min(plan.lines2, nz2 - part * plan.lines2) * nx2
        if count < plan.share:
            here = slice(part * LANES, (part + 1) * LANES)
            lines[count:, here] = jnp.zeros((plan.share - count, LANES), F32)
    total = right_dot(lines[...], as_table(near & ((fine >> 1) == coarse), 0.5))
    share[...] = total
    pay[plan.edge:plan.edge + plan.share, :] = total
    later[plan.edge:plan.edge + plan.share, :] = total

    start = plan.first_layer(iz)
    for k in range(plan.window[0]):
        r1_ref[k] = r1[start + k]
        x1_ref[k] = x1[start + k]
    per_tile = LANES // 16
    for group in range(plan.window[0] // per_tile):
        tiles = []
        for which in range(2):
            total = jnp.zeros((nx1, LANES), F32)
            for j in range(per_tile):
                k = group * per_tile + j
                first = half - 3 if which == 0 else LANES - 4
                total = total + moved(r1_ref[k], first, 7, 16 * j)
                first = half - 2 if which == 0 else LANES - 3
                total = total + moved(x1_ref[k], first, 5, 16 * j + 7)
            tiles.append(total)
        here = slice(plan.fine_rows + group * nx1, plan.fine_rows + (group + 1) * nx1)
        pay[here, :] = jnp.where(up, tiles[0], tiles[1])
        later[here, :] = jnp.where(up_inner, tiles[0], tiles[1])


def level_lateral(shape):
    row = iota(shape, 0)
    not_first = jnp.where(row > 0, 1.0, 0.0).astype(F32)
    not_last = jnp.where(row < shape[0] - 1, 1.0, 0.0).astype(F32)

    def beside(v):
        return (
            not_first * pltpu.roll(v, 1, 0) + not_last * pltpu.roll(v, shape[0] - 1, 0)
            + pltpu.roll(v, 1, 1) + pltpu.roll(v, LANES - 1, 1)
        )

    return beside


def line_cycle(source, step):
    lane = iota((8, LANES), 1)
    count = len(source)

    def inside(s, v):
        if s == 0:
            return v
        return only(lane < LANES - s * step if s > 0 else lane >= -s * step, v)

    def op(v, width):
        out = {}
        for s in range(-width, width + 1):
            out[s] = []
            for k in range(count):
                beside = v[s - 1][k] + v[s + 1][k]
                if k > 0:
                    beside = beside + v[s][k - 1]
                if k < count - 1:
                    beside = beside + v[s][k + 1]
                out[s].append(inside(s, 6.0 * v[s][k] - beside))
        return out

    def mix(width, *terms):
        return {
            s: [sum(c * v[s][k] for c, v in terms) for k in range(count)]
            for s in range(-width, width + 1)
        }

    b = {s: [inside(s, shifted(v, -s * step)) for v in source] for s in range(-3, 4)}
    d = mix(3, (first_scale, b))
    r = mix(2, (1.0, b), (-1.0, op(d, 2)))
    d2 = mix(2, (carry_coef, d), (fresh_coef, r))
    x = mix(0, (1.0, d), (1.0, d2))
    r = mix(1, (1.0, r), (-1.0, op(d2, 1)))
    d = mix(1, (first_scale, r))
    r = mix(0, (1.0, r), (-1.0, op(d, 0)))
    x = mix(0, (1.0, x), (1.0 + carry_coef, d), (fresh_coef, r))[0]
    return x, x


def small_cycle(level, source):
    step = 1 << (level - 2)
    row, lane = iota((8, LANES), 0), iota((8, LANES), 1)
    count = len(source)
    if level == LEVELS - 1 and step >= 8:
        return line_cycle(source, step)
    shifts = []
    if step < 8:
        shifts += [(step, 0, row >= step), (8 - step, 0, row < 8 - step)]
    shifts += [(step, 1, lane >= step), (LANES - step, 1, lane < LANES - step)]

    def op(v):
        out = []
        for k in range(count):
            beside = None
            for shift, dim, keep in shifts:
                part = only(keep, pltpu.roll(v[k], shift, dim))
                beside = part if beside is None else beside + part
            if k > 0:
                beside = beside + v[k - 1]
            if k < count - 1:
                beside = beside + v[k + 1]
            out.append(6.0 * v[k] - beside)
        return out

    def moves(v, dim, places):
        size, shift = v.shape[dim], places * step
        if abs(shift) >= size:
            return jnp.zeros_like(v)
        index = row if dim == 0 else lane
        keep = index < size - shift if shift > 0 else index >= -shift
        return only(keep, pltpu.roll(v, -shift % size, dim))

    def at(values, k):
        return values[k] if 0 <= k < len(values) else None

    def added(*terms):
        total = None
        for term in terms:
            if term is not None:
                total = term if total is None else total + term
        return total

    d = [first_scale * v for v in source]
    before = [b - t for b, t in zip(source, op(d))]
    d2 = [carry_coef * v + fresh_coef * t for v, t in zip(d, before)]
    x = [v + t for v, t in zip(d, d2)]
    r = [v - t for v, t in zip(before, op(d2))]
    coarsest = None
    if level < LEVELS - 1:
        keep = only((row % (2 * step) == 0) & (lane % (2 * step) == 0), 0.5)
        coarse = []
        for k in range(0, count, 2):
            v = d2[k] + d2[k + 1]
            beyond = added(at(d2, k - 1), at(d2, k + 2))
            rest = before[k] + before[k + 1] - 5.0 * v
            rest = rest if beyond is None else rest + beyond
            along = [
                v + moves(v, dim, 1) + (moves(v, dim, -1) + moves(v, dim, 2)) for dim in range(2)
            ]
            first = rest + moves(rest, 0, 1) + along[0]
            coarse.append(keep * (
                first + moves(first, 1, 1) + (along[1] + moves(along[1], 0, 1))
            ))
        coarse, coarsest = small_cycle(level + 1, coarse)
        e, beside = [], []
        for v in coarse:
            back = [moves(v, dim, -1) for dim in range(2)]
            wide = v + back[0]
            e.append(wide + moves(wide, 1, -1))
            along = [
                v + back[dim] + (moves(v, dim, 1) + moves(v, dim, -2)) for dim in range(2)
            ]
            beside.append(
                along[0] + moves(along[0], 1, -1) + (along[1] + moves(along[1], 0, -1))
            )
        for k in range(count):
            own = e[k // 2]
            change = 5.0 * own - beside[k // 2]
            beyond = at(e, k // 2 + (1 if k % 2 else -1))
            if beyond is not None:
                change = change - beyond
            x[k] = x[k] + own
            r[k] = r[k] - change
    d = [first_scale * v for v in r]
    r = [v - t for v, t in zip(r, op(d))]
    x = [v + (t + (carry_coef * t + fresh_coef * u)) for v, t, u in zip(x, d, r)]
    return x, (x if level == LEVELS - 1 else coarsest)


def last_kernel(plan, r_in, x_in, r1_in, x1_in, ours, from_a, from_b, from_c, p_out, res_out, last_ref, *scratch):
    shares, p_ref, res_ref, r, q1, e1, e0, d0, d1, r1, lines, wide, sem = scratch
    bz, bx, by = plan.block
    ez, ex, ey = plan.ext
    nz1, nx1, _ = plan.window
    nz2, nx2, _ = plan.level2
    layers, half = plan.layers, by // 2
    iz, z_low, z_high = place("gz", plan.peers[0])
    ix, x_low, x_high = place("gx", plan.peers[1])
    iy, y_low, y_high = place("gy", plan.peers[2])

    shares[0] = ours[...]
    shares[1] = from_a[plan.edge:plan.edge + plan.share, :]
    shares[3] = from_b[plan.edge:plan.edge + plan.share, :]
    shares[2] = from_c[...]
    own2 = half // 2
    source = []
    for part in range(plan.fold):
        total = None
        for j in range(plan.peers[2]):
            v = moved(shares[iy ^ j], part * plan.wide2, plan.wide2, own2 * j - 2)
            total = v if total is None else total + v
        source += [total[nx2 * k:nx2 * (k + 1)] for k in range(plan.lines2)]
    source = source[:nz2]
    e2, coarsest = small_cycle(2, source)
    for k in range(nz2):
        lines[k * nx2:(k + 1) * nx2, :] = e2[k]
    thin = as_table(iota((LANES, LANES), 0) == 8 * iota((LANES, LANES), 1))
    for k in range(last_ref.shape[0]):
        last_ref[k] = right_dot(coarsest[k], thin)[0:1, 0:last_ref.shape[2]]

    up_a, _ = side(iy, 1)
    _, near_b = side(iy, 3)

    def sent(rows):
        a, b = from_a[rows[0]:rows[1], :], only(near_b, from_b[rows[0]:rows[1], :])
        return jnp.where(up_a, a, b), jnp.where(up_a, b, a)

    fine = signed(iota((LANES, LANES), 1), half, LANES)
    coarse = iota((LANES, LANES), 0) - iy * own2
    start = plan.first_layer(iz)
    here = pl.ds(pl.multiple_of(start // 2 * nx2, 8), nz1 // 2 * nx2)
    e2 = right_dot(lines[here, :], as_table((fine >> 1) == coarse))
    for zc in range(nz1 // 2):
        v = e2[zc * nx2:(zc + 1) * nx2]
        for part in range(2):
            q1.at[2 * zc + part][pl.ds(0, nx2, 2), :] = v
            q1.at[2 * zc + part][pl.ds(1, nx2, 2), :] = v
    per_tile = LANES // 16
    lateral1 = level_lateral((nx1, LANES))
    keep = wrapped_mask((nx1, LANES), {1: half}, (None, y_low), (None, y_high))
    for group in range(nz1 // per_tile):
        at = plan.fine_rows + group * nx1
        high, low = sent((at, at + nx1))
        for j in range(per_tile):
            k = group * per_tile + j
            s = 16 * j
            r1[k] = (
                r1_in[k] + landed(high, s, 7, half - 4) + landed(low, s, 7, LANES - 3)
                - apply_at(q1, k, lateral1)
            )
            e1[k + 2, 8:8 + nx1, :] = (
                x1_in[k] + q1[k]
                + landed(high, s + 7, 5, half - 3) + landed(low, s + 7, 5, LANES - 2)
            )
    for k in range(nz1):
        d1[k] = keep * (r1[k] * first_scale)
    nothing = jnp.zeros((8, LANES), F32)
    for k in range(nz1 + 4):
        e1[k, 0:8, :] = nothing
        e1[k, 8 + nx1:16 + nx1, :] = nothing
        if not 2 <= k < nz1 + 2:
            e1[k, 8:8 + nx1, :] = jnp.zeros((nx1, LANES), F32)
    for k in range(nz1):
        v = r1[k] - apply_at(d1, k, lateral1)
        e1[k + 2, 8:8 + nx1, :] += d1[k] + keep * (carry_coef * d1[k] + fresh_coef * v)

    coarse = signed(iota((LANES, ey), 0), half, LANES)
    fine = signed(iota((LANES, ey), 1), by, ey)
    double = as_table((fine >> 1) == coarse)
    half_z, half_x = bz // 2, bx // 2
    for zc in range(half_z + 4):
        here = pl.ds(pl.multiple_of(ix * half_x, 8), half_x + 16)
        v = e1[iz * half_z - start + zc, here, :]
        own, low, high = v[8:8 + half_x], v[0:8], v[8 + half_x:16 + half_x]
        at = zc * ex
        wide[pl.ds(at, half_x, 2), :] = own
        wide[pl.ds(at + 1, half_x, 2), :] = own
        for j in range(2):
            for twin in range(2):
                row = at + bx + 2 * j + twin
                wide[row:row + 1, :] = high[j:j + 1]
                row = at + ex - 4 + 2 * j + twin
                wide[row:row + 1, :] = low[6 + j:7 + j]
    origin = 8 + (iz >> 8)
    for zc in range(half_z + 4):
        v = right_dots(wide[zc * ex:(zc + 1) * ex, :], double)
        for k in (2 * zc - 1, 2 * zc):
            if 0 <= k < ez:
                put(e0, k, v)
    flat = wrapped_mask((ex, ey), {0: bx, 1: by}, (x_low, y_low), (x_high, y_high))
    below = jnp.where(z_low, 1.0, 0.0).astype(F32)
    above = jnp.where(z_high, 1.0, 0.0).astype(F32)

    def masked(k, v):
        v = v * flat
        if k < 3:
            v = v * below
        if k >= 3 + bz:
            v = v * above
        return v

    high, low = sent((0, ex))
    for k in range(layers):
        s, inner = plan.slots[k], plan.inner[k]
        v = r_in[k] - apply_padded(e0, k + 1, origin)
        own = v[:, 0:by] + landed(high, s, 3, LANES - 3) + landed(low, s + inner, 3, 0)
        spill = v[:, by:ey]
        if inner:
            spill = spill + landed(high, s + 3, inner, 0) + landed(low, s, inner, LANES - inner)
        r[k, :, 0:by] = own
        r[k, :, by:ey] = spill
        put(d0, k, masked(k + 1, r[k] * first_scale))
        if inner == 2:
            s = s + 3 + inner
            p_ref[k - 2] = (
                x_in[k - 2] + e0[0, k + 1, 8:8 + bx, :]
                + (landed(high, s, 2, LANES - 2) + landed(low, s, 2, 0))[0:bx]
            )
    for k in range(1, layers - 1):
        v = r[k] - apply_padded(d0, k, origin)
        r[k] = v
        d = rows_of(d0, k, 8)
        v = masked(k + 1, carry_coef * d + fresh_coef * v)
        put(e0, k, v)
        if 2 <= k < 2 + bz:
            p_ref[k - 2] += d[0:bx, 0:by] + v[0:bx, 0:by]
    copy = pltpu.make_async_copy(p_ref, p_out, sem.at[0])
    copy.start()
    copies = [copy]
    parts = 2
    for part in range(parts):
        here = range(part * bz // parts, (part + 1) * bz // parts)
        for j in here:
            v = r[j + 2] - apply_padded(e0, j + 2, origin)
            res_ref[j] = v[0:bx, 0:by]
        here = pl.ds(here[0], bz // parts)
        copy = pltpu.make_async_copy(res_ref.at[here], res_out.at[here], sem.at[1 + part])
        copy.start()
        copies.append(copy)
    for copy in copies:
        copy.wait()


def whole(shape):
    return jax.ShapeDtypeStruct(shape, F32)


VMEM = pl.BlockSpec(memory_space=pltpu.VMEM)
ANY = pl.BlockSpec(memory_space=pl.ANY)
VMEM_BYTES = 24 << 20


def run(kernel, plan, outs, scratch, *operands, out_specs=None, semaphores=0):
    scratch = [pltpu.VMEM(s, F32) for s in scratch]
    if semaphores:
        scratch.append(pltpu.SemaphoreType.DMA((semaphores,)))
    return pl.pallas_call(
        functools.partial(kernel, plan),
        out_shape=[whole(s) for s in outs],
        in_specs=[VMEM] * len(operands),
        out_specs=out_specs or [VMEM] * len(outs),
        scratch_shapes=scratch,
        compiler_params=pltpu.CompilerParams(vmem_limit_bytes=VMEM_BYTES),
    )(*operands)


def swap(values, partner):
    axes = ("gx", "gy", "gz")
    counts = [lax.axis_size(a) for a in axes]
    pairs = []
    for i in range(counts[0] * counts[1] * counts[2]):
        to = partner(i // (counts[1] * counts[2]), i // counts[2] % counts[1], i % counts[2])
        if to is not None:
            pairs.append((i, (to[0] * counts[1] + to[1]) * counts[2] + to[2]))
    return lax.ppermute(values, axes, pairs)


def body_fast(divergence, pressure_prev):
    plan = Plan(divergence.shape, tuple(lax.axis_size(a) for a in ("gz", "gx", "gy")))
    ext, level1 = plan.ext, plan.level1
    window, layers = plan.window, (plan.layers, plan.ex, plan.ey)
    payload = [(n + plan.coarse, LANES) for n in (plan.slab_z, plan.slab_x, plan.corner)]
    both = jnp.stack([pressure_prev, divergence])
    both = jnp.pad(both, ((0, 0), (3, 3), (0, plan.ex - plan.block[1]), (0, plan.ey - plan.block[2])))
    r, x, pay_z, pay_x, pay_d = run(
        first_kernel, plan, [ext, ext] + payload,
        [padded(plan), padded(plan), (2, 2 * plan.pairs * plan.ex, LANES),
         (2 * plan.lat_at, plan.ey)],
        both,
    )
    from_z = swap(pay_z, lambda x, y, z: (x, y, z ^ 3))
    from_x = swap(pay_x, lambda x, y, z: (x ^ 1, y, z))
    from_d = swap(pay_d, lambda x, y, z: (x ^ 1, y, z ^ 3))
    r, x, slab = run(
        chip_kernel, plan, [ext, ext, (plan.slab, LANES)], [], r, x, from_z, from_x, from_d
    )
    ours = jnp.concatenate([
        slab, pay_z[plan.slab_z:], from_z[plan.slab_z:], from_x[plan.slab_x:], from_d[plan.corner:]
    ], axis=0)
    got = swap(ours, lambda x, y, z: (x, y, z ^ 1))
    nz2, nx2, _ = plan.level2
    share = (plan.share, LANES)
    r, x, r1, x1, now, later, ours = run(
        plane_kernel, plan,
        [layers, plan.block, window, window, (plan.edge + plan.share, LANES),
         (plan.edge + plan.share, LANES), share],
        [ext, ext, level1, level1, level1, level1, level1, (nz2 * level1[1], LANES),
         (plan.share, plan.fold * LANES)],
        r, x, ours, got,
    )
    from_a = swap(now, lambda x, y, z: (x, y ^ 1, z))
    from_b = swap(later, lambda x, y, z: (x, y ^ 3, z))
    from_c = swap(ours, lambda x, y, z: (x, y ^ 2, z))
    return run(
        last_kernel, plan,
        [plan.block, plan.block, tuple(n >> 3 for n in plan.level2)],
        [(4,) + share, plan.block, plan.block, layers, window,
         (window[0] + 4, window[1] + 16, LANES), padded(plan), padded(plan), window, window,
         (nz2 * nx2, LANES), (2 * plan.pairs * plan.ex, LANES)],
        r, x, r1, x1, ours, from_a, from_b, from_c,
        out_specs=[ANY, ANY, VMEM], semaphores=3,
    )


def fits_fast(shape, peers):
    bz, bx, by = shape
    nz, nx, ny = peers
    return (
        nz == 4 and nx == 2 and ny == 4 and bz == 16 and by == LANES
        and nx * bx == 4 * 8 and ny * by == 4 * LANES
    )


def body(divergence, pressure_prev):
    peers = tuple(lax.axis_size(a) for a in ("gz", "gx", "gy"))
    if fits_fast(divergence.shape, peers):
        return tuple(body_fast(divergence, pressure_prev))
    return body_levels(divergence, pressure_prev)


def solution(mesh):
    in_specs = (P("gz", "gx", "gy"), P("gz", "gx", "gy"))
    out_specs = (P("gz", "gx", "gy"), P("gz", "gx", "gy"), P())
    return jax.shard_map(body, mesh=mesh, in_specs=in_specs, out_specs=out_specs, check_vma=False)
```
